32 devices in a mesh: bucket: 4 (over x, core), blk: 8 (over z, y).
Axes of the slice: x: 2, y: 2, z: 4, core: 2. Of those that a mesh axis runs over, the one named last changes fastest.
Arguments:
- tokens: bfloat16 [4, 1024, 2, 2048], P('bucket', 'blk'), may hold values from -6 to 6
- lengths: int32 [4, 2], P('bucket'), may hold values from 256 to 1024, as said below
- norm_gain: float32 [2048], P(('bucket', 'blk')), may hold values from 0.5 to 1.5
- norm_shift: float32 [2048], P(('bucket', 'blk')), may hold values from -4 to 4
- inward_weight: float32 [2048, 6144], P(('bucket', 'blk')), may hold values from -0.1875 to 0.1875
- inward_bias: float32 [4608], P(('bucket', 'blk')), may hold values from -0.3125 to 0.3125
- outward_weight: float32 [2048, 2048], P(('bucket', 'blk')), may hold values from -2 to 2
- gate_up_weight: float32 [2048, 11264], P(('bucket', 'blk')), may hold values from -0.125 to 0.125
- down_weight: float32 [5632, 2048], P(('bucket', 'blk')), may hold values from -0.078125 to 0.078125
- cotangent: bfloat16 [4, 1024, 2, 2048], P('bucket', 'blk'), may hold values from -6 to 6
Outputs:
- layer_out: bfloat16 [4, 1024, 2, 2048], P('bucket', 'blk')
- tokens_grad: bfloat16 [4, 1024, 2, 2048], P('bucket', 'blk')
- gain_grad: float32 [2048], P(('bucket', 'blk'))
- shift_grad: float32 [2048], P(('bucket', 'blk'))
- inward_grad: float32 [2048, 6144], P(('bucket', 'blk'))
- bias_grad: float32 [4608], P(('bucket', 'blk'))
- outward_grad: float32 [2048, 2048], P(('bucket', 'blk'))
- gate_up_grad: float32 [2048, 11264], P(('bucket', 'blk'))
- down_grad: float32 [5632, 2048], P(('bucket', 'blk'))
The draws below stay inside these ranges and needn't reach their ends.
Inputs may be any that keep to these rules, and one draw needn't show every extreme that they name: In every bucket one sequence, which one drawn from the seed, is exactly 1024 tokens long; the other lengths lean toward the short end. Positions at or past a sequence's length are padding.
All inputs are finite; a program needn't handle non-finite values.
Results may differ from the reference program's by a relative error of at most 0.014.
The reference program's roundings to bfloat16 on the way count: a program that leaves them out, or rounds other values in their place, can miss the bound.
Values may be sent and summed in bfloat16 or wider, within the bound.
A program may use at most 512 MiB of HBM per device.

```python
import jax
import jax.numpy as jnp
from jax import lax

D = 2048
HEADS = 32
HEAD_DIM = 64
ROT = 16
FF = 5632
GROUP = 128
SEQS = 2
LEN = 1024
BUCKETS = 4


def draw_lengths(key, part):
    key = jax.random.fold_in(key, 11)
    first_key, second_key, third_key = jax.random.split(key, 3)
    lowest = LEN // 4
    cubed_draw = jax.random.randint(first_key, (BUCKETS, SEQS), 0, 64)
    jitter = jax.random.randint(second_key, (BUCKETS, SEQS), 0, GROUP)
    spread = lowest + (LEN - lowest) * cubed_draw * cubed_draw * cubed_draw // 262144 + jitter
    spread = jnp.minimum(spread, LEN)
    longest = jax.random.randint(third_key, (BUCKETS, 1), 0, SEQS)
    chosen = jnp.arange(SEQS)[None, :] == longest
    return jnp.where(chosen, LEN, spread).astype(jnp.int32)


def steps_of(key, shape, cuts, low, largest):
    gain = 1.0
    for axis_at, shards_of in cuts:
        heights = jax.random.uniform(jax.random.fold_in(jax.random.fold_in(key, 6), axis_at), (shards_of,), jnp.float32, low / len(cuts), largest / len(cuts))
        gain = gain * jnp.repeat(jnp.exp(heights), shape[axis_at] // shards_of).reshape((-1,) + (1,) * (len(shape) - 1 - axis_at))
    return gain


def noise(own_key, dims, width, bound, pieces=(), kind=jnp.bfloat16):
    entries = jax.random.normal(own_key, dims, jnp.float32) * width
    if len(pieces) > 0:
        entries = steps_of(own_key, dims, pieces, -0.22, 0.18) * entries
    return jnp.clip(entries, min=-bound, max=bound).astype(kind)


def setup_inputs(seed: int = 0) -> dict:
    key_of = jax.random.split(jax.random.key(seed), 11)
    return {
        "tokens": noise(key_of[0], (BUCKETS, LEN, SEQS, D), 1.0, 6.0, ((0, 4), (1, 8))),
        "lengths": draw_lengths(jax.random.fold_in(key_of[10], 71), 0),
        "norm_gain": jnp.clip(1.0 + 0.1 * jax.random.normal(key_of[2], (D,), jnp.float32), 0.5, 1.5),
        "norm_shift": noise(key_of[3], (D,), 0.3, 4.0, ((0, 32),), jnp.float32),
        "inward_weight": noise(key_of[4], (D, 3 * D), (D // 2) ** -0.5, 0.1875, ((0, 32),), jnp.float32),
        "inward_bias": noise(key_of[5], (2 * D + HEADS * ROT,), 0.02, 0.3125, ((0, 32),), jnp.float32),
        "outward_weight": noise(key_of[6], (D, D), (max(D // 256, 1)) ** -0.5, 2.0, ((0, 32),), jnp.float32),
        "gate_up_weight": noise(key_of[7], (D, 2 * FF), D ** -0.5, 0.125, ((0, 32),), jnp.float32),
        "down_weight": noise(key_of[8], (FF, D), FF ** -0.5, 0.078125, ((0, 32),), jnp.float32),
        "cotangent": noise(key_of[9], (BUCKETS, LEN, SEQS, D), 1.0, 6.0, ((0, 4), (1, 8))),
    }


@jax.custom_vjp
def low(v):
    return lax.optimization_barrier(v.astype(jnp.bfloat16)).astype(jnp.float32)

@jax.custom_vjp
def low_back(v):
    return v

def low_keep(v):
    return (low(v), None)

def low_pass(kept, grad):
    return (grad,)

def back_keep(v):
    return (v, None)

def back_low(kept, grad):
    return (low(grad),)
low.defvjp(low_keep, low_pass)
low_back.defvjp(back_keep, back_low)
highest = lax.Precision.HIGHEST
epsilon = 1e-05
rotary_base = 10000.0
masked_score = -1e+30

def product(left, right):
    return jnp.dot(left, right, precision=highest)

def rotary_tables(positions):
    half_rot = ROT // 2
    frequency = rotary_base ** (-(2.0 * jnp.arange(half_rot).astype(jnp.float32)) / ROT)
    angles = positions.astype(jnp.float32)[:, None] * frequency[None, :]
    return (jnp.cos(angles), jnp.sin(angles))

def rotate(values, cos_table, sine_table):
    half_rot = ROT // 2
    front_half = values[..., :half_rot]
    back_half = values[..., half_rot:ROT]
    return jnp.concatenate([front_half * cos_table - back_half * sine_table, back_half * cos_table + front_half * sine_table, values[..., ROT:]], axis=-1)

def sequence_attention(queries, keys_all, values_all):
    block_count = LEN // GROUP
    query_blocks = queries.reshape(block_count, GROUP, HEADS, HEAD_DIM)
    key_pos = jnp.arange(LEN)

    def one_block(element):
        query_block, block_index = element
        scores = low_back(jnp.einsum('thd,uhd->htu', query_block, keys_all, precision=highest))
        query_pos = block_index * GROUP + jnp.arange(GROUP)
        allowed = key_pos[None, :] <= query_pos[:, None]
        scores = jnp.where(allowed[None], scores, masked_score)
        weights = low(jax.nn.softmax(scores, axis=-1))
        return jnp.einsum('htu,uhd->thd', weights, values_all, precision=highest)
    outputs = lax.map(jax.checkpoint(one_block), (query_blocks, jnp.arange(block_count)))
    return outputs.reshape(LEN, HEADS, HEAD_DIM)

def layer_forward(inputs, gain_vec, shifts, inward, biases, outward, gate_up, down_mat, valid_rows):
    centred = inputs - lax.optimization_barrier(jnp.mean(inputs, axis=-1, keepdims=True))
    variance = lax.optimization_barrier(jnp.mean(centred * centred, axis=-1, keepdims=True))
    normed = low(centred * lax.rsqrt(variance + epsilon) * low(gain_vec) + low(shifts))
    flat_rows = normed.reshape(-1, D)
    bias_low = low(biases)
    key_bias = jnp.pad(bias_low[2 * D:].reshape(HEADS, ROT), ((0, 0), (0, HEAD_DIM - ROT))).reshape(D)
    full_bias = jnp.concatenate([bias_low[:D], key_bias, bias_low[D:2 * D]])
    projected = low_back(product(flat_rows, low(inward)) + full_bias)
    projected = projected.reshape(BUCKETS, LEN, SEQS, 3, HEADS, HEAD_DIM)
    cos_table, sine_table = rotary_tables(jnp.arange(LEN))
    cos_table = cos_table.reshape(1, LEN, 1, 1, ROT // 2)
    sine_table = sine_table.reshape(1, LEN, 1, 1, ROT // 2)
    queries = low(rotate(projected[:, :, :, 0], cos_table, sine_table) * HEAD_DIM ** (-0.5))
    keys_low = low(rotate(projected[:, :, :, 1], cos_table, sine_table))
    values_low = low(projected[:, :, :, 2])

    def per_sequence(stacked):
        return jnp.transpose(stacked, (0, 2, 1, 3, 4)).reshape(BUCKETS * SEQS, LEN, HEADS, HEAD_DIM)

    def attend_one(triple):
        return sequence_attention(triple[0], triple[1], triple[2])
    attended = lax.map(attend_one, (per_sequence(queries), per_sequence(keys_low), per_sequence(values_low)))
    attended = jnp.transpose(attended.reshape(BUCKETS, SEQS, LEN, HEADS, HEAD_DIM), (0, 2, 1, 3, 4)).reshape(-1, D)
    attended = low(low_back(attended))
    attn_part = product(attended, low(outward))
    gate_up_rows = low_back(product(flat_rows, low(gate_up)))
    hidden = low(jax.nn.silu(gate_up_rows[:, :FF]) * gate_up_rows[:, FF:])
    branch = (attn_part + product(hidden, low(down_mat))).reshape(inputs.shape)
    return inputs + valid_rows * branch

def reference(tokens, lengths, norm_gain, norm_shift, inward_weight, inward_bias, outward_weight, gate_up_weight, down_weight, cotangent):
    positions = jnp.arange(LEN)
    valid_rows = (positions[None, :, None] < lengths[:, None, :]).astype(jnp.float32)[..., None]

    def forward(inputs, gain_vec, shifts, inward, biases, outward, gate_up, down_mat):
        return layer_forward(inputs, gain_vec, shifts, inward, biases, outward, gate_up, down_mat, valid_rows)
    result, pullback = jax.vjp(forward, tokens.astype(jnp.float32), norm_gain, norm_shift, inward_weight, inward_bias, outward_weight, gate_up_weight, down_weight)
    gradients = pullback(cotangent.astype(jnp.float32))
    return (result.astype(jnp.bfloat16), gradients[0].astype(jnp.bfloat16), gradients[1], gradients[2], gradients[3], gradients[4], gradients[5], gradients[6], gradients[7])
```

```python
import jax
import jax.numpy as jnp
from jax import lax
from jax.experimental import pallas as pl
from jax.experimental.pallas import tpu as pltpu
from jax.sharding import PartitionSpec as P

HEADS = 32
HEAD_DIM = 64
ROT = 16


epsilon = 1e-05
rotary_base = 10000.0
masked_score = -1e30


def shifted(value, axis, by):
    count = lax.axis_size(axis)
    pairs = [(i, i + by) for i in range(count) if 0 <= i + by < count]
    return lax.ppermute(value, axis, pairs)


def shifted_2(value, axis, steps):
    count = lax.axis_size(axis)
    pairs = [(source, (source + steps) % count) for source in range(count)]
    return lax.ppermute(value, axis, pairs)


def keep_same(value):
    return value


def transposed_times(left, right):
    return lax.dot_general(
        left, right, (((1,), (1,)), ((), ())), preferred_element_type=jnp.float32
    )


def times_transposed(left, right):
    return lax.dot_general(
        left, right, (((0,), (0,)), ((), ())), preferred_element_type=jnp.float32
    )


def rotary_tables(positions):
    half_rot = ROT // 2
    frequency = rotary_base ** (-(2.0 * jnp.arange(half_rot).astype(jnp.float32)) / ROT)
    angles = positions.astype(jnp.float32)[:, None] * frequency[None, :]
    return (jnp.cos(angles), jnp.sin(angles))


def rotate(values, cos_table, sine_table):
    half_rot = ROT // 2
    front_half = values[..., :half_rot]
    back_half = values[..., half_rot:ROT]
    return jnp.concatenate(
        [
            front_half * cos_table - back_half * sine_table,
            back_half * cos_table + front_half * sine_table,
            values[..., ROT:],
        ],
        axis=-1,
    )


def split_pairs(packed):
    rows_here, seq_count, both_width = packed.shape
    half_width = both_width // 2
    keys_part = packed[..., :half_width].reshape(rows_here, seq_count, HEADS, HEAD_DIM)
    values_part = packed[..., half_width:].reshape(rows_here, seq_count, HEADS, HEAD_DIM)
    return (keys_part, values_part)


def block_scores(queries, key_block, query_start, key_start):
    scores = jnp.einsum("tshd,ushd->shtu", queries, key_block, preferred_element_type=jnp.float32)
    query_pos = query_start + jnp.arange(queries.shape[0], dtype=jnp.int32)
    key_pos = key_start + jnp.arange(key_block.shape[0], dtype=jnp.int32)
    allowed = (key_pos[None, :] <= query_pos[:, None])[None, None]
    return (jnp.where(allowed, scores, masked_score), allowed)


def forward_block(carried, queries, key_block, value_block, query_start, key_start):
    running_max, running_sum, weighted = carried
    scores, allowed = block_scores(queries, key_block, query_start, key_start)
    new_max = jnp.maximum(running_max, jnp.max(scores, axis=-1))
    rescale = jnp.exp(running_max - new_max)
    weights = jnp.where(allowed, jnp.exp(scores - new_max[..., None]), 0.0)
    running_sum = running_sum * rescale + jnp.sum(weights, axis=-1)
    update = jnp.einsum(
        "shtu,ushd->tshd",
        weights.astype(jnp.bfloat16),
        value_block,
        preferred_element_type=jnp.float32,
    )
    weighted = weighted * jnp.transpose(rescale, (2, 0, 1))[..., None] + update
    return (new_max, running_sum, weighted)


def pair_grads(
    queries, out_grads, log_norm, deltas, key_block, value_block, query_start, key_start
):
    scores, allowed = block_scores(queries, key_block, query_start, key_start)
    probability = jnp.where(allowed, jnp.exp(scores - log_norm[..., None]), 0.0)
    value_grad = jnp.einsum(
        "shtu,tshd->ushd",
        probability.astype(jnp.bfloat16),
        out_grads,
        preferred_element_type=jnp.float32,
    )
    prob_grad = jnp.einsum(
        "tshd,ushd->shtu", out_grads, value_block, preferred_element_type=jnp.float32
    )
    score_grad = (probability * (prob_grad - deltas[..., None])).astype(jnp.bfloat16)
    query_grad = jnp.einsum(
        "shtu,ushd->tshd", score_grad, key_block, preferred_element_type=jnp.float32
    )
    key_grad = jnp.einsum(
        "shtu,tshd->ushd", score_grad, queries, preferred_element_type=jnp.float32
    )
    return (query_grad, key_grad, value_grad)


def over_blocks(running, incoming, unit_rows, handle):
    total_rows = incoming[0].shape[0]
    block_count = total_rows // unit_rows
    block_rows = total_rows // block_count
    stacked = tuple(
        (member.reshape((block_count, block_rows) + member.shape[1:]) for member in incoming)
    )

    def visit(carried, element):
        block_index, members = element
        return (handle(carried, members, block_index * block_rows), None)

    running, unused = lax.scan(visit, running, (jnp.arange(block_count, dtype=jnp.int32), stacked))
    return running


def shards_general(
    tokens,
    lengths,
    norm_gain,
    norm_shift,
    inward_weight,
    inward_bias,
    outward_weight,
    gate_up_weight,
    down_weight,
    cotangent,
):
    group_len = tokens.shape[1]
    seq_count = tokens.shape[2]
    model_width = tokens.shape[3]
    row_total = group_len * seq_count
    block_total = lax.axis_size("blk")
    position = lax.axis_index("blk")
    own_start = position * group_len
    longest = jnp.max(lengths[0])
    active = own_start < longest
    gathered = (
        lax.all_gather(inward_weight.astype(jnp.bfloat16), ("bucket", "blk"), axis=0, tiled=True),
        lax.all_gather(outward_weight.astype(jnp.bfloat16), ("bucket", "blk"), axis=0, tiled=True),
        lax.all_gather(gate_up_weight.astype(jnp.bfloat16), ("bucket", "blk"), axis=0, tiled=True),
        lax.all_gather(down_weight.astype(jnp.bfloat16), ("bucket", "blk"), axis=0, tiled=True),
        lax.all_gather(norm_gain.astype(jnp.bfloat16), ("bucket", "blk"), axis=0, tiled=True),
        lax.all_gather(norm_shift.astype(jnp.bfloat16), ("bucket", "blk"), axis=0, tiled=True),
        lax.all_gather(inward_bias.astype(jnp.bfloat16), ("bucket", "blk"), axis=0, tiled=True),
    )
    inward_full, outward_full, gate_up_full, down_full, gain_full, shift_full, bias_full = gathered
    inputs = tokens.reshape(row_total, model_width).astype(jnp.float32)
    centred = inputs - jnp.mean(inputs, axis=-1, keepdims=True)
    variance = jnp.mean(centred * centred, axis=-1, keepdims=True)
    inverse = lax.rsqrt(variance + epsilon)
    normal_hat = centred * inverse
    normed_low = (
        normal_hat * gain_full.astype(jnp.float32) + shift_full.astype(jnp.float32)
    ).astype(jnp.bfloat16)
    bias_float = bias_full.astype(jnp.float32)
    key_bias = jnp.pad(
        bias_float[2 * model_width :].reshape(HEADS, ROT), ((0, 0), (0, HEAD_DIM - ROT))
    ).reshape(model_width)
    full_bias = jnp.concatenate(
        [bias_float[:model_width], key_bias, bias_float[model_width : 2 * model_width]]
    )
    projected = jnp.dot(normed_low, inward_full, preferred_element_type=jnp.float32) + full_bias
    projected = projected.reshape(group_len, seq_count, 3, HEADS, HEAD_DIM)
    cos_table, sine_table = rotary_tables(own_start + jnp.arange(group_len, dtype=jnp.int32))
    cos_table = cos_table[:, None, None, :]
    sine_table = sine_table[:, None, None, :]
    query_scale = HEAD_DIM ** (-0.5)
    queries = (rotate(projected[:, :, 0], cos_table, sine_table) * query_scale).astype(jnp.bfloat16)
    keys_low = rotate(projected[:, :, 1], cos_table, sine_table).astype(jnp.bfloat16)
    values_low = projected[:, :, 2].astype(jnp.bfloat16)
    packed = jnp.concatenate(
        [
            keys_low.reshape(group_len, seq_count, model_width),
            values_low.reshape(group_len, seq_count, model_width),
        ],
        axis=-1,
    )

    def forward_handle(carried, members, key_start):
        keys_part, values_part = split_pairs(members[0])
        needed = active & (key_start <= own_start + group_len - 1)

        def forward_compute(state_in):
            return forward_block(state_in, queries, keys_part, values_part, own_start, key_start)

        return lax.cond(needed, forward_compute, keep_same, carried)

    start_state = (
        jnp.full((seq_count, HEADS, group_len), masked_score, jnp.float32),
        jnp.zeros((seq_count, HEADS, group_len), jnp.float32),
        jnp.zeros((group_len, seq_count, HEADS, HEAD_DIM), jnp.float32),
    )
    running_max, running_sum, weighted = over_blocks(
        start_state, (lax.all_gather(packed, "blk", axis=0, tiled=True),), group_len, forward_handle
    )
    bounded = jnp.maximum(running_sum, 1.0)
    log_norm = running_max + jnp.log(bounded)
    attended = weighted / jnp.transpose(bounded, (2, 0, 1))[..., None]
    attended_rows = attended.astype(jnp.bfloat16).reshape(row_total, model_width)
    gate_up = jnp.dot(normed_low, gate_up_full, preferred_element_type=jnp.float32)
    ff_width = gate_up.shape[1] // 2
    gate_part = gate_up[:, :ff_width]
    up_part = gate_up[:, ff_width:]
    sigmoid_gate = jax.nn.sigmoid(gate_part)
    silu_gate = gate_part * sigmoid_gate
    hidden_low = (silu_gate * up_part).astype(jnp.bfloat16)
    branch = jnp.dot(attended_rows, outward_full, preferred_element_type=jnp.float32) + jnp.dot(
        hidden_low, down_full, preferred_element_type=jnp.float32
    )
    query_pos = own_start + jnp.arange(group_len, dtype=jnp.int32)
    valid_rows = (
        (query_pos[:, None] < lengths[0][None, :]).astype(jnp.float32).reshape(row_total, 1)
    )
    layer_out = (inputs + valid_rows * branch).astype(jnp.bfloat16).reshape(tokens.shape)
    inward_back = gathered[0]
    outward_back = gathered[1]
    gate_up_back = gathered[2]
    down_back = gathered[3]
    gain_float = gathered[4].astype(jnp.float32)
    cotangent_rows = cotangent.reshape(row_total, model_width).astype(jnp.float32)
    branch_grad = (cotangent_rows * valid_rows).astype(jnp.bfloat16)
    hidden_grad = transposed_times(branch_grad, down_back)
    gate_grad = hidden_grad * up_part * (sigmoid_gate + silu_gate * (1.0 - sigmoid_gate))
    up_grad = hidden_grad * silu_gate
    gate_up_grad_low = jnp.concatenate([gate_grad, up_grad], axis=-1).astype(jnp.bfloat16)
    down_term = times_transposed(hidden_low, branch_grad)
    gate_up_term = times_transposed(normed_low, gate_up_grad_low)
    gate_up_sum, down_sum = (
        lax.psum_scatter(gate_up_term, ("bucket", "blk"), scatter_dimension=0, tiled=True),
        lax.psum_scatter(down_term, ("bucket", "blk"), scatter_dimension=0, tiled=True),
    )
    normed_grad = transposed_times(gate_up_grad_low, gate_up_back)
    attended_grad = (
        transposed_times(branch_grad, outward_back)
        .astype(jnp.bfloat16)
        .reshape(group_len, seq_count, HEADS, HEAD_DIM)
    )
    outward_term = times_transposed(attended_rows, branch_grad)
    deltas = jnp.transpose(
        jnp.sum(attended_grad.astype(jnp.float32) * attended, axis=-1), (1, 2, 0)
    )
    grad_zeros = jnp.zeros((group_len, seq_count, 2 * model_width), jnp.float32)
    query_zeros = jnp.zeros((group_len, seq_count, HEADS, HEAD_DIM), jnp.float32)

    def cycle_turn(turn_index, carried):
        visiting, sums_now, grads_now = carried
        owner_index = (position - turn_index) % block_total
        key_start = owner_index * group_len
        needed = active & (owner_index <= position)

        def cycle_compute(sums_in):
            keys_part, values_part = split_pairs(visiting)
            query_part, key_part, value_part = pair_grads(
                queries,
                attended_grad,
                log_norm,
                deltas,
                keys_part,
                values_part,
                own_start,
                key_start,
            )
            merged = jnp.concatenate(
                [
                    key_part.reshape(group_len, seq_count, model_width),
                    value_part.reshape(group_len, seq_count, model_width),
                ],
                axis=-1,
            )
            return (sums_in[0] + merged, sums_in[1] + query_part)

        sums_now, grads_now = lax.cond(needed, cycle_compute, keep_same, (sums_now, grads_now))
        visiting = shifted(visiting, "blk", 1)
        sums_now = shifted_2(sums_now.astype(jnp.bfloat16), "blk", 1).astype(sums_now.dtype)
        return (visiting, sums_now, grads_now)

    unused, pair_sums, query_grads = lax.fori_loop(
        0, block_total, cycle_turn, (packed, grad_zeros, query_zeros)
    )
    key_grad = pair_sums[..., :model_width].reshape(group_len, seq_count, HEADS, HEAD_DIM)
    value_grad = pair_sums[..., model_width:].reshape(group_len, seq_count, HEADS, HEAD_DIM)
    back_sine = -sine_table
    query_back = rotate(query_grads * query_scale, cos_table, back_sine)
    key_back = rotate(key_grad, cos_table, back_sine)
    projected_grad = (
        jnp.stack([query_back, key_back, value_grad], axis=2)
        .reshape(row_total, 3 * model_width)
        .astype(jnp.bfloat16)
    )
    inward_term = times_transposed(normed_low, projected_grad)
    column_sums = jnp.sum(projected_grad.astype(jnp.float32), axis=0)
    key_bias_grad = (
        column_sums[model_width : 2 * model_width]
        .reshape(HEADS, HEAD_DIM)[:, :ROT]
        .reshape(HEADS * ROT)
    )
    bias_term = jnp.concatenate(
        [column_sums[:model_width], column_sums[2 * model_width :], key_bias_grad]
    )
    normed_grad = normed_grad + transposed_times(projected_grad, inward_back)
    gain_term = jnp.sum(normed_grad * normal_hat, axis=0)
    shift_term = jnp.sum(normed_grad, axis=0)
    scaled_grad = normed_grad * gain_float
    input_grad = inverse * (
        scaled_grad
        - jnp.mean(scaled_grad, axis=-1, keepdims=True)
        - normal_hat * jnp.mean(scaled_grad * normal_hat, axis=-1, keepdims=True)
    )
    tokens_grad = (cotangent_rows + input_grad).astype(jnp.bfloat16).reshape(tokens.shape)
    inward_sum, outward_sum, bias_sum, gain_sum, shift_sum = (
        lax.psum_scatter(inward_term, ("bucket", "blk"), scatter_dimension=0, tiled=True),
        lax.psum_scatter(outward_term, ("bucket", "blk"), scatter_dimension=0, tiled=True),
        lax.psum_scatter(bias_term, ("bucket", "blk"), scatter_dimension=0, tiled=True),
        lax.psum_scatter(gain_term, ("bucket", "blk"), scatter_dimension=0, tiled=True),
        lax.psum_scatter(shift_term, ("bucket", "blk"), scatter_dimension=0, tiled=True),
    )
    return (
        layer_out,
        tokens_grad,
        gain_sum,
        shift_sum,
        inward_sum,
        bias_sum,
        outward_sum,
        gate_up_sum,
        down_sum,
    )


DEPTH = 4
PIECES = 2 * DEPTH
ROWS = 256
LOCAL_HEADS = 4
HEAD_COLS = LOCAL_HEADS * HEAD_DIM
CORE = [(i, i ^ 1) for i in range(4)]
ACROSS_X = [(i, i ^ 2) for i in range(4)]
ACROSS_Y = [(i, i ^ 1) for i in range(8)]
UPWARD = [(i, i + 2) for i in range(6)]
DOWNWARD = [(i + 2, i) for i in range(6)]
MIB = 1024 * 1024


def fits_groups(mesh):
    return mesh.shape["bucket"] == 4 and mesh.shape["blk"] == 2 * DEPTH


def around(step):
    return [(z * 2 + y, ((z + step) % DEPTH) * 2 + y) for z in range(DEPTH) for y in range(2)]


def in_order(own, other, index, axis):
    return jnp.where(
        index == 0, jnp.stack([own, other], axis), jnp.stack([other, own], axis)
    )


def gather_pieces(value, z):
    up, down = [value], [value]
    for step in range(DEPTH - 1):
        up.append(lax.ppermute(up[-1], "blk", UPWARD))
        down.append(lax.ppermute(down[-1], "blk", DOWNWARD))
    own = [value]
    for step in range(1, DEPTH):
        own.append(jnp.where(z >= step, up[step], down[DEPTH - step]))
    return own + [lax.ppermute(piece, "bucket", CORE) for piece in own]


def scatter_pieces(partial):
    total = None
    for step in range(DEPTH):
        both = partial[step].astype(jnp.float32) + lax.ppermute(
            partial[DEPTH + step], "bucket", CORE
        ).astype(jnp.float32)
        if step > 0:
            both = lax.ppermute(both.astype(jnp.bfloat16), "blk", around(-step)).astype(jnp.float32)
        total = both if total is None else total + both
    return total


def columns_of_group(rows, core, z):
    mine = lax.dynamic_index_in_dim(rows, core, 0, False)
    theirs = lax.dynamic_index_in_dim(rows, 1 - core, 0, False)
    got = lax.ppermute(theirs, "bucket", CORE)
    both = in_order(mine, got, core, 1)
    pieces = [lax.dynamic_index_in_dim(both, z, 0, False)]
    for step in range(1, DEPTH):
        chunk = lax.dynamic_index_in_dim(both, (z + step) % DEPTH, 0, False)
        pieces.append(lax.ppermute(chunk, "blk", around(step)))
    stacked = jnp.stack(pieces)
    return jnp.concatenate(
        [lax.dynamic_slice_in_dim(stacked, (z - j) % DEPTH, 1, 0) for j in range(DEPTH)]
    )


def over_columns(value, x, y):
    value = in_order(value, lax.ppermute(value, "blk", ACROSS_Y), y, 0)
    return in_order(value, lax.ppermute(value, "bucket", ACROSS_X), x, 0)


def sum_over_columns(value, x, y):
    keep = lax.dynamic_index_in_dim(value, x, 0, False)
    send = lax.dynamic_index_in_dim(value, 1 - x, 0, False).astype(jnp.bfloat16)
    value = keep + lax.ppermute(send, "bucket", ACROSS_X).astype(jnp.float32)
    keep = lax.dynamic_index_in_dim(value, y, 0, False)
    send = lax.dynamic_index_in_dim(value, 1 - y, 0, False).astype(jnp.bfloat16)
    return keep + lax.ppermute(send, "blk", ACROSS_Y).astype(jnp.float32)


def rows_of_device(value, core, z):
    low = value.astype(jnp.bfloat16)
    parts = [lax.dynamic_index_in_dim(low, z, 0, False)]
    for step in range(1, DEPTH):
        chunk = lax.dynamic_index_in_dim(low, (z + step) % DEPTH, 0, False)
        parts.append(lax.ppermute(chunk, "blk", around(step)))
    stacked = jnp.stack(parts)
    ordered = jnp.concatenate(
        [lax.dynamic_slice_in_dim(stacked, (z - j) % DEPTH, 1, 0) for j in range(DEPTH)]
    )
    mine = lax.dynamic_index_in_dim(ordered, core, 1, False)
    theirs = lax.dynamic_index_in_dim(ordered, 1 - core, 1, False)
    return in_order(mine, lax.ppermute(theirs, "bucket", CORE), core, 0)


def dot_rows(left, right):
    return lax.dot_general(
        left, right, (((1,), (0,)), ((), ())), preferred_element_type=jnp.float32
    )


def params(limit, **extra):
    return pltpu.CompilerParams(vmem_limit_bytes=limit * MIB, **extra)


def cost(flops, moved, exps=0):
    return pl.CostEstimate(flops=flops, bytes_accessed=moved, transcendentals=exps)


def piece_spec(width):
    return pl.BlockSpec((1, ROWS, width), lambda i: (i, 0, 0))


def whole_spec(shape):
    return pl.BlockSpec(shape, lambda i: (0,) * len(shape))


def normalised(rows):
    inputs = rows.astype(jnp.float32)
    centred = inputs - jnp.mean(inputs, axis=-1, keepdims=True)
    variance = jnp.mean(centred * centred, axis=-1, keepdims=True)
    inverse = lax.rsqrt(variance + epsilon)
    return centred * inverse, inverse


def turned(values, cos_ref, first_ref, second_ref, sign):
    half = ROT // 2
    cos = jnp.concatenate([cos_ref[0], cos_ref[0]], 0)
    first = jnp.concatenate([first_ref[0], first_ref[0]], 0)
    second = jnp.concatenate([second_ref[0], second_ref[0]], 0)
    ahead = pltpu.roll(values, HEAD_COLS - half, 1)
    behind = pltpu.roll(values, half, 1)
    return values * cos + sign * (ahead * first + behind * second)


def project_kernel(
    x_ref, gain_ref, shift_ref, w_ref, bias_ref, cos_ref, first_ref, second_ref, n_ref, q_ref, kv_ref
):
    hat, _ = normalised(x_ref[0])
    normed = (hat * gain_ref[...] + shift_ref[...]).astype(jnp.bfloat16)
    n_ref[0] = normed
    projected = dot_rows(normed, w_ref[...]) + bias_ref[...]
    tables = (cos_ref, first_ref, second_ref)
    query = turned(projected[:, :HEAD_COLS], *tables, 1.0) * (HEAD_DIM**-0.5)
    key = turned(projected[:, HEAD_COLS : 2 * HEAD_COLS], *tables, 1.0)
    q_ref[0] = query.astype(jnp.bfloat16)
    kv_ref[0, :, :HEAD_COLS] = key.astype(jnp.bfloat16)
    kv_ref[0, :, HEAD_COLS:] = projected[:, 2 * HEAD_COLS :].astype(jnp.bfloat16)


def project(pieces, gain, shift, weight, bias, tables):
    width = pieces.shape[-1]
    table_spec = pl.BlockSpec((1,) + tables[0].shape[1:], lambda i: (i % DEPTH, 0, 0))
    return pl.pallas_call(
        project_kernel,
        grid=(PIECES,),
        in_specs=[
            piece_spec(width),
            whole_spec((1, width)),
            whole_spec((1, width)),
            whole_spec(weight.shape),
            whole_spec(bias.shape),
            table_spec,
            table_spec,
            table_spec,
        ],
        out_specs=[piece_spec(width), piece_spec(HEAD_COLS), piece_spec(2 * HEAD_COLS)],
        out_shape=[
            jax.ShapeDtypeStruct((PIECES, ROWS, width), jnp.bfloat16),
            jax.ShapeDtypeStruct((PIECES, ROWS, HEAD_COLS), jnp.bfloat16),
            jax.ShapeDtypeStruct((PIECES, ROWS, 2 * HEAD_COLS), jnp.bfloat16),
        ],
        compiler_params=params(48),
        cost_estimate=cost(2 * PIECES * ROWS * width * 3 * HEAD_COLS, 24 * MIB),
        name="project",
    )(pieces, gain, shift, weight, bias, *tables)


def feed_kernel(n_ref, wg_ref, wu_ref, gate_ref, up_ref, hidden_ref):
    normed = n_ref[0]
    gate = dot_rows(normed, wg_ref[...])
    up = dot_rows(normed, wu_ref[...])
    gate_ref[0] = gate
    up_ref[0] = up
    hidden_ref[0] = (gate * jax.nn.sigmoid(gate) * up).astype(jnp.bfloat16)


def feed(normed, gate_weight, up_weight):
    width = normed.shape[-1]
    hidden = gate_weight.shape[1]
    return pl.pallas_call(
        feed_kernel,
        grid=(PIECES,),
        in_specs=[piece_spec(width), whole_spec(gate_weight.shape), whole_spec(up_weight.shape)],
        out_specs=[piece_spec(hidden)] * 3,
        out_shape=[
            jax.ShapeDtypeStruct((PIECES, ROWS, hidden), jnp.float32),
            jax.ShapeDtypeStruct((PIECES, ROWS, hidden), jnp.float32),
            jax.ShapeDtypeStruct((PIECES, ROWS, hidden), jnp.bfloat16),
        ],
        compiler_params=params(48),
        cost_estimate=cost(4 * PIECES * ROWS * width * hidden, 28 * MIB),
        name="feed",
    )(normed, gate_weight, up_weight)


def branch_kernel(a_ref, h_ref, wo_ref, wd_ref, out_ref):
    out_ref[0] = (dot_rows(a_ref[0], wo_ref[...]) + dot_rows(h_ref[0], wd_ref[...])).astype(
        jnp.bfloat16
    )


def branch_terms(attended, hidden, outward, down):
    width = outward.shape[1]
    return pl.pallas_call(
        branch_kernel,
        grid=(PIECES,),
        in_specs=[
            piece_spec(HEAD_COLS),
            piece_spec(hidden.shape[-1]),
            whole_spec(outward.shape),
            whole_spec(down.shape),
        ],
        out_specs=piece_spec(width),
        out_shape=jax.ShapeDtypeStruct((PIECES, ROWS, width), jnp.bfloat16),
        compiler_params=params(48),
        cost_estimate=cost(2 * PIECES * ROWS * width * (HEAD_COLS + hidden.shape[-1]), 16 * MIB),
        name="branch_terms",
    )(attended, hidden, outward, down)


def back_kernel(g_ref, gate_ref, up_ref, wo_ref, wd_ref, a_ref, gg_ref, ug_ref):
    grad = g_ref[0]
    a_ref[0] = transposed_times(grad, wo_ref[...]).astype(jnp.bfloat16)
    hidden_grad = transposed_times(grad, wd_ref[...])
    gate = gate_ref[0]
    sig = jax.nn.sigmoid(gate)
    silu = gate * sig
    gg_ref[0] = (hidden_grad * up_ref[0] * (sig + silu * (1.0 - sig))).astype(jnp.bfloat16)
    ug_ref[0] = (hidden_grad * silu).astype(jnp.bfloat16)


def back(grads, gate, up, outward, down):
    width = outward.shape[1]
    hidden = down.shape[0]
    return pl.pallas_call(
        back_kernel,
        grid=(PIECES,),
        in_specs=[
            piece_spec(width),
            piece_spec(hidden),
            piece_spec(hidden),
            whole_spec(outward.shape),
            whole_spec(down.shape),
        ],
        out_specs=[piece_spec(HEAD_COLS), piece_spec(hidden), piece_spec(hidden)],
        out_shape=[
            jax.ShapeDtypeStruct((PIECES, ROWS, HEAD_COLS), jnp.bfloat16),
            jax.ShapeDtypeStruct((PIECES, ROWS, hidden), jnp.bfloat16),
            jax.ShapeDtypeStruct((PIECES, ROWS, hidden), jnp.bfloat16),
        ],
        compiler_params=params(48),
        cost_estimate=cost(2 * PIECES * ROWS * width * (HEAD_COLS + hidden), 28 * MIB),
        name="back",
    )(grads, gate, up, outward, down)


def pair_rows(block):
    lane = lax.broadcasted_iota(jnp.int32, block.shape, 1)
    zero = jnp.zeros_like(block)
    return jnp.concatenate(
        [jnp.where(lane < HEAD_DIM, block, zero), jnp.where(lane < HEAD_DIM, zero, block)], 0
    )


def pair_lanes(rows):
    half = rows.shape[0] // 2
    lane = lax.broadcasted_iota(jnp.int32, (half, rows.shape[1]), 1)
    return jnp.where(lane < HEAD_DIM, rows[:half], rows[half:])


def block_probs(queries, keys, last, y):
    scores = transposed_times(queries, keys)
    rows, columns = scores.shape
    size = rows // 2
    row = lax.broadcasted_iota(jnp.int32, (rows, 2 * size), 0) % size
    column = lax.broadcasted_iota(jnp.int32, (rows, 2 * size), 1)
    allowed = (column <= row) | ((column >= size) & (y == 1))
    tail = jnp.where(allowed, scores[:, last * 2 * size :], masked_score)
    scores = tail if last == 0 else jnp.concatenate([scores[:, : last * 2 * size], tail], 1)
    weights = jnp.exp(scores - jnp.max(scores, axis=-1, keepdims=True))
    return weights * (1.0 / jnp.sum(weights, axis=-1, keepdims=True))


def both_columns(own_ref, other_ref, z, count):
    blocks = []
    for j in range(count):
        at = (z + DEPTH - j) % DEPTH
        blocks += [own_ref[0, at, 0], other_ref[0, at, 0]]
    return jnp.concatenate(blocks, 0)


def attend_kernel(place_ref, q_ref, k_ref, v_ref, ok_ref, ov_ref, out_ref):
    z, y = place_ref[0], place_ref[1]
    keys = both_columns(k_ref, ok_ref, z, DEPTH)
    values = both_columns(v_ref, ov_ref, z, DEPTH)
    size = keys.shape[0] // DEPTH
    for j in range(DEPTH):
        at = (z + DEPTH - j) % DEPTH
        count = (j + 1) * size
        probs = block_probs(pair_rows(q_ref[0, at, 0]), keys[:count], j, y)
        out = dot_rows(probs.astype(jnp.bfloat16), values[:count])
        out_ref[0, at, 0] = pair_lanes(out).astype(jnp.bfloat16)


def attend_back_kernel(
    place_ref,
    q_ref,
    k_ref,
    v_ref,
    ok_ref,
    ov_ref,
    grad_ref,
    dq_ref,
    dk_ref,
    dv_ref,
    odk_ref,
    odv_ref,
    key_sum,
    value_sum,
):
    z, y = place_ref[0], place_ref[1]
    keys = both_columns(k_ref, ok_ref, z, DEPTH)
    values = both_columns(v_ref, ov_ref, z, DEPTH)
    size = keys.shape[0] // DEPTH
    half = size // 2
    for j in reversed(range(DEPTH)):
        at = (z + DEPTH - j) % DEPTH
        count = (j + 1) * size
        queries = pair_rows(q_ref[0, at, 0])
        grads = pair_rows(grad_ref[0, at, 0])
        probs = block_probs(queries, keys[:count], j, y)
        low = probs.astype(jnp.bfloat16)
        prob_grad = transposed_times(grads, values[:count])
        delta = jnp.sum(low.astype(jnp.float32) * prob_grad, axis=-1, keepdims=True)
        score_grad = (probs * (prob_grad - delta)).astype(jnp.bfloat16)
        dq_ref[0, at, 0] = pair_lanes(dot_rows(score_grad, keys[:count]))
        key_term = times_transposed(score_grad, queries)
        value_term = times_transposed(low, grads)
        if j == DEPTH - 1:
            key_sum[...] = key_term
            value_sum[...] = value_term
        else:
            key_sum[:count] += key_term
            value_sum[:count] += value_term
    for j in range(DEPTH):
        at = (z + DEPTH - j) % DEPTH
        low = j * size
        dk_ref[0, at, 0] = key_sum[low : low + half]
        dv_ref[0, at, 0] = value_sum[low : low + half]
        odk_ref[0, at, 0] = key_sum[low + half : low + size].astype(jnp.bfloat16)
        odv_ref[0, at, 0] = value_sum[low + half : low + size].astype(jnp.bfloat16)


def sequence_specs(seqs, length):
    def spec(first):
        return pl.BlockSpec(
            (1, DEPTH, 1, length, 2 * HEAD_DIM), lambda b, s, p, place: (b, 0, s, 0, first + p)
        )

    return spec(0), spec(LOCAL_HEADS // 2)


def as_sequences(value, seqs):
    return value.reshape(2, DEPTH, seqs, ROWS // seqs, value.shape[-1])


def attend(place, queries, pairs, other_pairs, seqs):
    queries, pairs, other_pairs = (as_sequences(v, seqs) for v in (queries, pairs, other_pairs))
    first, second = sequence_specs(seqs, ROWS // seqs)
    out = pl.pallas_call(
        attend_kernel,
        grid_spec=pltpu.PrefetchScalarGridSpec(
            num_scalar_prefetch=1,
            grid=(2, seqs, LOCAL_HEADS // 2),
            in_specs=[first, first, second, first, second],
            out_specs=first,
        ),
        out_shape=jax.ShapeDtypeStruct(queries.shape, jnp.bfloat16),
        compiler_params=params(48),
        cost_estimate=cost(4 * 8 * 2 * 2 * 256 * 2560 * 128, 8 * MIB, 8 * 256 * 2560),
        name="attend",
    )(place, queries, pairs, pairs, other_pairs, other_pairs)
    return out.reshape(PIECES, ROWS, HEAD_COLS)


def attend_back(place, queries, pairs, other_pairs, grads, seqs):
    queries, pairs, other_pairs, grads = (
        as_sequences(v, seqs) for v in (queries, pairs, other_pairs, grads)
    )
    length = ROWS // seqs
    first, second = sequence_specs(seqs, length)
    wide = jax.ShapeDtypeStruct(queries.shape, jnp.float32)
    narrow = jax.ShapeDtypeStruct(queries.shape, jnp.bfloat16)
    outs = pl.pallas_call(
        attend_back_kernel,
        grid_spec=pltpu.PrefetchScalarGridSpec(
            num_scalar_prefetch=1,
            grid=(2, seqs, LOCAL_HEADS // 2),
            in_specs=[first, first, second, first, second, first],
            out_specs=[first] * 5,
            scratch_shapes=[
                pltpu.VMEM((2 * DEPTH * length, 2 * HEAD_DIM), jnp.float32),
                pltpu.VMEM((2 * DEPTH * length, 2 * HEAD_DIM), jnp.float32),
            ],
        ),
        out_shape=[wide, wide, wide, narrow, narrow],
        compiler_params=params(48),
        cost_estimate=cost(10 * 8 * 2 * 2 * 256 * 2560 * 128, 16 * MIB, 8 * 256 * 2560),
        name="attend_back",
    )(place, queries, pairs, pairs, other_pairs, other_pairs, grads)
    return [v.reshape(PIECES, ROWS, HEAD_COLS) for v in outs]


def input_grad_kernel(
    dq_ref,
    dk_ref,
    dv_ref,
    odk_ref,
    odv_ref,
    gg_ref,
    ug_ref,
    x_ref,
    wi_ref,
    wg_ref,
    wu_ref,
    cos_ref,
    first_ref,
    second_ref,
    pg_ref,
    out_ref,
    gain_ref,
    shift_ref,
    bias_ref,
):
    tables = (cos_ref, first_ref, second_ref)
    query = turned(dq_ref[0] * (HEAD_DIM**-0.5), *tables, -1.0)
    key = turned(dk_ref[0] + odk_ref[0].astype(jnp.float32), *tables, -1.0)
    value = dv_ref[0] + odv_ref[0].astype(jnp.float32)
    low = jnp.concatenate([query, key, value], 1).astype(jnp.bfloat16)
    pg_ref[0] = low
    grad = transposed_times(low, wi_ref[...])
    grad += transposed_times(gg_ref[0], wg_ref[...])
    grad += transposed_times(ug_ref[0], wu_ref[...])
    out_ref[0] = grad.astype(jnp.bfloat16)
    hat, _ = normalised(x_ref[0])

    @pl.when(pl.program_id(0) == 0)
    def _():
        gain_ref[...] = jnp.zeros_like(gain_ref)
        shift_ref[...] = jnp.zeros_like(shift_ref)
        bias_ref[...] = jnp.zeros_like(bias_ref)

    gain_ref[...] += jnp.sum(grad * hat, axis=0, keepdims=True)
    shift_ref[...] += jnp.sum(grad, axis=0, keepdims=True)
    bias_ref[...] += jnp.sum(low.astype(jnp.float32), axis=0, keepdims=True)


def input_grads(parts, other_key, other_value, gate_grad, up_grad, pieces, weights, tables):
    width = pieces.shape[-1]
    hidden = gate_grad.shape[-1]
    table_spec = pl.BlockSpec((1,) + tables[0].shape[1:], lambda i: (i % DEPTH, 0, 0))
    return pl.pallas_call(
        input_grad_kernel,
        grid=(PIECES,),
        in_specs=[piece_spec(HEAD_COLS)] * 5
        + [piece_spec(hidden)] * 2
        + [piece_spec(width)]
        + [whole_spec(w.shape) for w in weights]
        + [table_spec] * 3,
        out_specs=[
            piece_spec(3 * HEAD_COLS),
            piece_spec(width),
            whole_spec((1, width)),
            whole_spec((1, width)),
            whole_spec((1, 3 * HEAD_COLS)),
        ],
        out_shape=[
            jax.ShapeDtypeStruct((PIECES, ROWS, 3 * HEAD_COLS), jnp.bfloat16),
            jax.ShapeDtypeStruct((PIECES, ROWS, width), jnp.bfloat16),
            jax.ShapeDtypeStruct((1, width), jnp.float32),
            jax.ShapeDtypeStruct((1, width), jnp.float32),
            jax.ShapeDtypeStruct((1, 3 * HEAD_COLS), jnp.float32),
        ],
        compiler_params=params(56),
        cost_estimate=cost(2 * PIECES * ROWS * width * (3 * HEAD_COLS + 2 * hidden), 48 * MIB),
        name="input_grads",
    )(*parts, other_key, other_value, gate_grad, up_grad, pieces, *weights, *tables)


def lane_tables(positions):
    half = ROT // 2
    place = jnp.arange(HEAD_COLS, dtype=jnp.int32) % HEAD_DIM
    power = (place % half).astype(jnp.float32)
    frequency = jnp.where(place < ROT, rotary_base ** (-(2.0 * power) / ROT), 0.0)
    angles = positions.astype(jnp.float32)[..., None] * frequency
    sine = jnp.sin(angles)
    return (
        jnp.cos(angles),
        jnp.where(place < half, -sine, 0.0),
        jnp.where((place >= half) & (place < ROT), sine, 0.0),
    )


def shards_grouped(
    tokens,
    lengths,
    norm_gain,
    norm_shift,
    inward_weight,
    inward_bias,
    outward_weight,
    gate_up_weight,
    down_weight,
    cotangent,
):
    group_len, seqs, width = tokens.shape[1:]
    bucket, blk = lax.axis_index("bucket"), lax.axis_index("blk")
    x, core = bucket // 2, bucket % 2
    z, y = blk // 2, blk % 2
    devices = 4 * 2 * DEPTH

    shares = jnp.concatenate([norm_gain, norm_shift, inward_bias]).astype(jnp.bfloat16)
    shares = lax.all_gather(shares, ("bucket", "blk"), axis=0, tiled=False).astype(jnp.float32)
    gain_share, bias_share = norm_gain.shape[0], inward_bias.shape[0]
    gain = shares[:, :gain_share].reshape(1, width)
    shift = shares[:, gain_share : 2 * gain_share].reshape(1, width)
    bias = shares[:, 2 * gain_share :].reshape(-1)

    def own_columns(values, each):
        split = values.reshape(2, 2, DEPTH, each)
        split = lax.dynamic_index_in_dim(split, core, 1, False)
        return lax.dynamic_index_in_dim(split, z, 1, False)

    key_bias = jnp.pad(
        own_columns(bias[2 * width :], 2 * ROT).reshape(LOCAL_HEADS, ROT),
        ((0, 0), (0, HEAD_DIM - ROT)),
    )
    own_bias = jnp.concatenate(
        [
            own_columns(bias[:width], 2 * HEAD_DIM).reshape(-1),
            key_bias.reshape(-1),
            own_columns(bias[width : 2 * width], 2 * HEAD_DIM).reshape(-1),
        ]
    ).reshape(1, -1)

    own_rows = inward_weight.shape[0]
    hidden_each = gate_up_weight.shape[1] // (2 * 2 * 2 * DEPTH)
    inward = inward_weight.astype(jnp.bfloat16).reshape(own_rows, 3, 2, 2, DEPTH, 2 * HEAD_DIM)
    inward = jnp.transpose(inward, (3, 4, 0, 1, 2, 5)).reshape(2, DEPTH, own_rows, 3 * HEAD_COLS)
    gate_up = gate_up_weight.astype(jnp.bfloat16).reshape(own_rows, 2, 2, 2, DEPTH, hidden_each)
    gate_up = jnp.transpose(gate_up, (3, 4, 0, 1, 2, 5)).reshape(
        2, DEPTH, own_rows, 4 * hidden_each
    )
    inward = columns_of_group(inward, core, z)
    gate_up = columns_of_group(gate_up, core, z)
    rows_out = jnp.concatenate([outward_weight, down_weight]).astype(jnp.bfloat16)
    rows_out = over_columns(rows_out, x, y)
    outward = rows_out[:, :, : outward_weight.shape[0]].reshape(-1, width)
    down = rows_out[:, :, outward_weight.shape[0] :].reshape(-1, width)

    def full_rows(value):
        value = over_columns(value, x, y)
        return jnp.transpose(value, (0, 3, 2, 1, 4, 5)).reshape(width, -1)

    inward = full_rows(inward)
    gate_up = full_rows(gate_up)
    gate_weight = gate_up[:, : 2 * hidden_each]
    up_weight = gate_up[:, 2 * hidden_each :]

    own_tokens = jnp.transpose(tokens[0], (1, 0, 2))
    position = blk * group_len + jnp.arange(group_len, dtype=jnp.int32)
    valid = (position[None, :] < lengths[0][:, None]).astype(jnp.float32)[..., None]
    own_cotangent = jnp.transpose(cotangent[0], (1, 0, 2)).astype(jnp.float32)
    own_grad = (own_cotangent * valid).astype(jnp.bfloat16)
    pieces = jnp.stack(gather_pieces(own_tokens.reshape(ROWS, width), z))
    grads = jnp.stack(gather_pieces(own_grad.reshape(ROWS, width), z))

    turns = (z - jnp.arange(DEPTH, dtype=jnp.int32)) % DEPTH
    tables = lane_tables(
        ((2 * turns + y) * group_len)[:, None] + jnp.arange(group_len, dtype=jnp.int32)
    )
    place = jnp.stack([z, y]).astype(jnp.int32)

    normed, queries, pairs = project(pieces, gain, shift, inward, own_bias, tables)
    other_pairs = lax.ppermute(pairs, "blk", ACROSS_Y)
    gate, up, hidden = feed(normed, gate_weight, up_weight)
    attended = attend(place, queries, pairs, other_pairs, seqs)
    branch = scatter_pieces(branch_terms(attended, hidden, outward, down))
    branch = branch.reshape(seqs, group_len, width)
    inputs = own_tokens.astype(jnp.float32)
    layer_out = (inputs + valid * branch).astype(jnp.bfloat16)

    attended_grad, gate_grad, up_grad = back(grads, gate, up, outward, down)
    dq, dk, dv, other_dk, other_dv = attend_back(
        place, queries, pairs, other_pairs, attended_grad, seqs
    )
    other_dk = lax.ppermute(other_dk, "blk", ACROSS_Y)
    other_dv = lax.ppermute(other_dv, "blk", ACROSS_Y)
    total = PIECES * ROWS
    flat_normed = normed.reshape(total, width)
    flat_grads = grads.reshape(total, width)
    outward_term = times_transposed(attended.reshape(total, -1), flat_grads)
    down_term = times_transposed(hidden.reshape(total, -1), flat_grads)
    gate_term = times_transposed(flat_normed, gate_grad.reshape(total, -1))
    up_term = times_transposed(flat_normed, up_grad.reshape(total, -1))
    projected_grad, normed_grad, gain_term, shift_term, bias_term = input_grads(
        (dq, dk, dv),
        other_dk,
        other_dv,
        gate_grad,
        up_grad,
        pieces,
        (inward, gate_weight, up_weight),
        tables,
    )
    inward_term = times_transposed(flat_normed, projected_grad.reshape(total, -1))

    outward_sum = sum_over_columns(outward_term.reshape(2, 2, -1, width), x, y)
    down_sum = sum_over_columns(down_term.reshape(2, 2, -1, width), x, y)

    def device_rows(term, parts):
        term = term.reshape(2, 2, DEPTH, 2, own_rows, -1)
        term = sum_over_columns(jnp.transpose(term, (0, 3, 2, 1, 4, 5)), x, y)
        term = rows_of_device(term, core, z)
        term = term.reshape(2, DEPTH, own_rows, parts, 2, -1)
        return jnp.transpose(term, (2, 3, 4, 0, 1, 5)).reshape(own_rows, -1).astype(jnp.float32)

    gate_up_sum = device_rows(jnp.concatenate([gate_term, up_term], 1), 2)
    inward_sum = device_rows(inward_term, 3)

    bias_parts = bias_term.reshape(3, 2, 1, 1, 2 * HEAD_DIM)
    here = (
        (jnp.arange(2)[:, None] == core) & (jnp.arange(DEPTH)[None, :] == z)
    ).astype(jnp.float32)[None, None, :, :, None]
    spread = bias_parts * here
    key_rot = spread[1].reshape(2, 2, DEPTH, 2, HEAD_DIM)[..., :ROT]
    bias_all = jnp.concatenate(
        [spread[0].reshape(-1), spread[2].reshape(-1), key_rot.reshape(-1)]
    )
    vector_terms = jnp.concatenate(
        [
            gain_term.reshape(devices, -1),
            shift_term.reshape(devices, -1),
            bias_all.reshape(devices, -1),
        ],
        1,
    )
    vector_sums = lax.psum_scatter(
        vector_terms, ("bucket", "blk"), scatter_dimension=0, tiled=True
    ).reshape(-1)

    normed_grad = scatter_pieces(normed_grad).reshape(seqs, group_len, width)
    hat, inverse = normalised(own_tokens)
    scaled = normed_grad * gain.reshape(width)
    input_grad = inverse * (
        scaled
        - jnp.mean(scaled, axis=-1, keepdims=True)
        - hat * jnp.mean(scaled * hat, axis=-1, keepdims=True)
    )
    tokens_grad = (own_cotangent + input_grad).astype(jnp.bfloat16)

    def placed(value):
        return jnp.transpose(value, (1, 0, 2)).reshape(tokens.shape)

    return (
        placed(layer_out),
        placed(tokens_grad),
        vector_sums[:gain_share],
        vector_sums[gain_share : 2 * gain_share],
        inward_sum,
        vector_sums[2 * gain_share :],
        outward_sum,
        gate_up_sum,
        down_sum,
    )


def solution(mesh):
    in_specs = (
        P("bucket", "blk", None, None),
        P("bucket", None),
        P(("bucket", "blk")),
        P(("bucket", "blk")),
        P(("bucket", "blk"), None),
        P(("bucket", "blk")),
        P(("bucket", "blk"), None),
        P(("bucket", "blk"), None),
        P(("bucket", "blk"), None),
        P("bucket", "blk", None, None),
    )
    out_specs = (
        P("bucket", "blk", None, None),
        P("bucket", "blk", None, None),
        P(("bucket", "blk")),
        P(("bucket", "blk")),
        P(("bucket", "blk"), None),
        P(("bucket", "blk")),
        P(("bucket", "blk"), None),
        P(("bucket", "blk"), None),
        P(("bucket", "blk"), None),
    )
    body = shards_grouped if fits_groups(mesh) else shards_general
    return jax.shard_map(body, mesh=mesh, in_specs=in_specs, out_specs=out_specs, check_vma=False)
```

```python
import functools

import jax
import jax.numpy as jnp
from jax import lax
from jax.experimental import pallas as pl
from jax.experimental.pallas import tpu as pltpu
from jax.sharding import PartitionSpec as P

HEADS = 32
HEAD_DIM = 64
ROT = 16


epsilon = 1e-05
rotary_base = 10000.0
masked_score = -1e30


def shifted(value, axis, by):
    count = lax.axis_size(axis)
    pairs = [(i, i + by) for i in range(count) if 0 <= i + by < count]
    return lax.ppermute(value, axis, pairs)


def shifted_2(value, axis, steps):
    count = lax.axis_size(axis)
    pairs = [(source, (source + steps) % count) for source in range(count)]
    return lax.ppermute(value, axis, pairs)


def keep_same(value):
    return value


def transposed_times(left, right):
    return lax.dot_general(
        left, right, (((1,), (1,)), ((), ())), preferred_element_type=jnp.float32
    )


def times_transposed(left, right):
    return lax.dot_general(
        left, right, (((0,), (0,)), ((), ())), preferred_element_type=jnp.float32
    )


def rotary_tables(positions):
    half_rot = ROT // 2
    frequency = rotary_base ** (-(2.0 * jnp.arange(half_rot).astype(jnp.float32)) / ROT)
    angles = positions.astype(jnp.float32)[:, None] * frequency[None, :]
    return (jnp.cos(angles), jnp.sin(angles))


def rotate(values, cos_table, sine_table):
    half_rot = ROT // 2
    front_half = values[..., :half_rot]
    back_half = values[..., half_rot:ROT]
    return jnp.concatenate(
        [
            front_half * cos_table - back_half * sine_table,
            back_half * cos_table + front_half * sine_table,
            values[..., ROT:],
        ],
        axis=-1,
    )


def split_pairs(packed):
    rows_here, seq_count, both_width = packed.shape
    half_width = both_width // 2
    keys_part = packed[..., :half_width].reshape(rows_here, seq_count, HEADS, HEAD_DIM)
    values_part = packed[..., half_width:].reshape(rows_here, seq_count, HEADS, HEAD_DIM)
    return (keys_part, values_part)


def block_scores(queries, key_block, query_start, key_start):
    scores = jnp.einsum("tshd,ushd->shtu", queries, key_block, preferred_element_type=jnp.float32)
    query_pos = query_start + jnp.arange(queries.shape[0], dtype=jnp.int32)
    key_pos = key_start + jnp.arange(key_block.shape[0], dtype=jnp.int32)
    allowed = (key_pos[None, :] <= query_pos[:, None])[None, None]
    return (jnp.where(allowed, scores, masked_score), allowed)


def forward_block(carried, queries, key_block, value_block, query_start, key_start):
    running_max, running_sum, weighted = carried
    scores, allowed = block_scores(queries, key_block, query_start, key_start)
    new_max = jnp.maximum(running_max, jnp.max(scores, axis=-1))
    rescale = jnp.exp(running_max - new_max)
    weights = jnp.where(allowed, jnp.exp(scores - new_max[..., None]), 0.0)
    running_sum = running_sum * rescale + jnp.sum(weights, axis=-1)
    update = jnp.einsum(
        "shtu,ushd->tshd",
        weights.astype(jnp.bfloat16),
        value_block,
        preferred_element_type=jnp.float32,
    )
    weighted = weighted * jnp.transpose(rescale, (2, 0, 1))[..., None] + update
    return (new_max, running_sum, weighted)


def pair_grads(
    queries, out_grads, log_norm, deltas, key_block, value_block, query_start, key_start
):
    scores, allowed = block_scores(queries, key_block, query_start, key_start)
    probability = jnp.where(allowed, jnp.exp(scores - log_norm[..., None]), 0.0)
    value_grad = jnp.einsum(
        "shtu,tshd->ushd",
        probability.astype(jnp.bfloat16),
        out_grads,
        preferred_element_type=jnp.float32,
    )
    prob_grad = jnp.einsum(
        "tshd,ushd->shtu", out_grads, value_block, preferred_element_type=jnp.float32
    )
    score_grad = (probability * (prob_grad - deltas[..., None])).astype(jnp.bfloat16)
    query_grad = jnp.einsum(
        "shtu,ushd->tshd", score_grad, key_block, preferred_element_type=jnp.float32
    )
    key_grad = jnp.einsum(
        "shtu,tshd->ushd", score_grad, queries, preferred_element_type=jnp.float32
    )
    return (query_grad, key_grad, value_grad)


def over_blocks(running, incoming, unit_rows, handle):
    total_rows = incoming[0].shape[0]
    block_count = total_rows // unit_rows
    block_rows = total_rows // block_count
    stacked = tuple(
        (member.reshape((block_count, block_rows) + member.shape[1:]) for member in incoming)
    )

    def visit(carried, element):
        block_index, members = element
        return (handle(carried, members, block_index * block_rows), None)

    running, unused = lax.scan(visit, running, (jnp.arange(block_count, dtype=jnp.int32), stacked))
    return running


def shards_general(
    tokens,
    lengths,
    norm_gain,
    norm_shift,
    inward_weight,
    inward_bias,
    outward_weight,
    gate_up_weight,
    down_weight,
    cotangent,
):
    group_len = tokens.shape[1]
    seq_count = tokens.shape[2]
    model_width = tokens.shape[3]
    row_total = group_len * seq_count
    block_total = lax.axis_size("blk")
    position = lax.axis_index("blk")
    own_start = position * group_len
    longest = jnp.max(lengths[0])
    active = own_start < longest
    gathered = (
        lax.all_gather(inward_weight.astype(jnp.bfloat16), ("bucket", "blk"), axis=0, tiled=True),
        lax.all_gather(outward_weight.astype(jnp.bfloat16), ("bucket", "blk"), axis=0, tiled=True),
        lax.all_gather(gate_up_weight.astype(jnp.bfloat16), ("bucket", "blk"), axis=0, tiled=True),
        lax.all_gather(down_weight.astype(jnp.bfloat16), ("bucket", "blk"), axis=0, tiled=True),
        lax.all_gather(norm_gain.astype(jnp.bfloat16), ("bucket", "blk"), axis=0, tiled=True),
        lax.all_gather(norm_shift.astype(jnp.bfloat16), ("bucket", "blk"), axis=0, tiled=True),
        lax.all_gather(inward_bias.astype(jnp.bfloat16), ("bucket", "blk"), axis=0, tiled=True),
    )
    inward_full, outward_full, gate_up_full, down_full, gain_full, shift_full, bias_full = gathered
    inputs = tokens.reshape(row_total, model_width).astype(jnp.float32)
    centred = inputs - jnp.mean(inputs, axis=-1, keepdims=True)
    variance = jnp.mean(centred * centred, axis=-1, keepdims=True)
    inverse = lax.rsqrt(variance + epsilon)
    normal_hat = centred * inverse
    normed_low = (
        normal_hat * gain_full.astype(jnp.float32) + shift_full.astype(jnp.float32)
    ).astype(jnp.bfloat16)
    bias_float = bias_full.astype(jnp.float32)
    key_bias = jnp.pad(
        bias_float[2 * model_width :].reshape(HEADS, ROT), ((0, 0), (0, HEAD_DIM - ROT))
    ).reshape(model_width)
    full_bias = jnp.concatenate(
        [bias_float[:model_width], key_bias, bias_float[model_width : 2 * model_width]]
    )
    projected = jnp.dot(normed_low, inward_full, preferred_element_type=jnp.float32) + full_bias
    projected = projected.reshape(group_len, seq_count, 3, HEADS, HEAD_DIM)
    cos_table, sine_table = rotary_tables(own_start + jnp.arange(group_len, dtype=jnp.int32))
    cos_table = cos_table[:, None, None, :]
    sine_table = sine_table[:, None, None, :]
    query_scale = HEAD_DIM ** (-0.5)
    queries = (rotate(projected[:, :, 0], cos_table, sine_table) * query_scale).astype(jnp.bfloat16)
    keys_low = rotate(projected[:, :, 1], cos_table, sine_table).astype(jnp.bfloat16)
    values_low = projected[:, :, 2].astype(jnp.bfloat16)
    packed = jnp.concatenate(
        [
            keys_low.reshape(group_len, seq_count, model_width),
            values_low.reshape(group_len, seq_count, model_width),
        ],
        axis=-1,
    )

    def forward_handle(carried, members, key_start):
        keys_part, values_part = split_pairs(members[0])
        needed = active & (key_start <= own_start + group_len - 1)

        def forward_compute(state_in):
            return forward_block(state_in, queries, keys_part, values_part, own_start, key_start)

        return lax.cond(needed, forward_compute, keep_same, carried)

    start_state = (
        jnp.full((seq_count, HEADS, group_len), masked_score, jnp.float32),
        jnp.zeros((seq_count, HEADS, group_len), jnp.float32),
        jnp.zeros((group_len, seq_count, HEADS, HEAD_DIM), jnp.float32),
    )
    running_max, running_sum, weighted = over_blocks(
        start_state, (lax.all_gather(packed, "blk", axis=0, tiled=True),), group_len, forward_handle
    )
    bounded = jnp.maximum(running_sum, 1.0)
    log_norm = running_max + jnp.log(bounded)
    attended = weighted / jnp.transpose(bounded, (2, 0, 1))[..., None]
    attended_rows = attended.astype(jnp.bfloat16).reshape(row_total, model_width)
    gate_up = jnp.dot(normed_low, gate_up_full, preferred_element_type=jnp.float32)
    ff_width = gate_up.shape[1] // 2
    gate_part = gate_up[:, :ff_width]
    up_part = gate_up[:, ff_width:]
    sigmoid_gate = jax.nn.sigmoid(gate_part)
    silu_gate = gate_part * sigmoid_gate
    hidden_low = (silu_gate * up_part).astype(jnp.bfloat16)
    branch = jnp.dot(attended_rows, outward_full, preferred_element_type=jnp.float32) + jnp.dot(
        hidden_low, down_full, preferred_element_type=jnp.float32
    )
    query_pos = own_start + jnp.arange(group_len, dtype=jnp.int32)
    valid_rows = (
        (query_pos[:, None] < lengths[0][None, :]).astype(jnp.float32).reshape(row_total, 1)
    )
    layer_out = (inputs + valid_rows * branch).astype(jnp.bfloat16).reshape(tokens.shape)
    inward_back = gathered[0]
    outward_back = gathered[1]
    gate_up_back = gathered[2]
    down_back = gathered[3]
    gain_float = gathered[4].astype(jnp.float32)
    cotangent_rows = cotangent.reshape(row_total, model_width).astype(jnp.float32)
    branch_grad = (cotangent_rows * valid_rows).astype(jnp.bfloat16)
    hidden_grad = transposed_times(branch_grad, down_back)
    gate_grad = hidden_grad * up_part * (sigmoid_gate + silu_gate * (1.0 - sigmoid_gate))
    up_grad = hidden_grad * silu_gate
    gate_up_grad_low = jnp.concatenate([gate_grad, up_grad], axis=-1).astype(jnp.bfloat16)
    down_term = times_transposed(hidden_low, branch_grad)
    gate_up_term = times_transposed(normed_low, gate_up_grad_low)
    gate_up_sum, down_sum = (
        lax.psum_scatter(gate_up_term, ("bucket", "blk"), scatter_dimension=0, tiled=True),
        lax.psum_scatter(down_term, ("bucket", "blk"), scatter_dimension=0, tiled=True),
    )
    normed_grad = transposed_times(gate_up_grad_low, gate_up_back)
    attended_grad = (
        transposed_times(branch_grad, outward_back)
        .astype(jnp.bfloat16)
        .reshape(group_len, seq_count, HEADS, HEAD_DIM)
    )
    outward_term = times_transposed(attended_rows, branch_grad)
    deltas = jnp.transpose(
        jnp.sum(attended_grad.astype(jnp.float32) * attended, axis=-1), (1, 2, 0)
    )
    grad_zeros = jnp.zeros((group_len, seq_count, 2 * model_width), jnp.float32)
    query_zeros = jnp.zeros((group_len, seq_count, HEADS, HEAD_DIM), jnp.float32)

    def cycle_turn(turn_index, carried):
        visiting, sums_now, grads_now = carried
        owner_index = (position - turn_index) % block_total
        key_start = owner_index * group_len
        needed = active & (owner_index <= position)

        def cycle_compute(sums_in):
            keys_part, values_part = split_pairs(visiting)
            query_part, key_part, value_part = pair_grads(
                queries,
                attended_grad,
                log_norm,
                deltas,
                keys_part,
                values_part,
                own_start,
                key_start,
            )
            merged = jnp.concatenate(
                [
                    key_part.reshape(group_len, seq_count, model_width),
                    value_part.reshape(group_len, seq_count, model_width),
                ],
                axis=-1,
            )
            return (sums_in[0] + merged, sums_in[1] + query_part)

        sums_now, grads_now = lax.cond(needed, cycle_compute, keep_same, (sums_now, grads_now))
        visiting = shifted(visiting, "blk", 1)
        sums_now = shifted_2(sums_now.astype(jnp.bfloat16), "blk", 1).astype(sums_now.dtype)
        return (visiting, sums_now, grads_now)

    unused, pair_sums, query_grads = lax.fori_loop(
        0, block_total, cycle_turn, (packed, grad_zeros, query_zeros)
    )
    key_grad = pair_sums[..., :model_width].reshape(group_len, seq_count, HEADS, HEAD_DIM)
    value_grad = pair_sums[..., model_width:].reshape(group_len, seq_count, HEADS, HEAD_DIM)
    back_sine = -sine_table
    query_back = rotate(query_grads * query_scale, cos_table, back_sine)
    key_back = rotate(key_grad, cos_table, back_sine)
    projected_grad = (
        jnp.stack([query_back, key_back, value_grad], axis=2)
        .reshape(row_total, 3 * model_width)
        .astype(jnp.bfloat16)
    )
    inward_term = times_transposed(normed_low, projected_grad)
    column_sums = jnp.sum(projected_grad.astype(jnp.float32), axis=0)
    key_bias_grad = (
        column_sums[model_width : 2 * model_width]
        .reshape(HEADS, HEAD_DIM)[:, :ROT]
        .reshape(HEADS * ROT)
    )
    bias_term = jnp.concatenate(
        [column_sums[:model_width], column_sums[2 * model_width :], key_bias_grad]
    )
    normed_grad = normed_grad + transposed_times(projected_grad, inward_back)
    gain_term = jnp.sum(normed_grad * normal_hat, axis=0)
    shift_term = jnp.sum(normed_grad, axis=0)
    scaled_grad = normed_grad * gain_float
    input_grad = inverse * (
        scaled_grad
        - jnp.mean(scaled_grad, axis=-1, keepdims=True)
        - normal_hat * jnp.mean(scaled_grad * normal_hat, axis=-1, keepdims=True)
    )
    tokens_grad = (cotangent_rows + input_grad).astype(jnp.bfloat16).reshape(tokens.shape)
    inward_sum, outward_sum, bias_sum, gain_sum, shift_sum = (
        lax.psum_scatter(inward_term, ("bucket", "blk"), scatter_dimension=0, tiled=True),
        lax.psum_scatter(outward_term, ("bucket", "blk"), scatter_dimension=0, tiled=True),
        lax.psum_scatter(bias_term, ("bucket", "blk"), scatter_dimension=0, tiled=True),
        lax.psum_scatter(gain_term, ("bucket", "blk"), scatter_dimension=0, tiled=True),
        lax.psum_scatter(shift_term, ("bucket", "blk"), scatter_dimension=0, tiled=True),
    )
    return (
        layer_out,
        tokens_grad,
        gain_sum,
        shift_sum,
        inward_sum,
        bias_sum,
        outward_sum,
        gate_up_sum,
        down_sum,
    )


DEPTH = 4
PIECES = 2 * DEPTH
ROWS = 256
EXTRA = 16
LOCAL_HEADS = 4
HEAD_COLS = LOCAL_HEADS * HEAD_DIM
CORE = [(i, i ^ 1) for i in range(4)]
ACROSS_X = [(i, i ^ 2) for i in range(4)]
ACROSS_Y = [(i, i ^ 1) for i in range(8)]
MIB = 1024 * 1024


def fits_groups(mesh):
    return mesh.shape["bucket"] == 4 and mesh.shape["blk"] == 2 * DEPTH


def around(step):
    return [(z * 2 + y, ((z + step) % DEPTH) * 2 + y) for z in range(DEPTH) for y in range(2)]


def in_order(own, other, index, axis):
    return jnp.where(
        index == 0, jnp.stack([own, other], axis), jnp.stack([other, own], axis)
    )


def gather_pieces(value):
    own = [value]
    for step in range(1, DEPTH):
        own.append(lax.ppermute(value, "blk", around(step)))
    return own + [lax.ppermute(piece, "bucket", CORE) for piece in own]


def core_sums(own, other):
    other = lax.ppermute(other, "bucket", CORE)
    sums = [own[k].astype(jnp.float32) + other[k].astype(jnp.float32) for k in range(DEPTH)]
    return [sums[0]] + [value.astype(jnp.bfloat16) for value in sums[1:]]


def scatter_pieces(sums):
    total = sums[0]
    for step in range(1, DEPTH):
        got = lax.ppermute(sums[step], "blk", around(-step))
        total = total + got.astype(jnp.float32)
    return total


def after(value, *earlier):
    return lax.optimization_barrier((value,) + earlier)[0]


def one_of(value, index, axis):
    return lax.dynamic_index_in_dim(value, index, axis, False)


def summed(keep, send, over_x):
    send = send.astype(jnp.bfloat16)
    got = (
        lax.ppermute(send, "bucket", ACROSS_X) if over_x else lax.ppermute(send, "blk", ACROSS_Y)
    )
    return keep + got.astype(jnp.float32)


def rows_of_device(value, core, z):
    parts = [one_of(value, z, 0)]
    for step in range(1, DEPTH):
        chunk = one_of(value, (z + step) % DEPTH, 0).astype(jnp.bfloat16)
        parts.append(lax.ppermute(chunk, "blk", around(step)).astype(jnp.float32))
    stacked = jnp.stack(parts)
    ordered = jnp.concatenate(
        [lax.dynamic_slice_in_dim(stacked, (z - j) % DEPTH, 1, 0) for j in range(DEPTH)]
    )
    mine = one_of(ordered, core, 1)
    theirs = one_of(ordered, 1 - core, 1).astype(jnp.bfloat16)
    got = lax.ppermute(theirs, "bucket", CORE).astype(jnp.float32)
    return in_order(mine, got, core, 0)


def vector_sums(terms, x, y, core, z):
    for index, axis, name, pairs in ((x, 0, "bucket", ACROSS_X), (core, 0, "bucket", CORE)):
        keep, send = one_of(terms, index, axis), one_of(terms, 1 - index, axis)
        terms = keep + lax.ppermute(send, name, pairs)
    keep, send = one_of(terms, y, 1), one_of(terms, 1 - y, 1)
    terms = keep + lax.ppermute(send, "blk", ACROSS_Y)
    total = one_of(terms, z, 0)
    for step in range(1, DEPTH):
        total = total + lax.ppermute(one_of(terms, (z + step) % DEPTH, 0), "blk", around(step))
    return total


def dot_rows(left, right):
    return lax.dot_general(
        left, right, (((1,), (0,)), ((), ())), preferred_element_type=jnp.float32
    )


def params(limit, **extra):
    return pltpu.CompilerParams(vmem_limit_bytes=limit * MIB, **extra)


def cost(flops, moved, exps=0):
    return pl.CostEstimate(flops=flops // 64, bytes_accessed=moved // 64, transcendentals=exps // 64)


def piece_spec(width):
    return pl.BlockSpec((1, ROWS, width), lambda i: (i, 0, 0))


def whole_spec(shape):
    return pl.BlockSpec(shape, lambda i: (0,) * len(shape))


def remote(src, dst, sends, recvs, index, device):
    return pltpu.make_async_remote_copy(
        src_ref=src,
        dst_ref=dst,
        send_sem=sends.at[index],
        recv_sem=recvs.at[index],
        device_id=device,
        device_id_type=pl.DeviceIdType.MESH,
    )


def gather_kernel(
    x_ref,
    wi_ref,
    wg_ref,
    ro_ref,
    pieces,
    wi_out,
    wg_out,
    ro_out,
    group_s,
    group_r,
    across_s,
    across_r,
    rows_s,
    rows_r,
    up_s,
    down_s,
    piece_r,
    core_s,
    core_r,
    local_sems,
):
    bucket, blk = lax.axis_index("bucket"), lax.axis_index("blk")
    x, core = bucket // 2, bucket % 2
    z, y = blk // 2, blk % 2

    def device(xx, cc, zz, yy):
        return (xx * 2 + cc, zz * 2 + yy)

    x_mate, y_mate = device(1 - x, core, z, y), device(x, core, z, 1 - y)
    core_mate = device(x, 1 - core, z, y)
    members = [(flip, turn) for turn in (0, 1, 3, 2) for flip in (0, 1)]

    def target(flip, turn):
        return (core + flip) % 2, (z + turn) % DEPTH

    def source(flip, turn):
        return (core + flip) % 2, (z + DEPTH - turn) % DEPTH

    barrier = pltpu.get_barrier_semaphore()
    greeted = [device(x, *target(*m), y) for m in members[1:]] + [x_mate, y_mate]
    for mate in greeted:
        pl.semaphore_signal(
            barrier, inc=1, device_id=mate, device_id_type=pl.DeviceIdType.MESH
        )
    pl.semaphore_wait(barrier, len(greeted))

    started = []

    def begin(copy):
        copy.start()
        started.append(copy)
        return copy

    local = [
        pltpu.make_async_copy(wi_ref.at[core, z], wi_out.at[x, core, z, y], local_sems.at[0]),
        pltpu.make_async_copy(wg_ref.at[core, z], wg_out.at[x, core, z, y], local_sems.at[1]),
        pltpu.make_async_copy(ro_ref, ro_out.at[x, y], local_sems.at[2]),
        pltpu.make_async_copy(x_ref, pieces.at[0], local_sems.at[3]),
    ]
    for copy in local:
        copy.start()

    def send_group(which, ref, out):
        copies = {}
        for flip, turn in members[1:]:
            cc, zz = target(flip, turn)
            copies[flip, turn] = begin(
                remote(
                    ref.at[cc, zz],
                    out.at[x, core, z, y],
                    group_s,
                    group_r,
                    (which, flip * DEPTH + turn),
                    device(x, cc, zz, y),
                )
            )
        return copies

    def piece_copy(src, slot, sends, number, dz):
        return pltpu.make_async_remote_copy(
            src_ref=src,
            dst_ref=pieces.at[slot],
            send_sem=sends.at[number],
            recv_sem=piece_r.at[slot],
            device_id=device(x, core, z + dz, y),
            device_id_type=pl.DeviceIdType.MESH,
        )

    def core_copy(slot):
        src = x_ref if slot == 0 else pieces.at[slot]
        return remote(src, pieces.at[DEPTH + slot], core_s, core_r, slot, core_mate)

    ups = [piece_copy(x_ref if k == 0 else pieces.at[k], k + 1, up_s, k, 1) for k in range(3)]
    downs = [
        piece_copy(x_ref if k == 0 else pieces.at[DEPTH - k], 3 - k, down_s, k, -1)
        for k in range(3)
    ]

    def start_if(condition, copy):
        @pl.when(condition)
        def _():
            copy.start()

    def sent_if(condition, copy):
        @pl.when(condition)
        def _():
            copy.wait_send()

    inward = send_group(0, wi_ref, wi_out)
    start_if(z < DEPTH - 1, ups[0])
    start_if(z > 0, downs[0])
    core_copies = [core_copy(slot) for slot in range(DEPTH)]
    core_copies[0].start()
    rows_x = begin(remote(ro_ref, ro_out.at[x, y], rows_s, rows_r, 0, x_mate))
    rows_y = begin(remote(ro_ref, ro_out.at[x, y], rows_s, rows_r, 1, y_mate))
    gate_up = send_group(1, wg_ref, wg_out)

    def spread(which, ref, out, copies):
        pairs = {}
        for member in members:
            flip, turn = member
            cc, zz = source(flip, turn)
            if member == (0, 0):
                src = ref.at[core, z]
            else:
                copies[member].wait_recv()
                src = out.at[x, cc, zz, y]
            number = flip * DEPTH + turn
            pairs[member] = (
                begin(
                    remote(
                        src, out.at[x, cc, zz, y], across_s, across_r, (which, 0, number), x_mate
                    )
                ),
                begin(
                    remote(
                        src, out.at[x, cc, zz, y], across_s, across_r, (which, 1, number), y_mate
                    )
                ),
            )
        return pairs

    def corner(which, out, pairs):
        copies = []
        for member in members:
            flip, turn = member
            cc, zz = source(flip, turn)
            number = flip * DEPTH + turn
            if flip == 0:
                pairs[member][1].wait_recv()
                part = out.at[x, cc, zz, 1 - y]
                mate = x_mate
            else:
                pairs[member][0].wait_recv()
                part = out.at[1 - x, cc, zz, y]
                mate = y_mate
            copies.append(
                begin(remote(part, part, across_s, across_r, (which, 2, number), mate))
            )
        return copies

    inward_pairs = spread(0, wi_ref, wi_out, inward)

    @pl.when(z > 0)
    def _():
        ups[0].wait_recv()
        core_copies[1].start()

    start_if((z > 0) & (z < DEPTH - 1), ups[1])

    @pl.when(z < DEPTH - 1)
    def _():
        downs[0].wait_recv()
        core_copies[3].start()

    start_if((z > 0) & (z < DEPTH - 1), downs[1])

    inward_corner = corner(0, wi_out, inward_pairs)
    gate_up_pairs = spread(1, wg_ref, wg_out, gate_up)

    ups[1].wait_recv()
    core_copies[2].start()
    start_if(z == 2, ups[2])
    start_if(z == 1, downs[2])

    cut = (ro_ref.shape[0] // 32) * 16
    rows_y.wait_recv()
    low = ro_out.at[x, 1 - y, pl.ds(0, cut)]
    low_copy = begin(remote(low, low, rows_s, rows_r, 2, x_mate))
    rows_x.wait_recv()
    high = ro_out.at[1 - x, y, pl.ds(cut, ro_ref.shape[0] - cut)]
    high_copy = begin(remote(high, high, rows_s, rows_r, 3, y_mate))
    gate_up_corner = corner(1, wg_out, gate_up_pairs)

    @pl.when(z == DEPTH - 1)
    def _():
        ups[2].wait_recv()
        core_copies[3].start()

    @pl.when(z == 0)
    def _():
        downs[2].wait_recv()
        core_copies[1].start()

    for pairs in (inward_pairs, gate_up_pairs):
        for flip, turn in members:
            pairs[flip, turn][0 if flip == 0 else 1].wait_recv()
    for copy in inward_corner + gate_up_corner + [low_copy, high_copy]:
        copy.wait_recv()
    for copy in core_copies:
        copy.wait_recv()
        copy.wait_send()
    for copy in started:
        copy.wait_send()
    sent_if(z < DEPTH - 1, ups[0])
    sent_if(z > 0, downs[0])
    sent_if((z > 0) & (z < DEPTH - 1), ups[1])
    sent_if((z > 0) & (z < DEPTH - 1), downs[1])
    sent_if(z == 2, ups[2])
    sent_if(z == 1, downs[2])
    for copy in local:
        copy.wait()


def gather(tokens, inward, gate_up, rows_out):
    anywhere = pl.BlockSpec(memory_space=pl.ANY)
    low = jnp.bfloat16
    dma = pltpu.SemaphoreType.DMA
    return pl.pallas_call(
        gather_kernel,
        in_specs=[anywhere] * 4,
        out_specs=[anywhere] * 4,
        out_shape=[
            jax.ShapeDtypeStruct((PIECES,) + tokens.shape, low),
            jax.ShapeDtypeStruct((2, 2, DEPTH, 2) + inward.shape[2:], low),
            jax.ShapeDtypeStruct((2, 2, DEPTH, 2) + gate_up.shape[2:], low),
            jax.ShapeDtypeStruct((2, 2) + rows_out.shape, low),
        ],
        scratch_shapes=[
            dma((2, PIECES)),
            dma((2, PIECES)),
            dma((2, 3, PIECES)),
            dma((2, 3, PIECES)),
            dma((4,)),
            dma((4,)),
            dma((3,)),
            dma((3,)),
            dma((DEPTH,)),
            dma((DEPTH,)),
            dma((DEPTH,)),
            dma((4,)),
        ],
        compiler_params=params(32, collective_id=0, has_side_effects=True),
        cost_estimate=cost(0, 64 * MIB),
        name="gather",
    )(tokens, inward, gate_up, rows_out)


def inward_rows(ref):
    blocks, rows, columns = ref.shape
    return ref[:, : rows - EXTRA].reshape(blocks * (rows - EXTRA), columns)


def outward_rows(ref):
    blocks, rows, columns = ref.shape
    return ref[:, :HEAD_DIM].reshape(blocks * HEAD_DIM, columns)


def down_rows(ref):
    blocks, rows, columns = ref.shape
    return ref[:, HEAD_DIM:].reshape(blocks * (rows - HEAD_DIM), columns)


def normalised(rows):
    inputs = rows.astype(jnp.float32)
    centred = inputs - jnp.mean(inputs, axis=-1, keepdims=True)
    variance = jnp.mean(centred * centred, axis=-1, keepdims=True)
    inverse = lax.rsqrt(variance + epsilon)
    return centred * inverse, inverse


def turned(values, cos_ref, first_ref, second_ref, sign):
    half = ROT // 2
    cos = jnp.concatenate([cos_ref[0], cos_ref[0]], 0)
    first = jnp.concatenate([first_ref[0], first_ref[0]], 0)
    second = jnp.concatenate([second_ref[0], second_ref[0]], 0)
    ahead = pltpu.roll(values, HEAD_COLS - half, 1)
    behind = pltpu.roll(values, half, 1)
    return values * cos + sign * (ahead * first + behind * second)


def project_kernel(
    x_ref, gain_ref, shift_ref, w_ref, bias_ref, cos_ref, first_ref, second_ref, n_ref, q_ref, kv_ref
):
    hat, _ = normalised(x_ref[0])
    normed = (hat * gain_ref[...] + shift_ref[...]).astype(jnp.bfloat16)
    n_ref[0] = normed
    projected = dot_rows(normed, inward_rows(w_ref)) + bias_ref[...]
    tables = (cos_ref, first_ref, second_ref)
    query = turned(projected[:, :HEAD_COLS], *tables, 1.0) * (HEAD_DIM**-0.5)
    key = turned(projected[:, HEAD_COLS : 2 * HEAD_COLS], *tables, 1.0)
    q_ref[0] = query.astype(jnp.bfloat16)
    kv_ref[0, :, :HEAD_COLS] = key.astype(jnp.bfloat16)
    kv_ref[0, :, HEAD_COLS:] = projected[:, 2 * HEAD_COLS :].astype(jnp.bfloat16)


def project(pieces, gain, shift, weight, bias, tables):
    width = pieces.shape[-1]
    table_spec = pl.BlockSpec((1,) + tables[0].shape[1:], lambda i: (i % DEPTH, 0, 0))
    return pl.pallas_call(
        project_kernel,
        grid=(PIECES,),
        in_specs=[
            piece_spec(width),
            whole_spec((1, width)),
            whole_spec((1, width)),
            whole_spec(weight.shape),
            whole_spec(bias.shape),
            table_spec,
            table_spec,
            table_spec,
        ],
        out_specs=[piece_spec(width), piece_spec(HEAD_COLS), piece_spec(2 * HEAD_COLS)],
        out_shape=[
            jax.ShapeDtypeStruct((PIECES, ROWS, width), jnp.bfloat16),
            jax.ShapeDtypeStruct((PIECES, ROWS, HEAD_COLS), jnp.bfloat16),
            jax.ShapeDtypeStruct((PIECES, ROWS, 2 * HEAD_COLS), jnp.bfloat16),
        ],
        compiler_params=params(48),
        cost_estimate=cost(2 * PIECES * ROWS * width * 3 * HEAD_COLS, 24 * MIB),
        name="project",
    )(pieces, gain, shift, weight, bias, *tables)


def feed_kernel(n_ref, w_ref, gate_ref, up_ref, hidden_ref):
    both = dot_rows(n_ref[0], w_ref[...])
    hidden = both.shape[1] // 2
    gate, up = both[:, :hidden], both[:, hidden:]
    gate_ref[0] = gate
    up_ref[0] = up
    hidden_ref[0] = (gate * jax.nn.sigmoid(gate) * up).astype(jnp.bfloat16)


def feed(normed, weight):
    width = normed.shape[-1]
    hidden = weight.shape[1] // 2
    return pl.pallas_call(
        feed_kernel,
        grid=(PIECES,),
        in_specs=[piece_spec(width), whole_spec(weight.shape)],
        out_specs=[piece_spec(hidden)] * 3,
        out_shape=[
            jax.ShapeDtypeStruct((PIECES, ROWS, hidden), jnp.float32),
            jax.ShapeDtypeStruct((PIECES, ROWS, hidden), jnp.float32),
            jax.ShapeDtypeStruct((PIECES, ROWS, hidden), jnp.bfloat16),
        ],
        compiler_params=params(48),
        cost_estimate=cost(4 * PIECES * ROWS * width * hidden, 28 * MIB),
        name="feed",
    )(normed, weight)


def store_split(value, own_ref, other_ref):
    late = pl.program_id(0) >= DEPTH

    @pl.when(jnp.logical_not(late))
    def _():
        other_ref[0] = value

    @pl.when(late)
    def _():
        own_ref[0] = value


def other_first(width):
    return pl.BlockSpec((1, ROWS, width), lambda i: ((i + DEPTH) % PIECES, 0, 0))


def split_specs(width):
    return [
        pl.BlockSpec((1, ROWS, width), lambda i: (jnp.maximum(i - DEPTH, 0), 0, 0)),
        pl.BlockSpec((1, ROWS, width), lambda i: (jnp.minimum(i, DEPTH - 1), 0, 0)),
    ]


def branch_kernel(a_ref, h_ref, w_ref, own_ref, other_ref):
    term = dot_rows(a_ref[0], outward_rows(w_ref)) + dot_rows(h_ref[0], down_rows(w_ref))
    store_split(term.astype(jnp.bfloat16), own_ref, other_ref)


def branch_terms(attended, hidden, rows_out):
    width = rows_out.shape[-1]
    return pl.pallas_call(
        branch_kernel,
        grid=(PIECES,),
        in_specs=[
            other_first(HEAD_COLS),
            other_first(hidden.shape[-1]),
            whole_spec(rows_out.shape),
        ],
        out_specs=split_specs(width),
        out_shape=[jax.ShapeDtypeStruct((DEPTH, ROWS, width), jnp.bfloat16)] * 2,
        compiler_params=params(48),
        cost_estimate=cost(2 * PIECES * ROWS * width * (HEAD_COLS + hidden.shape[-1]), 16 * MIB),
        name="branch_terms",
    )(attended, hidden, rows_out)


def back_kernel(g_ref, gate_ref, up_ref, w_ref, a_ref, gu_ref):
    grad = g_ref[0]
    a_ref[0] = transposed_times(grad, outward_rows(w_ref)).astype(jnp.bfloat16)
    hidden_grad = transposed_times(grad, down_rows(w_ref))
    gate = gate_ref[0]
    sig = jax.nn.sigmoid(gate)
    silu = gate * sig
    gate_grad = hidden_grad * up_ref[0] * (sig + silu * (1.0 - sig))
    up_grad = hidden_grad * silu
    gu_ref[0] = jnp.concatenate([gate_grad, up_grad], 1).astype(jnp.bfloat16)


def back(grads, gate, up, rows_out):
    width = rows_out.shape[-1]
    hidden = gate.shape[-1]
    return pl.pallas_call(
        back_kernel,
        grid=(PIECES,),
        in_specs=[
            piece_spec(width),
            piece_spec(hidden),
            piece_spec(hidden),
            whole_spec(rows_out.shape),
        ],
        out_specs=[piece_spec(HEAD_COLS), piece_spec(2 * hidden)],
        out_shape=[
            jax.ShapeDtypeStruct((PIECES, ROWS, HEAD_COLS), jnp.bfloat16),
            jax.ShapeDtypeStruct((PIECES, ROWS, 2 * hidden), jnp.bfloat16),
        ],
        compiler_params=params(48),
        cost_estimate=cost(2 * PIECES * ROWS * width * (HEAD_COLS + hidden), 28 * MIB),
        name="back",
    )(grads, gate, up, rows_out)


def pair_rows(block):
    lane = lax.broadcasted_iota(jnp.int32, block.shape, 1)
    zero = jnp.zeros_like(block)
    return jnp.concatenate(
        [jnp.where(lane < HEAD_DIM, block, zero), jnp.where(lane < HEAD_DIM, zero, block)], 0
    )


def pair_lanes(rows):
    half = rows.shape[0] // 2
    lane = lax.broadcasted_iota(jnp.int32, (half, rows.shape[1]), 1)
    return jnp.where(lane < HEAD_DIM, rows[:half], rows[half:])


def block_probs(queries, keys, last, y):
    scores = transposed_times(queries, keys)
    rows, columns = scores.shape
    size = rows // 2
    row = lax.broadcasted_iota(jnp.int32, (rows, 2 * size), 0) % size
    column = lax.broadcasted_iota(jnp.int32, (rows, 2 * size), 1)
    allowed = (column <= row) | ((column >= size) & (y == 1))
    tail = jnp.where(allowed, scores[:, last * 2 * size :], masked_score)
    scores = tail if last == 0 else jnp.concatenate([scores[:, : last * 2 * size], tail], 1)
    weights = jnp.exp(scores - jnp.max(scores, axis=-1, keepdims=True))
    return weights * (1.0 / jnp.sum(weights, axis=-1, keepdims=True))


def both_columns(own_ref, other_ref, z, count):
    blocks = []
    for j in range(count):
        at = (z + DEPTH - j) % DEPTH
        blocks += [own_ref[0, at, 0], other_ref[0, at, 0]]
    return jnp.concatenate(blocks, 0)


def attend_kernel(place_ref, q_ref, k_ref, v_ref, ok_ref, ov_ref, out_ref):
    z, y = place_ref[0], place_ref[1]
    keys = both_columns(k_ref, ok_ref, z, DEPTH)
    values = both_columns(v_ref, ov_ref, z, DEPTH)
    size = keys.shape[0] // DEPTH
    for j in range(DEPTH):
        at = (z + DEPTH - j) % DEPTH
        count = (j + 1) * size
        probs = block_probs(pair_rows(q_ref[0, at, 0]), keys[:count], j, y)
        out = dot_rows(probs.astype(jnp.bfloat16), values[:count])
        out_ref[0, at, 0] = pair_lanes(out).astype(jnp.bfloat16)


def attend_back_kernel(
    place_ref,
    q_ref,
    k_ref,
    v_ref,
    ok_ref,
    ov_ref,
    grad_ref,
    dq_ref,
    dk_ref,
    dv_ref,
    odk_ref,
    odv_ref,
    key_sum,
    value_sum,
):
    z, y = place_ref[0], place_ref[1]
    keys = both_columns(k_ref, ok_ref, z, DEPTH)
    values = both_columns(v_ref, ov_ref, z, DEPTH)
    size = keys.shape[0] // DEPTH
    half = size // 2
    for j in reversed(range(DEPTH)):
        at = (z + DEPTH - j) % DEPTH
        count = (j + 1) * size
        queries = pair_rows(q_ref[0, at, 0])
        grads = pair_rows(grad_ref[0, at, 0])
        probs = block_probs(queries, keys[:count], j, y)
        low = probs.astype(jnp.bfloat16)
        prob_grad = transposed_times(grads, values[:count])
        delta = jnp.sum(low.astype(jnp.float32) * prob_grad, axis=-1, keepdims=True)
        score_grad = (probs * (prob_grad - delta)).astype(jnp.bfloat16)
        dq_ref[0, at, 0] = pair_lanes(dot_rows(score_grad, keys[:count]))
        key_term = times_transposed(score_grad, queries)
        value_term = times_transposed(low, grads)
        if j == DEPTH - 1:
            key_sum[...] = key_term
            value_sum[...] = value_term
        else:
            key_sum[:count] += key_term
            value_sum[:count] += value_term
    for j in range(DEPTH):
        at = (z + DEPTH - j) % DEPTH
        low = j * size
        dk_ref[0, at, 0] = key_sum[low : low + half]
        dv_ref[0, at, 0] = value_sum[low : low + half]
        odk_ref[0, at, 0] = key_sum[low + half : low + size].astype(jnp.bfloat16)
        odv_ref[0, at, 0] = value_sum[low + half : low + size].astype(jnp.bfloat16)


def sequence_specs(seqs, length):
    def spec(first):
        return pl.BlockSpec(
            (1, DEPTH, 1, length, 2 * HEAD_DIM), lambda b, s, p, place: (b, 0, s, 0, first + p)
        )

    return spec(0), spec(LOCAL_HEADS // 2)


def as_sequences(value, seqs):
    return value.reshape(2, DEPTH, seqs, ROWS // seqs, value.shape[-1])


def attend(place, queries, pairs, other_pairs, seqs):
    queries, pairs, other_pairs = (as_sequences(v, seqs) for v in (queries, pairs, other_pairs))
    first, second = sequence_specs(seqs, ROWS // seqs)
    out = pl.pallas_call(
        attend_kernel,
        grid_spec=pltpu.PrefetchScalarGridSpec(
            num_scalar_prefetch=1,
            grid=(2, seqs, LOCAL_HEADS // 2),
            in_specs=[first, first, second, first, second],
            out_specs=first,
        ),
        out_shape=jax.ShapeDtypeStruct(queries.shape, jnp.bfloat16),
        compiler_params=params(48),
        cost_estimate=cost(4 * 8 * 2 * 2 * 256 * 2560 * 128, 8 * MIB, 8 * 256 * 2560),
        name="attend",
    )(place, queries, pairs, pairs, other_pairs, other_pairs)
    return out.reshape(PIECES, ROWS, HEAD_COLS)


def attend_back(place, queries, pairs, other_pairs, grads, seqs):
    queries, pairs, other_pairs, grads = (
        as_sequences(v, seqs) for v in (queries, pairs, other_pairs, grads)
    )
    length = ROWS // seqs
    first, second = sequence_specs(seqs, length)
    wide = jax.ShapeDtypeStruct(queries.shape, jnp.float32)
    narrow = jax.ShapeDtypeStruct(queries.shape, jnp.bfloat16)
    outs = pl.pallas_call(
        attend_back_kernel,
        grid_spec=pltpu.PrefetchScalarGridSpec(
            num_scalar_prefetch=1,
            grid=(2, seqs, LOCAL_HEADS // 2),
            in_specs=[first, first, second, first, second, first],
            out_specs=[first] * 5,
            scratch_shapes=[
                pltpu.VMEM((2 * DEPTH * length, 2 * HEAD_DIM), jnp.float32),
                pltpu.VMEM((2 * DEPTH * length, 2 * HEAD_DIM), jnp.float32),
            ],
        ),
        out_shape=[wide, wide, wide, narrow, narrow],
        compiler_params=params(48),
        cost_estimate=cost(10 * 8 * 2 * 2 * 256 * 2560 * 128, 16 * MIB, 8 * 256 * 2560),
        name="attend_back",
    )(place, queries, pairs, pairs, other_pairs, other_pairs, grads)
    return [v.reshape(PIECES, ROWS, HEAD_COLS) for v in outs]


def input_grad_kernel(
    dq_ref,
    dk_ref,
    dv_ref,
    odk_ref,
    odv_ref,
    gu_ref,
    x_ref,
    wi_ref,
    wg_ref,
    cos_ref,
    first_ref,
    second_ref,
    pg_ref,
    own_ref,
    other_ref,
    gain_ref,
    shift_ref,
    bias_ref,
):
    tables = (cos_ref, first_ref, second_ref)
    query = turned(dq_ref[0] * (HEAD_DIM**-0.5), *tables, -1.0)
    key = turned(dk_ref[0] + odk_ref[0].astype(jnp.float32), *tables, -1.0)
    value = dv_ref[0] + odv_ref[0].astype(jnp.float32)
    low = jnp.concatenate([query, key, value], 1).astype(jnp.bfloat16)
    pg_ref[0] = low
    grad = transposed_times(low, inward_rows(wi_ref))
    grad += transposed_times(gu_ref[0], wg_ref[...])
    store_split(grad.astype(jnp.bfloat16), own_ref, other_ref)
    hat, _ = normalised(x_ref[0])

    @pl.when(pl.program_id(0) == 0)
    def _():
        gain_ref[...] = jnp.zeros_like(gain_ref)
        shift_ref[...] = jnp.zeros_like(shift_ref)
        bias_ref[...] = jnp.zeros_like(bias_ref)

    gain_ref[...] += jnp.sum(grad * hat, axis=0, keepdims=True)
    shift_ref[...] += jnp.sum(grad, axis=0, keepdims=True)
    bias_ref[...] += jnp.sum(low.astype(jnp.float32), axis=0, keepdims=True)


def input_grads(parts, other_key, other_value, gate_up_grad, pieces, weights, tables):
    width = pieces.shape[-1]
    hidden = gate_up_grad.shape[-1]
    table_spec = pl.BlockSpec((1,) + tables[0].shape[1:], lambda i: (i % DEPTH, 0, 0))
    return pl.pallas_call(
        input_grad_kernel,
        grid=(PIECES,),
        in_specs=[other_first(HEAD_COLS)] * 5
        + [other_first(hidden)]
        + [other_first(width)]
        + [whole_spec(w.shape) for w in weights]
        + [table_spec] * 3,
        out_specs=[other_first(3 * HEAD_COLS)]
        + split_specs(width)
        + [
            whole_spec((1, width)),
            whole_spec((1, width)),
            whole_spec((1, 3 * HEAD_COLS)),
        ],
        out_shape=[jax.ShapeDtypeStruct((PIECES, ROWS, 3 * HEAD_COLS), jnp.bfloat16)]
        + [jax.ShapeDtypeStruct((DEPTH, ROWS, width), jnp.bfloat16)] * 2
        + [
            jax.ShapeDtypeStruct((1, width), jnp.float32),
            jax.ShapeDtypeStruct((1, width), jnp.float32),
            jax.ShapeDtypeStruct((1, 3 * HEAD_COLS), jnp.float32),
        ],
        compiler_params=params(56),
        cost_estimate=cost(2 * PIECES * ROWS * width * (3 * HEAD_COLS + hidden), 48 * MIB),
        name="input_grads",
    )(*parts, other_key, other_value, gate_up_grad, pieces, *weights, *tables)


def rows_kernel(first, last, place_ref, left_ref, right_ref, out_ref):
    term = times_transposed(left_ref[...], right_ref[:, first:last])
    out_ref[0] = term.astype(out_ref.dtype)


def split_rows_kernel(first, last, place_ref, left_ref, right_ref, keep_ref, send_ref):
    y = place_ref[1]
    term = times_transposed(left_ref[...], right_ref[:, first:last])
    rows = term.shape[0] // 4
    even = jnp.concatenate([term[:rows], term[2 * rows : 3 * rows]], 0)
    odd = jnp.concatenate([term[rows : 2 * rows], term[3 * rows :]], 0)
    keep_ref[0] = jnp.where(y == 0, even, odd)
    send_ref[0] = jnp.where(y == 0, odd, even).astype(jnp.bfloat16)


def weight_grad(place, left, right, first, last, part):
    total, width = left.shape
    columns = last - first
    blocks = PIECES if part == "split" else PIECES // 2
    if part == "split":
        where = lambda i, place: (0, i)
    elif part == "keep":
        where = lambda i, place: (0, place[2] * DEPTH + i)
    else:
        where = lambda i, place: (0, (1 - place[2]) * DEPTH + i)
    size = width // PIECES
    high = size // 2 if part == "split" else size
    spec = pl.BlockSpec((1, high, columns), lambda i, place: (i, 0, 0))
    shape = (blocks, high, columns)
    if part == "split":
        specs = [spec, spec]
        shapes = [
            jax.ShapeDtypeStruct(shape, jnp.float32),
            jax.ShapeDtypeStruct(shape, jnp.bfloat16),
        ]
    else:
        specs = spec
        shapes = jax.ShapeDtypeStruct(shape, jnp.float32 if part == "keep" else jnp.bfloat16)
    return pl.pallas_call(
        functools.partial(
            split_rows_kernel if part == "split" else rows_kernel, first, last
        ),
        grid_spec=pltpu.PrefetchScalarGridSpec(
            num_scalar_prefetch=1,
            grid=(blocks,),
            in_specs=[
                pl.BlockSpec((total, size), where),
                pl.BlockSpec(right.shape, lambda i, place: (0, 0)),
            ],
            out_specs=specs,
        ),
        out_shape=shapes,
        compiler_params=params(48),
        cost_estimate=cost(2 * total * size * blocks * columns, 10 * MIB),
        name="weight_grad_" + part,
    )(place, left, right)


def lane_tables(positions):
    half = ROT // 2
    place = jnp.arange(HEAD_COLS, dtype=jnp.int32) % HEAD_DIM
    power = (place % half).astype(jnp.float32)
    frequency = jnp.where(place < ROT, rotary_base ** (-(2.0 * power) / ROT), 0.0)
    angles = positions.astype(jnp.float32)[..., None] * frequency
    sine = jnp.sin(angles)
    return (
        jnp.cos(angles),
        jnp.where(place < half, -sine, 0.0),
        jnp.where((place >= half) & (place < ROT), sine, 0.0),
    )


def shards_grouped(
    tokens,
    lengths,
    norm_gain,
    norm_shift,
    inward_weight,
    inward_bias,
    outward_weight,
    gate_up_weight,
    down_weight,
    cotangent,
):
    group_len, seqs, width = tokens.shape[1:]
    bucket, blk = lax.axis_index("bucket"), lax.axis_index("blk")
    x, core = bucket // 2, bucket % 2
    z, y = blk // 2, blk % 2

    own_rows = inward_weight.shape[0]
    hidden_each = gate_up_weight.shape[1] // (2 * 2 * 2 * DEPTH)
    gain_share, bias_share = norm_gain.shape[0], inward_bias.shape[0]
    shares = jnp.concatenate([norm_gain, norm_shift, inward_bias]).astype(jnp.bfloat16)
    shares = jnp.pad(shares, (0, 3 * HEAD_COLS - shares.shape[0]))
    inward = inward_weight.astype(jnp.bfloat16).reshape(own_rows, 3, 2, 2, DEPTH, 2 * HEAD_DIM)
    inward = jnp.transpose(inward, (3, 4, 0, 1, 2, 5)).reshape(2, DEPTH, own_rows, 3 * HEAD_COLS)
    inward = jnp.concatenate(
        [inward, jnp.broadcast_to(shares, (2, DEPTH, EXTRA, 3 * HEAD_COLS))], 2
    )
    gate_up = gate_up_weight.astype(jnp.bfloat16).reshape(own_rows, 2, 2, 2, DEPTH, hidden_each)
    gate_up = jnp.transpose(gate_up, (3, 4, 0, 1, 2, 5)).reshape(
        2, DEPTH, own_rows, 4 * hidden_each
    )
    rows_out = jnp.concatenate([outward_weight, down_weight]).astype(jnp.bfloat16)
    own_tokens = jnp.transpose(tokens[0], (1, 0, 2))
    pieces, inward, gate_up, rows_out = gather(
        own_tokens.reshape(ROWS, width), inward, gate_up, rows_out
    )
    vectors = inward[..., own_rows, :].reshape(-1, 3 * HEAD_COLS).astype(jnp.float32)
    inward = inward.reshape((-1,) + inward.shape[4:])
    gate_up = gate_up.reshape(width, -1)
    rows_out = rows_out.reshape((-1,) + rows_out.shape[2:])

    gain = vectors[:, :gain_share].reshape(1, width)
    shift = vectors[:, gain_share : 2 * gain_share].reshape(1, width)
    bias = vectors[:, 2 * gain_share : 2 * gain_share + bias_share].reshape(-1)

    def own_columns(values, each):
        split = values.reshape(2, 2, DEPTH, each)
        return one_of(one_of(split, core, 1), z, 1)

    key_bias = jnp.pad(
        own_columns(bias[2 * width :], 2 * ROT).reshape(LOCAL_HEADS, ROT),
        ((0, 0), (0, HEAD_DIM - ROT)),
    )
    own_bias = jnp.concatenate(
        [
            own_columns(bias[:width], 2 * HEAD_DIM).reshape(-1),
            key_bias.reshape(-1),
            own_columns(bias[width : 2 * width], 2 * HEAD_DIM).reshape(-1),
        ]
    ).reshape(1, -1)

    position = blk * group_len + jnp.arange(group_len, dtype=jnp.int32)
    valid = (position[None, :] < lengths[0][:, None]).astype(jnp.float32)[..., None]
    own_cotangent = jnp.transpose(cotangent[0], (1, 0, 2)).astype(jnp.float32)
    own_grad = (own_cotangent * valid).astype(jnp.bfloat16)
    grads = after(own_grad.reshape(ROWS, width), pieces)
    grads = jnp.stack(gather_pieces(grads))

    turns = (z - jnp.arange(DEPTH, dtype=jnp.int32)) % DEPTH
    tables = lane_tables(
        ((2 * turns + y) * group_len)[:, None] + jnp.arange(group_len, dtype=jnp.int32)
    )
    place = jnp.stack([z, y, x]).astype(jnp.int32)

    normed, queries, pairs = project(pieces, gain, shift, inward, own_bias, tables)
    other_pairs = lax.ppermute(pairs, "blk", ACROSS_Y)
    gate, up, hidden = feed(normed, gate_up)
    attended = attend(place, after(queries, hidden), pairs, other_pairs, seqs)
    branch_own, branch_other = branch_terms(attended, hidden, rows_out)
    branch_sums = core_sums(branch_own, branch_other)
    branch = scatter_pieces(branch_sums)
    branch = branch.reshape(seqs, group_len, width)
    inputs = own_tokens.astype(jnp.float32)
    layer_out = (inputs + valid * branch).astype(jnp.bfloat16)

    attended_grad, gate_up_grad = back(after(grads, branch_own), gate, up, rows_out)
    attended_grad = after(attended_grad, *branch_sums)
    dq, dk, dv, other_dk, other_dv = attend_back(
        place, queries, pairs, other_pairs, attended_grad, seqs
    )
    got_dk = lax.ppermute(other_dk, "blk", ACROSS_Y)
    got_dv = lax.ppermute(other_dv, "blk", ACROSS_Y)
    total = PIECES * ROWS
    flat_normed = after(normed, other_dk).reshape(total, width)
    flat_grads = after(grads, other_dk).reshape(total, width)

    def row_sums(right):
        rows, columns = own_rows, right.shape[-1]
        right = right.reshape(total, columns)
        cut = -(-columns // 256) * 128
        send = weight_grad(place, flat_normed, right, 0, cut, "send")
        y_keep, y_send = weight_grad(place, flat_normed, right, cut, columns, "split")
        keep = weight_grad(place, flat_normed, right, 0, cut, "keep")
        first = summed(keep, send, True).reshape(2, DEPTH, 2, rows, -1)
        first = summed(one_of(first, y, 2), one_of(first, 1 - y, 2), False)
        second = summed(y_keep, y_send, False).reshape(2, 2, DEPTH, rows, -1)
        second = summed(one_of(second, x, 0), one_of(second, 1 - x, 0), True)
        return jnp.transpose(jnp.concatenate([first, second], -1), (1, 0, 2, 3))

    def device_rows(term, parts):
        term = rows_of_device(term, core, z).reshape(2, DEPTH, own_rows, parts, 2, -1)
        return jnp.transpose(term, (2, 3, 4, 0, 1, 5)).reshape(own_rows, -1)

    gate_up_term = row_sums(gate_up_grad)
    outward_term = times_transposed(attended.reshape(total, -1), flat_grads)
    down_term = times_transposed(hidden.reshape(total, -1), flat_grads)

    def owner_sums(term):
        term = term.reshape(2, 2, -1, width)
        term = summed(one_of(term, x, 0), one_of(term, 1 - x, 0), True)
        return summed(one_of(term, y, 0), one_of(term, 1 - y, 0), False)

    outward_sum = owner_sums(outward_term)
    down_sum = owner_sums(down_term)
    projected_grad, normed_own, normed_other, gain_term, shift_term, bias_term = input_grads(
        (after(dq, branch), dk, dv),
        got_dk,
        got_dv,
        gate_up_grad,
        pieces,
        (inward, gate_up),
        tables,
    )
    normed_sums = core_sums(normed_own, normed_other)
    normed_grad = scatter_pieces(normed_sums).reshape(seqs, group_len, width)
    inward_term = row_sums(after(projected_grad, *normed_sums))
    gate_up_sum = device_rows(gate_up_term, 2)
    inward_sum = device_rows(inward_term, 3)

    bias_parts = bias_term.reshape(3, 2, 1, 1, 2 * HEAD_DIM)
    here = (
        (jnp.arange(2)[:, None] == core) & (jnp.arange(DEPTH)[None, :] == z)
    ).astype(jnp.float32)[None, None, :, :, None]
    spread = bias_parts * here
    key_rot = spread[1].reshape(2, 2, DEPTH, 2, HEAD_DIM)[..., :ROT]
    bias_all = jnp.concatenate(
        [spread[0].reshape(-1), spread[2].reshape(-1), key_rot.reshape(-1)]
    )
    grid = (2, 2, DEPTH, 2, -1)
    vector_sum = vector_sums(
        jnp.concatenate(
            [gain_term.reshape(grid), shift_term.reshape(grid), bias_all.reshape(grid)], -1
        ),
        x,
        y,
        core,
        z,
    )

    hat, inverse = normalised(own_tokens)
    scaled = normed_grad * gain.reshape(width)
    input_grad = inverse * (
        scaled
        - jnp.mean(scaled, axis=-1, keepdims=True)
        - hat * jnp.mean(scaled * hat, axis=-1, keepdims=True)
    )
    tokens_grad = (own_cotangent + input_grad).astype(jnp.bfloat16)

    def placed(value):
        return jnp.transpose(value, (1, 0, 2)).reshape(tokens.shape)

    return (
        placed(layer_out),
        placed(tokens_grad),
        vector_sum[:gain_share],
        vector_sum[gain_share : 2 * gain_share],
        inward_sum,
        vector_sum[2 * gain_share :],
        outward_sum,
        gate_up_sum,
        down_sum,
    )


def solution(mesh):
    in_specs = (
        P("bucket", "blk", None, None),
        P("bucket", None),
        P(("bucket", "blk")),
        P(("bucket", "blk")),
        P(("bucket", "blk"), None),
        P(("bucket", "blk")),
        P(("bucket", "blk"), None),
        P(("bucket", "blk"), None),
        P(("bucket", "blk"), None),
        P("bucket", "blk", None, None),
    )
    out_specs = (
        P("bucket", "blk", None, None),
        P("bucket", "blk", None, None),
        P(("bucket", "blk")),
        P(("bucket", "blk")),
        P(("bucket", "blk"), None),
        P(("bucket", "blk")),
        P(("bucket", "blk"), None),
        P(("bucket", "blk"), None),
        P(("bucket", "blk"), None),
    )
    body = shards_grouped if fits_groups(mesh) else shards_general
    return jax.shard_map(body, mesh=mesh, in_specs=in_specs, out_specs=out_specs, check_vma=False)
```

```python
import functools

import jax
import jax.numpy as jnp
from jax import lax
from jax.experimental import pallas as pl
from jax.experimental.pallas import tpu as pltpu
from jax.sharding import PartitionSpec as P

HEADS = 32
HEAD_DIM = 64
ROT = 16


epsilon = 1e-05
rotary_base = 10000.0
masked_score = -1e30


def shifted(value, axis, by):
    count = lax.axis_size(axis)
    pairs = [(i, i + by) for i in range(count) if 0 <= i + by < count]
    return lax.ppermute(value, axis, pairs)


def shifted_2(value, axis, steps):
    count = lax.axis_size(axis)
    pairs = [(source, (source + steps) % count) for source in range(count)]
    return lax.ppermute(value, axis, pairs)


def keep_same(value):
    return value


def transposed_times(left, right):
    return lax.dot_general(
        left, right, (((1,), (1,)), ((), ())), preferred_element_type=jnp.float32
    )


def times_transposed(left, right):
    return lax.dot_general(
        left, right, (((0,), (0,)), ((), ())), preferred_element_type=jnp.float32
    )


def rotary_tables(positions):
    half_rot = ROT // 2
    frequency = rotary_base ** (-(2.0 * jnp.arange(half_rot).astype(jnp.float32)) / ROT)
    angles = positions.astype(jnp.float32)[:, None] * frequency[None, :]
    return (jnp.cos(angles), jnp.sin(angles))


def rotate(values, cos_table, sine_table):
    half_rot = ROT // 2
    front_half = values[..., :half_rot]
    back_half = values[..., half_rot:ROT]
    return jnp.concatenate(
        [
            front_half * cos_table - back_half * sine_table,
            back_half * cos_table + front_half * sine_table,
            values[..., ROT:],
        ],
        axis=-1,
    )


def split_pairs(packed):
    rows_here, seq_count, both_width = packed.shape
    half_width = both_width // 2
    keys_part = packed[..., :half_width].reshape(rows_here, seq_count, HEADS, HEAD_DIM)
    values_part = packed[..., half_width:].reshape(rows_here, seq_count, HEADS, HEAD_DIM)
    return (keys_part, values_part)


def block_scores(queries, key_block, query_start, key_start):
    scores = jnp.einsum("tshd,ushd->shtu", queries, key_block, preferred_element_type=jnp.float32)
    query_pos = query_start + jnp.arange(queries.shape[0], dtype=jnp.int32)
    key_pos = key_start + jnp.arange(key_block.shape[0], dtype=jnp.int32)
    allowed = (key_pos[None, :] <= query_pos[:, None])[None, None]
    return (jnp.where(allowed, scores, masked_score), allowed)


def forward_block(carried, queries, key_block, value_block, query_start, key_start):
    running_max, running_sum, weighted = carried
    scores, allowed = block_scores(queries, key_block, query_start, key_start)
    new_max = jnp.maximum(running_max, jnp.max(scores, axis=-1))
    rescale = jnp.exp(running_max - new_max)
    weights = jnp.where(allowed, jnp.exp(scores - new_max[..., None]), 0.0)
    running_sum = running_sum * rescale + jnp.sum(weights, axis=-1)
    update = jnp.einsum(
        "shtu,ushd->tshd",
        weights.astype(jnp.bfloat16),
        value_block,
        preferred_element_type=jnp.float32,
    )
    weighted = weighted * jnp.transpose(rescale, (2, 0, 1))[..., None] + update
    return (new_max, running_sum, weighted)


def pair_grads(
    queries, out_grads, log_norm, deltas, key_block, value_block, query_start, key_start
):
    scores, allowed = block_scores(queries, key_block, query_start, key_start)
    probability = jnp.where(allowed, jnp.exp(scores - log_norm[..., None]), 0.0)
    value_grad = jnp.einsum(
        "shtu,tshd->ushd",
        probability.astype(jnp.bfloat16),
        out_grads,
        preferred_element_type=jnp.float32,
    )
    prob_grad = jnp.einsum(
        "tshd,ushd->shtu", out_grads, value_block, preferred_element_type=jnp.float32
    )
    score_grad = (probability * (prob_grad - deltas[..., None])).astype(jnp.bfloat16)
    query_grad = jnp.einsum(
        "shtu,ushd->tshd", score_grad, key_block, preferred_element_type=jnp.float32
    )
    key_grad = jnp.einsum(
        "shtu,tshd->ushd", score_grad, queries, preferred_element_type=jnp.float32
    )
    return (query_grad, key_grad, value_grad)


def over_blocks(running, incoming, unit_rows, handle):
    total_rows = incoming[0].shape[0]
    block_count = total_rows // unit_rows
    block_rows = total_rows // block_count
    stacked = tuple(
        (member.reshape((block_count, block_rows) + member.shape[1:]) for member in incoming)
    )

    def visit(carried, element):
        block_index, members = element
        return (handle(carried, members, block_index * block_rows), None)

    running, unused = lax.scan(visit, running, (jnp.arange(block_count, dtype=jnp.int32), stacked))
    return running


def shards_general(
    tokens,
    lengths,
    norm_gain,
    norm_shift,
    inward_weight,
    inward_bias,
    outward_weight,
    gate_up_weight,
    down_weight,
    cotangent,
):
    group_len = tokens.shape[1]
    seq_count = tokens.shape[2]
    model_width = tokens.shape[3]
    row_total = group_len * seq_count
    block_total = lax.axis_size("blk")
    position = lax.axis_index("blk")
    own_start = position * group_len
    longest = jnp.max(lengths[0])
    active = own_start < longest
    gathered = (
        lax.all_gather(inward_weight.astype(jnp.bfloat16), ("bucket", "blk"), axis=0, tiled=True),
        lax.all_gather(outward_weight.astype(jnp.bfloat16), ("bucket", "blk"), axis=0, tiled=True),
        lax.all_gather(gate_up_weight.astype(jnp.bfloat16), ("bucket", "blk"), axis=0, tiled=True),
        lax.all_gather(down_weight.astype(jnp.bfloat16), ("bucket", "blk"), axis=0, tiled=True),
        lax.all_gather(norm_gain.astype(jnp.bfloat16), ("bucket", "blk"), axis=0, tiled=True),
        lax.all_gather(norm_shift.astype(jnp.bfloat16), ("bucket", "blk"), axis=0, tiled=True),
        lax.all_gather(inward_bias.astype(jnp.bfloat16), ("bucket", "blk"), axis=0, tiled=True),
    )
    inward_full, outward_full, gate_up_full, down_full, gain_full, shift_full, bias_full = gathered
    inputs = tokens.reshape(row_total, model_width).astype(jnp.float32)
    centred = inputs - jnp.mean(inputs, axis=-1, keepdims=True)
    variance = jnp.mean(centred * centred, axis=-1, keepdims=True)
    inverse = lax.rsqrt(variance + epsilon)
    normal_hat = centred * inverse
    normed_low = (
        normal_hat * gain_full.astype(jnp.float32) + shift_full.astype(jnp.float32)
    ).astype(jnp.bfloat16)
    bias_float = bias_full.astype(jnp.float32)
    key_bias = jnp.pad(
        bias_float[2 * model_width :].reshape(HEADS, ROT), ((0, 0), (0, HEAD_DIM - ROT))
    ).reshape(model_width)
    full_bias = jnp.concatenate(
        [bias_float[:model_width], key_bias, bias_float[model_width : 2 * model_width]]
    )
    projected = jnp.dot(normed_low, inward_full, preferred_element_type=jnp.float32) + full_bias
    projected = projected.reshape(group_len, seq_count, 3, HEADS, HEAD_DIM)
    cos_table, sine_table = rotary_tables(own_start + jnp.arange(group_len, dtype=jnp.int32))
    cos_table = cos_table[:, None, None, :]
    sine_table = sine_table[:, None, None, :]
    query_scale = HEAD_DIM ** (-0.5)
    queries = (rotate(projected[:, :, 0], cos_table, sine_table) * query_scale).astype(jnp.bfloat16)
    keys_low = rotate(projected[:, :, 1], cos_table, sine_table).astype(jnp.bfloat16)
    values_low = projected[:, :, 2].astype(jnp.bfloat16)
    packed = jnp.concatenate(
        [
            keys_low.reshape(group_len, seq_count, model_width),
            values_low.reshape(group_len, seq_count, model_width),
        ],
        axis=-1,
    )

    def forward_handle(carried, members, key_start):
        keys_part, values_part = split_pairs(members[0])
        needed = active & (key_start <= own_start + group_len - 1)

        def forward_compute(state_in):
            return forward_block(state_in, queries, keys_part, values_part, own_start, key_start)

        return lax.cond(needed, forward_compute, keep_same, carried)

    start_state = (
        jnp.full((seq_count, HEADS, group_len), masked_score, jnp.float32),
        jnp.zeros((seq_count, HEADS, group_len), jnp.float32),
        jnp.zeros((group_len, seq_count, HEADS, HEAD_DIM), jnp.float32),
    )
    running_max, running_sum, weighted = over_blocks(
        start_state, (lax.all_gather(packed, "blk", axis=0, tiled=True),), group_len, forward_handle
    )
    bounded = jnp.maximum(running_sum, 1.0)
    log_norm = running_max + jnp.log(bounded)
    attended = weighted / jnp.transpose(bounded, (2, 0, 1))[..., None]
    attended_rows = attended.astype(jnp.bfloat16).reshape(row_total, model_width)
    gate_up = jnp.dot(normed_low, gate_up_full, preferred_element_type=jnp.float32)
    ff_width = gate_up.shape[1] // 2
    gate_part = gate_up[:, :ff_width]
    up_part = gate_up[:, ff_width:]
    sigmoid_gate = jax.nn.sigmoid(gate_part)
    silu_gate = gate_part * sigmoid_gate
    hidden_low = (silu_gate * up_part).astype(jnp.bfloat16)
    branch = jnp.dot(attended_rows, outward_full, preferred_element_type=jnp.float32) + jnp.dot(
        hidden_low, down_full, preferred_element_type=jnp.float32
    )
    query_pos = own_start + jnp.arange(group_len, dtype=jnp.int32)
    valid_rows = (
        (query_pos[:, None] < lengths[0][None, :]).astype(jnp.float32).reshape(row_total, 1)
    )
    layer_out = (inputs + valid_rows * branch).astype(jnp.bfloat16).reshape(tokens.shape)
    inward_back = gathered[0]
    outward_back = gathered[1]
    gate_up_back = gathered[2]
    down_back = gathered[3]
    gain_float = gathered[4].astype(jnp.float32)
    cotangent_rows = cotangent.reshape(row_total, model_width).astype(jnp.float32)
    branch_grad = (cotangent_rows * valid_rows).astype(jnp.bfloat16)
    hidden_grad = transposed_times(branch_grad, down_back)
    gate_grad = hidden_grad * up_part * (sigmoid_gate + silu_gate * (1.0 - sigmoid_gate))
    up_grad = hidden_grad * silu_gate
    gate_up_grad_low = jnp.concatenate([gate_grad, up_grad], axis=-1).astype(jnp.bfloat16)
    down_term = times_transposed(hidden_low, branch_grad)
    gate_up_term = times_transposed(normed_low, gate_up_grad_low)
    gate_up_sum, down_sum = (
        lax.psum_scatter(gate_up_term, ("bucket", "blk"), scatter_dimension=0, tiled=True),
        lax.psum_scatter(down_term, ("bucket", "blk"), scatter_dimension=0, tiled=True),
    )
    normed_grad = transposed_times(gate_up_grad_low, gate_up_back)
    attended_grad = (
        transposed_times(branch_grad, outward_back)
        .astype(jnp.bfloat16)
        .reshape(group_len, seq_count, HEADS, HEAD_DIM)
    )
    outward_term = times_transposed(attended_rows, branch_grad)
    deltas = jnp.transpose(
        jnp.sum(attended_grad.astype(jnp.float32) * attended, axis=-1), (1, 2, 0)
    )
    grad_zeros = jnp.zeros((group_len, seq_count, 2 * model_width), jnp.float32)
    query_zeros = jnp.zeros((group_len, seq_count, HEADS, HEAD_DIM), jnp.float32)

    def cycle_turn(turn_index, carried):
        visiting, sums_now, grads_now = carried
        owner_index = (position - turn_index) % block_total
        key_start = owner_index * group_len
        needed = active & (owner_index <= position)

        def cycle_compute(sums_in):
            keys_part, values_part = split_pairs(visiting)
            query_part, key_part, value_part = pair_grads(
                queries,
                attended_grad,
                log_norm,
                deltas,
                keys_part,
                values_part,
                own_start,
                key_start,
            )
            merged = jnp.concatenate(
                [
                    key_part.reshape(group_len, seq_count, model_width),
                    value_part.reshape(group_len, seq_count, model_width),
                ],
                axis=-1,
            )
            return (sums_in[0] + merged, sums_in[1] + query_part)

        sums_now, grads_now = lax.cond(needed, cycle_compute, keep_same, (sums_now, grads_now))
        visiting = shifted(visiting, "blk", 1)
        sums_now = shifted_2(sums_now.astype(jnp.bfloat16), "blk", 1).astype(sums_now.dtype)
        return (visiting, sums_now, grads_now)

    unused, pair_sums, query_grads = lax.fori_loop(
        0, block_total, cycle_turn, (packed, grad_zeros, query_zeros)
    )
    key_grad = pair_sums[..., :model_width].reshape(group_len, seq_count, HEADS, HEAD_DIM)
    value_grad = pair_sums[..., model_width:].reshape(group_len, seq_count, HEADS, HEAD_DIM)
    back_sine = -sine_table
    query_back = rotate(query_grads * query_scale, cos_table, back_sine)
    key_back = rotate(key_grad, cos_table, back_sine)
    projected_grad = (
        jnp.stack([query_back, key_back, value_grad], axis=2)
        .reshape(row_total, 3 * model_width)
        .astype(jnp.bfloat16)
    )
    inward_term = times_transposed(normed_low, projected_grad)
    column_sums = jnp.sum(projected_grad.astype(jnp.float32), axis=0)
    key_bias_grad = (
        column_sums[model_width : 2 * model_width]
        .reshape(HEADS, HEAD_DIM)[:, :ROT]
        .reshape(HEADS * ROT)
    )
    bias_term = jnp.concatenate(
        [column_sums[:model_width], column_sums[2 * model_width :], key_bias_grad]
    )
    normed_grad = normed_grad + transposed_times(projected_grad, inward_back)
    gain_term = jnp.sum(normed_grad * normal_hat, axis=0)
    shift_term = jnp.sum(normed_grad, axis=0)
    scaled_grad = normed_grad * gain_float
    input_grad = inverse * (
        scaled_grad
        - jnp.mean(scaled_grad, axis=-1, keepdims=True)
        - normal_hat * jnp.mean(scaled_grad * normal_hat, axis=-1, keepdims=True)
    )
    tokens_grad = (cotangent_rows + input_grad).astype(jnp.bfloat16).reshape(tokens.shape)
    inward_sum, outward_sum, bias_sum, gain_sum, shift_sum = (
        lax.psum_scatter(inward_term, ("bucket", "blk"), scatter_dimension=0, tiled=True),
        lax.psum_scatter(outward_term, ("bucket", "blk"), scatter_dimension=0, tiled=True),
        lax.psum_scatter(bias_term, ("bucket", "blk"), scatter_dimension=0, tiled=True),
        lax.psum_scatter(gain_term, ("bucket", "blk"), scatter_dimension=0, tiled=True),
        lax.psum_scatter(shift_term, ("bucket", "blk"), scatter_dimension=0, tiled=True),
    )
    return (
        layer_out,
        tokens_grad,
        gain_sum,
        shift_sum,
        inward_sum,
        bias_sum,
        outward_sum,
        gate_up_sum,
        down_sum,
    )


DEPTH = 4
PIECES = 2 * DEPTH
ROWS = 256
EXTRA = 16
LOCAL_HEADS = 4
HEAD_COLS = LOCAL_HEADS * HEAD_DIM
CORE = [(i, i ^ 1) for i in range(4)]
ACROSS_X = [(i, i ^ 2) for i in range(4)]
ACROSS_Y = [(i, i ^ 1) for i in range(8)]
MIB = 1024 * 1024


def fits_groups(mesh):
    return mesh.shape["bucket"] == 4 and mesh.shape["blk"] == 2 * DEPTH


def around(step):
    return [(z * 2 + y, ((z + step) % DEPTH) * 2 + y) for z in range(DEPTH) for y in range(2)]


def in_order(own, other, index, axis):
    return jnp.where(
        index == 0, jnp.stack([own, other], axis), jnp.stack([other, own], axis)
    )


def gather_pieces(value):
    own = [value]
    for step in range(1, DEPTH):
        own.append(lax.ppermute(value, "blk", around(step)))
    return own + [lax.ppermute(piece, "bucket", CORE) for piece in own]


def core_sums(own, other):
    other = lax.ppermute(other, "bucket", CORE)
    sums = [own[k].astype(jnp.float32) + other[k].astype(jnp.float32) for k in range(DEPTH)]
    return [sums[0]] + [value.astype(jnp.bfloat16) for value in sums[1:]]


def scatter_pieces(sums):
    total = sums[0]
    for step in range(1, DEPTH):
        got = lax.ppermute(sums[step], "blk", around(-step))
        total = total + got.astype(jnp.float32)
    return total


def after(value, *earlier):
    return lax.optimization_barrier((value,) + earlier)[0]


def one_of(value, index, axis):
    return lax.dynamic_index_in_dim(value, index, axis, False)


def dot_rows(left, right):
    return lax.dot_general(
        left, right, (((1,), (0,)), ((), ())), preferred_element_type=jnp.float32
    )


def params(limit, **extra):
    return pltpu.CompilerParams(vmem_limit_bytes=limit * MIB, **extra)


def cost(flops, moved, exps=0):
    return pl.CostEstimate(flops=flops // 64, bytes_accessed=moved // 64, transcendentals=exps // 64)


def piece_spec(width):
    return pl.BlockSpec((1, ROWS, width), lambda i: (i, 0, 0))


def whole_spec(shape):
    return pl.BlockSpec(shape, lambda i: (0,) * len(shape))


def remote(src, dst, sends, recvs, index, device):
    return pltpu.make_async_remote_copy(
        src_ref=src,
        dst_ref=dst,
        send_sem=sends.at[index],
        recv_sem=recvs.at[index],
        device_id=device,
        device_id_type=pl.DeviceIdType.MESH,
    )


def gather_kernel(
    x_ref,
    wi_ref,
    wg_ref,
    ro_ref,
    pieces,
    wi_out,
    wg_out,
    ro_out,
    group_s,
    group_r,
    across_s,
    across_r,
    rows_s,
    rows_r,
    up_s,
    down_s,
    piece_r,
    core_s,
    core_r,
    local_sems,
):
    bucket, blk = lax.axis_index("bucket"), lax.axis_index("blk")
    x, core = bucket // 2, bucket % 2
    z, y = blk // 2, blk % 2

    def device(xx, cc, zz, yy):
        return (xx * 2 + cc, zz * 2 + yy)

    x_mate, y_mate = device(1 - x, core, z, y), device(x, core, z, 1 - y)
    core_mate = device(x, 1 - core, z, y)
    members = [(flip, turn) for turn in (0, 1, 3, 2) for flip in (0, 1)]

    def target(flip, turn):
        return (core + flip) % 2, (z + turn) % DEPTH

    def source(flip, turn):
        return (core + flip) % 2, (z + DEPTH - turn) % DEPTH

    barrier = pltpu.get_barrier_semaphore()
    greeted = [device(x, *target(*m), y) for m in members[1:]] + [x_mate, y_mate]
    for mate in greeted:
        pl.semaphore_signal(
            barrier, inc=1, device_id=mate, device_id_type=pl.DeviceIdType.MESH
        )
    pl.semaphore_wait(barrier, len(greeted))

    started = []

    def begin(copy):
        copy.start()
        started.append(copy)
        return copy

    local = [
        pltpu.make_async_copy(wi_ref.at[core, z], wi_out.at[x, core, z, y], local_sems.at[0]),
        pltpu.make_async_copy(wg_ref.at[core, z], wg_out.at[x, core, z, y], local_sems.at[1]),
        pltpu.make_async_copy(ro_ref, ro_out.at[x, y], local_sems.at[2]),
        pltpu.make_async_copy(x_ref, pieces.at[0], local_sems.at[3]),
    ]
    for copy in local:
        copy.start()

    def send_group(which, ref, out):
        copies = {}
        for flip, turn in members[1:]:
            cc, zz = target(flip, turn)
            copies[flip, turn] = begin(
                remote(
                    ref.at[cc, zz],
                    out.at[x, core, z, y],
                    group_s,
                    group_r,
                    (which, flip * DEPTH + turn),
                    device(x, cc, zz, y),
                )
            )
        return copies

    def piece_copy(src, slot, sends, number, dz):
        return pltpu.make_async_remote_copy(
            src_ref=src,
            dst_ref=pieces.at[slot],
            send_sem=sends.at[number],
            recv_sem=piece_r.at[slot],
            device_id=device(x, core, z + dz, y),
            device_id_type=pl.DeviceIdType.MESH,
        )

    def core_copy(slot):
        src = x_ref if slot == 0 else pieces.at[slot]
        return remote(src, pieces.at[DEPTH + slot], core_s, core_r, slot, core_mate)

    ups = [piece_copy(x_ref if k == 0 else pieces.at[k], k + 1, up_s, k, 1) for k in range(3)]
    downs = [
        piece_copy(x_ref if k == 0 else pieces.at[DEPTH - k], 3 - k, down_s, k, -1)
        for k in range(3)
    ]

    def start_if(condition, copy):
        @pl.when(condition)
        def _():
            copy.start()

    def sent_if(condition, copy):
        @pl.when(condition)
        def _():
            copy.wait_send()

    inward = send_group(0, wi_ref, wi_out)
    start_if(z < DEPTH - 1, ups[0])
    start_if(z > 0, downs[0])
    core_copies = [core_copy(slot) for slot in range(DEPTH)]
    core_copies[0].start()
    rows_x = begin(remote(ro_ref, ro_out.at[x, y], rows_s, rows_r, 0, x_mate))
    rows_y = begin(remote(ro_ref, ro_out.at[x, y], rows_s, rows_r, 1, y_mate))
    gate_up = send_group(1, wg_ref, wg_out)

    def spread(which, ref, out, copies):
        pairs = {}
        for member in members:
            flip, turn = member
            cc, zz = source(flip, turn)
            if member == (0, 0):
                src = ref.at[core, z]
            else:
                copies[member].wait_recv()
                src = out.at[x, cc, zz, y]
            number = flip * DEPTH + turn
            pairs[member] = (
                begin(
                    remote(
                        src, out.at[x, cc, zz, y], across_s, across_r, (which, 0, number), x_mate
                    )
                ),
                begin(
                    remote(
                        src, out.at[x, cc, zz, y], across_s, across_r, (which, 1, number), y_mate
                    )
                ),
            )
        return pairs

    def corner(which, out, pairs):
        copies = []
        for member in members:
            flip, turn = member
            cc, zz = source(flip, turn)
            number = flip * DEPTH + turn
            if flip == 0:
                pairs[member][1].wait_recv()
                part = out.at[x, cc, zz, 1 - y]
                mate = x_mate
            else:
                pairs[member][0].wait_recv()
                part = out.at[1 - x, cc, zz, y]
                mate = y_mate
            copies.append(
                begin(remote(part, part, across_s, across_r, (which, 2, number), mate))
            )
        return copies

    inward_pairs = spread(0, wi_ref, wi_out, inward)

    @pl.when(z > 0)
    def _():
        ups[0].wait_recv()
        core_copies[1].start()

    start_if((z > 0) & (z < DEPTH - 1), ups[1])

    @pl.when(z < DEPTH - 1)
    def _():
        downs[0].wait_recv()
        core_copies[3].start()

    start_if((z > 0) & (z < DEPTH - 1), downs[1])

    inward_corner = corner(0, wi_out, inward_pairs)
    gate_up_pairs = spread(1, wg_ref, wg_out, gate_up)

    ups[1].wait_recv()
    core_copies[2].start()
    start_if(z == 2, ups[2])
    start_if(z == 1, downs[2])

    cut = (ro_ref.shape[0] // 32) * 16
    rows_y.wait_recv()
    low = ro_out.at[x, 1 - y, pl.ds(0, cut)]
    low_copy = begin(remote(low, low, rows_s, rows_r, 2, x_mate))
    rows_x.wait_recv()
    high = ro_out.at[1 - x, y, pl.ds(cut, ro_ref.shape[0] - cut)]
    high_copy = begin(remote(high, high, rows_s, rows_r, 3, y_mate))
    gate_up_corner = corner(1, wg_out, gate_up_pairs)

    @pl.when(z == DEPTH - 1)
    def _():
        ups[2].wait_recv()
        core_copies[3].start()

    @pl.when(z == 0)
    def _():
        downs[2].wait_recv()
        core_copies[1].start()

    for pairs in (inward_pairs, gate_up_pairs):
        for flip, turn in members:
            pairs[flip, turn][0 if flip == 0 else 1].wait_recv()
    for copy in inward_corner + gate_up_corner + [low_copy, high_copy]:
        copy.wait_recv()
    for copy in core_copies:
        copy.wait_recv()
        copy.wait_send()
    for copy in started:
        copy.wait_send()
    sent_if(z < DEPTH - 1, ups[0])
    sent_if(z > 0, downs[0])
    sent_if((z > 0) & (z < DEPTH - 1), ups[1])
    sent_if((z > 0) & (z < DEPTH - 1), downs[1])
    sent_if(z == 2, ups[2])
    sent_if(z == 1, downs[2])
    for copy in local:
        copy.wait()


def gather(tokens, inward, gate_up, rows_out):
    anywhere = pl.BlockSpec(memory_space=pl.ANY)
    low = jnp.bfloat16
    dma = pltpu.SemaphoreType.DMA
    return pl.pallas_call(
        gather_kernel,
        in_specs=[anywhere] * 4,
        out_specs=[anywhere] * 4,
        out_shape=[
            jax.ShapeDtypeStruct((PIECES,) + tokens.shape, low),
            jax.ShapeDtypeStruct((2, 2, DEPTH, 2) + inward.shape[2:], low),
            jax.ShapeDtypeStruct((2, 2, DEPTH, 2) + gate_up.shape[2:], low),
            jax.ShapeDtypeStruct((2, 2) + rows_out.shape, low),
        ],
        scratch_shapes=[
            dma((2, PIECES)),
            dma((2, PIECES)),
            dma((2, 3, PIECES)),
            dma((2, 3, PIECES)),
            dma((4,)),
            dma((4,)),
            dma((3,)),
            dma((3,)),
            dma((DEPTH,)),
            dma((DEPTH,)),
            dma((DEPTH,)),
            dma((4,)),
        ],
        compiler_params=params(32, collective_id=0, has_side_effects=True),
        cost_estimate=cost(0, 64 * MIB),
        name="gather",
    )(tokens, inward, gate_up, rows_out)


def inward_rows(ref):
    blocks, rows, columns = ref.shape
    return ref[:, : rows - EXTRA].reshape(blocks * (rows - EXTRA), columns)


def outward_rows(ref):
    blocks, rows, columns = ref.shape
    return ref[:, :HEAD_DIM].reshape(blocks * HEAD_DIM, columns)


def down_rows(ref):
    blocks, rows, columns = ref.shape
    return ref[:, HEAD_DIM:].reshape(blocks * (rows - HEAD_DIM), columns)


def normalised(rows):
    inputs = rows.astype(jnp.float32)
    centred = inputs - jnp.mean(inputs, axis=-1, keepdims=True)
    variance = jnp.mean(centred * centred, axis=-1, keepdims=True)
    inverse = lax.rsqrt(variance + epsilon)
    return centred * inverse, inverse


def turned(values, cos_ref, first_ref, second_ref, sign):
    half = ROT // 2
    cos = jnp.concatenate([cos_ref[0], cos_ref[0]], 0)
    first = jnp.concatenate([first_ref[0], first_ref[0]], 0)
    second = jnp.concatenate([second_ref[0], second_ref[0]], 0)
    ahead = pltpu.roll(values, HEAD_COLS - half, 1)
    behind = pltpu.roll(values, half, 1)
    return values * cos + sign * (ahead * first + behind * second)


def project_kernel(
    x_ref, gain_ref, shift_ref, w_ref, bias_ref, cos_ref, first_ref, second_ref, n_ref, q_ref, kv_ref
):
    hat, _ = normalised(x_ref[0])
    normed = (hat * gain_ref[...] + shift_ref[...]).astype(jnp.bfloat16)
    n_ref[0] = normed
    projected = dot_rows(normed, inward_rows(w_ref)) + bias_ref[...]
    tables = (cos_ref, first_ref, second_ref)
    query = turned(projected[:, :HEAD_COLS], *tables, 1.0) * (HEAD_DIM**-0.5)
    key = turned(projected[:, HEAD_COLS : 2 * HEAD_COLS], *tables, 1.0)
    q_ref[0] = query.astype(jnp.bfloat16)
    kv_ref[0, :, :HEAD_COLS] = key.astype(jnp.bfloat16)
    kv_ref[0, :, HEAD_COLS:] = projected[:, 2 * HEAD_COLS :].astype(jnp.bfloat16)


def project(pieces, gain, shift, weight, bias, tables):
    width = pieces.shape[-1]
    table_spec = pl.BlockSpec((1,) + tables[0].shape[1:], lambda i: (i % DEPTH, 0, 0))
    return pl.pallas_call(
        project_kernel,
        grid=(PIECES,),
        in_specs=[
            piece_spec(width),
            whole_spec((1, width)),
            whole_spec((1, width)),
            whole_spec(weight.shape),
            whole_spec(bias.shape),
            table_spec,
            table_spec,
            table_spec,
        ],
        out_specs=[piece_spec(width), piece_spec(HEAD_COLS), piece_spec(2 * HEAD_COLS)],
        out_shape=[
            jax.ShapeDtypeStruct((PIECES, ROWS, width), jnp.bfloat16),
            jax.ShapeDtypeStruct((PIECES, ROWS, HEAD_COLS), jnp.bfloat16),
            jax.ShapeDtypeStruct((PIECES, ROWS, 2 * HEAD_COLS), jnp.bfloat16),
        ],
        compiler_params=params(48),
        cost_estimate=cost(2 * PIECES * ROWS * width * 3 * HEAD_COLS, 24 * MIB),
        name="project",
    )(pieces, gain, shift, weight, bias, *tables)


def feed_kernel(n_ref, w_ref, gate_ref, up_ref, hidden_ref):
    both = dot_rows(n_ref[0], w_ref[...])
    hidden = both.shape[1] // 2
    gate, up = both[:, :hidden], both[:, hidden:]
    gate_ref[0] = gate
    up_ref[0] = up
    hidden_ref[0] = (gate * jax.nn.sigmoid(gate) * up).astype(jnp.bfloat16)


def feed(normed, weight):
    width = normed.shape[-1]
    hidden = weight.shape[1] // 2
    return pl.pallas_call(
        feed_kernel,
        grid=(PIECES,),
        in_specs=[piece_spec(width), whole_spec(weight.shape)],
        out_specs=[piece_spec(hidden)] * 3,
        out_shape=[
            jax.ShapeDtypeStruct((PIECES, ROWS, hidden), jnp.float32),
            jax.ShapeDtypeStruct((PIECES, ROWS, hidden), jnp.float32),
            jax.ShapeDtypeStruct((PIECES, ROWS, hidden), jnp.bfloat16),
        ],
        compiler_params=params(48),
        cost_estimate=cost(4 * PIECES * ROWS * width * hidden, 28 * MIB),
        name="feed",
    )(normed, weight)


def store_split(value, own_ref, other_ref):
    late = pl.program_id(0) >= DEPTH

    @pl.when(jnp.logical_not(late))
    def _():
        other_ref[0] = value

    @pl.when(late)
    def _():
        own_ref[0] = value


def other_first(width):
    return pl.BlockSpec((1, ROWS, width), lambda i: ((i + DEPTH) % PIECES, 0, 0))


def split_specs(width):
    return [
        pl.BlockSpec((1, ROWS, width), lambda i: (jnp.maximum(i - DEPTH, 0), 0, 0)),
        pl.BlockSpec((1, ROWS, width), lambda i: (jnp.minimum(i, DEPTH - 1), 0, 0)),
    ]


def branch_kernel(a_ref, h_ref, w_ref, own_ref, other_ref):
    term = dot_rows(a_ref[0], outward_rows(w_ref)) + dot_rows(h_ref[0], down_rows(w_ref))
    store_split(term.astype(jnp.bfloat16), own_ref, other_ref)


def branch_terms(attended, hidden, rows_out):
    width = rows_out.shape[-1]
    return pl.pallas_call(
        branch_kernel,
        grid=(PIECES,),
        in_specs=[
            other_first(HEAD_COLS),
            other_first(hidden.shape[-1]),
            whole_spec(rows_out.shape),
        ],
        out_specs=split_specs(width),
        out_shape=[jax.ShapeDtypeStruct((DEPTH, ROWS, width), jnp.bfloat16)] * 2,
        compiler_params=params(48),
        cost_estimate=cost(2 * PIECES * ROWS * width * (HEAD_COLS + hidden.shape[-1]), 16 * MIB),
        name="branch_terms",
    )(attended, hidden, rows_out)


def back_kernel(g_ref, gate_ref, up_ref, w_ref, a_ref, gu_ref):
    grad = g_ref[0]
    a_ref[0] = transposed_times(grad, outward_rows(w_ref)).astype(jnp.bfloat16)
    hidden_grad = transposed_times(grad, down_rows(w_ref))
    gate = gate_ref[0]
    sig = jax.nn.sigmoid(gate)
    silu = gate * sig
    gate_grad = hidden_grad * up_ref[0] * (sig + silu * (1.0 - sig))
    up_grad = hidden_grad * silu
    gu_ref[0] = jnp.concatenate([gate_grad, up_grad], 1).astype(jnp.bfloat16)


def back(grads, gate, up, rows_out):
    width = rows_out.shape[-1]
    hidden = gate.shape[-1]
    return pl.pallas_call(
        back_kernel,
        grid=(PIECES,),
        in_specs=[
            piece_spec(width),
            piece_spec(hidden),
            piece_spec(hidden),
            whole_spec(rows_out.shape),
        ],
        out_specs=[piece_spec(HEAD_COLS), piece_spec(2 * hidden)],
        out_shape=[
            jax.ShapeDtypeStruct((PIECES, ROWS, HEAD_COLS), jnp.bfloat16),
            jax.ShapeDtypeStruct((PIECES, ROWS, 2 * hidden), jnp.bfloat16),
        ],
        compiler_params=params(48),
        cost_estimate=cost(2 * PIECES * ROWS * width * (HEAD_COLS + hidden), 28 * MIB),
        name="back",
    )(grads, gate, up, rows_out)


def pair_rows(block):
    lane = lax.broadcasted_iota(jnp.int32, block.shape, 1)
    zero = jnp.zeros_like(block)
    return jnp.concatenate(
        [jnp.where(lane < HEAD_DIM, block, zero), jnp.where(lane < HEAD_DIM, zero, block)], 0
    )


def pair_lanes(rows):
    half = rows.shape[0] // 2
    lane = lax.broadcasted_iota(jnp.int32, (half, rows.shape[1]), 1)
    return jnp.where(lane < HEAD_DIM, rows[:half], rows[half:])


def block_probs(queries, keys, last, y):
    scores = transposed_times(queries, keys)
    rows, columns = scores.shape
    size = rows // 2
    row = lax.broadcasted_iota(jnp.int32, (rows, 2 * size), 0) % size
    column = lax.broadcasted_iota(jnp.int32, (rows, 2 * size), 1)
    allowed = (column <= row) | ((column >= size) & (y == 1))
    tail = jnp.where(allowed, scores[:, last * 2 * size :], masked_score)
    scores = tail if last == 0 else jnp.concatenate([scores[:, : last * 2 * size], tail], 1)
    weights = jnp.exp(scores - jnp.max(scores, axis=-1, keepdims=True))
    return weights * (1.0 / jnp.sum(weights, axis=-1, keepdims=True))


def both_columns(own_ref, other_ref, z, count):
    blocks = []
    for j in range(count):
        at = (z + DEPTH - j) % DEPTH
        blocks += [own_ref[0, at, 0], other_ref[0, at, 0]]
    return jnp.concatenate(blocks, 0)


def attend_kernel(place_ref, q_ref, k_ref, v_ref, ok_ref, ov_ref, out_ref):
    z, y = place_ref[0], place_ref[1]
    keys = both_columns(k_ref, ok_ref, z, DEPTH)
    values = both_columns(v_ref, ov_ref, z, DEPTH)
    size = keys.shape[0] // DEPTH
    for j in range(DEPTH):
        at = (z + DEPTH - j) % DEPTH
        count = (j + 1) * size
        probs = block_probs(pair_rows(q_ref[0, at, 0]), keys[:count], j, y)
        out = dot_rows(probs.astype(jnp.bfloat16), values[:count])
        out_ref[0, at, 0] = pair_lanes(out).astype(jnp.bfloat16)


def attend_back_kernel(
    place_ref,
    q_ref,
    k_ref,
    v_ref,
    ok_ref,
    ov_ref,
    grad_ref,
    dq_ref,
    dk_ref,
    dv_ref,
    odk_ref,
    odv_ref,
    key_sum,
    value_sum,
):
    z, y = place_ref[0], place_ref[1]
    keys = both_columns(k_ref, ok_ref, z, DEPTH)
    values = both_columns(v_ref, ov_ref, z, DEPTH)
    size = keys.shape[0] // DEPTH
    half = size // 2
    for j in reversed(range(DEPTH)):
        at = (z + DEPTH - j) % DEPTH
        count = (j + 1) * size
        queries = pair_rows(q_ref[0, at, 0])
        grads = pair_rows(grad_ref[0, at, 0])
        probs = block_probs(queries, keys[:count], j, y)
        low = probs.astype(jnp.bfloat16)
        prob_grad = transposed_times(grads, values[:count])
        delta = jnp.sum(low.astype(jnp.float32) * prob_grad, axis=-1, keepdims=True)
        score_grad = (probs * (prob_grad - delta)).astype(jnp.bfloat16)
        dq_ref[0, at, 0] = pair_lanes(dot_rows(score_grad, keys[:count]))
        key_term = times_transposed(score_grad, queries)
        value_term = times_transposed(low, grads)
        if j == DEPTH - 1:
            key_sum[...] = key_term
            value_sum[...] = value_term
        else:
            key_sum[:count] += key_term
            value_sum[:count] += value_term
    for j in range(DEPTH):
        at = (z + DEPTH - j) % DEPTH
        low = j * size
        dk_ref[0, at, 0] = key_sum[low : low + half]
        dv_ref[0, at, 0] = value_sum[low : low + half]
        odk_ref[0, at, 0] = key_sum[low + half : low + size].astype(jnp.bfloat16)
        odv_ref[0, at, 0] = value_sum[low + half : low + size].astype(jnp.bfloat16)


def sequence_specs(seqs, length):
    def spec(first):
        return pl.BlockSpec(
            (1, DEPTH, 1, length, 2 * HEAD_DIM), lambda b, s, p, place: (b, 0, s, 0, first + p)
        )

    return spec(0), spec(LOCAL_HEADS // 2)


def as_sequences(value, seqs):
    return value.reshape(2, DEPTH, seqs, ROWS // seqs, value.shape[-1])


def attend(place, queries, pairs, other_pairs, seqs):
    queries, pairs, other_pairs = (as_sequences(v, seqs) for v in (queries, pairs, other_pairs))
    first, second = sequence_specs(seqs, ROWS // seqs)
    out = pl.pallas_call(
        attend_kernel,
        grid_spec=pltpu.PrefetchScalarGridSpec(
            num_scalar_prefetch=1,
            grid=(2, seqs, LOCAL_HEADS // 2),
            in_specs=[first, first, second, first, second],
            out_specs=first,
        ),
        out_shape=jax.ShapeDtypeStruct(queries.shape, jnp.bfloat16),
        compiler_params=params(48),
        cost_estimate=cost(4 * 8 * 2 * 2 * 256 * 2560 * 128, 8 * MIB, 8 * 256 * 2560),
        name="attend",
    )(place, queries, pairs, pairs, other_pairs, other_pairs)
    return out.reshape(PIECES, ROWS, HEAD_COLS)


def attend_back(place, queries, pairs, other_pairs, grads, seqs):
    queries, pairs, other_pairs, grads = (
        as_sequences(v, seqs) for v in (queries, pairs, other_pairs, grads)
    )
    length = ROWS // seqs
    first, second = sequence_specs(seqs, length)
    wide = jax.ShapeDtypeStruct(queries.shape, jnp.float32)
    narrow = jax.ShapeDtypeStruct(queries.shape, jnp.bfloat16)
    outs = pl.pallas_call(
        attend_back_kernel,
        grid_spec=pltpu.PrefetchScalarGridSpec(
            num_scalar_prefetch=1,
            grid=(2, seqs, LOCAL_HEADS // 2),
            in_specs=[first, first, second, first, second, first],
            out_specs=[first] * 5,
            scratch_shapes=[
                pltpu.VMEM((2 * DEPTH * length, 2 * HEAD_DIM), jnp.float32),
                pltpu.VMEM((2 * DEPTH * length, 2 * HEAD_DIM), jnp.float32),
            ],
        ),
        out_shape=[wide, wide, wide, narrow, narrow],
        compiler_params=params(48),
        cost_estimate=cost(10 * 8 * 2 * 2 * 256 * 2560 * 128, 16 * MIB, 8 * 256 * 2560),
        name="attend_back",
    )(place, queries, pairs, pairs, other_pairs, other_pairs, grads)
    return [v.reshape(PIECES, ROWS, HEAD_COLS) for v in outs]


def finish_kernel(
    dq_ref,
    dk_ref,
    dv_ref,
    odk_ref,
    odv_ref,
    gu_ref,
    pieces_ref,
    cos_ref,
    first_ref,
    second_ref,
    normed_ref,
    gate_xs,
    gate_xk,
    gate_ys,
    gate_yk,
    heads_term,
    hidden_term,
    wi_ref,
    wg_ref,
    gain_ref,
    cot_ref,
    tokens_out,
    heads_out,
    hidden_out,
    gate_rows,
    inward_rows_out,
    vec_out,
    inward_xs,
    inward_xk,
    inward_ys,
    inward_yk,
    gate_xr,
    gate_yr,
    gate_y2s,
    gate_y2r,
    gate_x2s,
    gate_x2r,
    gate_fin,
    inward_xr,
    inward_yr,
    inward_y2s,
    inward_y2r,
    inward_x2s,
    inward_x2r,
    inward_fin,
    heads_r,
    heads_2s,
    heads_2r,
    hidden_r,
    hidden_2s,
    hidden_2r,
    core_send,
    core_recv,
    z_send,
    z_recv,
    own_sum,
    pg_ref,
    token_rows,
    vec_sum,
    vec_x,
    vec_y,
    core_s,
    core_r,
    z_s,
    z_r,
    stage_s,
    stage_r,
    rows_s,
    rows_r,
    vec_s,
    vec_r,
    local_sems,
):
    bucket, blk = lax.axis_index("bucket"), lax.axis_index("blk")
    x, core = bucket // 2, bucket % 2
    z, y = blk // 2, blk % 2
    low = jnp.bfloat16
    wide = jnp.float32

    def device(xx, cc, zz, yy):
        return (xx * 2 + cc, zz * 2 + yy)

    x_mate, y_mate = device(1 - x, core, z, y), device(x, core, z, 1 - y)
    core_mate = device(x, 1 - core, z, y)
    members = [(flip, turn) for turn in (2, 1, 3, 0) for flip in (1, 0)][:-1]

    def target(flip, turn):
        return (core + flip) % 2, (z + turn) % DEPTH

    barrier = pltpu.get_barrier_semaphore()
    greeted = [device(x, *target(*m), y) for m in members] + [x_mate, y_mate]
    for mate in greeted:
        pl.semaphore_signal(
            barrier, inc=1, device_id=mate, device_id_type=pl.DeviceIdType.MESH
        )
    pl.semaphore_wait(barrier, len(greeted))

    started = []

    def begin(copy):
        copy.start()
        started.append(copy)
        return copy

    gate_x = begin(remote(gate_xs, gate_xr, stage_s, stage_r, (0, 0), x_mate))
    gate_y = begin(remote(gate_ys, gate_yr, stage_s, stage_r, (0, 1), y_mate))
    heads_x = begin(remote(heads_term.at[1 - x], heads_r, stage_s, stage_r, (2, 0), x_mate))
    hidden_y = [
        begin(
            remote(hidden_term.at[i, 1 - y], hidden_r.at[i], stage_s, stage_r, (3, i), y_mate)
        )
        for i in range(2)
    ]
    own_tokens = pltpu.make_async_copy(pieces_ref.at[0], token_rows, local_sems.at[0])
    own_tokens.start()

    vec_sum[...] = jnp.zeros_like(vec_sum)

    def core_copy(k):
        return remote(core_send.at[k], core_recv.at[k], core_s, core_r, k, core_mate)

    def z_copy(k):
        goal = device(x, core, (z + DEPTH - k) % DEPTH, y)
        return remote(z_send.at[k - 1], z_recv.at[k - 1], z_s, z_r, k - 1, goal)

    def piece_of(i):
        k = DEPTH - 1 - i // 2
        return k + DEPTH * (1 - i % 2)

    def piece_body(
        dq, dk, dv, odk, odv, gu, tokens, cos, first, second
    ):
        step = pl.program_id(0)
        k = DEPTH - 1 - step // 2
        piece = piece_of(step)
        tables = (cos, first, second)
        query = turned(dq[0] * (HEAD_DIM**-0.5), *tables, -1.0)
        key = turned(dk[0] + odk[0].astype(wide), *tables, -1.0)
        value = dv[0] + odv[0].astype(wide)
        narrow = jnp.concatenate([query, key, value], 1).astype(low)
        pg_ref[piece] = narrow
        grad = transposed_times(narrow, inward_rows(wi_ref))
        grad += transposed_times(gu[0], wg_ref[...])
        hat, _ = normalised(tokens[0])
        half = grad.shape[1] // 2
        for row, total in (
            (0, jnp.sum(grad * hat, axis=0, keepdims=True)),
            (2, jnp.sum(grad, axis=0, keepdims=True)),
        ):
            vec_sum[row : row + 1] += total[:, :half]
            vec_sum[row + 1 : row + 2] += total[:, half:]
        vec_sum[4:5, : 3 * HEAD_COLS] += jnp.sum(narrow.astype(wide), axis=0, keepdims=True)

        @pl.when(step % 2 == 0)
        def _():
            core_send[k] = grad.astype(low)
            core_copy(k).start()

        @pl.when(step % 2 == 1)
        def _():
            core_copy(k).wait_recv()
            both = grad + core_recv[k].astype(wide)

            @pl.when(k > 0)
            def _():
                z_send[k - 1] = both.astype(low)
                z_copy(k).start()

            @pl.when(k == 0)
            def _():
                own_sum[...] = both

    def by_piece(width):
        return pl.BlockSpec((1, ROWS, width), lambda i: (piece_of(i), 0, 0))

    table_spec = pl.BlockSpec(
        (1,) + cos_ref.shape[1:], lambda i: (piece_of(i) % DEPTH, 0, 0)
    )
    pltpu.emit_pipeline(
        piece_body,
        grid=(PIECES,),
        in_specs=[by_piece(HEAD_COLS)] * 5
        + [by_piece(gu_ref.shape[-1]), by_piece(pieces_ref.shape[-1])]
        + [table_spec] * 3,
    )(
        dq_ref,
        dk_ref,
        dv_ref,
        odk_ref,
        odv_ref,
        gu_ref,
        pieces_ref,
        cos_ref,
        first_ref,
        second_ref,
    )
    vector_x = remote(vec_sum, vec_x, vec_s, vec_r, 0, x_mate)
    vector_x.start()

    total, width = normed_ref.shape
    size = width // PIECES
    cut = 3 * HEAD_COLS // 2

    def projected(first, last):
        return pg_ref[...].reshape(total, 3 * HEAD_COLS)[:, first:last]

    def send_body(left, out):
        out[0] = times_transposed(left[...], projected(0, cut)).astype(low)

    def keep_body(left, out):
        out[0] = times_transposed(left[...], projected(0, cut))

    def split_body(left, keep, send):
        term = times_transposed(left[...], projected(cut, 2 * cut))
        split_rows(term, y, keep, send)

    def from_block(base):
        return pl.BlockSpec((total, size), lambda i: (0, base + i))

    def block_of(array):
        return pl.BlockSpec((1,) + array.shape[1:], lambda i: (i, 0, 0))

    pltpu.emit_pipeline(
        send_body,
        grid=(DEPTH,),
        in_specs=[from_block((1 - x) * DEPTH)],
        out_specs=[block_of(inward_xs)],
    )(normed_ref, inward_xs)
    inward_x = begin(remote(inward_xs, inward_xr, stage_s, stage_r, (1, 0), x_mate))
    pltpu.emit_pipeline(
        split_body,
        grid=(PIECES,),
        in_specs=[from_block(0)],
        out_specs=[block_of(inward_yk), block_of(inward_ys)],
    )(normed_ref, inward_yk, inward_ys)
    inward_y = begin(remote(inward_ys, inward_yr, stage_s, stage_r, (1, 1), y_mate))

    vector_x.wait_recv()
    vec_sum_x = vec_sum[...] + vec_x[...]
    vector_x.wait_send()
    vec_sum[...] = vec_sum_x
    vector_y = remote(vec_sum, vec_y, vec_s, vec_r, 1, y_mate)
    vector_y.start()

    def add_two(one, two, out):
        out[...] = (one[...].astype(wide) + two[...].astype(wide)).astype(out.dtype)

    def second_stage(which, xk, xr, yk, yr, y2s, y2r, x2s, x2r, first_x, first_y):
        quarter = xk.shape[1] // 4
        rows_at = pl.BlockSpec(
            (1, quarter, xk.shape[2]), lambda i: (i // 2, (i % 2) * 2 + (1 - y), 0)
        )
        first_x.wait_recv()
        pltpu.emit_pipeline(
            add_two, grid=(PIECES,), in_specs=[rows_at, rows_at], out_specs=[block_of(y2s)]
        )(xk, xr, y2s)
        over_y = begin(remote(y2s, y2r, stage_s, stage_r, (which, 2), y_mate))
        part = pl.BlockSpec((1,) + yk.shape[1:], lambda i: ((1 - x) * DEPTH + i, 0, 0))
        first_y.wait_recv()
        pltpu.emit_pipeline(
            add_two, grid=(DEPTH,), in_specs=[part, part], out_specs=[block_of(x2s)]
        )(yk, yr, x2s)
        over_x = begin(remote(x2s, x2r, stage_s, stage_r, (which, 3), x_mate))
        return over_y, over_x

    def last_stage(which, xk, xr, yk, yr, y2r, x2r, fin, rows, over_y, over_x):
        quarter = xk.shape[1] // 4
        cut = xk.shape[2]
        rows_at = pl.BlockSpec((1, quarter, cut), lambda i: (i // 2, (i % 2) * 2 + y, 0))
        part = pl.BlockSpec(
            (1, quarter, yk.shape[2]), lambda i: (x * DEPTH + i // 2, i % 2, 0)
        )
        last = pl.BlockSpec((1, quarter, yk.shape[2]), lambda i: (i // 2, i % 2, 0))

        def body(one, two, three, four, five, six, out):
            left = one[0] + two[0].astype(wide) + three[0].astype(wide)
            right = four[0] + five[0].astype(wide) + six[0].astype(wide)
            out[0] = jnp.concatenate([left, right], 1).astype(low)

        over_y.wait_recv()
        over_x.wait_recv()
        pltpu.emit_pipeline(
            body,
            grid=(PIECES,),
            in_specs=[rows_at, rows_at, block_of(y2r), part, part, last],
            out_specs=[block_of(fin)],
        )(xk, xr, y2r, yk, yr, x2r, fin)
        slot = core * DEPTH + z
        copies = []
        for flip, turn in members:
            cc, zz = target(flip, turn)
            copies.append(
                begin(
                    remote(
                        fin.at[cc * DEPTH + zz],
                        rows.at[slot],
                        rows_s,
                        rows_r,
                        (which, flip * DEPTH + turn),
                        device(x, cc, zz, y),
                    )
                )
            )
        own = pltpu.make_async_copy(fin.at[slot], rows.at[slot], local_sems.at[1 + which])
        own.start()
        return copies, own

    gate_second = second_stage(
        0,
        gate_xk,
        gate_xr,
        gate_yk,
        gate_yr,
        gate_y2s,
        gate_y2r,
        gate_x2s,
        gate_x2r,
        gate_x,
        gate_y,
    )

    chunk = heads_term.shape[-1] // DEPTH

    def flat_spec(rows):
        return pl.BlockSpec((rows, chunk), lambda i: (0, i))

    def row_sum(one, two, out):
        spec = flat_spec(one.shape[0])
        pltpu.emit_pipeline(
            add_two, grid=(DEPTH,), in_specs=[spec, spec], out_specs=[spec]
        )(one, two, out)

    def row_total(one, two, three, out):
        spec = flat_spec(one.shape[0])

        def body(one, two, three, out):
            out[...] = one[...].astype(wide) + two[...].astype(wide) + three[...].astype(wide)

        pltpu.emit_pipeline(
            body, grid=(DEPTH,), in_specs=[spec] * 3, out_specs=[spec]
        )(one, two, three, out)

    heads_x.wait_recv()
    row_sum(heads_term.at[x, 1 - y], heads_r.at[1 - y], heads_2s)
    heads_y = begin(remote(heads_2s, heads_2r, stage_s, stage_r, (2, 2), y_mate))
    for copy in hidden_y:
        copy.wait_recv()
    row_sum(hidden_term.at[1 - x, y], hidden_r.at[1 - x], hidden_2s)
    hidden_x = begin(remote(hidden_2s, hidden_2r, stage_s, stage_r, (3, 2), x_mate))

    pltpu.emit_pipeline(
        keep_body,
        grid=(DEPTH,),
        in_specs=[from_block(x * DEPTH)],
        out_specs=[block_of(inward_xk)],
    )(normed_ref, inward_xk)

    vector_y.wait_recv()
    vec_sum_y = vec_sum[...] + vec_y[...]
    vector_y.wait_send()
    slot = core * DEPTH + z
    vec_out[slot] = vec_sum_y
    vectors = []
    for flip, turn in members:
        cc, zz = target(flip, turn)
        vectors.append(
            begin(
                remote(
                    vec_out.at[slot],
                    vec_out.at[slot],
                    rows_s,
                    rows_r,
                    (2, flip * DEPTH + turn),
                    device(x, cc, zz, y),
                )
            )
        )

    gate_rest = last_stage(
        0,
        gate_xk,
        gate_xr,
        gate_yk,
        gate_yr,
        gate_y2r,
        gate_x2r,
        gate_fin,
        gate_rows,
        *gate_second,
    )
    inward_second = second_stage(
        1,
        inward_xk,
        inward_xr,
        inward_yk,
        inward_yr,
        inward_y2s,
        inward_y2r,
        inward_x2s,
        inward_x2r,
        inward_x,
        inward_y,
    )
    heads_y.wait_recv()
    row_total(heads_term.at[x, y], heads_r.at[y], heads_2r, heads_out)
    hidden_x.wait_recv()
    row_total(hidden_term.at[x, y], hidden_r.at[x], hidden_2r, hidden_out)
    inward_rest = last_stage(
        1,
        inward_xk,
        inward_xr,
        inward_yk,
        inward_yr,
        inward_y2r,
        inward_x2r,
        inward_fin,
        inward_rows_out,
        *inward_second,
    )

    own_tokens.wait()
    for k in range(1, DEPTH):
        z_copy(k).wait_recv()
    for first in range(0, ROWS, 64):
        rows = pl.ds(first, 64)
        grad = own_sum[rows]
        for k in range(DEPTH - 1):
            grad = grad + z_recv[k, rows].astype(wide)
        hat, inverse = normalised(token_rows[rows])
        scaled = grad * gain_ref[...]
        input_grad = inverse * (
            scaled
            - jnp.mean(scaled, axis=-1, keepdims=True)
            - hat * jnp.mean(scaled * hat, axis=-1, keepdims=True)
        )
        tokens_out[rows] = (cot_ref[rows].astype(wide) + input_grad).astype(low)

    for copies, own in (gate_rest, inward_rest):
        own.wait()
        for copy in copies:
            copy.wait_recv()
    for copy in vectors:
        copy.wait_recv()
    for copy in started:
        copy.wait_send()
    for k in range(DEPTH):
        core_copy(k).wait_send()
        if k > 0:
            z_copy(k).wait_send()


def finish(
    parts, got_dk, got_dv, gate_up_grad, pieces, tables, normed, gate_up, heads, hidden, weights,
    gain, cot
):
    low, wide = jnp.bfloat16, jnp.float32
    width = pieces.shape[-1]
    gate_xs, gate_xk, gate_ys, gate_yk = gate_up
    rows = width // 32
    anywhere = pl.BlockSpec(memory_space=pl.ANY)
    inside = pl.BlockSpec(memory_space=pltpu.VMEM)
    shape = jax.ShapeDtypeStruct
    half = 3 * HEAD_COLS // 2

    def staged(a, b):
        return [
            shape((DEPTH, 4 * rows, a), low),
            shape((PIECES, 2 * rows, b), low),
            shape((PIECES, rows, a), low),
            shape((PIECES, rows, a), low),
            shape((DEPTH, 2 * rows, b), low),
            shape((DEPTH, 2 * rows, b), low),
            shape((PIECES, rows, a + b), low),
        ]

    a, b = gate_xs.shape[-1], gate_ys.shape[-1]
    heads_rows, hidden_rows = heads.shape[2], hidden.shape[2]
    out_shapes = [
        shape((ROWS, width), low),
        shape((heads_rows, width), wide),
        shape((hidden_rows, width), wide),
        shape((PIECES, rows, a + b), low),
        shape((PIECES, rows, 2 * half), low),
        shape((PIECES, 8, width // 2), wide),
        shape((DEPTH, 4 * rows, half), low),
        shape((DEPTH, 4 * rows, half), wide),
        shape((PIECES, 2 * rows, half), low),
        shape((PIECES, 2 * rows, half), wide),
    ]
    out_shapes += staged(a, b) + staged(half, half)
    out_shapes += [
        shape((2, heads_rows, width), low),
        shape((heads_rows, width), low),
        shape((heads_rows, width), low),
        shape((2, hidden_rows, width), low),
        shape((hidden_rows, width), low),
        shape((hidden_rows, width), low),
    ]
    out_specs = [inside] + [anywhere] * 4 + [inside] + [anywhere] * (len(out_shapes) - 6)
    dma = pltpu.SemaphoreType.DMA
    outs = pl.pallas_call(
        finish_kernel,
        in_specs=[anywhere] * 17 + [inside] * 4,
        out_specs=out_specs,
        out_shape=out_shapes,
        scratch_shapes=[
            pltpu.VMEM((DEPTH, ROWS, width), low),
            pltpu.VMEM((DEPTH, ROWS, width), low),
            pltpu.VMEM((DEPTH - 1, ROWS, width), low),
            pltpu.VMEM((DEPTH - 1, ROWS, width), low),
            pltpu.VMEM((ROWS, width), wide),
            pltpu.VMEM((PIECES, ROWS, 3 * HEAD_COLS), low),
            pltpu.VMEM((ROWS, width), low),
            pltpu.VMEM((8, width // 2), wide),
            pltpu.VMEM((8, width // 2), wide),
            pltpu.VMEM((8, width // 2), wide),
            dma((DEPTH,)),
            dma((DEPTH,)),
            dma((DEPTH - 1,)),
            dma((DEPTH - 1,)),
            dma((4, 4)),
            dma((4, 4)),
            dma((3, PIECES)),
            dma((3, PIECES)),
            dma((2,)),
            dma((2,)),
            dma((3,)),
        ],
        compiler_params=params(60, collective_id=1, has_side_effects=True),
        cost_estimate=cost(0, 64 * MIB),
        name="finish",
    )(
        *parts,
        got_dk,
        got_dv,
        gate_up_grad,
        pieces,
        *tables,
        normed,
        *gate_up,
        heads,
        hidden,
        *weights,
        gain,
        cot,
    )
    return outs[:6]


def split_rows(term, y, keep_ref, send_ref):
    rows = term.shape[0] // 4
    even = jnp.concatenate([term[:rows], term[2 * rows : 3 * rows]], 0)
    odd = jnp.concatenate([term[rows : 2 * rows], term[3 * rows :]], 0)
    keep_ref[0] = jnp.where(y == 0, even, odd)
    send_ref[0] = jnp.where(y == 0, odd, even).astype(jnp.bfloat16)


def place_kernel(parts, in_ref, out_ref):
    each = in_ref.shape[2] // parts
    for part in range(parts):
        columns = slice(part * each, (part + 1) * each)
        line = jnp.concatenate([in_ref[n, :, columns] for n in range(PIECES)], 1)
        out_ref[:, part * PIECES * each : (part + 1) * PIECES * each] = line.astype(jnp.float32)


def place_rows(value, parts):
    rows, columns = value.shape[1], value.shape[2]
    return pl.pallas_call(
        functools.partial(place_kernel, parts),
        out_shape=jax.ShapeDtypeStruct((rows, PIECES * columns), jnp.float32),
        compiler_params=params(32),
        cost_estimate=cost(0, 4 * MIB),
        name="place_rows",
    )(value)


def rows_kernel(first, last, place_ref, left_ref, right_ref, out_ref):
    term = times_transposed(left_ref[...], right_ref[:, first:last])
    out_ref[0] = term.astype(out_ref.dtype)


def split_rows_kernel(first, last, place_ref, left_ref, right_ref, keep_ref, send_ref):
    y = place_ref[1]
    term = times_transposed(left_ref[...], right_ref[:, first:last])
    split_rows(term, y, keep_ref, send_ref)


def weight_grad(place, left, right, first, last, part):
    total, width = left.shape
    columns = last - first
    blocks = PIECES if part == "split" else PIECES // 2
    if part == "split":
        where = lambda i, place: (0, i)
    elif part == "keep":
        where = lambda i, place: (0, place[2] * DEPTH + i)
    else:
        where = lambda i, place: (0, (1 - place[2]) * DEPTH + i)
    size = width // PIECES
    high = size // 2 if part == "split" else size
    spec = pl.BlockSpec((1, high, columns), lambda i, place: (i, 0, 0))
    shape = (blocks, high, columns)
    if part == "split":
        specs = [spec, spec]
        shapes = [
            jax.ShapeDtypeStruct(shape, jnp.float32),
            jax.ShapeDtypeStruct(shape, jnp.bfloat16),
        ]
    else:
        specs = spec
        shapes = jax.ShapeDtypeStruct(shape, jnp.float32 if part == "keep" else jnp.bfloat16)
    return pl.pallas_call(
        functools.partial(
            split_rows_kernel if part == "split" else rows_kernel, first, last
        ),
        grid_spec=pltpu.PrefetchScalarGridSpec(
            num_scalar_prefetch=1,
            grid=(blocks,),
            in_specs=[
                pl.BlockSpec((total, size), where),
                pl.BlockSpec(right.shape, lambda i, place: (0, 0)),
            ],
            out_specs=specs,
        ),
        out_shape=shapes,
        compiler_params=params(48),
        cost_estimate=cost(2 * total * size * blocks * columns, 10 * MIB),
        name="weight_grad_" + part,
    )(place, left, right)


def lane_tables(positions):
    half = ROT // 2
    place = jnp.arange(HEAD_COLS, dtype=jnp.int32) % HEAD_DIM
    power = (place % half).astype(jnp.float32)
    frequency = jnp.where(place < ROT, rotary_base ** (-(2.0 * power) / ROT), 0.0)
    angles = positions.astype(jnp.float32)[..., None] * frequency
    sine = jnp.sin(angles)
    return (
        jnp.cos(angles),
        jnp.where(place < half, -sine, 0.0),
        jnp.where((place >= half) & (place < ROT), sine, 0.0),
    )


def shards_grouped(
    tokens,
    lengths,
    norm_gain,
    norm_shift,
    inward_weight,
    inward_bias,
    outward_weight,
    gate_up_weight,
    down_weight,
    cotangent,
):
    group_len, seqs, width = tokens.shape[1:]
    bucket, blk = lax.axis_index("bucket"), lax.axis_index("blk")
    x, core = bucket // 2, bucket % 2
    z, y = blk // 2, blk % 2

    own_rows = inward_weight.shape[0]
    hidden_each = gate_up_weight.shape[1] // (2 * 2 * 2 * DEPTH)
    gain_share, bias_share = norm_gain.shape[0], inward_bias.shape[0]
    shares = jnp.concatenate([norm_gain, norm_shift, inward_bias]).astype(jnp.bfloat16)
    shares = jnp.pad(shares, (0, 3 * HEAD_COLS - shares.shape[0]))
    inward = inward_weight.astype(jnp.bfloat16).reshape(own_rows, 3, 2, 2, DEPTH, 2 * HEAD_DIM)
    inward = jnp.transpose(inward, (3, 4, 0, 1, 2, 5)).reshape(2, DEPTH, own_rows, 3 * HEAD_COLS)
    inward = jnp.concatenate(
        [inward, jnp.broadcast_to(shares, (2, DEPTH, EXTRA, 3 * HEAD_COLS))], 2
    )
    gate_up = gate_up_weight.astype(jnp.bfloat16).reshape(own_rows, 2, 2, 2, DEPTH, hidden_each)
    gate_up = jnp.transpose(gate_up, (3, 4, 0, 1, 2, 5)).reshape(
        2, DEPTH, own_rows, 4 * hidden_each
    )
    rows_out = jnp.concatenate([outward_weight, down_weight]).astype(jnp.bfloat16)
    own_tokens = jnp.transpose(tokens[0], (1, 0, 2))
    pieces, inward, gate_up, rows_out = gather(
        own_tokens.reshape(ROWS, width), inward, gate_up, rows_out
    )
    vectors = inward[..., own_rows, :].reshape(-1, 3 * HEAD_COLS).astype(jnp.float32)
    inward = inward.reshape((-1,) + inward.shape[4:])
    gate_up = gate_up.reshape(width, -1)
    rows_out = rows_out.reshape((-1,) + rows_out.shape[2:])

    gain = vectors[:, :gain_share].reshape(1, width)
    shift = vectors[:, gain_share : 2 * gain_share].reshape(1, width)
    bias = vectors[:, 2 * gain_share : 2 * gain_share + bias_share].reshape(-1)

    def own_columns(values, each):
        split = values.reshape(2, 2, DEPTH, each)
        return one_of(one_of(split, core, 1), z, 1)

    key_bias = jnp.pad(
        own_columns(bias[2 * width :], 2 * ROT).reshape(LOCAL_HEADS, ROT),
        ((0, 0), (0, HEAD_DIM - ROT)),
    )
    own_bias = jnp.concatenate(
        [
            own_columns(bias[:width], 2 * HEAD_DIM).reshape(-1),
            key_bias.reshape(-1),
            own_columns(bias[width : 2 * width], 2 * HEAD_DIM).reshape(-1),
        ]
    ).reshape(1, -1)

    position = blk * group_len + jnp.arange(group_len, dtype=jnp.int32)
    valid = (position[None, :] < lengths[0][:, None]).astype(jnp.float32)[..., None]
    own_cotangent = jnp.transpose(cotangent[0], (1, 0, 2)).astype(jnp.float32)
    own_grad = (own_cotangent * valid).astype(jnp.bfloat16)
    grads = after(own_grad.reshape(ROWS, width), pieces)
    grads = jnp.stack(gather_pieces(grads))

    turns = (z - jnp.arange(DEPTH, dtype=jnp.int32)) % DEPTH
    tables = lane_tables(
        ((2 * turns + y) * group_len)[:, None] + jnp.arange(group_len, dtype=jnp.int32)
    )
    place = jnp.stack([z, y, x]).astype(jnp.int32)

    normed, queries, pairs = project(pieces, gain, shift, inward, own_bias, tables)
    other_pairs = lax.ppermute(pairs, "blk", ACROSS_Y)
    gate, up, hidden = feed(normed, gate_up)
    attended = attend(place, after(queries, hidden), pairs, other_pairs, seqs)
    branch_own, branch_other = branch_terms(attended, hidden, rows_out)
    branch_sums = core_sums(branch_own, branch_other)
    branch_sums = list(lax.optimization_barrier((*branch_sums, grads)))[:DEPTH]
    branch = scatter_pieces(branch_sums)
    branch = branch.reshape(seqs, group_len, width)
    inputs = own_tokens.astype(jnp.float32)
    layer_out = (inputs + valid * branch).astype(jnp.bfloat16)

    attended_grad, gate_up_grad = back(after(grads, branch_own), gate, up, rows_out)
    attended_grad = after(attended_grad, *branch_sums)
    dq, dk, dv, other_dk, other_dv = attend_back(
        place, queries, pairs, other_pairs, attended_grad, seqs
    )
    got_dk = lax.ppermute(other_dk, "blk", ACROSS_Y)
    got_dv = lax.ppermute(other_dv, "blk", ACROSS_Y)
    total = PIECES * ROWS
    flat_normed = after(normed, other_dk).reshape(total, width)
    flat_grads = after(grads, other_dk).reshape(total, width)

    right = gate_up_grad.reshape(total, -1)
    columns = right.shape[1]
    cut = -(-columns // 256) * 128
    gate_up_send = weight_grad(place, flat_normed, right, 0, cut, "send")
    gate_up_kept, gate_up_sent = weight_grad(place, flat_normed, right, cut, columns, "split")
    gate_up_keep = weight_grad(place, flat_normed, right, 0, cut, "keep")
    heads_term = times_transposed(attended.reshape(total, -1), flat_grads).astype(jnp.bfloat16)
    hidden_term = times_transposed(hidden.reshape(total, -1), flat_grads).astype(jnp.bfloat16)
    tokens_grad, outward_sum, down_sum, gate_up_rows, inward_rows_own, vectors = finish(
        (after(dq, layer_out), dk, dv),
        got_dk,
        got_dv,
        gate_up_grad,
        pieces,
        tables,
        normed.reshape(total, width),
        (gate_up_send, gate_up_keep, gate_up_sent, gate_up_kept),
        heads_term.reshape(2, 2, -1, width),
        hidden_term.reshape(2, 2, -1, width),
        (inward, gate_up),
        gain,
        jnp.transpose(cotangent[0], (1, 0, 2)).reshape(ROWS, width),
    )
    gate_up_sum = place_rows(gate_up_rows, 4)
    inward_sum = place_rows(inward_rows_own, 6)

    device = bucket * 2 * DEPTH + blk
    sums = jnp.sum(vectors[:, :4], axis=0).reshape(2, -1, gain_share)
    gain_sum = one_of(sums[0], device, 0)
    shift_sum = one_of(sums[1], device, 0)
    columns_sum = vectors[:, 4, : 3 * HEAD_COLS].reshape(PIECES, 3, 2, 2 * HEAD_DIM)
    columns_sum = jnp.transpose(columns_sum, (1, 2, 0, 3)).reshape(3, -1)
    key_rot = columns_sum[1].reshape(HEADS, HEAD_DIM)[:, :ROT]
    bias_all = jnp.concatenate([columns_sum[0], columns_sum[2], key_rot.reshape(-1)])
    bias_sum = one_of(bias_all.reshape(-1, bias_share), device, 0)

    def placed(value):
        value = value.reshape(seqs, group_len, width)
        return jnp.transpose(value, (1, 0, 2)).reshape(tokens.shape)

    return (
        placed(layer_out),
        placed(tokens_grad),
        gain_sum,
        shift_sum,
        inward_sum,
        bias_sum,
        outward_sum,
        gate_up_sum,
        down_sum,
    )


def solution(mesh):
    in_specs = (
        P("bucket", "blk", None, None),
        P("bucket", None),
        P(("bucket", "blk")),
        P(("bucket", "blk")),
        P(("bucket", "blk"), None),
        P(("bucket", "blk")),
        P(("bucket", "blk"), None),
        P(("bucket", "blk"), None),
        P(("bucket", "blk"), None),
        P("bucket", "blk", None, None),
    )
    out_specs = (
        P("bucket", "blk", None, None),
        P("bucket", "blk", None, None),
        P(("bucket", "blk")),
        P(("bucket", "blk")),
        P(("bucket", "blk"), None),
        P(("bucket", "blk")),
        P(("bucket", "blk"), None),
        P(("bucket", "blk"), None),
        P(("bucket", "blk"), None),
    )
    body = shards_grouped if fits_groups(mesh) else shards_general
    return jax.shard_map(body, mesh=mesh, in_specs=in_specs, out_specs=out_specs, check_vma=False)
```

```python
import functools

import jax
import jax.numpy as jnp
from jax import lax
from jax.experimental import pallas as pl
from jax.experimental.pallas import tpu as pltpu
from jax.sharding import PartitionSpec as P

HEADS = 32
HEAD_DIM = 64
ROT = 16


epsilon = 1e-05
rotary_base = 10000.0
masked_score = -1e30


def shifted(value, axis, by):
    count = lax.axis_size(axis)
    pairs = [(i, i + by) for i in range(count) if 0 <= i + by < count]
    return lax.ppermute(value, axis, pairs)


def shifted_2(value, axis, steps):
    count = lax.axis_size(axis)
    pairs = [(source, (source + steps) % count) for source in range(count)]
    return lax.ppermute(value, axis, pairs)


def keep_same(value):
    return value


def transposed_times(left, right):
    return lax.dot_general(
        left, right, (((1,), (1,)), ((), ())), preferred_element_type=jnp.float32
    )


def times_transposed(left, right):
    return lax.dot_general(
        left, right, (((0,), (0,)), ((), ())), preferred_element_type=jnp.float32
    )


def rotary_tables(positions):
    half_rot = ROT // 2
    frequency = rotary_base ** (-(2.0 * jnp.arange(half_rot).astype(jnp.float32)) / ROT)
    angles = positions.astype(jnp.float32)[:, None] * frequency[None, :]
    return (jnp.cos(angles), jnp.sin(angles))


def rotate(values, cos_table, sine_table):
    half_rot = ROT // 2
    front_half = values[..., :half_rot]
    back_half = values[..., half_rot:ROT]
    return jnp.concatenate(
        [
            front_half * cos_table - back_half * sine_table,
            back_half * cos_table + front_half * sine_table,
            values[..., ROT:],
        ],
        axis=-1,
    )


def split_pairs(packed):
    rows_here, seq_count, both_width = packed.shape
    half_width = both_width // 2
    keys_part = packed[..., :half_width].reshape(rows_here, seq_count, HEADS, HEAD_DIM)
    values_part = packed[..., half_width:].reshape(rows_here, seq_count, HEADS, HEAD_DIM)
    return (keys_part, values_part)


def block_scores(queries, key_block, query_start, key_start):
    scores = jnp.einsum("tshd,ushd->shtu", queries, key_block, preferred_element_type=jnp.float32)
    query_pos = query_start + jnp.arange(queries.shape[0], dtype=jnp.int32)
    key_pos = key_start + jnp.arange(key_block.shape[0], dtype=jnp.int32)
    allowed = (key_pos[None, :] <= query_pos[:, None])[None, None]
    return (jnp.where(allowed, scores, masked_score), allowed)


def forward_block(carried, queries, key_block, value_block, query_start, key_start):
    running_max, running_sum, weighted = carried
    scores, allowed = block_scores(queries, key_block, query_start, key_start)
    new_max = jnp.maximum(running_max, jnp.max(scores, axis=-1))
    rescale = jnp.exp(running_max - new_max)
    weights = jnp.where(allowed, jnp.exp(scores - new_max[..., None]), 0.0)
    running_sum = running_sum * rescale + jnp.sum(weights, axis=-1)
    update = jnp.einsum(
        "shtu,ushd->tshd",
        weights.astype(jnp.bfloat16),
        value_block,
        preferred_element_type=jnp.float32,
    )
    weighted = weighted * jnp.transpose(rescale, (2, 0, 1))[..., None] + update
    return (new_max, running_sum, weighted)


def pair_grads(
    queries, out_grads, log_norm, deltas, key_block, value_block, query_start, key_start
):
    scores, allowed = block_scores(queries, key_block, query_start, key_start)
    probability = jnp.where(allowed, jnp.exp(scores - log_norm[..., None]), 0.0)
    value_grad = jnp.einsum(
        "shtu,tshd->ushd",
        probability.astype(jnp.bfloat16),
        out_grads,
        preferred_element_type=jnp.float32,
    )
    prob_grad = jnp.einsum(
        "tshd,ushd->shtu", out_grads, value_block, preferred_element_type=jnp.float32
    )
    score_grad = (probability * (prob_grad - deltas[..., None])).astype(jnp.bfloat16)
    query_grad = jnp.einsum(
        "shtu,ushd->tshd", score_grad, key_block, preferred_element_type=jnp.float32
    )
    key_grad = jnp.einsum(
        "shtu,tshd->ushd", score_grad, queries, preferred_element_type=jnp.float32
    )
    return (query_grad, key_grad, value_grad)


def over_blocks(running, incoming, unit_rows, handle):
    total_rows = incoming[0].shape[0]
    block_count = total_rows // unit_rows
    block_rows = total_rows // block_count
    stacked = tuple(
        (member.reshape((block_count, block_rows) + member.shape[1:]) for member in incoming)
    )

    def visit(carried, element):
        block_index, members = element
        return (handle(carried, members, block_index * block_rows), None)

    running, unused = lax.scan(visit, running, (jnp.arange(block_count, dtype=jnp.int32), stacked))
    return running


def shards_general(
    tokens,
    lengths,
    norm_gain,
    norm_shift,
    inward_weight,
    inward_bias,
    outward_weight,
    gate_up_weight,
    down_weight,
    cotangent,
):
    group_len = tokens.shape[1]
    seq_count = tokens.shape[2]
    model_width = tokens.shape[3]
    row_total = group_len * seq_count
    block_total = lax.axis_size("blk")
    position = lax.axis_index("blk")
    own_start = position * group_len
    longest = jnp.max(lengths[0])
    active = own_start < longest
    gathered = (
        lax.all_gather(inward_weight.astype(jnp.bfloat16), ("bucket", "blk"), axis=0, tiled=True),
        lax.all_gather(outward_weight.astype(jnp.bfloat16), ("bucket", "blk"), axis=0, tiled=True),
        lax.all_gather(gate_up_weight.astype(jnp.bfloat16), ("bucket", "blk"), axis=0, tiled=True),
        lax.all_gather(down_weight.astype(jnp.bfloat16), ("bucket", "blk"), axis=0, tiled=True),
        lax.all_gather(norm_gain.astype(jnp.bfloat16), ("bucket", "blk"), axis=0, tiled=True),
        lax.all_gather(norm_shift.astype(jnp.bfloat16), ("bucket", "blk"), axis=0, tiled=True),
        lax.all_gather(inward_bias.astype(jnp.bfloat16), ("bucket", "blk"), axis=0, tiled=True),
    )
    inward_full, outward_full, gate_up_full, down_full, gain_full, shift_full, bias_full = gathered
    inputs = tokens.reshape(row_total, model_width).astype(jnp.float32)
    centred = inputs - jnp.mean(inputs, axis=-1, keepdims=True)
    variance = jnp.mean(centred * centred, axis=-1, keepdims=True)
    inverse = lax.rsqrt(variance + epsilon)
    normal_hat = centred * inverse
    normed_low = (
        normal_hat * gain_full.astype(jnp.float32) + shift_full.astype(jnp.float32)
    ).astype(jnp.bfloat16)
    bias_float = bias_full.astype(jnp.float32)
    key_bias = jnp.pad(
        bias_float[2 * model_width :].reshape(HEADS, ROT), ((0, 0), (0, HEAD_DIM - ROT))
    ).reshape(model_width)
    full_bias = jnp.concatenate(
        [bias_float[:model_width], key_bias, bias_float[model_width : 2 * model_width]]
    )
    projected = jnp.dot(normed_low, inward_full, preferred_element_type=jnp.float32) + full_bias
    projected = projected.reshape(group_len, seq_count, 3, HEADS, HEAD_DIM)
    cos_table, sine_table = rotary_tables(own_start + jnp.arange(group_len, dtype=jnp.int32))
    cos_table = cos_table[:, None, None, :]
    sine_table = sine_table[:, None, None, :]
    query_scale = HEAD_DIM ** (-0.5)
    queries = (rotate(projected[:, :, 0], cos_table, sine_table) * query_scale).astype(jnp.bfloat16)
    keys_low = rotate(projected[:, :, 1], cos_table, sine_table).astype(jnp.bfloat16)
    values_low = projected[:, :, 2].astype(jnp.bfloat16)
    packed = jnp.concatenate(
        [
            keys_low.reshape(group_len, seq_count, model_width),
            values_low.reshape(group_len, seq_count, model_width),
        ],
        axis=-1,
    )

    def forward_handle(carried, members, key_start):
        keys_part, values_part = split_pairs(members[0])
        needed = active & (key_start <= own_start + group_len - 1)

        def forward_compute(state_in):
            return forward_block(state_in, queries, keys_part, values_part, own_start, key_start)

        return lax.cond(needed, forward_compute, keep_same, carried)

    start_state = (
        jnp.full((seq_count, HEADS, group_len), masked_score, jnp.float32),
        jnp.zeros((seq_count, HEADS, group_len), jnp.float32),
        jnp.zeros((group_len, seq_count, HEADS, HEAD_DIM), jnp.float32),
    )
    running_max, running_sum, weighted = over_blocks(
        start_state, (lax.all_gather(packed, "blk", axis=0, tiled=True),), group_len, forward_handle
    )
    bounded = jnp.maximum(running_sum, 1.0)
    log_norm = running_max + jnp.log(bounded)
    attended = weighted / jnp.transpose(bounded, (2, 0, 1))[..., None]
    attended_rows = attended.astype(jnp.bfloat16).reshape(row_total, model_width)
    gate_up = jnp.dot(normed_low, gate_up_full, preferred_element_type=jnp.float32)
    ff_width = gate_up.shape[1] // 2
    gate_part = gate_up[:, :ff_width]
    up_part = gate_up[:, ff_width:]
    sigmoid_gate = jax.nn.sigmoid(gate_part)
    silu_gate = gate_part * sigmoid_gate
    hidden_low = (silu_gate * up_part).astype(jnp.bfloat16)
    branch = jnp.dot(attended_rows, outward_full, preferred_element_type=jnp.float32) + jnp.dot(
        hidden_low, down_full, preferred_element_type=jnp.float32
    )
    query_pos = own_start + jnp.arange(group_len, dtype=jnp.int32)
    valid_rows = (
        (query_pos[:, None] < lengths[0][None, :]).astype(jnp.float32).reshape(row_total, 1)
    )
    layer_out = (inputs + valid_rows * branch).astype(jnp.bfloat16).reshape(tokens.shape)
    inward_back = gathered[0]
    outward_back = gathered[1]
    gate_up_back = gathered[2]
    down_back = gathered[3]
    gain_float = gathered[4].astype(jnp.float32)
    cotangent_rows = cotangent.reshape(row_total, model_width).astype(jnp.float32)
    branch_grad = (cotangent_rows * valid_rows).astype(jnp.bfloat16)
    hidden_grad = transposed_times(branch_grad, down_back)
    gate_grad = hidden_grad * up_part * (sigmoid_gate + silu_gate * (1.0 - sigmoid_gate))
    up_grad = hidden_grad * silu_gate
    gate_up_grad_low = jnp.concatenate([gate_grad, up_grad], axis=-1).astype(jnp.bfloat16)
    down_term = times_transposed(hidden_low, branch_grad)
    gate_up_term = times_transposed(normed_low, gate_up_grad_low)
    gate_up_sum, down_sum = (
        lax.psum_scatter(gate_up_term, ("bucket", "blk"), scatter_dimension=0, tiled=True),
        lax.psum_scatter(down_term, ("bucket", "blk"), scatter_dimension=0, tiled=True),
    )
    normed_grad = transposed_times(gate_up_grad_low, gate_up_back)
    attended_grad = (
        transposed_times(branch_grad, outward_back)
        .astype(jnp.bfloat16)
        .reshape(group_len, seq_count, HEADS, HEAD_DIM)
    )
    outward_term = times_transposed(attended_rows, branch_grad)
    deltas = jnp.transpose(
        jnp.sum(attended_grad.astype(jnp.float32) * attended, axis=-1), (1, 2, 0)
    )
    grad_zeros = jnp.zeros((group_len, seq_count, 2 * model_width), jnp.float32)
    query_zeros = jnp.zeros((group_len, seq_count, HEADS, HEAD_DIM), jnp.float32)

    def cycle_turn(turn_index, carried):
        visiting, sums_now, grads_now = carried
        owner_index = (position - turn_index) % block_total
        key_start = owner_index * group_len
        needed = active & (owner_index <= position)

        def cycle_compute(sums_in):
            keys_part, values_part = split_pairs(visiting)
            query_part, key_part, value_part = pair_grads(
                queries,
                attended_grad,
                log_norm,
                deltas,
                keys_part,
                values_part,
                own_start,
                key_start,
            )
            merged = jnp.concatenate(
                [
                    key_part.reshape(group_len, seq_count, model_width),
                    value_part.reshape(group_len, seq_count, model_width),
                ],
                axis=-1,
            )
            return (sums_in[0] + merged, sums_in[1] + query_part)

        sums_now, grads_now = lax.cond(needed, cycle_compute, keep_same, (sums_now, grads_now))
        visiting = shifted(visiting, "blk", 1)
        sums_now = shifted_2(sums_now.astype(jnp.bfloat16), "blk", 1).astype(sums_now.dtype)
        return (visiting, sums_now, grads_now)

    unused, pair_sums, query_grads = lax.fori_loop(
        0, block_total, cycle_turn, (packed, grad_zeros, query_zeros)
    )
    key_grad = pair_sums[..., :model_width].reshape(group_len, seq_count, HEADS, HEAD_DIM)
    value_grad = pair_sums[..., model_width:].reshape(group_len, seq_count, HEADS, HEAD_DIM)
    back_sine = -sine_table
    query_back = rotate(query_grads * query_scale, cos_table, back_sine)
    key_back = rotate(key_grad, cos_table, back_sine)
    projected_grad = (
        jnp.stack([query_back, key_back, value_grad], axis=2)
        .reshape(row_total, 3 * model_width)
        .astype(jnp.bfloat16)
    )
    inward_term = times_transposed(normed_low, projected_grad)
    column_sums = jnp.sum(projected_grad.astype(jnp.float32), axis=0)
    key_bias_grad = (
        column_sums[model_width : 2 * model_width]
        .reshape(HEADS, HEAD_DIM)[:, :ROT]
        .reshape(HEADS * ROT)
    )
    bias_term = jnp.concatenate(
        [column_sums[:model_width], column_sums[2 * model_width :], key_bias_grad]
    )
    normed_grad = normed_grad + transposed_times(projected_grad, inward_back)
    gain_term = jnp.sum(normed_grad * normal_hat, axis=0)
    shift_term = jnp.sum(normed_grad, axis=0)
    scaled_grad = normed_grad * gain_float
    input_grad = inverse * (
        scaled_grad
        - jnp.mean(scaled_grad, axis=-1, keepdims=True)
        - normal_hat * jnp.mean(scaled_grad * normal_hat, axis=-1, keepdims=True)
    )
    tokens_grad = (cotangent_rows + input_grad).astype(jnp.bfloat16).reshape(tokens.shape)
    inward_sum, outward_sum, bias_sum, gain_sum, shift_sum = (
        lax.psum_scatter(inward_term, ("bucket", "blk"), scatter_dimension=0, tiled=True),
        lax.psum_scatter(outward_term, ("bucket", "blk"), scatter_dimension=0, tiled=True),
        lax.psum_scatter(bias_term, ("bucket", "blk"), scatter_dimension=0, tiled=True),
        lax.psum_scatter(gain_term, ("bucket", "blk"), scatter_dimension=0, tiled=True),
        lax.psum_scatter(shift_term, ("bucket", "blk"), scatter_dimension=0, tiled=True),
    )
    return (
        layer_out,
        tokens_grad,
        gain_sum,
        shift_sum,
        inward_sum,
        bias_sum,
        outward_sum,
        gate_up_sum,
        down_sum,
    )


DEPTH = 4
PIECES = 2 * DEPTH
ROWS = 256
EXTRA = 16
LOCAL_HEADS = 4
HEAD_COLS = LOCAL_HEADS * HEAD_DIM


MIB = 1024 * 1024


def fits_groups(mesh):
    return mesh.shape["bucket"] == 4 and mesh.shape["blk"] == 2 * DEPTH


def around(step):
    return [(z * 2 + y, ((z + step) % DEPTH) * 2 + y) for z in range(DEPTH) for y in range(2)]


def in_order(own, other, index, axis):
    return jnp.where(
        index == 0, jnp.stack([own, other], axis), jnp.stack([other, own], axis)
    )


def one_of(value, index, axis):
    return lax.dynamic_index_in_dim(value, index, axis, False)


def dot_rows(left, right):
    return lax.dot_general(
        left, right, (((1,), (0,)), ((), ())), preferred_element_type=jnp.float32
    )


def params(limit, **extra):
    return pltpu.CompilerParams(vmem_limit_bytes=limit * MIB, **extra)


def cost(flops, moved, exps=0):
    return pl.CostEstimate(flops=flops // 64, bytes_accessed=moved // 64, transcendentals=exps // 64)


def piece_spec(width):
    return pl.BlockSpec((1, ROWS, width), lambda i: (i, 0, 0))


def whole_spec(shape):
    return pl.BlockSpec(shape, lambda i: (0,) * len(shape))


def remote(src, dst, sends, recvs, index, device):
    return pltpu.make_async_remote_copy(
        src_ref=src,
        dst_ref=dst,
        send_sem=sends.at[index],
        recv_sem=recvs.at[index],
        device_id=device,
        device_id_type=pl.DeviceIdType.MESH,
    )


class Chain:
    def __init__(self, src, out, x, core, z, y, sems):
        up_s, down_s, arrive, core_s, core_r, local = sems
        self.z = z
        self.out = out

        def hop(k, src, slot, sends, dz):
            return pltpu.make_async_remote_copy(
                src_ref=src,
                dst_ref=out.at[slot],
                send_sem=sends.at[k],
                recv_sem=arrive.at[slot],
                device_id=(x * 2 + core, (z + dz) * 2 + y),
                device_id_type=pl.DeviceIdType.MESH,
            )

        mate = (x * 2 + 1 - core, z * 2 + y)
        self.ups = [hop(k, src if k == 0 else out.at[k], k + 1, up_s, 1) for k in range(3)]
        self.downs = [
            hop(k, src if k == 0 else out.at[DEPTH - k], 3 - k, down_s, -1) for k in range(3)
        ]
        self.cores = [
            remote(src if k == 0 else out.at[k], out.at[DEPTH + k], core_s, core_r, k, mate)
            for k in range(DEPTH)
        ]
        self.local = pltpu.make_async_copy(src, out.at[0], local)
        inner = (z > 0) & (z < DEPTH - 1)
        self.sent = [
            (z < DEPTH - 1, self.ups[0]),
            (z > 0, self.downs[0]),
            (inner, self.ups[1]),
            (inner, self.downs[1]),
            (z == DEPTH - 2, self.ups[2]),
            (z == 1, self.downs[2]),
        ]

    def start(self, *numbers):
        for number in numbers:
            condition, copy = self.sent[number]
            pl.when(condition)(copy.start)

    def first(self):
        self.start(0, 1)
        self.cores[0].start()
        self.local.start()

    def second(self):
        @pl.when(self.z > 0)
        def _():
            self.ups[0].wait_recv()
            self.cores[1].start()

        self.start(2)

        @pl.when(self.z < DEPTH - 1)
        def _():
            self.downs[0].wait_recv()
            self.cores[3].start()

        self.start(3)

    def third(self):
        self.ups[1].wait_recv()
        self.cores[2].start()
        self.start(4, 5)

    def fourth(self):
        @pl.when(self.z == DEPTH - 1)
        def _():
            self.ups[2].wait_recv()
            self.cores[3].start()

        @pl.when(self.z == 0)
        def _():
            self.downs[2].wait_recv()
            self.cores[1].start()

    def end(self):
        for copy in self.cores:
            copy.wait_recv()
            copy.wait_send()
        for condition, copy in self.sent:
            pl.when(condition)(copy.wait_send)
        self.local.wait()


def chain_sems():
    dma = pltpu.SemaphoreType.DMA
    return [dma((3,)), dma((3,)), dma((DEPTH,)), dma((DEPTH,)), dma((DEPTH,)), dma(())]


def greet(mates):
    barrier = pltpu.get_barrier_semaphore()
    for mate in mates:
        pl.semaphore_signal(
            barrier, inc=1, device_id=mate, device_id_type=pl.DeviceIdType.MESH
        )
    pl.semaphore_wait(barrier, len(mates))


def coordinates():
    bucket, blk = lax.axis_index("bucket"), lax.axis_index("blk")
    return bucket // 2, bucket % 2, blk // 2, blk % 2


def gather_kernel(
    x_ref,
    wi_ref,
    wg_ref,
    ro_ref,
    pieces,
    wi_out,
    wg_out,
    ro_out,
    group_s,
    group_r,
    across_s,
    across_r,
    rows_s,
    rows_r,
    local_sems,
    *chain,
):
    x, core, z, y = coordinates()

    def device(xx, cc, zz, yy):
        return (xx * 2 + cc, zz * 2 + yy)

    x_mate, y_mate = device(1 - x, core, z, y), device(x, core, z, 1 - y)
    members = [(flip, turn) for turn in (0, 1, 3, 2) for flip in (0, 1)]

    def target(flip, turn):
        return (core + flip) % 2, (z + turn) % DEPTH

    def source(flip, turn):
        return (core + flip) % 2, (z + DEPTH - turn) % DEPTH

    greet([device(x, *target(*m), y) for m in members[1:]] + [x_mate, y_mate])
    started = []

    def begin(copy):
        copy.start()
        started.append(copy)
        return copy

    local = [
        pltpu.make_async_copy(wi_ref.at[core, z], wi_out.at[x, core, z, y], local_sems.at[0]),
        pltpu.make_async_copy(wg_ref.at[core, z], wg_out.at[x, core, z, y], local_sems.at[1]),
        pltpu.make_async_copy(ro_ref, ro_out.at[x, y], local_sems.at[2]),
    ]
    for copy in local:
        copy.start()

    def send_group(which, ref, out):
        copies = {}
        for flip, turn in members[1:]:
            cc, zz = target(flip, turn)
            copies[flip, turn] = begin(
                remote(
                    ref.at[cc, zz],
                    out.at[x, core, z, y],
                    group_s,
                    group_r,
                    (which, flip * DEPTH + turn),
                    device(x, cc, zz, y),
                )
            )
        return copies

    inward = send_group(0, wi_ref, wi_out)
    tokens = Chain(x_ref, pieces, x, core, z, y, chain)
    tokens.first()
    rows_x = begin(remote(ro_ref, ro_out.at[x, y], rows_s, rows_r, 0, x_mate))
    rows_y = begin(remote(ro_ref, ro_out.at[x, y], rows_s, rows_r, 1, y_mate))
    gate_up = send_group(1, wg_ref, wg_out)

    def spread(which, ref, out, copies):
        pairs = {}
        for member in members:
            flip, turn = member
            cc, zz = source(flip, turn)
            if member == (0, 0):
                src = ref.at[core, z]
            else:
                copies[member].wait_recv()
                src = out.at[x, cc, zz, y]
            number = flip * DEPTH + turn
            pairs[member] = (
                begin(
                    remote(
                        src, out.at[x, cc, zz, y], across_s, across_r, (which, 0, number), x_mate
                    )
                ),
                begin(
                    remote(
                        src, out.at[x, cc, zz, y], across_s, across_r, (which, 1, number), y_mate
                    )
                ),
            )
        return pairs

    def corner(which, out, pairs):
        copies = []
        for member in members:
            flip, turn = member
            cc, zz = source(flip, turn)
            number = flip * DEPTH + turn
            if flip == 0:
                pairs[member][1].wait_recv()
                part = out.at[x, cc, zz, 1 - y]
                mate = x_mate
            else:
                pairs[member][0].wait_recv()
                part = out.at[1 - x, cc, zz, y]
                mate = y_mate
            copies.append(
                begin(remote(part, part, across_s, across_r, (which, 2, number), mate))
            )
        return copies

    inward_pairs = spread(0, wi_ref, wi_out, inward)

    tokens.second()
    inward_corner = corner(0, wi_out, inward_pairs)
    gate_up_pairs = spread(1, wg_ref, wg_out, gate_up)

    tokens.third()
    cut = (ro_ref.shape[0] // 32) * 16
    rows_y.wait_recv()
    low = ro_out.at[x, 1 - y, pl.ds(0, cut)]
    low_copy = begin(remote(low, low, rows_s, rows_r, 2, x_mate))
    rows_x.wait_recv()
    high = ro_out.at[1 - x, y, pl.ds(cut, ro_ref.shape[0] - cut)]
    high_copy = begin(remote(high, high, rows_s, rows_r, 3, y_mate))
    gate_up_corner = corner(1, wg_out, gate_up_pairs)

    tokens.fourth()

    for pairs in (inward_pairs, gate_up_pairs):
        for flip, turn in members:
            pairs[flip, turn][0 if flip == 0 else 1].wait_recv()
    for copy in inward_corner + gate_up_corner + [low_copy, high_copy]:
        copy.wait_recv()
    for copy in started:
        copy.wait_send()
    tokens.end()
    for copy in local:
        copy.wait()


def gather(tokens, inward, gate_up, rows_out):
    anywhere = pl.BlockSpec(memory_space=pl.ANY)
    low = jnp.bfloat16
    dma = pltpu.SemaphoreType.DMA
    return pl.pallas_call(
        gather_kernel,
        in_specs=[anywhere] * 4,
        out_specs=[anywhere] * 4,
        out_shape=[
            jax.ShapeDtypeStruct((PIECES,) + tokens.shape, low),
            jax.ShapeDtypeStruct((2, 2, DEPTH, 2) + inward.shape[2:], low),
            jax.ShapeDtypeStruct((2, 2, DEPTH, 2) + gate_up.shape[2:], low),
            jax.ShapeDtypeStruct((2, 2) + rows_out.shape, low),
        ],
        scratch_shapes=[
            dma((2, PIECES)),
            dma((2, PIECES)),
            dma((2, 3, PIECES)),
            dma((2, 3, PIECES)),
            dma((4,)),
            dma((4,)),
            dma((3,)),
        ]
        + chain_sems(),
        compiler_params=params(32, collective_id=0, has_side_effects=True),
        cost_estimate=cost(0, 64 * MIB),
        name="gather",
    )(tokens, inward, gate_up, rows_out)


def inward_rows(ref):
    blocks, rows, columns = ref.shape
    return ref[:, : rows - EXTRA].reshape(blocks * (rows - EXTRA), columns)


def outward_rows(ref):
    blocks, rows, columns = ref.shape
    return ref[:, :HEAD_DIM].reshape(blocks * HEAD_DIM, columns)


def down_rows(ref):
    blocks, rows, columns = ref.shape
    return ref[:, HEAD_DIM:].reshape(blocks * (rows - HEAD_DIM), columns)


def normalised(rows):
    inputs = rows.astype(jnp.float32)
    centred = inputs - jnp.mean(inputs, axis=-1, keepdims=True)
    variance = jnp.mean(centred * centred, axis=-1, keepdims=True)
    inverse = lax.rsqrt(variance + epsilon)
    return centred * inverse, inverse


def turned(values, cos_ref, first_ref, second_ref, sign):
    half = ROT // 2
    cos = jnp.concatenate([cos_ref[0], cos_ref[0]], 0)
    first = jnp.concatenate([first_ref[0], first_ref[0]], 0)
    second = jnp.concatenate([second_ref[0], second_ref[0]], 0)
    ahead = pltpu.roll(values, HEAD_COLS - half, 1)
    behind = pltpu.roll(values, half, 1)
    return values * cos + sign * (ahead * first + behind * second)


def forward_kernel(
    pieces_ref,
    grad_ref,
    cos_ref,
    first_ref,
    second_ref,
    gain_ref,
    shift_ref,
    bias_ref,
    wi_ref,
    wg_ref,
    rows_ref,
    normed_out,
    gate_out,
    up_out,
    grads_out,
    q_ref,
    kv_ref,
    okv_ref,
    hidden_ref,
    att_ref,
    own_sum,
    terms,
    core_send,
    core_recv,
    kv_s,
    kv_r,
    core_s,
    core_r,
    *chain,
):
    x, core, z, y = coordinates()
    low, wide = jnp.bfloat16, jnp.float32
    core_mate = (x * 2 + 1 - core, z * 2 + y)
    y_mate = (x * 2 + core, z * 2 + 1 - y)
    below = (x * 2 + core, lax.rem(z + DEPTH - 1, DEPTH) * 2 + y)
    above = (x * 2 + core, lax.rem(z + 1, DEPTH) * 2 + y)
    greet([core_mate, y_mate, below, above])
    grads = Chain(grad_ref, grads_out, x, core, z, y, chain)
    grads.first()

    def pair_copy(piece):
        return remote(kv_ref.at[piece], okv_ref.at[piece], kv_s, kv_r, piece, y_mate)

    def piece_body(tokens, cos, first, second, normed, gate_part, up_part):
        piece = pl.program_id(0)
        hat, _ = normalised(tokens[0])
        narrow = (hat * gain_ref[...] + shift_ref[...]).astype(low)
        normed[0] = narrow
        projected = dot_rows(narrow, inward_rows(wi_ref)) + bias_ref[...]
        tables = (cos, first, second)
        query = turned(projected[:, :HEAD_COLS], *tables, 1.0) * (HEAD_DIM**-0.5)
        key = turned(projected[:, HEAD_COLS : 2 * HEAD_COLS], *tables, 1.0)
        kv_ref[piece] = jnp.concatenate([key, projected[:, 2 * HEAD_COLS :]], 1).astype(low)
        pair_copy(piece).start()
        q_ref[piece] = query.astype(low)
        both = dot_rows(narrow, wg_ref[...])
        hidden = both.shape[1] // 2
        gate, up = both[:, :hidden], both[:, hidden:]
        gate_part[0] = gate
        up_part[0] = up
        hidden_ref[piece] = (gate * jax.nn.sigmoid(gate) * up).astype(low)

        @pl.when(piece == PIECES - 2)
        def _():
            grads.second()

    table_spec = pl.BlockSpec((1,) + cos_ref.shape[1:], lambda i: (i % DEPTH, 0, 0))
    pltpu.emit_pipeline(
        piece_body,
        grid=(PIECES,),
        in_specs=[piece_spec(pieces_ref.shape[-1])] + [table_spec] * 3,
        out_specs=[piece_spec(r.shape[-1]) for r in (normed_out, gate_out, up_out)],
    )(pieces_ref, cos_ref, first_ref, second_ref, normed_out, gate_out, up_out)

    for b in range(2):
        for j in range(DEPTH):
            pair_copy(b * DEPTH + j).wait_recv()

        def attend(t, carry):
            attend_one(Heads(b, t, z, y, q_ref, kv_ref, okv_ref), att_ref)
            return carry

        lax.fori_loop(0, 2 * LOCAL_HEADS // 2, attend, 0)
        if b == 0:
            grads.third()

    def core_copy(k):
        return remote(core_send.at[k], core_recv.at[k], core_s, core_r, k, core_mate)

    def term(piece):
        return dot_rows(att_ref[piece], outward_rows(rows_ref)) + dot_rows(
            hidden_ref[piece], down_rows(rows_ref)
        )

    def branch(i, carry):
        k = DEPTH - 1 - i
        core_send[k] = term(DEPTH + k).astype(low)
        core_copy(k).start()
        own = term(k)
        core_copy(k).wait_recv()
        both = own + core_recv[k].astype(wide)

        @pl.when(k > 0)
        def _():
            terms[k - 1] = both.astype(low)

        @pl.when(k == 0)
        def _():
            own_sum[...] = both

        return carry

    lax.fori_loop(0, DEPTH, branch, 0)
    grads.fourth()
    grads.end()
    for piece in range(PIECES):
        pair_copy(piece).wait_send()
    for k in range(DEPTH):
        core_copy(k).wait_send()


def forward(pieces, own_grad, tables, gain, shift, bias, inward, gate_up, rows_out):
    low, wide = jnp.bfloat16, jnp.float32
    width = pieces.shape[-1]
    hidden = gate_up.shape[1] // 2
    anywhere = pl.BlockSpec(memory_space=pl.ANY)
    inside = pl.BlockSpec(memory_space=pltpu.VMEM)
    shape = jax.ShapeDtypeStruct
    dma = pltpu.SemaphoreType.DMA
    return pl.pallas_call(
        forward_kernel,
        in_specs=[anywhere] * 5 + [inside] * 6,
        out_specs=[anywhere] * 4 + [inside] * 7,
        out_shape=[
            shape((PIECES, ROWS, width), low),
            shape((PIECES, ROWS, hidden), wide),
            shape((PIECES, ROWS, hidden), wide),
            shape((PIECES, ROWS, width), low),
            shape((PIECES, ROWS, HEAD_COLS), low),
            shape((PIECES, ROWS, 2 * HEAD_COLS), low),
            shape((PIECES, ROWS, 2 * HEAD_COLS), low),
            shape((PIECES, ROWS, hidden), low),
            shape((PIECES, ROWS, HEAD_COLS), low),
            shape((ROWS, width), wide),
            shape((DEPTH - 1, ROWS, width), low),
        ],
        scratch_shapes=[
            pltpu.VMEM((DEPTH, ROWS, width), low),
            pltpu.VMEM((DEPTH, ROWS, width), low),
            dma((PIECES,)),
            dma((PIECES,)),
            dma((DEPTH,)),
            dma((DEPTH,)),
        ]
        + chain_sems(),
        compiler_params=params(60, collective_id=2, has_side_effects=True),
        cost_estimate=cost(0, 64 * MIB),
        name="forward",
    )(pieces, own_grad, *tables, gain, shift, bias, inward, gate_up, rows_out)


def pair_rows(block):
    lane = lax.broadcasted_iota(jnp.int32, block.shape, 1)
    zero = jnp.zeros_like(block)
    return jnp.concatenate(
        [jnp.where(lane < HEAD_DIM, block, zero), jnp.where(lane < HEAD_DIM, zero, block)], 0
    )


def pair_lanes(rows):
    half = rows.shape[0] // 2
    lane = lax.broadcasted_iota(jnp.int32, (half, rows.shape[1]), 1)
    return jnp.where(lane < HEAD_DIM, rows[:half], rows[half:])


def block_probs(queries, keys, last, y):
    scores = transposed_times(queries, keys)
    rows, columns = scores.shape
    size = rows // 2
    row = lax.broadcasted_iota(jnp.int32, (rows, 2 * size), 0) % size
    column = lax.broadcasted_iota(jnp.int32, (rows, 2 * size), 1)
    allowed = (column <= row) | ((column >= size) & (y == 1))
    tail = jnp.where(allowed, scores[:, last * 2 * size :], masked_score)
    scores = tail if last == 0 else jnp.concatenate([scores[:, : last * 2 * size], tail], 1)
    weights = jnp.exp(scores - jnp.max(scores, axis=-1, keepdims=True))
    return weights * (1.0 / jnp.sum(weights, axis=-1, keepdims=True))


class Heads:
    def __init__(self, b, t, z, y, q_ref, kv_ref, okv_ref):
        size = ROWS // 2
        pair = 2 * HEAD_DIM
        self.b, self.z, self.y = b, z, y
        self.rows = pl.ds(pl.multiple_of((t // 2) * size, size), size)
        self.lanes = pl.ds(pl.multiple_of((t % 2) * pair, pair), pair)
        value_lanes = pl.ds(pl.multiple_of(HEAD_COLS + (t % 2) * pair, pair), pair)
        self.q_ref = q_ref

        def both(lanes):
            blocks = []
            for j in range(DEPTH):
                place = (self.piece(j), self.rows, lanes)
                blocks += [kv_ref[place], okv_ref[place]]
            return jnp.concatenate(blocks, 0)

        self.keys, self.values = both(self.lanes), both(value_lanes)

    def piece(self, j):
        return self.b * DEPTH + lax.rem(self.z + DEPTH - j, DEPTH)

    def place(self, j):
        return self.piece(j), self.rows, self.lanes

    def queries(self, j):
        return pair_rows(self.q_ref[self.place(j)])


def attend_one(heads, out_ref):
    for j in range(DEPTH):
        count = (j + 1) * ROWS
        probs = block_probs(heads.queries(j), heads.keys[:count], j, heads.y)
        out = dot_rows(probs.astype(jnp.bfloat16), heads.values[:count])
        out_ref[heads.place(j)] = pair_lanes(out).astype(jnp.bfloat16)


def attend_back_one(heads, grad_ref, dq_ref, dk_ref, dv_ref, odk_ref, odv_ref, key_sum, value_sum):
    half = ROWS // 2
    for j in reversed(range(DEPTH)):
        count = (j + 1) * ROWS
        queries = heads.queries(j)
        grads = pair_rows(grad_ref[heads.place(j)])
        keys, values = heads.keys[:count], heads.values[:count]
        probs = block_probs(queries, keys, j, heads.y)
        low = probs.astype(jnp.bfloat16)
        prob_grad = transposed_times(grads, values)
        delta = jnp.sum(low.astype(jnp.float32) * prob_grad, axis=-1, keepdims=True)
        score_grad = (probs * (prob_grad - delta)).astype(jnp.bfloat16)
        dq_ref[heads.place(j)] = pair_lanes(dot_rows(score_grad, keys))
        key_term = times_transposed(score_grad, queries)
        value_term = times_transposed(low, grads)
        if j == DEPTH - 1:
            key_sum[...] = key_term
            value_sum[...] = value_term
        else:
            key_sum[:count] += key_term
            value_sum[:count] += value_term
    for j in range(DEPTH):
        low = j * ROWS
        place = heads.place(j)
        dk_ref[place] = key_sum[low : low + half]
        dv_ref[place] = value_sum[low : low + half]
        odk_ref[place] = key_sum[low + half : low + ROWS].astype(jnp.bfloat16)
        odv_ref[place] = value_sum[low + half : low + ROWS].astype(jnp.bfloat16)


def backward_kernel(
    grads_ref,
    gate_ref,
    up_ref,
    normed_ref,
    pieces_ref,
    q_ref,
    kv_ref,
    okv_ref,
    hidden_ref,
    att_ref,
    rows_ref,
    own_sum,
    terms,
    valid_ref,
    gate_xs,
    gate_xk,
    gate_ys,
    gate_yk,
    heads_out,
    hidden_out,
    gu_ref,
    dq_ref,
    dk_ref,
    dv_ref,
    got_dk,
    got_dv,
    layer_out,
    attended_grad,
    odk_ref,
    odv_ref,
    key_sum,
    value_sum,
    z_recv,
    token_rows,
    z_s,
    z_r,
    pair_s,
    pair_r,
    local_sem,
):
    x, core, z, y = coordinates()
    low, wide = jnp.bfloat16, jnp.float32
    y_mate = (x * 2 + core, z * 2 + 1 - y)

    def z_mate(turn):
        return (x * 2 + core, lax.rem(z + turn, DEPTH) * 2 + y)

    greet([y_mate] + [z_mate(turn) for turn in range(1, DEPTH)])
    scattered = [
        remote(terms.at[k - 1], z_recv.at[k - 1], z_s, z_r, k - 1, z_mate(DEPTH - k))
        for k in range(1, DEPTH)
    ]
    for copy in scattered:
        copy.start()
    own_tokens = pltpu.make_async_copy(pieces_ref.at[0], token_rows, local_sem)
    own_tokens.start()

    def piece_body(grad_part, gate_part, up_part):
        piece = pl.program_id(0)
        grad = grad_part[0]
        attended_grad[piece] = transposed_times(grad, outward_rows(rows_ref)).astype(low)
        hidden_grad = transposed_times(grad, down_rows(rows_ref))
        gate = gate_part[0]
        sig = jax.nn.sigmoid(gate)
        silu = gate * sig
        gate_grad = hidden_grad * up_part[0] * (sig + silu * (1.0 - sig))
        up_grad = hidden_grad * silu
        gu_ref[piece] = jnp.concatenate([gate_grad, up_grad], 1).astype(low)

    pltpu.emit_pipeline(
        piece_body,
        grid=(PIECES,),
        in_specs=[piece_spec(r.shape[-1]) for r in (grads_ref, gate_ref, up_ref)],
    )(grads_ref, gate_ref, up_ref)

    def pair_copies(b, t):
        size, pair = ROWS // 2, 2 * HEAD_DIM
        at = (
            pl.ds(b * DEPTH, DEPTH),
            pl.ds(pl.multiple_of((t // 2) * size, size), size),
            pl.ds(pl.multiple_of((t % 2) * pair, pair), pair),
        )
        number = b * DEPTH + t
        return (
            remote(odk_ref.at[at], got_dk.at[at], pair_s, pair_r, (0, number), y_mate),
            remote(odv_ref.at[at], got_dv.at[at], pair_s, pair_r, (1, number), y_mate),
        )

    def attend_back(i, carry):
        b, t = i // DEPTH, i % DEPTH
        heads = Heads(b, t, z, y, q_ref, kv_ref, okv_ref)
        attend_back_one(
            heads, attended_grad, dq_ref, dk_ref, dv_ref, odk_ref, odv_ref, key_sum, value_sum
        )
        for copy in pair_copies(b, t):
            copy.start()
        return carry

    lax.fori_loop(0, PIECES, attend_back, 0)

    total, width = normed_ref.shape
    size = width // PIECES
    columns = gu_ref.shape[-1]
    cut = gate_xs.shape[-1]

    def right(first, last):
        return gu_ref[...].reshape(total, columns)[:, first:last]

    def whole_body(left, out):
        out[0] = times_transposed(left[...], right(0, cut)).astype(out.dtype)

    def split_body(left, keep, send):
        split_rows(times_transposed(left[...], right(cut, columns)), y, keep, send)

    def from_block(base):
        return pl.BlockSpec((total, size), lambda i: (0, base + i))

    def block_of(array):
        return pl.BlockSpec((1,) + array.shape[1:], lambda i: (i, 0, 0))

    pltpu.emit_pipeline(
        whole_body,
        grid=(DEPTH,),
        in_specs=[from_block((1 - x) * DEPTH)],
        out_specs=[block_of(gate_xs)],
    )(normed_ref, gate_xs)
    pltpu.emit_pipeline(
        split_body,
        grid=(PIECES,),
        in_specs=[from_block(0)],
        out_specs=[block_of(gate_yk), block_of(gate_ys)],
    )(normed_ref, gate_yk, gate_ys)
    pltpu.emit_pipeline(
        whole_body,
        grid=(DEPTH,),
        in_specs=[from_block(x * DEPTH)],
        out_specs=[block_of(gate_xk)],
    )(normed_ref, gate_xk)

    flat_grads = grads_ref.reshape(total, width)
    wide_size = 2 * size

    def rows_body(right, heads, hidden):
        grad = right[...]
        attended = att_ref[...].reshape(total, HEAD_COLS)
        term = times_transposed(attended, grad).astype(low)
        heads[...] = term.reshape(heads.shape)
        hidden_rows = hidden_ref[...].reshape(total, hidden_ref.shape[-1])
        term = times_transposed(hidden_rows, grad).astype(low)
        hidden[...] = term.reshape(hidden.shape)

    def column_block(array):
        return pl.BlockSpec(array.shape[:2] + (wide_size,), lambda i: (0, 0, i))

    pltpu.emit_pipeline(
        rows_body,
        grid=(width // wide_size,),
        in_specs=[pl.BlockSpec((total, wide_size), lambda i: (0, i))],
        out_specs=[column_block(heads_out), column_block(hidden_out)],
    )(flat_grads, heads_out, hidden_out)

    own_tokens.wait()
    for copy in scattered:
        copy.wait_recv()
    for first in range(0, ROWS, 64):
        rows = pl.ds(first, 64)
        branch = own_sum[rows]
        for k in range(DEPTH - 1):
            branch = branch + z_recv[k, rows].astype(wide)
        layer_out[rows] = (token_rows[rows].astype(wide) + valid_ref[rows] * branch).astype(low)

    for b in range(2):
        for t in range(DEPTH):
            for copy in pair_copies(b, t):
                copy.wait_recv()
                copy.wait_send()
    for copy in scattered:
        copy.wait_send()


def backward(
    grads, gate, up, normed, pieces, queries, pairs, other_pairs, hidden, attended, rows_out,
    own_sum, terms, valid
):
    low, wide = jnp.bfloat16, jnp.float32
    width = pieces.shape[-1]
    each = hidden.shape[-1]
    columns = 2 * each
    cut = -(-columns // 256) * 128
    rows = width // 32
    head_rows = HEAD_DIM
    anywhere = pl.BlockSpec(memory_space=pl.ANY)
    inside = pl.BlockSpec(memory_space=pltpu.VMEM)
    shape = jax.ShapeDtypeStruct
    dma = pltpu.SemaphoreType.DMA
    return pl.pallas_call(
        backward_kernel,
        in_specs=[anywhere] * 5 + [inside] * 9,
        out_specs=[anywhere] * 6 + [inside] * 7,
        out_shape=[
            shape((DEPTH, 4 * rows, cut), low),
            shape((DEPTH, 4 * rows, cut), wide),
            shape((PIECES, 2 * rows, columns - cut), low),
            shape((PIECES, 2 * rows, columns - cut), wide),
            shape((4, head_rows, width), low),
            shape((4, each // 4, width), low),
            shape((PIECES, ROWS, columns), low),
            shape((PIECES, ROWS, HEAD_COLS), wide),
            shape((PIECES, ROWS, HEAD_COLS), wide),
            shape((PIECES, ROWS, HEAD_COLS), wide),
            shape((PIECES, ROWS, HEAD_COLS), low),
            shape((PIECES, ROWS, HEAD_COLS), low),
            shape((ROWS, width), low),
        ],
        scratch_shapes=[
            pltpu.VMEM((PIECES, ROWS, HEAD_COLS), low),
            pltpu.VMEM((PIECES, ROWS, HEAD_COLS), low),
            pltpu.VMEM((PIECES, ROWS, HEAD_COLS), low),
            pltpu.VMEM((DEPTH * ROWS, 2 * HEAD_DIM), wide),
            pltpu.VMEM((DEPTH * ROWS, 2 * HEAD_DIM), wide),
            pltpu.VMEM((DEPTH - 1, ROWS, width), low),
            pltpu.VMEM((ROWS, width), low),
            dma((DEPTH - 1,)),
            dma((DEPTH - 1,)),
            dma((2, PIECES)),
            dma((2, PIECES)),
            dma(()),
        ],
        compiler_params=params(62, collective_id=3, has_side_effects=True),
        cost_estimate=cost(0, 64 * MIB),
        name="backward",
    )(
        grads, gate, up, normed, pieces, queries, pairs, other_pairs, hidden, attended, rows_out,
        own_sum, terms, valid
    )


def finish_kernel(
    dq_ref,
    dk_ref,
    dv_ref,
    odk_ref,
    odv_ref,
    gu_ref,
    pieces_ref,
    cos_ref,
    first_ref,
    second_ref,
    normed_ref,
    gate_xs,
    gate_xk,
    gate_ys,
    gate_yk,
    heads_term,
    hidden_term,
    wi_ref,
    wg_ref,
    gain_ref,
    cot_ref,
    tokens_out,
    heads_out,
    hidden_out,
    gate_rows,
    inward_rows_out,
    vec_out,
    inward_xs,
    inward_xk,
    inward_ys,
    inward_yk,
    gate_xr,
    gate_yr,
    gate_y2s,
    gate_y2r,
    gate_x2s,
    gate_x2r,
    gate_fin,
    inward_xr,
    inward_yr,
    inward_y2s,
    inward_y2r,
    inward_x2s,
    inward_x2r,
    inward_fin,
    heads_r,
    heads_2s,
    heads_2r,
    hidden_r,
    hidden_2s,
    hidden_2r,
    core_send,
    core_recv,
    z_send,
    z_recv,
    own_sum,
    pg_ref,
    token_rows,
    vec_sum,
    vec_x,
    vec_y,
    core_s,
    core_r,
    z_s,
    z_r,
    stage_s,
    stage_r,
    rows_s,
    rows_r,
    vec_s,
    vec_r,
    local_sems,
):
    x, core, z, y = coordinates()
    low = jnp.bfloat16
    wide = jnp.float32

    def device(xx, cc, zz, yy):
        return (xx * 2 + cc, zz * 2 + yy)

    x_mate, y_mate = device(1 - x, core, z, y), device(x, core, z, 1 - y)
    core_mate = device(x, 1 - core, z, y)
    members = [(flip, turn) for turn in (2, 1, 3, 0) for flip in (1, 0)][:-1]

    def target(flip, turn):
        return (core + flip) % 2, (z + turn) % DEPTH

    greet([device(x, *target(*m), y) for m in members] + [x_mate, y_mate])

    started = []

    def begin(copy):
        copy.start()
        started.append(copy)
        return copy

    gate_x = begin(remote(gate_xs, gate_xr, stage_s, stage_r, (0, 0), x_mate))
    gate_y = begin(remote(gate_ys, gate_yr, stage_s, stage_r, (0, 1), y_mate))
    heads_x = begin(remote(heads_term.at[1 - x], heads_r, stage_s, stage_r, (2, 0), x_mate))
    hidden_y = [
        begin(
            remote(hidden_term.at[i, 1 - y], hidden_r.at[i], stage_s, stage_r, (3, i), y_mate)
        )
        for i in range(2)
    ]
    own_tokens = pltpu.make_async_copy(pieces_ref.at[0], token_rows, local_sems.at[0])
    own_tokens.start()

    vec_sum[...] = jnp.zeros_like(vec_sum)

    def core_copy(k):
        return remote(core_send.at[k], core_recv.at[k], core_s, core_r, k, core_mate)

    def z_copy(k):
        goal = device(x, core, (z + DEPTH - k) % DEPTH, y)
        return remote(z_send.at[k - 1], z_recv.at[k - 1], z_s, z_r, k - 1, goal)

    def piece_of(i):
        k = DEPTH - 1 - i // 2
        return k + DEPTH * (1 - i % 2)

    def piece_body(
        dq, dk, dv, odk, odv, gu, tokens, cos, first, second
    ):
        step = pl.program_id(0)
        k = DEPTH - 1 - step // 2
        piece = piece_of(step)
        tables = (cos, first, second)
        query = turned(dq[0] * (HEAD_DIM**-0.5), *tables, -1.0)
        key = turned(dk[0] + odk[0].astype(wide), *tables, -1.0)
        value = dv[0] + odv[0].astype(wide)
        narrow = jnp.concatenate([query, key, value], 1).astype(low)
        pg_ref[piece] = narrow
        grad = transposed_times(narrow, inward_rows(wi_ref))
        grad += transposed_times(gu[0], wg_ref[...])
        hat, _ = normalised(tokens[0])
        half = grad.shape[1] // 2
        for row, total in (
            (0, jnp.sum(grad * hat, axis=0, keepdims=True)),
            (2, jnp.sum(grad, axis=0, keepdims=True)),
        ):
            vec_sum[row : row + 1] += total[:, :half]
            vec_sum[row + 1 : row + 2] += total[:, half:]
        vec_sum[4:5, : 3 * HEAD_COLS] += jnp.sum(narrow.astype(wide), axis=0, keepdims=True)

        @pl.when(step % 2 == 0)
        def _():
            core_send[k] = grad.astype(low)
            core_copy(k).start()

        @pl.when(step % 2 == 1)
        def _():
            core_copy(k).wait_recv()
            both = grad + core_recv[k].astype(wide)

            @pl.when(k > 0)
            def _():
                z_send[k - 1] = both.astype(low)
                z_copy(k).start()

            @pl.when(k == 0)
            def _():
                own_sum[...] = both

    def by_piece(width):
        return pl.BlockSpec((1, ROWS, width), lambda i: (piece_of(i), 0, 0))

    table_spec = pl.BlockSpec(
        (1,) + cos_ref.shape[1:], lambda i: (piece_of(i) % DEPTH, 0, 0)
    )
    pltpu.emit_pipeline(
        piece_body,
        grid=(PIECES,),
        in_specs=[by_piece(HEAD_COLS)] * 5
        + [by_piece(gu_ref.shape[-1]), by_piece(pieces_ref.shape[-1])]
        + [table_spec] * 3,
    )(
        dq_ref,
        dk_ref,
        dv_ref,
        odk_ref,
        odv_ref,
        gu_ref,
        pieces_ref,
        cos_ref,
        first_ref,
        second_ref,
    )
    vector_x = remote(vec_sum, vec_x, vec_s, vec_r, 0, x_mate)
    vector_x.start()

    total, width = normed_ref.shape
    size = width // PIECES
    cut = 3 * HEAD_COLS // 2

    def projected(first, last):
        return pg_ref[...].reshape(total, 3 * HEAD_COLS)[:, first:last]

    def send_body(left, out):
        out[0] = times_transposed(left[...], projected(0, cut)).astype(low)

    def keep_body(left, out):
        out[0] = times_transposed(left[...], projected(0, cut))

    def split_body(left, keep, send):
        term = times_transposed(left[...], projected(cut, 2 * cut))
        split_rows(term, y, keep, send)

    def from_block(base):
        return pl.BlockSpec((total, size), lambda i: (0, base + i))

    def block_of(array):
        return pl.BlockSpec((1,) + array.shape[1:], lambda i: (i, 0, 0))

    pltpu.emit_pipeline(
        send_body,
        grid=(DEPTH,),
        in_specs=[from_block((1 - x) * DEPTH)],
        out_specs=[block_of(inward_xs)],
    )(normed_ref, inward_xs)
    inward_x = begin(remote(inward_xs, inward_xr, stage_s, stage_r, (1, 0), x_mate))
    pltpu.emit_pipeline(
        split_body,
        grid=(PIECES,),
        in_specs=[from_block(0)],
        out_specs=[block_of(inward_yk), block_of(inward_ys)],
    )(normed_ref, inward_yk, inward_ys)
    inward_y = begin(remote(inward_ys, inward_yr, stage_s, stage_r, (1, 1), y_mate))

    vector_x.wait_recv()
    vec_sum_x = vec_sum[...] + vec_x[...]
    vector_x.wait_send()
    vec_sum[...] = vec_sum_x
    vector_y = remote(vec_sum, vec_y, vec_s, vec_r, 1, y_mate)
    vector_y.start()

    def add_two(one, two, out):
        out[...] = (one[...].astype(wide) + two[...].astype(wide)).astype(out.dtype)

    def second_stage(which, xk, xr, yk, yr, y2s, y2r, x2s, x2r, first_x, first_y):
        quarter = xk.shape[1] // 4
        rows_at = pl.BlockSpec(
            (1, quarter, xk.shape[2]), lambda i: (i // 2, (i % 2) * 2 + (1 - y), 0)
        )
        first_x.wait_recv()
        pltpu.emit_pipeline(
            add_two, grid=(PIECES,), in_specs=[rows_at, rows_at], out_specs=[block_of(y2s)]
        )(xk, xr, y2s)
        over_y = begin(remote(y2s, y2r, stage_s, stage_r, (which, 2), y_mate))
        part = pl.BlockSpec((1,) + yk.shape[1:], lambda i: ((1 - x) * DEPTH + i, 0, 0))
        first_y.wait_recv()
        pltpu.emit_pipeline(
            add_two, grid=(DEPTH,), in_specs=[part, part], out_specs=[block_of(x2s)]
        )(yk, yr, x2s)
        over_x = begin(remote(x2s, x2r, stage_s, stage_r, (which, 3), x_mate))
        return over_y, over_x

    def last_stage(which, xk, xr, yk, yr, y2r, x2r, fin, rows, over_y, over_x):
        quarter = xk.shape[1] // 4
        cut = xk.shape[2]
        rows_at = pl.BlockSpec((1, quarter, cut), lambda i: (i // 2, (i % 2) * 2 + y, 0))
        part = pl.BlockSpec(
            (1, quarter, yk.shape[2]), lambda i: (x * DEPTH + i // 2, i % 2, 0)
        )
        last = pl.BlockSpec((1, quarter, yk.shape[2]), lambda i: (i // 2, i % 2, 0))

        def body(one, two, three, four, five, six, out):
            left = one[0] + two[0].astype(wide) + three[0].astype(wide)
            right = four[0] + five[0].astype(wide) + six[0].astype(wide)
            out[0] = jnp.concatenate([left, right], 1).astype(low)

        over_y.wait_recv()
        over_x.wait_recv()
        pltpu.emit_pipeline(
            body,
            grid=(PIECES,),
            in_specs=[rows_at, rows_at, block_of(y2r), part, part, last],
            out_specs=[block_of(fin)],
        )(xk, xr, y2r, yk, yr, x2r, fin)
        slot = core * DEPTH + z
        copies = []
        for flip, turn in members:
            cc, zz = target(flip, turn)
            copies.append(
                begin(
                    remote(
                        fin.at[cc * DEPTH + zz],
                        rows.at[slot],
                        rows_s,
                        rows_r,
                        (which, flip * DEPTH + turn),
                        device(x, cc, zz, y),
                    )
                )
            )
        own = pltpu.make_async_copy(fin.at[slot], rows.at[slot], local_sems.at[1 + which])
        own.start()
        return copies, own

    gate_second = second_stage(
        0,
        gate_xk,
        gate_xr,
        gate_yk,
        gate_yr,
        gate_y2s,
        gate_y2r,
        gate_x2s,
        gate_x2r,
        gate_x,
        gate_y,
    )

    chunk = heads_term.shape[-1] // DEPTH

    def flat_spec(rows):
        return pl.BlockSpec((rows, chunk), lambda i: (0, i))

    def row_sum(one, two, out):
        spec = flat_spec(one.shape[0])
        pltpu.emit_pipeline(
            add_two, grid=(DEPTH,), in_specs=[spec, spec], out_specs=[spec]
        )(one, two, out)

    def row_total(one, two, three, out):
        spec = flat_spec(one.shape[0])

        def body(one, two, three, out):
            out[...] = one[...].astype(wide) + two[...].astype(wide) + three[...].astype(wide)

        pltpu.emit_pipeline(
            body, grid=(DEPTH,), in_specs=[spec] * 3, out_specs=[spec]
        )(one, two, three, out)

    heads_x.wait_recv()
    row_sum(heads_term.at[x, 1 - y], heads_r.at[1 - y], heads_2s)
    heads_y = begin(remote(heads_2s, heads_2r, stage_s, stage_r, (2, 2), y_mate))
    for copy in hidden_y:
        copy.wait_recv()
    row_sum(hidden_term.at[1 - x, y], hidden_r.at[1 - x], hidden_2s)
    hidden_x = begin(remote(hidden_2s, hidden_2r, stage_s, stage_r, (3, 2), x_mate))

    pltpu.emit_pipeline(
        keep_body,
        grid=(DEPTH,),
        in_specs=[from_block(x * DEPTH)],
        out_specs=[block_of(inward_xk)],
    )(normed_ref, inward_xk)

    vector_y.wait_recv()
    vec_sum_y = vec_sum[...] + vec_y[...]
    vector_y.wait_send()
    slot = core * DEPTH + z
    vec_out[slot] = vec_sum_y
    vectors = []
    for flip, turn in members:
        cc, zz = target(flip, turn)
        vectors.append(
            begin(
                remote(
                    vec_out.at[slot],
                    vec_out.at[slot],
                    rows_s,
                    rows_r,
                    (2, flip * DEPTH + turn),
                    device(x, cc, zz, y),
                )
            )
        )

    gate_rest = last_stage(
        0,
        gate_xk,
        gate_xr,
        gate_yk,
        gate_yr,
        gate_y2r,
        gate_x2r,
        gate_fin,
        gate_rows,
        *gate_second,
    )
    inward_second = second_stage(
        1,
        inward_xk,
        inward_xr,
        inward_yk,
        inward_yr,
        inward_y2s,
        inward_y2r,
        inward_x2s,
        inward_x2r,
        inward_x,
        inward_y,
    )
    heads_y.wait_recv()
    row_total(heads_term.at[x, y], heads_r.at[y], heads_2r, heads_out)
    hidden_x.wait_recv()
    row_total(hidden_term.at[x, y], hidden_r.at[x], hidden_2r, hidden_out)
    inward_rest = last_stage(
        1,
        inward_xk,
        inward_xr,
        inward_yk,
        inward_yr,
        inward_y2r,
        inward_x2r,
        inward_fin,
        inward_rows_out,
        *inward_second,
    )

    own_tokens.wait()
    for k in range(1, DEPTH):
        z_copy(k).wait_recv()
    for first in range(0, ROWS, 64):
        rows = pl.ds(first, 64)
        grad = own_sum[rows]
        for k in range(DEPTH - 1):
            grad = grad + z_recv[k, rows].astype(wide)
        hat, inverse = normalised(token_rows[rows])
        scaled = grad * gain_ref[...]
        input_grad = inverse * (
            scaled
            - jnp.mean(scaled, axis=-1, keepdims=True)
            - hat * jnp.mean(scaled * hat, axis=-1, keepdims=True)
        )
        tokens_out[rows] = (cot_ref[rows].astype(wide) + input_grad).astype(low)

    for copies, own in (gate_rest, inward_rest):
        own.wait()
        for copy in copies:
            copy.wait_recv()
    for copy in vectors:
        copy.wait_recv()
    for copy in started:
        copy.wait_send()
    for k in range(DEPTH):
        core_copy(k).wait_send()
        if k > 0:
            z_copy(k).wait_send()


def finish(
    parts, gate_up_grad, pieces, tables, normed, gate_up, heads, hidden, weights, gain, cot
):
    low, wide = jnp.bfloat16, jnp.float32
    width = pieces.shape[-1]
    gate_xs, gate_xk, gate_ys, gate_yk = gate_up
    rows = width // 32
    anywhere = pl.BlockSpec(memory_space=pl.ANY)
    inside = pl.BlockSpec(memory_space=pltpu.VMEM)
    shape = jax.ShapeDtypeStruct
    half = 3 * HEAD_COLS // 2

    def staged(a, b):
        return [
            shape((DEPTH, 4 * rows, a), low),
            shape((PIECES, 2 * rows, b), low),
            shape((PIECES, rows, a), low),
            shape((PIECES, rows, a), low),
            shape((DEPTH, 2 * rows, b), low),
            shape((DEPTH, 2 * rows, b), low),
            shape((PIECES, rows, a + b), low),
        ]

    a, b = gate_xs.shape[-1], gate_ys.shape[-1]
    heads_rows, hidden_rows = heads.shape[2], hidden.shape[2]
    out_shapes = [
        shape((ROWS, width), low),
        shape((heads_rows, width), wide),
        shape((hidden_rows, width), wide),
        shape((PIECES, rows, a + b), low),
        shape((PIECES, rows, 2 * half), low),
        shape((PIECES, 8, width // 2), wide),
        shape((DEPTH, 4 * rows, half), low),
        shape((DEPTH, 4 * rows, half), wide),
        shape((PIECES, 2 * rows, half), low),
        shape((PIECES, 2 * rows, half), wide),
    ]
    out_shapes += staged(a, b) + staged(half, half)
    out_shapes += [
        shape((2, heads_rows, width), low),
        shape((heads_rows, width), low),
        shape((heads_rows, width), low),
        shape((2, hidden_rows, width), low),
        shape((hidden_rows, width), low),
        shape((hidden_rows, width), low),
    ]
    out_specs = [inside] + [anywhere] * 4 + [inside] + [anywhere] * (len(out_shapes) - 6)
    dma = pltpu.SemaphoreType.DMA
    outs = pl.pallas_call(
        finish_kernel,
        in_specs=[anywhere] * 17 + [inside] * 4,
        out_specs=out_specs,
        out_shape=out_shapes,
        scratch_shapes=[
            pltpu.VMEM((DEPTH, ROWS, width), low),
            pltpu.VMEM((DEPTH, ROWS, width), low),
            pltpu.VMEM((DEPTH - 1, ROWS, width), low),
            pltpu.VMEM((DEPTH - 1, ROWS, width), low),
            pltpu.VMEM((ROWS, width), wide),
            pltpu.VMEM((PIECES, ROWS, 3 * HEAD_COLS), low),
            pltpu.VMEM((ROWS, width), low),
            pltpu.VMEM((8, width // 2), wide),
            pltpu.VMEM((8, width // 2), wide),
            pltpu.VMEM((8, width // 2), wide),
            dma((DEPTH,)),
            dma((DEPTH,)),
            dma((DEPTH - 1,)),
            dma((DEPTH - 1,)),
            dma((4, 4)),
            dma((4, 4)),
            dma((3, PIECES)),
            dma((3, PIECES)),
            dma((2,)),
            dma((2,)),
            dma((3,)),
        ],
        compiler_params=params(60, collective_id=1, has_side_effects=True),
        cost_estimate=cost(0, 64 * MIB),
        name="finish",
    )(
        *parts,
        gate_up_grad,
        pieces,
        *tables,
        normed,
        *gate_up,
        heads,
        hidden,
        *weights,
        gain,
        cot,
    )
    return outs[:6]


def split_rows(term, y, keep_ref, send_ref):
    rows = term.shape[0] // 4
    even = jnp.concatenate([term[:rows], term[2 * rows : 3 * rows]], 0)
    odd = jnp.concatenate([term[rows : 2 * rows], term[3 * rows :]], 0)
    keep_ref[0] = jnp.where(y == 0, even, odd)
    send_ref[0] = jnp.where(y == 0, odd, even).astype(jnp.bfloat16)


def place_kernel(parts, in_ref, out_ref):
    each = in_ref.shape[2] // parts
    for part in range(parts):
        columns = slice(part * each, (part + 1) * each)
        line = jnp.concatenate([in_ref[n, :, columns] for n in range(PIECES)], 1)
        out_ref[:, part * PIECES * each : (part + 1) * PIECES * each] = line.astype(jnp.float32)


def place_rows(value, parts):
    rows, columns = value.shape[1], value.shape[2]
    return pl.pallas_call(
        functools.partial(place_kernel, parts),
        out_shape=jax.ShapeDtypeStruct((rows, PIECES * columns), jnp.float32),
        compiler_params=params(32),
        cost_estimate=cost(0, 4 * MIB),
        name="place_rows",
    )(value)


def lane_tables(positions):
    half = ROT // 2
    place = jnp.arange(HEAD_COLS, dtype=jnp.int32) % HEAD_DIM
    power = (place % half).astype(jnp.float32)
    frequency = jnp.where(place < ROT, rotary_base ** (-(2.0 * power) / ROT), 0.0)
    angles = positions.astype(jnp.float32)[..., None] * frequency
    sine = jnp.sin(angles)
    return (
        jnp.cos(angles),
        jnp.where(place < half, -sine, 0.0),
        jnp.where((place >= half) & (place < ROT), sine, 0.0),
    )


def shards_grouped(
    tokens,
    lengths,
    norm_gain,
    norm_shift,
    inward_weight,
    inward_bias,
    outward_weight,
    gate_up_weight,
    down_weight,
    cotangent,
):
    group_len, seqs, width = tokens.shape[1:]
    bucket, blk = lax.axis_index("bucket"), lax.axis_index("blk")
    _, core, z, y = coordinates()

    own_rows = inward_weight.shape[0]
    hidden_each = gate_up_weight.shape[1] // (2 * 2 * 2 * DEPTH)
    gain_share, bias_share = norm_gain.shape[0], inward_bias.shape[0]
    shares = jnp.concatenate([norm_gain, norm_shift, inward_bias]).astype(jnp.bfloat16)
    shares = jnp.pad(shares, (0, 3 * HEAD_COLS - shares.shape[0]))
    inward = inward_weight.astype(jnp.bfloat16).reshape(own_rows, 3, 2, 2, DEPTH, 2 * HEAD_DIM)
    inward = jnp.transpose(inward, (3, 4, 0, 1, 2, 5)).reshape(2, DEPTH, own_rows, 3 * HEAD_COLS)
    inward = jnp.concatenate(
        [inward, jnp.broadcast_to(shares, (2, DEPTH, EXTRA, 3 * HEAD_COLS))], 2
    )
    gate_up = gate_up_weight.astype(jnp.bfloat16).reshape(own_rows, 2, 2, 2, DEPTH, hidden_each)
    gate_up = jnp.transpose(gate_up, (3, 4, 0, 1, 2, 5)).reshape(
        2, DEPTH, own_rows, 4 * hidden_each
    )
    rows_out = jnp.concatenate([outward_weight, down_weight]).astype(jnp.bfloat16)
    own_tokens = jnp.transpose(tokens[0], (1, 0, 2))
    pieces, inward, gate_up, rows_out = gather(
        own_tokens.reshape(ROWS, width), inward, gate_up, rows_out
    )
    vectors = inward[..., own_rows, :].reshape(-1, 3 * HEAD_COLS).astype(jnp.float32)
    inward = inward.reshape((-1,) + inward.shape[4:])
    gate_up = gate_up.reshape(width, -1)
    rows_out = rows_out.reshape((-1,) + rows_out.shape[2:])

    gain = vectors[:, :gain_share].reshape(1, width)
    shift = vectors[:, gain_share : 2 * gain_share].reshape(1, width)
    bias = vectors[:, 2 * gain_share : 2 * gain_share + bias_share].reshape(-1)

    def own_columns(values, each):
        split = values.reshape(2, 2, DEPTH, each)
        return one_of(one_of(split, core, 1), z, 1)

    key_bias = jnp.pad(
        own_columns(bias[2 * width :], 2 * ROT).reshape(LOCAL_HEADS, ROT),
        ((0, 0), (0, HEAD_DIM - ROT)),
    )
    own_bias = jnp.concatenate(
        [
            own_columns(bias[:width], 2 * HEAD_DIM).reshape(-1),
            key_bias.reshape(-1),
            own_columns(bias[width : 2 * width], 2 * HEAD_DIM).reshape(-1),
        ]
    ).reshape(1, -1)

    position = blk * group_len + jnp.arange(group_len, dtype=jnp.int32)
    valid = (position[None, :] < lengths[0][:, None]).astype(jnp.float32)[..., None]
    own_cotangent = jnp.transpose(cotangent[0], (1, 0, 2))
    own_grad = (own_cotangent.astype(jnp.float32) * valid).astype(jnp.bfloat16)
    turns = (z - jnp.arange(DEPTH, dtype=jnp.int32)) % DEPTH
    tables = lane_tables(
        ((2 * turns + y) * group_len)[:, None] + jnp.arange(group_len, dtype=jnp.int32)
    )

    normed, gate, up, grads, queries, pairs, other_pairs, hidden, attended, own_sum, terms = forward(
        pieces,
        own_grad.reshape(ROWS, width),
        tables,
        gain,
        shift,
        own_bias,
        inward,
        gate_up,
        rows_out,
    )
    normed = normed.reshape(PIECES * ROWS, width)
    gate_xs, gate_xk, gate_ys, gate_yk, heads_term, hidden_term, gate_up_grad, *parts, layer_out = (
        backward(
            grads,
            gate,
            up,
            normed,
            pieces,
            queries,
            pairs,
            other_pairs,
            hidden,
            attended,
            rows_out,
            own_sum,
            terms,
            valid.reshape(ROWS, 1),
        )
    )
    tokens_grad, outward_sum, down_sum, gate_up_rows, inward_rows_own, vectors = finish(
        parts,
        gate_up_grad,
        pieces,
        tables,
        normed,
        (gate_xs, gate_xk, gate_ys, gate_yk),
        heads_term.reshape(2, 2, -1, width),
        hidden_term.reshape(2, 2, -1, width),
        (inward, gate_up),
        gain,
        own_cotangent.reshape(ROWS, width),
    )
    gate_up_sum = place_rows(gate_up_rows, 4)
    inward_sum = place_rows(inward_rows_own, 6)

    device = bucket * 2 * DEPTH + blk
    sums = jnp.sum(vectors[:, :4], axis=0).reshape(2, -1, gain_share)
    gain_sum = one_of(sums[0], device, 0)
    shift_sum = one_of(sums[1], device, 0)
    columns_sum = vectors[:, 4, : 3 * HEAD_COLS].reshape(PIECES, 3, 2, 2 * HEAD_DIM)
    columns_sum = jnp.transpose(columns_sum, (1, 2, 0, 3)).reshape(3, -1)
    key_rot = columns_sum[1].reshape(HEADS, HEAD_DIM)[:, :ROT]
    bias_all = jnp.concatenate([columns_sum[0], columns_sum[2], key_rot.reshape(-1)])
    bias_sum = one_of(bias_all.reshape(-1, bias_share), device, 0)

    def placed(value):
        value = value.reshape(seqs, group_len, width)
        return jnp.transpose(value, (1, 0, 2)).reshape(tokens.shape)

    return (
        placed(layer_out),
        placed(tokens_grad),
        gain_sum,
        shift_sum,
        inward_sum,
        bias_sum,
        outward_sum,
        gate_up_sum,
        down_sum,
    )


def solution(mesh):
    in_specs = (
        P("bucket", "blk", None, None),
        P("bucket", None),
        P(("bucket", "blk")),
        P(("bucket", "blk")),
        P(("bucket", "blk"), None),
        P(("bucket", "blk")),
        P(("bucket", "blk"), None),
        P(("bucket", "blk"), None),
        P(("bucket", "blk"), None),
        P("bucket", "blk", None, None),
    )
    out_specs = (
        P("bucket", "blk", None, None),
        P("bucket", "blk", None, None),
        P(("bucket", "blk")),
        P(("bucket", "blk")),
        P(("bucket", "blk"), None),
        P(("bucket", "blk")),
        P(("bucket", "blk"), None),
        P(("bucket", "blk"), None),
        P(("bucket", "blk"), None),
    )
    body = shards_grouped if fits_groups(mesh) else shards_general
    return jax.shard_map(body, mesh=mesh, in_specs=in_specs, out_specs=out_specs, check_vma=False)
```

```python
import functools

import jax
import jax.numpy as jnp
from jax import lax
from jax.experimental import pallas as pl
from jax.experimental.pallas import tpu as pltpu
from jax.sharding import PartitionSpec as P

HEADS = 32
HEAD_DIM = 64
ROT = 16


epsilon = 1e-05
rotary_base = 10000.0
masked_score = -1e30


def shifted(value, axis, by):
    count = lax.axis_size(axis)
    pairs = [(i, i + by) for i in range(count) if 0 <= i + by < count]
    return lax.ppermute(value, axis, pairs)


def shifted_2(value, axis, steps):
    count = lax.axis_size(axis)
    pairs = [(source, (source + steps) % count) for source in range(count)]
    return lax.ppermute(value, axis, pairs)


def keep_same(value):
    return value


def transposed_times(left, right):
    return lax.dot_general(
        left, right, (((1,), (1,)), ((), ())), preferred_element_type=jnp.float32
    )


def times_transposed(left, right):
    return lax.dot_general(
        left, right, (((0,), (0,)), ((), ())), preferred_element_type=jnp.float32
    )


def rotary_tables(positions):
    half_rot = ROT // 2
    frequency = rotary_base ** (-(2.0 * jnp.arange(half_rot).astype(jnp.float32)) / ROT)
    angles = positions.astype(jnp.float32)[:, None] * frequency[None, :]
    return (jnp.cos(angles), jnp.sin(angles))


def rotate(values, cos_table, sine_table):
    half_rot = ROT // 2
    front_half = values[..., :half_rot]
    back_half = values[..., half_rot:ROT]
    return jnp.concatenate(
        [
            front_half * cos_table - back_half * sine_table,
            back_half * cos_table + front_half * sine_table,
            values[..., ROT:],
        ],
        axis=-1,
    )


def split_pairs(packed):
    rows_here, seq_count, both_width = packed.shape
    half_width = both_width // 2
    keys_part = packed[..., :half_width].reshape(rows_here, seq_count, HEADS, HEAD_DIM)
    values_part = packed[..., half_width:].reshape(rows_here, seq_count, HEADS, HEAD_DIM)
    return (keys_part, values_part)


def block_scores(queries, key_block, query_start, key_start):
    scores = jnp.einsum("tshd,ushd->shtu", queries, key_block, preferred_element_type=jnp.float32)
    query_pos = query_start + jnp.arange(queries.shape[0], dtype=jnp.int32)
    key_pos = key_start + jnp.arange(key_block.shape[0], dtype=jnp.int32)
    allowed = (key_pos[None, :] <= query_pos[:, None])[None, None]
    return (jnp.where(allowed, scores, masked_score), allowed)


def forward_block(carried, queries, key_block, value_block, query_start, key_start):
    running_max, running_sum, weighted = carried
    scores, allowed = block_scores(queries, key_block, query_start, key_start)
    new_max = jnp.maximum(running_max, jnp.max(scores, axis=-1))
    rescale = jnp.exp(running_max - new_max)
    weights = jnp.where(allowed, jnp.exp(scores - new_max[..., None]), 0.0)
    running_sum = running_sum * rescale + jnp.sum(weights, axis=-1)
    update = jnp.einsum(
        "shtu,ushd->tshd",
        weights.astype(jnp.bfloat16),
        value_block,
        preferred_element_type=jnp.float32,
    )
    weighted = weighted * jnp.transpose(rescale, (2, 0, 1))[..., None] + update
    return (new_max, running_sum, weighted)


def pair_grads(
    queries, out_grads, log_norm, deltas, key_block, value_block, query_start, key_start
):
    scores, allowed = block_scores(queries, key_block, query_start, key_start)
    probability = jnp.where(allowed, jnp.exp(scores - log_norm[..., None]), 0.0)
    value_grad = jnp.einsum(
        "shtu,tshd->ushd",
        probability.astype(jnp.bfloat16),
        out_grads,
        preferred_element_type=jnp.float32,
    )
    prob_grad = jnp.einsum(
        "tshd,ushd->shtu", out_grads, value_block, preferred_element_type=jnp.float32
    )
    score_grad = (probability * (prob_grad - deltas[..., None])).astype(jnp.bfloat16)
    query_grad = jnp.einsum(
        "shtu,ushd->tshd", score_grad, key_block, preferred_element_type=jnp.float32
    )
    key_grad = jnp.einsum(
        "shtu,tshd->ushd", score_grad, queries, preferred_element_type=jnp.float32
    )
    return (query_grad, key_grad, value_grad)


def over_blocks(running, incoming, unit_rows, handle):
    total_rows = incoming[0].shape[0]
    block_count = total_rows // unit_rows
    block_rows = total_rows // block_count
    stacked = tuple(
        (member.reshape((block_count, block_rows) + member.shape[1:]) for member in incoming)
    )

    def visit(carried, element):
        block_index, members = element
        return (handle(carried, members, block_index * block_rows), None)

    running, unused = lax.scan(visit, running, (jnp.arange(block_count, dtype=jnp.int32), stacked))
    return running


def shards_general(
    tokens,
    lengths,
    norm_gain,
    norm_shift,
    inward_weight,
    inward_bias,
    outward_weight,
    gate_up_weight,
    down_weight,
    cotangent,
):
    group_len = tokens.shape[1]
    seq_count = tokens.shape[2]
    model_width = tokens.shape[3]
    row_total = group_len * seq_count
    block_total = lax.axis_size("blk")
    position = lax.axis_index("blk")
    own_start = position * group_len
    longest = jnp.max(lengths[0])
    active = own_start < longest
    gathered = (
        lax.all_gather(inward_weight.astype(jnp.bfloat16), ("bucket", "blk"), axis=0, tiled=True),
        lax.all_gather(outward_weight.astype(jnp.bfloat16), ("bucket", "blk"), axis=0, tiled=True),
        lax.all_gather(gate_up_weight.astype(jnp.bfloat16), ("bucket", "blk"), axis=0, tiled=True),
        lax.all_gather(down_weight.astype(jnp.bfloat16), ("bucket", "blk"), axis=0, tiled=True),
        lax.all_gather(norm_gain.astype(jnp.bfloat16), ("bucket", "blk"), axis=0, tiled=True),
        lax.all_gather(norm_shift.astype(jnp.bfloat16), ("bucket", "blk"), axis=0, tiled=True),
        lax.all_gather(inward_bias.astype(jnp.bfloat16), ("bucket", "blk"), axis=0, tiled=True),
    )
    inward_full, outward_full, gate_up_full, down_full, gain_full, shift_full, bias_full = gathered
    inputs = tokens.reshape(row_total, model_width).astype(jnp.float32)
    centred = inputs - jnp.mean(inputs, axis=-1, keepdims=True)
    variance = jnp.mean(centred * centred, axis=-1, keepdims=True)
    inverse = lax.rsqrt(variance + epsilon)
    normal_hat = centred * inverse
    normed_low = (
        normal_hat * gain_full.astype(jnp.float32) + shift_full.astype(jnp.float32)
    ).astype(jnp.bfloat16)
    bias_float = bias_full.astype(jnp.float32)
    key_bias = jnp.pad(
        bias_float[2 * model_width :].reshape(HEADS, ROT), ((0, 0), (0, HEAD_DIM - ROT))
    ).reshape(model_width)
    full_bias = jnp.concatenate(
        [bias_float[:model_width], key_bias, bias_float[model_width : 2 * model_width]]
    )
    projected = jnp.dot(normed_low, inward_full, preferred_element_type=jnp.float32) + full_bias
    projected = projected.reshape(group_len, seq_count, 3, HEADS, HEAD_DIM)
    cos_table, sine_table = rotary_tables(own_start + jnp.arange(group_len, dtype=jnp.int32))
    cos_table = cos_table[:, None, None, :]
    sine_table = sine_table[:, None, None, :]
    query_scale = HEAD_DIM ** (-0.5)
    queries = (rotate(projected[:, :, 0], cos_table, sine_table) * query_scale).astype(jnp.bfloat16)
    keys_low = rotate(projected[:, :, 1], cos_table, sine_table).astype(jnp.bfloat16)
    values_low = projected[:, :, 2].astype(jnp.bfloat16)
    packed = jnp.concatenate(
        [
            keys_low.reshape(group_len, seq_count, model_width),
            values_low.reshape(group_len, seq_count, model_width),
        ],
        axis=-1,
    )

    def forward_handle(carried, members, key_start):
        keys_part, values_part = split_pairs(members[0])
        needed = active & (key_start <= own_start + group_len - 1)

        def forward_compute(state_in):
            return forward_block(state_in, queries, keys_part, values_part, own_start, key_start)

        return lax.cond(needed, forward_compute, keep_same, carried)

    start_state = (
        jnp.full((seq_count, HEADS, group_len), masked_score, jnp.float32),
        jnp.zeros((seq_count, HEADS, group_len), jnp.float32),
        jnp.zeros((group_len, seq_count, HEADS, HEAD_DIM), jnp.float32),
    )
    running_max, running_sum, weighted = over_blocks(
        start_state, (lax.all_gather(packed, "blk", axis=0, tiled=True),), group_len, forward_handle
    )
    bounded = jnp.maximum(running_sum, 1.0)
    log_norm = running_max + jnp.log(bounded)
    attended = weighted / jnp.transpose(bounded, (2, 0, 1))[..., None]
    attended_rows = attended.astype(jnp.bfloat16).reshape(row_total, model_width)
    gate_up = jnp.dot(normed_low, gate_up_full, preferred_element_type=jnp.float32)
    ff_width = gate_up.shape[1] // 2
    gate_part = gate_up[:, :ff_width]
    up_part = gate_up[:, ff_width:]
    sigmoid_gate = jax.nn.sigmoid(gate_part)
    silu_gate = gate_part * sigmoid_gate
    hidden_low = (silu_gate * up_part).astype(jnp.bfloat16)
    branch = jnp.dot(attended_rows, outward_full, preferred_element_type=jnp.float32) + jnp.dot(
        hidden_low, down_full, preferred_element_type=jnp.float32
    )
    query_pos = own_start + jnp.arange(group_len, dtype=jnp.int32)
    valid_rows = (
        (query_pos[:, None] < lengths[0][None, :]).astype(jnp.float32).reshape(row_total, 1)
    )
    layer_out = (inputs + valid_rows * branch).astype(jnp.bfloat16).reshape(tokens.shape)
    inward_back = gathered[0]
    outward_back = gathered[1]
    gate_up_back = gathered[2]
    down_back = gathered[3]
    gain_float = gathered[4].astype(jnp.float32)
    cotangent_rows = cotangent.reshape(row_total, model_width).astype(jnp.float32)
    branch_grad = (cotangent_rows * valid_rows).astype(jnp.bfloat16)
    hidden_grad = transposed_times(branch_grad, down_back)
    gate_grad = hidden_grad * up_part * (sigmoid_gate + silu_gate * (1.0 - sigmoid_gate))
    up_grad = hidden_grad * silu_gate
    gate_up_grad_low = jnp.concatenate([gate_grad, up_grad], axis=-1).astype(jnp.bfloat16)
    down_term = times_transposed(hidden_low, branch_grad)
    gate_up_term = times_transposed(normed_low, gate_up_grad_low)
    gate_up_sum, down_sum = (
        lax.psum_scatter(gate_up_term, ("bucket", "blk"), scatter_dimension=0, tiled=True),
        lax.psum_scatter(down_term, ("bucket", "blk"), scatter_dimension=0, tiled=True),
    )
    normed_grad = transposed_times(gate_up_grad_low, gate_up_back)
    attended_grad = (
        transposed_times(branch_grad, outward_back)
        .astype(jnp.bfloat16)
        .reshape(group_len, seq_count, HEADS, HEAD_DIM)
    )
    outward_term = times_transposed(attended_rows, branch_grad)
    deltas = jnp.transpose(
        jnp.sum(attended_grad.astype(jnp.float32) * attended, axis=-1), (1, 2, 0)
    )
    grad_zeros = jnp.zeros((group_len, seq_count, 2 * model_width), jnp.float32)
    query_zeros = jnp.zeros((group_len, seq_count, HEADS, HEAD_DIM), jnp.float32)

    def cycle_turn(turn_index, carried):
        visiting, sums_now, grads_now = carried
        owner_index = (position - turn_index) % block_total
        key_start = owner_index * group_len
        needed = active & (owner_index <= position)

        def cycle_compute(sums_in):
            keys_part, values_part = split_pairs(visiting)
            query_part, key_part, value_part = pair_grads(
                queries,
                attended_grad,
                log_norm,
                deltas,
                keys_part,
                values_part,
                own_start,
                key_start,
            )
            merged = jnp.concatenate(
                [
                    key_part.reshape(group_len, seq_count, model_width),
                    value_part.reshape(group_len, seq_count, model_width),
                ],
                axis=-1,
            )
            return (sums_in[0] + merged, sums_in[1] + query_part)

        sums_now, grads_now = lax.cond(needed, cycle_compute, keep_same, (sums_now, grads_now))
        visiting = shifted(visiting, "blk", 1)
        sums_now = shifted_2(sums_now.astype(jnp.bfloat16), "blk", 1).astype(sums_now.dtype)
        return (visiting, sums_now, grads_now)

    unused, pair_sums, query_grads = lax.fori_loop(
        0, block_total, cycle_turn, (packed, grad_zeros, query_zeros)
    )
    key_grad = pair_sums[..., :model_width].reshape(group_len, seq_count, HEADS, HEAD_DIM)
    value_grad = pair_sums[..., model_width:].reshape(group_len, seq_count, HEADS, HEAD_DIM)
    back_sine = -sine_table
    query_back = rotate(query_grads * query_scale, cos_table, back_sine)
    key_back = rotate(key_grad, cos_table, back_sine)
    projected_grad = (
        jnp.stack([query_back, key_back, value_grad], axis=2)
        .reshape(row_total, 3 * model_width)
        .astype(jnp.bfloat16)
    )
    inward_term = times_transposed(normed_low, projected_grad)
    column_sums = jnp.sum(projected_grad.astype(jnp.float32), axis=0)
    key_bias_grad = (
        column_sums[model_width : 2 * model_width]
        .reshape(HEADS, HEAD_DIM)[:, :ROT]
        .reshape(HEADS * ROT)
    )
    bias_term = jnp.concatenate(
        [column_sums[:model_width], column_sums[2 * model_width :], key_bias_grad]
    )
    normed_grad = normed_grad + transposed_times(projected_grad, inward_back)
    gain_term = jnp.sum(normed_grad * normal_hat, axis=0)
    shift_term = jnp.sum(normed_grad, axis=0)
    scaled_grad = normed_grad * gain_float
    input_grad = inverse * (
        scaled_grad
        - jnp.mean(scaled_grad, axis=-1, keepdims=True)
        - normal_hat * jnp.mean(scaled_grad * normal_hat, axis=-1, keepdims=True)
    )
    tokens_grad = (cotangent_rows + input_grad).astype(jnp.bfloat16).reshape(tokens.shape)
    inward_sum, outward_sum, bias_sum, gain_sum, shift_sum = (
        lax.psum_scatter(inward_term, ("bucket", "blk"), scatter_dimension=0, tiled=True),
        lax.psum_scatter(outward_term, ("bucket", "blk"), scatter_dimension=0, tiled=True),
        lax.psum_scatter(bias_term, ("bucket", "blk"), scatter_dimension=0, tiled=True),
        lax.psum_scatter(gain_term, ("bucket", "blk"), scatter_dimension=0, tiled=True),
        lax.psum_scatter(shift_term, ("bucket", "blk"), scatter_dimension=0, tiled=True),
    )
    return (
        layer_out,
        tokens_grad,
        gain_sum,
        shift_sum,
        inward_sum,
        bias_sum,
        outward_sum,
        gate_up_sum,
        down_sum,
    )


DEPTH = 4
PIECES = 2 * DEPTH
ROWS = 256
EXTRA = 16
GATE_STEP = 4
LOCAL_HEADS = 4
HEAD_COLS = LOCAL_HEADS * HEAD_DIM


MIB = 1024 * 1024


def fits_groups(mesh):
    return mesh.shape["bucket"] == 4 and mesh.shape["blk"] == 2 * DEPTH


def around(step):
    return [(z * 2 + y, ((z + step) % DEPTH) * 2 + y) for z in range(DEPTH) for y in range(2)]


def in_order(own, other, index, axis):
    return jnp.where(
        index == 0, jnp.stack([own, other], axis), jnp.stack([other, own], axis)
    )


def one_of(value, index, axis):
    return lax.dynamic_index_in_dim(value, index, axis, False)


def dot_rows(left, right):
    return lax.dot_general(
        left, right, (((1,), (0,)), ((), ())), preferred_element_type=jnp.float32
    )


def params(limit, **extra):
    return pltpu.CompilerParams(vmem_limit_bytes=limit * MIB, **extra)


def cost(flops, moved, exps=0):
    return pl.CostEstimate(flops=flops // 64, bytes_accessed=moved // 64, transcendentals=exps // 64)


def piece_spec(width):
    return pl.BlockSpec((1, ROWS, width), lambda i: (i, 0, 0))


def whole_spec(shape):
    return pl.BlockSpec(shape, lambda i: (0,) * len(shape))


def remote_to(src, dst, send_sem, recv_sem, device):
    return pltpu.make_async_remote_copy(
        src_ref=src,
        dst_ref=dst,
        send_sem=send_sem,
        recv_sem=recv_sem,
        device_id=device,
        device_id_type=pl.DeviceIdType.MESH,
    )


def remote(src, dst, sends, recvs, index, device):
    return remote_to(src, dst, sends.at[index], recvs.at[index], device)


def select(i, first, second, third):
    return jnp.where(i == 0, first, jnp.where(i == 1, second, jnp.where(i == 2, third, 0)))


class Chain:
    def __init__(self, src, out, x, core, z, y, sems):
        up_s, down_s, arrive, core_s, core_r, local = sems
        self.z = z
        self.out = out

        def hop(k, src, slot, sends, dz):
            return pltpu.make_async_remote_copy(
                src_ref=src,
                dst_ref=out.at[slot],
                send_sem=sends.at[k],
                recv_sem=arrive.at[slot],
                device_id=(x * 2 + core, (z + dz) * 2 + y),
                device_id_type=pl.DeviceIdType.MESH,
            )

        mate = (x * 2 + 1 - core, z * 2 + y)
        self.ups = [hop(k, src if k == 0 else out.at[k], k + 1, up_s, 1) for k in range(3)]
        self.downs = [
            hop(k, src if k == 0 else out.at[DEPTH - k], 3 - k, down_s, -1) for k in range(3)
        ]
        self.cores = [
            remote(src if k == 0 else out.at[k], out.at[DEPTH + k], core_s, core_r, k, mate)
            for k in range(DEPTH)
        ]
        self.local = pltpu.make_async_copy(src, out.at[0], local)
        inner = (z > 0) & (z < DEPTH - 1)
        self.sent = [
            (z < DEPTH - 1, self.ups[0]),
            (z > 0, self.downs[0]),
            (inner, self.ups[1]),
            (inner, self.downs[1]),
            (z == DEPTH - 2, self.ups[2]),
            (z == 1, self.downs[2]),
        ]

    def start(self, *numbers):
        for number in numbers:
            condition, copy = self.sent[number]
            pl.when(condition)(copy.start)

    def first(self):
        self.start(0, 1)
        self.cores[0].start()
        self.local.start()

    def second(self):
        @pl.when(self.z > 0)
        def _():
            self.ups[0].wait_recv()
            self.cores[1].start()

        self.start(2)

        @pl.when(self.z < DEPTH - 1)
        def _():
            self.downs[0].wait_recv()
            self.cores[3].start()

        self.start(3)

    def third(self):
        self.ups[1].wait_recv()
        self.cores[2].start()
        self.start(4, 5)

    def fourth(self):
        @pl.when(self.z == DEPTH - 1)
        def _():
            self.ups[2].wait_recv()
            self.cores[3].start()

        @pl.when(self.z == 0)
        def _():
            self.downs[2].wait_recv()
            self.cores[1].start()

    def end(self):
        for copy in self.cores:
            copy.wait_recv()
            copy.wait_send()
        for condition, copy in self.sent:
            pl.when(condition)(copy.wait_send)
        self.local.wait()


def chain_sems():
    dma = pltpu.SemaphoreType.DMA
    return [dma((3,)), dma((3,)), dma((DEPTH,)), dma((DEPTH,)), dma((DEPTH,)), dma(())]


def greet(mates):
    barrier = pltpu.get_barrier_semaphore()
    for mate in mates:
        pl.semaphore_signal(
            barrier, inc=1, device_id=mate, device_id_type=pl.DeviceIdType.MESH
        )
    pl.semaphore_wait(barrier, len(mates))


def coordinates():
    bucket, blk = lax.axis_index("bucket"), lax.axis_index("blk")
    return bucket // 2, bucket % 2, blk // 2, blk % 2


def gather_kernel(
    x_ref,
    wi_ref,
    wg_ref,
    ro_ref,
    pieces,
    wi_out,
    wg_out,
    ro_out,
    group_s,
    group_r,
    across_s,
    across_r,
    rows_s,
    rows_r,
    local_sems,
    *chain,
):
    x, core, z, y = coordinates()

    def device(xx, cc, zz, yy):
        return (xx * 2 + cc, zz * 2 + yy)

    x_mate, y_mate = device(1 - x, core, z, y), device(x, core, z, 1 - y)
    members = [(flip, turn) for turn in (0, 1, 3, 2) for flip in (0, 1)]

    def target(flip, turn):
        return (core + flip) % 2, (z + turn) % DEPTH

    def source(flip, turn):
        return (core + flip) % 2, (z + DEPTH - turn) % DEPTH

    greet([device(x, *target(*m), y) for m in members[1:]] + [x_mate, y_mate])
    started = []

    def begin(copy):
        copy.start()
        started.append(copy)
        return copy

    local = [
        pltpu.make_async_copy(wi_ref.at[core, z], wi_out.at[x, core, z, y], local_sems.at[0]),
        pltpu.make_async_copy(wg_ref.at[core, z], wg_out.at[x, core, z, y], local_sems.at[1]),
        pltpu.make_async_copy(ro_ref, ro_out.at[x, y], local_sems.at[2]),
    ]
    for copy in local:
        copy.start()

    def send_group(which, ref, out):
        copies = {}
        for flip, turn in members[1:]:
            cc, zz = target(flip, turn)
            copies[flip, turn] = begin(
                remote(
                    ref.at[cc, zz],
                    out.at[x, core, z, y],
                    group_s,
                    group_r,
                    (which, flip * DEPTH + turn),
                    device(x, cc, zz, y),
                )
            )
        return copies

    inward = send_group(0, wi_ref, wi_out)
    tokens = Chain(x_ref, pieces, x, core, z, y, chain)
    tokens.first()
    rows_x = begin(remote(ro_ref, ro_out.at[x, y], rows_s, rows_r, 0, x_mate))
    rows_y = begin(remote(ro_ref, ro_out.at[x, y], rows_s, rows_r, 1, y_mate))
    gate_up = send_group(1, wg_ref, wg_out)

    def spread(which, ref, out, copies):
        pairs = {}
        for member in members:
            flip, turn = member
            cc, zz = source(flip, turn)
            if member == (0, 0):
                src = ref.at[core, z]
            else:
                copies[member].wait_recv()
                src = out.at[x, cc, zz, y]
            number = flip * DEPTH + turn
            pairs[member] = (
                begin(
                    remote(
                        src, out.at[x, cc, zz, y], across_s, across_r, (which, 0, number), x_mate
                    )
                ),
                begin(
                    remote(
                        src, out.at[x, cc, zz, y], across_s, across_r, (which, 1, number), y_mate
                    )
                ),
            )
        return pairs

    def corner(which, out, pairs):
        copies = []
        for member in members:
            flip, turn = member
            cc, zz = source(flip, turn)
            number = flip * DEPTH + turn
            if flip == 0:
                pairs[member][1].wait_recv()
                part = out.at[x, cc, zz, 1 - y]
                mate = x_mate
            else:
                pairs[member][0].wait_recv()
                part = out.at[1 - x, cc, zz, y]
                mate = y_mate
            copies.append(
                begin(remote(part, part, across_s, across_r, (which, 2, number), mate))
            )
        return copies

    inward_pairs = spread(0, wi_ref, wi_out, inward)

    tokens.second()
    inward_corner = corner(0, wi_out, inward_pairs)
    gate_up_pairs = spread(1, wg_ref, wg_out, gate_up)

    tokens.third()
    cut = (ro_ref.shape[0] // 32) * 16
    rows_y.wait_recv()
    low = ro_out.at[x, 1 - y, pl.ds(0, cut)]
    low_copy = begin(remote(low, low, rows_s, rows_r, 2, x_mate))
    rows_x.wait_recv()
    high = ro_out.at[1 - x, y, pl.ds(cut, ro_ref.shape[0] - cut)]
    high_copy = begin(remote(high, high, rows_s, rows_r, 3, y_mate))
    gate_up_corner = corner(1, wg_out, gate_up_pairs)

    tokens.fourth()

    for pairs in (inward_pairs, gate_up_pairs):
        for flip, turn in members:
            pairs[flip, turn][0 if flip == 0 else 1].wait_recv()
    for copy in inward_corner + gate_up_corner + [low_copy, high_copy]:
        copy.wait_recv()
    for copy in started:
        copy.wait_send()
    tokens.end()
    for copy in local:
        copy.wait()


def gather(tokens, inward, gate_up, rows_out):
    anywhere = pl.BlockSpec(memory_space=pl.ANY)
    low = jnp.bfloat16
    dma = pltpu.SemaphoreType.DMA
    return pl.pallas_call(
        gather_kernel,
        in_specs=[anywhere] * 4,
        out_specs=[anywhere] * 4,
        out_shape=[
            jax.ShapeDtypeStruct((PIECES,) + tokens.shape, low),
            jax.ShapeDtypeStruct((2, 2, DEPTH, 2) + inward.shape[2:], low),
            jax.ShapeDtypeStruct((2, 2, DEPTH, 2) + gate_up.shape[2:], low),
            jax.ShapeDtypeStruct((2, 2) + rows_out.shape, low),
        ],
        scratch_shapes=[
            dma((2, PIECES)),
            dma((2, PIECES)),
            dma((2, 3, PIECES)),
            dma((2, 3, PIECES)),
            dma((4,)),
            dma((4,)),
            dma((3,)),
        ]
        + chain_sems(),
        compiler_params=params(32, collective_id=0, has_side_effects=True),
        cost_estimate=cost(0, 64 * MIB),
        name="gather",
    )(tokens, inward, gate_up, rows_out)


def inward_rows(ref):
    blocks, rows, columns = ref.shape
    return ref[:, : rows - EXTRA].reshape(blocks * (rows - EXTRA), columns)


def outward_rows(ref):
    blocks, rows, columns = ref.shape
    return ref[:, :HEAD_DIM].reshape(blocks * HEAD_DIM, columns)


def down_rows(ref):
    blocks, rows, columns = ref.shape
    return ref[:, HEAD_DIM:].reshape(blocks * (rows - HEAD_DIM), columns)


def normalised(rows):
    inputs = rows.astype(jnp.float32)
    centred = inputs - jnp.mean(inputs, axis=-1, keepdims=True)
    variance = jnp.mean(centred * centred, axis=-1, keepdims=True)
    inverse = lax.rsqrt(variance + epsilon)
    return centred * inverse, inverse


def turned(values, cos_ref, first_ref, second_ref, sign):
    half = ROT // 2
    cos = jnp.concatenate([cos_ref[0], cos_ref[0]], 0)
    first = jnp.concatenate([first_ref[0], first_ref[0]], 0)
    second = jnp.concatenate([second_ref[0], second_ref[0]], 0)
    ahead = pltpu.roll(values, HEAD_COLS - half, 1)
    behind = pltpu.roll(values, half, 1)
    return values * cos + sign * (ahead * first + behind * second)


def forward_kernel(
    pieces_ref,
    grad_ref,
    cos_ref,
    first_ref,
    second_ref,
    gain_ref,
    shift_ref,
    bias_ref,
    wi_ref,
    wg_ref,
    rows_ref,
    normed_out,
    gate_out,
    up_out,
    grads_out,
    q_ref,
    kv_ref,
    okv_ref,
    hidden_ref,
    att_ref,
    own_sum,
    terms,
    core_send,
    core_recv,
    kv_s,
    kv_r,
    core_s,
    core_r,
    *chain,
):
    x, core, z, y = coordinates()
    low, wide = jnp.bfloat16, jnp.float32
    core_mate = (x * 2 + 1 - core, z * 2 + y)
    y_mate = (x * 2 + core, z * 2 + 1 - y)
    below = (x * 2 + core, lax.rem(z + DEPTH - 1, DEPTH) * 2 + y)
    above = (x * 2 + core, lax.rem(z + 1, DEPTH) * 2 + y)
    greet([core_mate, y_mate, below, above])
    grads = Chain(grad_ref, grads_out, x, core, z, y, chain)
    grads.first()

    def pair_copy(piece):
        return remote(kv_ref.at[piece], okv_ref.at[piece], kv_s, kv_r, piece, y_mate)

    def piece_body(tokens, cos, first, second, normed, gate_part, up_part):
        piece = pl.program_id(0)
        hat, _ = normalised(tokens[0])
        narrow = (hat * gain_ref[...] + shift_ref[...]).astype(low)
        normed[0] = narrow
        projected = dot_rows(narrow, inward_rows(wi_ref)) + bias_ref[...]
        tables = (cos, first, second)
        query = turned(projected[:, :HEAD_COLS], *tables, 1.0) * (HEAD_DIM**-0.5)
        key = turned(projected[:, HEAD_COLS : 2 * HEAD_COLS], *tables, 1.0)
        kv_ref[piece] = jnp.concatenate([key, projected[:, 2 * HEAD_COLS :]], 1).astype(low)
        pair_copy(piece).start()
        q_ref[piece] = query.astype(low)
        both = dot_rows(narrow, wg_ref[...])
        hidden = both.shape[1] // 2
        gate, up = both[:, :hidden], both[:, hidden:]
        gate_part[0] = gate
        up_part[0] = up
        hidden_ref[piece] = (gate * jax.nn.sigmoid(gate) * up).astype(low)

        @pl.when(piece == PIECES - 2)
        def _():
            grads.second()

    table_spec = pl.BlockSpec((1,) + cos_ref.shape[1:], lambda i: (i % DEPTH, 0, 0))
    pltpu.emit_pipeline(
        piece_body,
        grid=(PIECES,),
        in_specs=[piece_spec(pieces_ref.shape[-1])] + [table_spec] * 3,
        out_specs=[piece_spec(r.shape[-1]) for r in (normed_out, gate_out, up_out)],
    )(pieces_ref, cos_ref, first_ref, second_ref, normed_out, gate_out, up_out)

    for b in range(2):
        for j in range(DEPTH):
            pair_copy(b * DEPTH + j).wait_recv()

        def attend(t, carry):
            attend_one(Heads(b, t, z, y, q_ref, kv_ref, okv_ref), att_ref)
            return carry

        lax.fori_loop(0, 2 * LOCAL_HEADS // 2, attend, 0)
        if b == 0:
            grads.third()

    def core_copy(k):
        return remote(core_send.at[k], core_recv.at[k], core_s, core_r, k, core_mate)

    def term(piece):
        return dot_rows(att_ref[piece], outward_rows(rows_ref)) + dot_rows(
            hidden_ref[piece], down_rows(rows_ref)
        )

    def branch(i, carry):
        k = DEPTH - 1 - i
        core_send[k] = term(DEPTH + k).astype(low)
        core_copy(k).start()
        own = term(k)
        core_copy(k).wait_recv()
        both = own + core_recv[k].astype(wide)

        @pl.when(k > 0)
        def _():
            terms[k - 1] = both.astype(low)

        @pl.when(k == 0)
        def _():
            own_sum[...] = both

        return carry

    lax.fori_loop(0, DEPTH, branch, 0)
    grads.fourth()
    grads.end()
    for piece in range(PIECES):
        pair_copy(piece).wait_send()
    for k in range(DEPTH):
        core_copy(k).wait_send()


def forward(pieces, own_grad, tables, gain, shift, bias, inward, gate_up, rows_out):
    low, wide = jnp.bfloat16, jnp.float32
    width = pieces.shape[-1]
    hidden = gate_up.shape[1] // 2
    anywhere = pl.BlockSpec(memory_space=pl.ANY)
    inside = pl.BlockSpec(memory_space=pltpu.VMEM)
    shape = jax.ShapeDtypeStruct
    dma = pltpu.SemaphoreType.DMA
    return pl.pallas_call(
        forward_kernel,
        in_specs=[anywhere] * 5 + [inside] * 6,
        out_specs=[anywhere] * 4 + [inside] * 7,
        out_shape=[
            shape((PIECES, ROWS, width), low),
            shape((PIECES, ROWS, hidden), wide),
            shape((PIECES, ROWS, hidden), wide),
            shape((PIECES, ROWS, width), low),
            shape((PIECES, ROWS, HEAD_COLS), low),
            shape((PIECES, ROWS, 2 * HEAD_COLS), low),
            shape((PIECES, ROWS, 2 * HEAD_COLS), low),
            shape((PIECES, ROWS, hidden), low),
            shape((PIECES, ROWS, HEAD_COLS), low),
            shape((ROWS, width), wide),
            shape((DEPTH - 1, ROWS, width), low),
        ],
        scratch_shapes=[
            pltpu.VMEM((DEPTH, ROWS, width), low),
            pltpu.VMEM((DEPTH, ROWS, width), low),
            dma((PIECES,)),
            dma((PIECES,)),
            dma((DEPTH,)),
            dma((DEPTH,)),
        ]
        + chain_sems(),
        compiler_params=params(60, collective_id=2, has_side_effects=True),
        cost_estimate=cost(0, 64 * MIB),
        name="forward",
    )(pieces, own_grad, *tables, gain, shift, bias, inward, gate_up, rows_out)


def pair_rows(block):
    lane = lax.broadcasted_iota(jnp.int32, block.shape, 1)
    zero = jnp.zeros_like(block)
    return jnp.concatenate(
        [jnp.where(lane < HEAD_DIM, block, zero), jnp.where(lane < HEAD_DIM, zero, block)], 0
    )


def pair_lanes(rows):
    half = rows.shape[0] // 2
    lane = lax.broadcasted_iota(jnp.int32, (half, rows.shape[1]), 1)
    return jnp.where(lane < HEAD_DIM, rows[:half], rows[half:])


def block_probs(queries, keys, last, y):
    scores = transposed_times(queries, keys)
    rows, columns = scores.shape
    size = rows // 2
    row = lax.broadcasted_iota(jnp.int32, (rows, 2 * size), 0) % size
    column = lax.broadcasted_iota(jnp.int32, (rows, 2 * size), 1)
    allowed = (column <= row) | ((column >= size) & (y == 1))
    tail = jnp.where(allowed, scores[:, last * 2 * size :], masked_score)
    scores = tail if last == 0 else jnp.concatenate([scores[:, : last * 2 * size], tail], 1)
    weights = jnp.exp(scores - jnp.max(scores, axis=-1, keepdims=True))
    return weights * (1.0 / jnp.sum(weights, axis=-1, keepdims=True))


class Heads:
    def __init__(self, b, t, z, y, q_ref, kv_ref, okv_ref):
        size = ROWS // 2
        pair = 2 * HEAD_DIM
        self.b, self.z, self.y = b, z, y
        self.rows = pl.ds(pl.multiple_of((t // 2) * size, size), size)
        self.lanes = pl.ds(pl.multiple_of((t % 2) * pair, pair), pair)
        value_lanes = pl.ds(pl.multiple_of(HEAD_COLS + (t % 2) * pair, pair), pair)
        self.q_ref = q_ref

        def both(lanes):
            blocks = []
            for j in range(DEPTH):
                place = (self.piece(j), self.rows, lanes)
                blocks += [kv_ref[place], okv_ref[place]]
            return jnp.concatenate(blocks, 0)

        self.keys, self.values = both(self.lanes), both(value_lanes)

    def piece(self, j):
        return self.b * DEPTH + lax.rem(self.z + DEPTH - j, DEPTH)

    def place(self, j):
        return self.piece(j), self.rows, self.lanes

    def queries(self, j):
        return pair_rows(self.q_ref[self.place(j)])


def attend_one(heads, out_ref):
    for j in range(DEPTH):
        count = (j + 1) * ROWS
        probs = block_probs(heads.queries(j), heads.keys[:count], j, heads.y)
        out = dot_rows(probs.astype(jnp.bfloat16), heads.values[:count])
        out_ref[heads.place(j)] = pair_lanes(out).astype(jnp.bfloat16)


def attend_back_one(heads, grad_ref, dq_ref, dk_ref, dv_ref, odk_ref, odv_ref, key_sum, value_sum):
    half = ROWS // 2
    for j in reversed(range(DEPTH)):
        count = (j + 1) * ROWS
        queries = heads.queries(j)
        grads = pair_rows(grad_ref[heads.place(j)])
        keys, values = heads.keys[:count], heads.values[:count]
        probs = block_probs(queries, keys, j, heads.y)
        low = probs.astype(jnp.bfloat16)
        prob_grad = transposed_times(grads, values)
        delta = jnp.sum(low.astype(jnp.float32) * prob_grad, axis=-1, keepdims=True)
        score_grad = (probs * (prob_grad - delta)).astype(jnp.bfloat16)
        dq_ref[heads.place(j)] = pair_lanes(dot_rows(score_grad, keys))
        key_term = times_transposed(score_grad, queries)
        value_term = times_transposed(low, grads)
        if j == DEPTH - 1:
            key_sum[...] = key_term
            value_sum[...] = value_term
        else:
            key_sum[:count] += key_term
            value_sum[:count] += value_term
    for j in range(DEPTH):
        low = j * ROWS
        place = heads.place(j)
        dk_ref[place] = key_sum[low : low + half]
        dv_ref[place] = value_sum[low : low + half]
        odk_ref[place] = key_sum[low + half : low + ROWS].astype(jnp.bfloat16)
        odv_ref[place] = value_sum[low + half : low + ROWS].astype(jnp.bfloat16)


def backward_kernel(
    grads_ref,
    gate_ref,
    up_ref,
    normed_ref,
    pieces_ref,
    q_ref,
    kv_ref,
    okv_ref,
    hidden_ref,
    att_ref,
    rows_ref,
    own_sum,
    terms,
    valid_ref,
    gate_xs,
    gate_xk,
    gate_ys,
    gate_yk,
    gate_xr,
    gate_yr,
    gate_y2s,
    gate_x2s,
    gate_own_x,
    gate_own_y,
    heads_out,
    hidden_out,
    gu_ref,
    dq_ref,
    dk_ref,
    dv_ref,
    got_dk,
    got_dv,
    layer_out,
    attended_grad,
    odk_ref,
    odv_ref,
    key_sum,
    value_sum,
    z_recv,
    token_rows,
    z_s,
    z_r,
    pair_s,
    pair_r,
    stage_s,
    stage_r,
    local_sem,
):
    x, core, z, y = coordinates()
    low, wide = jnp.bfloat16, jnp.float32
    y_mate = (x * 2 + core, z * 2 + 1 - y)

    def z_mate(turn):
        return (x * 2 + core, lax.rem(z + turn, DEPTH) * 2 + y)

    x_mate = (2 - x * 2 + core, z * 2 + y)
    greet([x_mate, y_mate] + [z_mate(turn) for turn in range(1, DEPTH)])
    scattered = [
        remote(terms.at[k - 1], z_recv.at[k - 1], z_s, z_r, k - 1, z_mate(DEPTH - k))
        for k in range(1, DEPTH)
    ]
    for copy in scattered:
        copy.start()
    own_tokens = pltpu.make_async_copy(pieces_ref.at[0], token_rows, local_sem)
    own_tokens.start()

    def piece_body(grad_part, gate_part, up_part):
        piece = pl.program_id(0)
        grad = grad_part[0]
        attended_grad[piece] = transposed_times(grad, outward_rows(rows_ref)).astype(low)
        hidden_grad = transposed_times(grad, down_rows(rows_ref))
        gate = gate_part[0]
        sig = jax.nn.sigmoid(gate)
        silu = gate * sig
        gate_grad = hidden_grad * up_part[0] * (sig + silu * (1.0 - sig))
        up_grad = hidden_grad * silu
        gu_ref[piece] = jnp.concatenate([gate_grad, up_grad], 1).astype(low)

    pltpu.emit_pipeline(
        piece_body,
        grid=(PIECES,),
        in_specs=[piece_spec(r.shape[-1]) for r in (grads_ref, gate_ref, up_ref)],
    )(grads_ref, gate_ref, up_ref)

    def pair_copies(b, t):
        size, pair = ROWS // 2, 2 * HEAD_DIM
        at = (
            pl.ds(b * DEPTH, DEPTH),
            pl.ds(pl.multiple_of((t // 2) * size, size), size),
            pl.ds(pl.multiple_of((t % 2) * pair, pair), pair),
        )
        number = b * DEPTH + t
        return (
            remote(odk_ref.at[at], got_dk.at[at], pair_s, pair_r, (0, number), y_mate),
            remote(odv_ref.at[at], got_dv.at[at], pair_s, pair_r, (1, number), y_mate),
        )

    def attend_back(i, carry):
        b, t = i // DEPTH, i % DEPTH
        heads = Heads(b, t, z, y, q_ref, kv_ref, okv_ref)
        attend_back_one(
            heads, attended_grad, dq_ref, dk_ref, dv_ref, odk_ref, odv_ref, key_sum, value_sum
        )
        for copy in pair_copies(b, t):
            copy.start()
        return carry

    lax.fori_loop(0, PIECES, attend_back, 0)

    total, width = normed_ref.shape
    size = width // PIECES
    columns = gu_ref.shape[-1]
    cut = gate_xs.shape[-1]

    def right(first, last):
        return gu_ref[...].reshape(total, columns)[:, first:last]

    def whole_body(left, out):
        term = times_transposed(left[...], right(0, cut)).astype(out.dtype)
        out[...] = term.reshape(out.shape)

    def split_body(left, keep, send):
        split_rows(times_transposed(left[...], right(cut, columns)), y, keep, send)

    def from_block(base):
        return pl.BlockSpec((total, size), lambda i: (0, base + i))

    def block_of(array):
        return pl.BlockSpec((2,) + array.shape[1:], lambda i: (i,) + (0,) * (len(array.shape) - 1))

    pltpu.emit_pipeline(
        whole_body,
        grid=(DEPTH,),
        in_specs=[from_block((1 - x) * DEPTH)],
        out_specs=[block_of(gate_xs)],
    )(normed_ref, gate_xs)
    gate_x = remote(gate_xs, gate_xr, stage_s, stage_r, 0, x_mate)
    gate_x.start()
    pltpu.emit_pipeline(
        split_body,
        grid=(PIECES,),
        in_specs=[from_block(0)],
        out_specs=[block_of(gate_yk), block_of(gate_ys)],
    )(normed_ref, gate_yk, gate_ys)
    gate_y = remote(gate_ys, gate_yr, stage_s, stage_r, 1, y_mate)
    gate_y.start()

    flat_grads = grads_ref.reshape(total, width)
    wide_size = 2 * size

    def rows_body(right, heads, hidden):
        grad = right[...]
        attended = att_ref[...].reshape(total, HEAD_COLS)
        term = times_transposed(attended, grad).astype(low)
        heads[...] = term.reshape(heads.shape)
        hidden_rows = hidden_ref[...].reshape(total, hidden_ref.shape[-1])
        term = times_transposed(hidden_rows, grad).astype(low)
        hidden[...] = term.reshape(hidden.shape)

    def column_block(array):
        return pl.BlockSpec(array.shape[:2] + (wide_size,), lambda i: (0, 0, i))

    pltpu.emit_pipeline(
        rows_body,
        grid=(width // wide_size,),
        in_specs=[pl.BlockSpec((total, wide_size), lambda i: (0, i))],
        out_specs=[column_block(heads_out), column_block(hidden_out)],
    )(flat_grads, heads_out, hidden_out)

    pltpu.emit_pipeline(
        whole_body,
        grid=(DEPTH,),
        in_specs=[from_block(x * DEPTH)],
        out_specs=[block_of(gate_xk)],
    )(normed_ref, gate_xk)

    def sums_body(xk, xr, yk, yr, yk_own, yr_own, y2s, x2s, own_x, own_y):
        y2s[0] = (xk[0, 1 - y] + xr[0, 1 - y].astype(wide)).astype(low)
        own_x[0] = xk[0, y] + xr[0, y].astype(wide)
        x2s[0] = (yk[0] + yr[0].astype(wide)).astype(low)
        own_y[0] = yk_own[0] + yr_own[0].astype(wide)

    def one_block(array, base=0):
        return pl.BlockSpec(
            (1,) + array.shape[1:], lambda i: (base + i,) + (0,) * (len(array.shape) - 1)
        )

    gate_x.wait_recv()
    gate_y.wait_recv()
    theirs, ours = (1 - x) * PIECES, x * PIECES
    pltpu.emit_pipeline(
        sums_body,
        grid=(PIECES,),
        in_specs=[
            one_block(gate_xk),
            one_block(gate_xr),
            one_block(gate_yk, theirs),
            one_block(gate_yr, theirs),
            one_block(gate_yk, ours),
            one_block(gate_yr, ours),
        ],
        out_specs=[one_block(r) for r in (gate_y2s, gate_x2s, gate_own_x, gate_own_y)],
    )(
        gate_xk,
        gate_xr,
        gate_yk,
        gate_yr,
        gate_yk,
        gate_yr,
        gate_y2s,
        gate_x2s,
        gate_own_x,
        gate_own_y,
    )
    own_tokens.wait()
    for copy in scattered:
        copy.wait_recv()
    for first in range(0, ROWS, 64):
        rows = pl.ds(first, 64)
        branch = own_sum[rows]
        for k in range(DEPTH - 1):
            branch = branch + z_recv[k, rows].astype(wide)
        layer_out[rows] = (token_rows[rows].astype(wide) + valid_ref[rows] * branch).astype(low)

    for b in range(2):
        for t in range(DEPTH):
            for copy in pair_copies(b, t):
                copy.wait_recv()
                copy.wait_send()
    for copy in scattered:
        copy.wait_send()
    for copy in (gate_x, gate_y):
        copy.wait_send()


def backward(
    grads, gate, up, normed, pieces, queries, pairs, other_pairs, hidden, attended, rows_out,
    own_sum, terms, valid
):
    low, wide = jnp.bfloat16, jnp.float32
    width = pieces.shape[-1]
    each = hidden.shape[-1]
    columns = 2 * each
    cut = -(-columns // 256) * 128
    rows = width // 32
    head_rows = HEAD_DIM
    anywhere = pl.BlockSpec(memory_space=pl.ANY)
    inside = pl.BlockSpec(memory_space=pltpu.VMEM)
    shape = jax.ShapeDtypeStruct
    dma = pltpu.SemaphoreType.DMA
    return pl.pallas_call(
        backward_kernel,
        in_specs=[anywhere] * 5 + [inside] * 9,
        out_specs=[anywhere] * 12 + [inside] * 7,
        out_shape=[
            shape((PIECES, 2, rows, cut), low),
            shape((PIECES, 2, rows, cut), wide),
            shape((2 * PIECES, rows, columns - cut), low),
            shape((2 * PIECES, rows, columns - cut), wide),
            shape((PIECES, 2, rows, cut), low),
            shape((2 * PIECES, rows, columns - cut), low),
            shape((PIECES, rows, cut), low),
            shape((PIECES, rows, columns - cut), low),
            shape((PIECES, rows, cut), wide),
            shape((PIECES, rows, columns - cut), wide),
            shape((4, head_rows, width), low),
            shape((4, each // 4, width), low),
            shape((PIECES, ROWS, columns), low),
            shape((PIECES, ROWS, HEAD_COLS), wide),
            shape((PIECES, ROWS, HEAD_COLS), wide),
            shape((PIECES, ROWS, HEAD_COLS), wide),
            shape((PIECES, ROWS, HEAD_COLS), low),
            shape((PIECES, ROWS, HEAD_COLS), low),
            shape((ROWS, width), low),
        ],
        scratch_shapes=[
            pltpu.VMEM((PIECES, ROWS, HEAD_COLS), low),
            pltpu.VMEM((PIECES, ROWS, HEAD_COLS), low),
            pltpu.VMEM((PIECES, ROWS, HEAD_COLS), low),
            pltpu.VMEM((DEPTH * ROWS, 2 * HEAD_DIM), wide),
            pltpu.VMEM((DEPTH * ROWS, 2 * HEAD_DIM), wide),
            pltpu.VMEM((DEPTH - 1, ROWS, width), low),
            pltpu.VMEM((ROWS, width), low),
            dma((DEPTH - 1,)),
            dma((DEPTH - 1,)),
            dma((2, PIECES)),
            dma((2, PIECES)),
            dma((2,)),
            dma((2,)),
            dma(()),
        ],
        compiler_params=params(62, collective_id=3, has_side_effects=True),
        cost_estimate=cost(0, 64 * MIB),
        name="backward",
    )(
        grads, gate, up, normed, pieces, queries, pairs, other_pairs, hidden, attended, rows_out,
        own_sum, terms, valid
    )


def finish_kernel(
    dq_ref,
    dk_ref,
    dv_ref,
    odk_ref,
    odv_ref,
    gu_ref,
    pieces_ref,
    cos_ref,
    first_ref,
    second_ref,
    normed_ref,
    gate_y2s,
    gate_x2s,
    gate_sum_x,
    gate_sum_y,
    heads_term,
    hidden_term,
    wi_ref,
    wg_ref,
    gain_ref,
    cot_ref,
    tokens_out,
    heads_out,
    hidden_out,
    gate_rows,
    inward_rows_out,
    vec_out,
    heads_r,
    heads_2s,
    heads_2r,
    hidden_r,
    hidden_2s,
    hidden_2r,
    core_send,
    core_recv,
    z_send,
    below,
    above,
    own_sum,
    pg_ref,
    token_rows,
    vec_sum,
    vec_x,
    vec_y,
    gate_own_x,
    gate_own_y,
    gate_y2r,
    gate_x2r,
    gate_fin,
    inward_xs,
    inward_xr,
    inward_xk,
    inward_ys,
    inward_yr,
    inward_yk,
    inward_y2s,
    inward_y2r,
    inward_x2s,
    inward_x2r,
    inward_fin,
    core_s,
    core_r,
    up_s,
    down_s,
    below_r,
    above_r,
    stage_s,
    stage_r,
    rows_s,
    rows_r,
    vec_s,
    vec_r,
    local_sems,
):
    x, core, z, y = coordinates()
    low = jnp.bfloat16
    wide = jnp.float32

    def device(xx, cc, zz, yy):
        return (xx * 2 + cc, zz * 2 + yy)

    x_mate, y_mate = device(1 - x, core, z, y), device(x, core, z, 1 - y)
    core_mate = device(x, 1 - core, z, y)
    members = [(flip, turn) for turn in (2, 1, 3, 0) for flip in (1, 0)][:-1]

    def target(flip, turn):
        return (core + flip) % 2, (z + turn) % DEPTH

    greet([device(x, *target(*m), y) for m in members] + [x_mate, y_mate])

    started = []

    def begin(copy):
        copy.start()
        started.append(copy)
        return copy

    loads = [
        pltpu.make_async_copy(gate_sum_x, gate_own_x, local_sems.at[2]),
        pltpu.make_async_copy(gate_sum_y, gate_own_y, local_sems.at[3]),
    ]
    for load in loads:
        load.start()
    gate_y = begin(remote(gate_y2s, gate_y2r, stage_s, stage_r, (0, 2), y_mate))
    gate_x = begin(remote(gate_x2s, gate_x2r, stage_s, stage_r, (0, 3), x_mate))
    heads_x = begin(remote(heads_term.at[1 - x], heads_r, stage_s, stage_r, (2, 0), x_mate))
    hidden_y = [
        remote(hidden_term.at[i, 1 - y], hidden_r.at[i], stage_s, stage_r, (3, i), y_mate)
        for i in range(2)
    ]
    own_tokens = pltpu.make_async_copy(pieces_ref.at[0], token_rows, local_sems.at[4])
    own_tokens.start()

    vec_sum[...] = jnp.zeros_like(vec_sum)

    def core_copy(k):
        return remote(core_send.at[k % 2], core_recv.at[k], core_s, core_r, k, core_mate)

    def up_copy(slot, number):
        goal = device(x, core, z + 1, y)
        return remote_to(
            z_send.at[slot], below.at[number], up_s.at[slot], below_r.at[number], goal
        )

    def down_copy(slot, number):
        goal = device(x, core, z - 1, y)
        return remote_to(
            z_send.at[slot], above.at[number], down_s.at[slot], above_r.at[number], goal
        )

    def order(i):
        inner = jnp.where(z == 1, select(i, 2, 1, 3), select(i, 2, 3, 1))
        outer = jnp.where(z == 0, select(i, 1, 2, 3), select(i, 3, 2, 1))
        return jnp.where((z == 0) | (z == DEPTH - 1), outer, inner)

    def piece_of(i):
        return order(i // 2) + DEPTH * (1 - i % 2)

    def arrived(box, recvs, number):
        copy = remote_to(box.at[number], box.at[number], up_s.at[0], recvs.at[number], core_mate)
        copy.wait_recv()

    def add_and(slot, box, recvs, number, copy):
        arrived(box, recvs, number)
        z_send[slot] = (z_send[slot].astype(wide) + box[number].astype(wide)).astype(low)
        copy.start()

    def first_hop():
        @pl.when(z == 1)
        def _():
            add_and(0, below, below_r, 0, up_copy(0, 0))

        @pl.when(z == DEPTH - 2)
        def _():
            add_and(0, above, above_r, 0, down_copy(0, 0))

    def second_hop():
        @pl.when(z == 1)
        def _():
            add_and(2, below, below_r, 1, up_copy(2, 1))

        @pl.when(z == DEPTH - 2)
        def _():
            add_and(2, above, above_r, 1, down_copy(2, 1))

    def third_hop():
        @pl.when(z == 1)
        def _():
            add_and(1, above, above_r, 0, down_copy(1, 0))

        @pl.when(z == DEPTH - 2)
        def _():
            add_and(1, below, below_r, 0, up_copy(1, 0))

    def last_hop():
        @pl.when(z == 0)
        def _():
            arrived(above, above_r, 0)
            own_sum[...] += above[0].astype(wide)

        @pl.when(z == 1)
        def _():
            arrived(below, below_r, 2)
            arrived(above, above_r, 1)
            own_sum[...] += below[2].astype(wide) + above[1].astype(wide)

        @pl.when(z == DEPTH - 2)
        def _():
            arrived(below, below_r, 1)
            arrived(above, above_r, 2)
            own_sum[...] += below[1].astype(wide) + above[2].astype(wide)

        @pl.when(z == DEPTH - 1)
        def _():
            arrived(below, below_r, 0)
            own_sum[...] += below[0].astype(wide)

    def sent_all():
        @pl.when(z == 0)
        def _():
            for slot in range(DEPTH - 1):
                up_copy(slot, slot).wait_send()

        @pl.when(z == DEPTH - 1)
        def _():
            for slot in range(DEPTH - 1):
                down_copy(slot, slot).wait_send()

        @pl.when(z == 1)
        def _():
            up_copy(0, 0).wait_send()
            up_copy(2, 1).wait_send()
            down_copy(1, 0).wait_send()

        @pl.when(z == DEPTH - 2)
        def _():
            down_copy(0, 0).wait_send()
            down_copy(2, 1).wait_send()
            up_copy(1, 0).wait_send()

    def to_rows(which, fin, rows):
        slot = core * DEPTH + z
        copies = []
        for flip, turn in members:
            cc, zz = target(flip, turn)
            copies.append(
                remote(
                    fin.at[cc * DEPTH + zz],
                    rows.at[slot],
                    rows_s,
                    rows_r,
                    (which, flip * DEPTH + turn),
                    device(x, cc, zz, y),
                )
            )
        copies.append(pltpu.make_async_copy(fin.at[slot], rows.at[slot], local_sems.at[which]))
        return copies

    def gate_done():
        gate_y.wait_recv()
        gate_x.wait_recv()
        for load in loads:
            load.wait()
        gate_fin[...] = jnp.concatenate(
            [
                gate_own_x[...] + gate_y2r[...].astype(wide),
                gate_own_y[...] + gate_x2r[...].astype(wide),
            ],
            2,
        ).astype(low)
        for copy in to_rows(0, gate_fin, gate_rows) + hidden_y:
            copy.start()

    def piece_body(
        dq, dk, dv, odk, odv, gu, tokens, cos, first, second
    ):
        step = pl.program_id(0)
        turn = step // 2
        piece = piece_of(step)
        tables = (cos, first, second)
        query = turned(dq[0] * (HEAD_DIM**-0.5), *tables, -1.0)
        key = turned(dk[0] + odk[0].astype(wide), *tables, -1.0)
        value = dv[0] + odv[0].astype(wide)
        narrow = jnp.concatenate([query, key, value], 1).astype(low)
        pg_ref[piece] = narrow
        grad = transposed_times(narrow, inward_rows(wi_ref))
        grad += transposed_times(gu[0], wg_ref[...])
        hat, _ = normalised(tokens[0])
        half = grad.shape[1] // 2
        for row, total in (
            (0, jnp.sum(grad * hat, axis=0, keepdims=True)),
            (2, jnp.sum(grad, axis=0, keepdims=True)),
        ):
            vec_sum[row : row + 1] += total[:, :half]
            vec_sum[row + 1 : row + 2] += total[:, half:]
        vec_sum[4:5, : 3 * HEAD_COLS] += jnp.sum(narrow.astype(wide), axis=0, keepdims=True)

        pl.when(step == GATE_STEP)(gate_done)
        pl.when(step == PIECES - 1)(first_hop)

        @pl.when(step % 2 == 0)
        def _():
            @pl.when(turn >= 2)
            def _():
                core_copy(turn - 2).wait_send()

            core_send[turn % 2] = grad.astype(low)
            core_copy(turn).start()

        @pl.when(step % 2 == 1)
        def _():
            core_copy(turn).wait_recv()
            both = grad + core_recv[turn].astype(wide)

            @pl.when(turn < DEPTH - 1)
            def _():
                z_send[turn] = both.astype(low)

                @pl.when(z == 0)
                def _():
                    up_copy(turn, turn).start()

                @pl.when(z == DEPTH - 1)
                def _():
                    down_copy(turn, turn).start()

            @pl.when(turn == DEPTH - 1)
            def _():
                own_sum[...] = both

    def by_piece(width):
        return pl.BlockSpec((1, ROWS, width), lambda i: (piece_of(i), 0, 0))

    table_spec = pl.BlockSpec(
        (1,) + cos_ref.shape[1:], lambda i: (piece_of(i) % DEPTH, 0, 0)
    )
    pltpu.emit_pipeline(
        piece_body,
        grid=(PIECES,),
        in_specs=[by_piece(HEAD_COLS)] * 5
        + [by_piece(gu_ref.shape[-1]), by_piece(pieces_ref.shape[-1])]
        + [table_spec] * 3,
    )(
        dq_ref,
        dk_ref,
        dv_ref,
        odk_ref,
        odv_ref,
        gu_ref,
        pieces_ref,
        cos_ref,
        first_ref,
        second_ref,
    )
    vector_x = remote(vec_sum, vec_x, vec_s, vec_r, 0, x_mate)
    vector_x.start()

    total, width = normed_ref.shape
    size = width // PIECES
    cut = 3 * HEAD_COLS // 2

    def block(i):
        return jnp.where(i < DEPTH, (1 - x) * DEPTH + i, x * DEPTH + i - DEPTH)

    inward_x = remote(inward_xs, inward_xr, stage_s, stage_r, (1, 0), x_mate)

    def inward_body(left):
        i = pl.program_id(0)
        rhs = pg_ref[...].reshape(total, 3 * HEAD_COLS)
        term = times_transposed(left[...], rhs)
        first = term[:, :cut].reshape(2, 2, size // 4, cut)
        at = pl.ds((i % DEPTH) * 2, 2)

        @pl.when(i < DEPTH)
        def _():
            inward_xs[at] = first.astype(low)

        @pl.when(i >= DEPTH)
        def _():
            inward_xk[at] = first

        at = pl.ds(block(i) * 2, 2)
        split_rows(term[:, cut:], y, inward_yk.at[at], inward_ys.at[at])

        @pl.when(i == DEPTH - 1)
        def _():
            inward_x.start()

    pltpu.emit_pipeline(
        inward_body,
        grid=(PIECES,),
        in_specs=[pl.BlockSpec((total, size), lambda i: (0, block(i)))],
    )(normed_ref)
    started.append(inward_x)
    inward_y = begin(remote(inward_ys, inward_yr, stage_s, stage_r, (1, 1), y_mate))

    vector_x.wait_recv()
    vec_sum_x = vec_sum[...] + vec_x[...]
    vector_x.wait_send()
    vec_sum[...] = vec_sum_x
    vector_y = remote(vec_sum, vec_y, vec_s, vec_r, 1, y_mate)
    vector_y.start()

    def add_two(one, two, out):
        out[...] = (one[...].astype(wide) + two[...].astype(wide)).astype(out.dtype)

    second_hop()
    third_hop()

    chunk = heads_term.shape[-1] // 2

    def flat_spec(rows):
        return pl.BlockSpec((rows, chunk), lambda i: (0, i))

    def row_sum(one, two, out):
        spec = flat_spec(one.shape[0])
        pltpu.emit_pipeline(
            add_two, grid=(2,), in_specs=[spec, spec], out_specs=[spec]
        )(one, two, out)

    def row_total(one, two, three, out):
        spec = flat_spec(one.shape[0])

        def body(one, two, three, out):
            out[...] = one[...].astype(wide) + two[...].astype(wide) + three[...].astype(wide)

        pltpu.emit_pipeline(
            body, grid=(2,), in_specs=[spec] * 3, out_specs=[spec]
        )(one, two, three, out)

    heads_x.wait_recv()
    row_sum(heads_term.at[x, 1 - y], heads_r.at[1 - y], heads_2s)
    heads_y = begin(remote(heads_2s, heads_2r, stage_s, stage_r, (2, 2), y_mate))
    for copy in hidden_y:
        copy.wait_recv()
    row_sum(hidden_term.at[1 - x, y], hidden_r.at[1 - x], hidden_2s)
    hidden_x = begin(remote(hidden_2s, hidden_2r, stage_s, stage_r, (3, 2), x_mate))

    vector_y.wait_recv()
    vec_sum_y = vec_sum[...] + vec_y[...]
    vector_y.wait_send()
    slot = core * DEPTH + z
    vec_out[slot] = vec_sum_y
    vectors = []
    for flip, turn in members:
        cc, zz = target(flip, turn)
        vectors.append(
            begin(
                remote(
                    vec_out.at[slot],
                    vec_out.at[slot],
                    rows_s,
                    rows_r,
                    (2, flip * DEPTH + turn),
                    device(x, cc, zz, y),
                )
            )
        )

    inward_x.wait_recv()
    inward_y2s[...] = (inward_xk[:, 1 - y] + inward_xr[:, 1 - y].astype(wide)).astype(low)
    inward_over_y = begin(remote(inward_y2s, inward_y2r, stage_s, stage_r, (1, 2), y_mate))
    inward_y.wait_recv()
    other = pl.ds((1 - x) * PIECES, PIECES)
    inward_x2s[...] = (inward_yk[other] + inward_yr[other].astype(wide)).astype(low)
    inward_over_x = begin(remote(inward_x2s, inward_x2r, stage_s, stage_r, (1, 3), x_mate))
    heads_y.wait_recv()
    row_total(heads_term.at[x, y], heads_r.at[y], heads_2r, heads_out)
    hidden_x.wait_recv()
    row_total(hidden_term.at[x, y], hidden_r.at[x], hidden_2r, hidden_out)
    inward_over_y.wait_recv()
    inward_over_x.wait_recv()
    own = pl.ds(x * PIECES, PIECES)
    inward_fin[...] = jnp.concatenate(
        [
            inward_xk[:, y] + inward_xr[:, y].astype(wide) + inward_y2r[...].astype(wide),
            inward_yk[own] + inward_yr[own].astype(wide) + inward_x2r[...].astype(wide),
        ],
        2,
    ).astype(low)
    inward_rest = to_rows(1, inward_fin, inward_rows_out)
    for copy in inward_rest:
        copy.start()

    own_tokens.wait()
    last_hop()
    for first in range(0, ROWS, 64):
        rows = pl.ds(first, 64)
        grad = own_sum[rows]
        hat, inverse = normalised(token_rows[rows])
        scaled = grad * gain_ref[...]
        input_grad = inverse * (
            scaled
            - jnp.mean(scaled, axis=-1, keepdims=True)
            - hat * jnp.mean(scaled * hat, axis=-1, keepdims=True)
        )
        tokens_out[rows] = (cot_ref[rows].astype(wide) + input_grad).astype(low)

    for copy in to_rows(0, gate_fin, gate_rows) + inward_rest:
        copy.wait()
    for copy in hidden_y:
        copy.wait_send()
    for copy in vectors:
        copy.wait_recv()
    for copy in started:
        copy.wait_send()
    for turn in range(DEPTH - 2, DEPTH):
        core_copy(turn).wait_send()
    sent_all()


def finish(
    parts, gate_up_grad, pieces, tables, normed, gate_up, heads, hidden, weights, gain, cot
):
    low, wide = jnp.bfloat16, jnp.float32
    width = pieces.shape[-1]
    rows = width // 32
    anywhere = pl.BlockSpec(memory_space=pl.ANY)
    inside = pl.BlockSpec(memory_space=pltpu.VMEM)
    shape = jax.ShapeDtypeStruct
    half = 3 * HEAD_COLS // 2

    a, b = (value.shape[-1] for value in gate_up[:2])
    heads_rows, hidden_rows = heads.shape[2], hidden.shape[2]
    out_shapes = [
        shape((ROWS, width), low),
        shape((heads_rows, width), wide),
        shape((hidden_rows, width), wide),
        shape((PIECES, rows, a + b), low),
        shape((PIECES, rows, 2 * half), low),
        shape((PIECES, 8, width // 2), wide),
    ]
    out_shapes += [
        shape((2, heads_rows, width), low),
        shape((heads_rows, width), low),
        shape((heads_rows, width), low),
        shape((2, hidden_rows, width), low),
        shape((hidden_rows, width), low),
        shape((hidden_rows, width), low),
    ]
    out_specs = [inside] + [anywhere] * 4 + [inside] + [anywhere] * (len(out_shapes) - 6)
    dma = pltpu.SemaphoreType.DMA
    outs = pl.pallas_call(
        finish_kernel,
        in_specs=[anywhere] * 17 + [inside] * 4,
        out_specs=out_specs,
        out_shape=out_shapes,
        scratch_shapes=[
            pltpu.VMEM((2, ROWS, width), low),
            pltpu.VMEM((DEPTH, ROWS, width), low),
            pltpu.VMEM((DEPTH - 1, ROWS, width), low),
            pltpu.VMEM((DEPTH - 1, ROWS, width), low),
            pltpu.VMEM((DEPTH - 1, ROWS, width), low),
            pltpu.VMEM((ROWS, width), wide),
            pltpu.VMEM((PIECES, ROWS, 3 * HEAD_COLS), low),
            pltpu.VMEM((ROWS, width), low),
            pltpu.VMEM((8, width // 2), wide),
            pltpu.VMEM((8, width // 2), wide),
            pltpu.VMEM((8, width // 2), wide),
            pltpu.VMEM((PIECES, rows, a), wide),
            pltpu.VMEM((PIECES, rows, b), wide),
            pltpu.VMEM((PIECES, rows, a), low),
            pltpu.VMEM((PIECES, rows, b), low),
            pltpu.VMEM((PIECES, rows, a + b), low),
            pltpu.VMEM((PIECES, 2, rows, half), low),
            pltpu.VMEM((PIECES, 2, rows, half), low),
            pltpu.VMEM((PIECES, 2, rows, half), wide),
            pltpu.VMEM((2 * PIECES, rows, half), low),
            pltpu.VMEM((2 * PIECES, rows, half), low),
            pltpu.VMEM((2 * PIECES, rows, half), wide),
            pltpu.VMEM((PIECES, rows, half), low),
            pltpu.VMEM((PIECES, rows, half), low),
            pltpu.VMEM((PIECES, rows, half), low),
            pltpu.VMEM((PIECES, rows, half), low),
            pltpu.VMEM((PIECES, rows, 2 * half), low),
            dma((DEPTH,)),
            dma((DEPTH,)),
            dma((DEPTH - 1,)),
            dma((DEPTH - 1,)),
            dma((DEPTH - 1,)),
            dma((DEPTH - 1,)),
            dma((4, 4)),
            dma((4, 4)),
            dma((3, PIECES)),
            dma((3, PIECES)),
            dma((2,)),
            dma((2,)),
            dma((5,)),
        ],
        compiler_params=params(63, collective_id=1, has_side_effects=True),
        cost_estimate=cost(0, 64 * MIB),
        name="finish",
    )(
        *parts,
        gate_up_grad,
        pieces,
        *tables,
        normed,
        *gate_up,
        heads,
        hidden,
        *weights,
        gain,
        cot,
    )
    return outs[:6]


def split_rows(term, y, keep_ref, send_ref):
    rows = term.shape[0] // 4
    even = jnp.concatenate([term[:rows], term[2 * rows : 3 * rows]], 0)
    odd = jnp.concatenate([term[rows : 2 * rows], term[3 * rows :]], 0)
    keep_ref[...] = jnp.where(y == 0, even, odd).reshape(keep_ref.shape)
    send_ref[...] = jnp.where(y == 0, odd, even).astype(jnp.bfloat16).reshape(send_ref.shape)


def place_kernel(parts, in_ref, out_ref):
    each = in_ref.shape[2] // parts
    for part in range(parts):
        columns = slice(part * each, (part + 1) * each)
        line = jnp.concatenate([in_ref[n, :, columns] for n in range(PIECES)], 1)
        out_ref[:, part * PIECES * each : (part + 1) * PIECES * each] = line.astype(jnp.float32)


def place_rows(value, parts):
    rows, columns = value.shape[1], value.shape[2]
    return pl.pallas_call(
        functools.partial(place_kernel, parts),
        out_shape=jax.ShapeDtypeStruct((rows, PIECES * columns), jnp.float32),
        compiler_params=params(32),
        cost_estimate=cost(0, 4 * MIB),
        name="place_rows",
    )(value)


def lane_tables(positions):
    half = ROT // 2
    place = jnp.arange(HEAD_COLS, dtype=jnp.int32) % HEAD_DIM
    power = (place % half).astype(jnp.float32)
    frequency = jnp.where(place < ROT, rotary_base ** (-(2.0 * power) / ROT), 0.0)
    angles = positions.astype(jnp.float32)[..., None] * frequency
    sine = jnp.sin(angles)
    return (
        jnp.cos(angles),
        jnp.where(place < half, -sine, 0.0),
        jnp.where((place >= half) & (place < ROT), sine, 0.0),
    )


def shards_grouped(
    tokens,
    lengths,
    norm_gain,
    norm_shift,
    inward_weight,
    inward_bias,
    outward_weight,
    gate_up_weight,
    down_weight,
    cotangent,
):
    group_len, seqs, width = tokens.shape[1:]
    bucket, blk = lax.axis_index("bucket"), lax.axis_index("blk")
    _, core, z, y = coordinates()

    own_rows = inward_weight.shape[0]
    hidden_each = gate_up_weight.shape[1] // (2 * 2 * 2 * DEPTH)
    gain_share, bias_share = norm_gain.shape[0], inward_bias.shape[0]
    shares = jnp.concatenate([norm_gain, norm_shift, inward_bias]).astype(jnp.bfloat16)
    shares = jnp.pad(shares, (0, 3 * HEAD_COLS - shares.shape[0]))
    inward = inward_weight.astype(jnp.bfloat16).reshape(own_rows, 3, 2, 2, DEPTH, 2 * HEAD_DIM)
    inward = jnp.transpose(inward, (3, 4, 0, 1, 2, 5)).reshape(2, DEPTH, own_rows, 3 * HEAD_COLS)
    inward = jnp.concatenate(
        [inward, jnp.broadcast_to(shares, (2, DEPTH, EXTRA, 3 * HEAD_COLS))], 2
    )
    gate_up = gate_up_weight.astype(jnp.bfloat16).reshape(own_rows, 2, 2, 2, DEPTH, hidden_each)
    gate_up = jnp.transpose(gate_up, (3, 4, 0, 1, 2, 5)).reshape(
        2, DEPTH, own_rows, 4 * hidden_each
    )
    rows_out = jnp.concatenate([outward_weight, down_weight]).astype(jnp.bfloat16)
    own_tokens = jnp.transpose(tokens[0], (1, 0, 2))
    pieces, inward, gate_up, rows_out = gather(
        own_tokens.reshape(ROWS, width), inward, gate_up, rows_out
    )
    vectors = inward[..., own_rows, :].reshape(-1, 3 * HEAD_COLS).astype(jnp.float32)
    inward = inward.reshape((-1,) + inward.shape[4:])
    gate_up = gate_up.reshape(width, -1)
    rows_out = rows_out.reshape((-1,) + rows_out.shape[2:])

    gain = vectors[:, :gain_share].reshape(1, width)
    shift = vectors[:, gain_share : 2 * gain_share].reshape(1, width)
    bias = vectors[:, 2 * gain_share : 2 * gain_share + bias_share].reshape(-1)

    def own_columns(values, each):
        split = values.reshape(2, 2, DEPTH, each)
        return one_of(one_of(split, core, 1), z, 1)

    key_bias = jnp.pad(
        own_columns(bias[2 * width :], 2 * ROT).reshape(LOCAL_HEADS, ROT),
        ((0, 0), (0, HEAD_DIM - ROT)),
    )
    own_bias = jnp.concatenate(
        [
            own_columns(bias[:width], 2 * HEAD_DIM).reshape(-1),
            key_bias.reshape(-1),
            own_columns(bias[width : 2 * width], 2 * HEAD_DIM).reshape(-1),
        ]
    ).reshape(1, -1)

    position = blk * group_len + jnp.arange(group_len, dtype=jnp.int32)
    valid = (position[None, :] < lengths[0][:, None]).astype(jnp.float32)[..., None]
    own_cotangent = jnp.transpose(cotangent[0], (1, 0, 2))
    own_grad = (own_cotangent.astype(jnp.float32) * valid).astype(jnp.bfloat16)
    turns = (z - jnp.arange(DEPTH, dtype=jnp.int32)) % DEPTH
    tables = lane_tables(
        ((2 * turns + y) * group_len)[:, None] + jnp.arange(group_len, dtype=jnp.int32)
    )

    normed, gate, up, grads, queries, pairs, other_pairs, hidden, attended, own_sum, terms = forward(
        pieces,
        own_grad.reshape(ROWS, width),
        tables,
        gain,
        shift,
        own_bias,
        inward,
        gate_up,
        rows_out,
    )
    normed = normed.reshape(PIECES * ROWS, width)
    outs = backward(
        grads,
        gate,
        up,
        normed,
        pieces,
        queries,
        pairs,
        other_pairs,
        hidden,
        attended,
        rows_out,
        own_sum,
        terms,
        valid.reshape(ROWS, 1),
    )
    heads_term, hidden_term, gate_up_grad, *parts, layer_out = outs[10:]
    tokens_grad, outward_sum, down_sum, gate_up_rows, inward_rows_own, vectors = finish(
        parts,
        gate_up_grad,
        pieces,
        tables,
        normed,
        outs[6:10],
        heads_term.reshape(2, 2, -1, width),
        hidden_term.reshape(2, 2, -1, width),
        (inward, gate_up),
        gain,
        own_cotangent.reshape(ROWS, width),
    )
    gate_up_sum = place_rows(gate_up_rows, 4)
    inward_sum = place_rows(inward_rows_own, 6)

    device = bucket * 2 * DEPTH + blk
    sums = jnp.sum(vectors[:, :4], axis=0).reshape(2, -1, gain_share)
    gain_sum = one_of(sums[0], device, 0)
    shift_sum = one_of(sums[1], device, 0)
    columns_sum = vectors[:, 4, : 3 * HEAD_COLS].reshape(PIECES, 3, 2, 2 * HEAD_DIM)
    columns_sum = jnp.transpose(columns_sum, (1, 2, 0, 3)).reshape(3, -1)
    key_rot = columns_sum[1].reshape(HEADS, HEAD_DIM)[:, :ROT]
    bias_all = jnp.concatenate([columns_sum[0], columns_sum[2], key_rot.reshape(-1)])
    bias_sum = one_of(bias_all.reshape(-1, bias_share), device, 0)

    def placed(value):
        value = value.reshape(seqs, group_len, width)
        return jnp.transpose(value, (1, 0, 2)).reshape(tokens.shape)

    return (
        placed(layer_out),
        placed(tokens_grad),
        gain_sum,
        shift_sum,
        inward_sum,
        bias_sum,
        outward_sum,
        gate_up_sum,
        down_sum,
    )


def solution(mesh):
    in_specs = (
        P("bucket", "blk", None, None),
        P("bucket", None),
        P(("bucket", "blk")),
        P(("bucket", "blk")),
        P(("bucket", "blk"), None),
        P(("bucket", "blk")),
        P(("bucket", "blk"), None),
        P(("bucket", "blk"), None),
        P(("bucket", "blk"), None),
        P("bucket", "blk", None, None),
    )
    out_specs = (
        P("bucket", "blk", None, None),
        P("bucket", "blk", None, None),
        P(("bucket", "blk")),
        P(("bucket", "blk")),
        P(("bucket", "blk"), None),
        P(("bucket", "blk")),
        P(("bucket", "blk"), None),
        P(("bucket", "blk"), None),
        P(("bucket", "blk"), None),
    )
    body = shards_grouped if fits_groups(mesh) else shards_general
    return jax.shard_map(body, mesh=mesh, in_specs=in_specs, out_specs=out_specs, check_vma=False)
```

```python
import functools

import jax
import jax.numpy as jnp
from jax import lax
from jax.experimental import pallas as pl
from jax.experimental.pallas import tpu as pltpu
from jax.sharding import PartitionSpec as P

HEADS = 32
HEAD_DIM = 64
ROT = 16


epsilon = 1e-05
rotary_base = 10000.0
masked_score = -1e30


def shifted(value, axis, by):
    count = lax.axis_size(axis)
    pairs = [(i, i + by) for i in range(count) if 0 <= i + by < count]
    return lax.ppermute(value, axis, pairs)


def shifted_2(value, axis, steps):
    count = lax.axis_size(axis)
    pairs = [(source, (source + steps) % count) for source in range(count)]
    return lax.ppermute(value, axis, pairs)


def keep_same(value):
    return value


def transposed_times(left, right):
    return lax.dot_general(
        left, right, (((1,), (1,)), ((), ())), preferred_element_type=jnp.float32
    )


def times_transposed(left, right):
    return lax.dot_general(
        left, right, (((0,), (0,)), ((), ())), preferred_element_type=jnp.float32
    )


def rotary_tables(positions):
    half_rot = ROT // 2
    frequency = rotary_base ** (-(2.0 * jnp.arange(half_rot).astype(jnp.float32)) / ROT)
    angles = positions.astype(jnp.float32)[:, None] * frequency[None, :]
    return (jnp.cos(angles), jnp.sin(angles))


def rotate(values, cos_table, sine_table):
    half_rot = ROT // 2
    front_half = values[..., :half_rot]
    back_half = values[..., half_rot:ROT]
    return jnp.concatenate(
        [
            front_half * cos_table - back_half * sine_table,
            back_half * cos_table + front_half * sine_table,
            values[..., ROT:],
        ],
        axis=-1,
    )


def split_pairs(packed):
    rows_here, seq_count, both_width = packed.shape
    half_width = both_width // 2
    keys_part = packed[..., :half_width].reshape(rows_here, seq_count, HEADS, HEAD_DIM)
    values_part = packed[..., half_width:].reshape(rows_here, seq_count, HEADS, HEAD_DIM)
    return (keys_part, values_part)


def block_scores(queries, key_block, query_start, key_start):
    scores = jnp.einsum("tshd,ushd->shtu", queries, key_block, preferred_element_type=jnp.float32)
    query_pos = query_start + jnp.arange(queries.shape[0], dtype=jnp.int32)
    key_pos = key_start + jnp.arange(key_block.shape[0], dtype=jnp.int32)
    allowed = (key_pos[None, :] <= query_pos[:, None])[None, None]
    return (jnp.where(allowed, scores, masked_score), allowed)


def forward_block(carried, queries, key_block, value_block, query_start, key_start):
    running_max, running_sum, weighted = carried
    scores, allowed = block_scores(queries, key_block, query_start, key_start)
    new_max = jnp.maximum(running_max, jnp.max(scores, axis=-1))
    rescale = jnp.exp(running_max - new_max)
    weights = jnp.where(allowed, jnp.exp(scores - new_max[..., None]), 0.0)
    running_sum = running_sum * rescale + jnp.sum(weights, axis=-1)
    update = jnp.einsum(
        "shtu,ushd->tshd",
        weights.astype(jnp.bfloat16),
        value_block,
        preferred_element_type=jnp.float32,
    )
    weighted = weighted * jnp.transpose(rescale, (2, 0, 1))[..., None] + update
    return (new_max, running_sum, weighted)


def pair_grads(
    queries, out_grads, log_norm, deltas, key_block, value_block, query_start, key_start
):
    scores, allowed = block_scores(queries, key_block, query_start, key_start)
    probability = jnp.where(allowed, jnp.exp(scores - log_norm[..., None]), 0.0)
    value_grad = jnp.einsum(
        "shtu,tshd->ushd",
        probability.astype(jnp.bfloat16),
        out_grads,
        preferred_element_type=jnp.float32,
    )
    prob_grad = jnp.einsum(
        "tshd,ushd->shtu", out_grads, value_block, preferred_element_type=jnp.float32
    )
    score_grad = (probability * (prob_grad - deltas[..., None])).astype(jnp.bfloat16)
    query_grad = jnp.einsum(
        "shtu,ushd->tshd", score_grad, key_block, preferred_element_type=jnp.float32
    )
    key_grad = jnp.einsum(
        "shtu,tshd->ushd", score_grad, queries, preferred_element_type=jnp.float32
    )
    return (query_grad, key_grad, value_grad)


def over_blocks(running, incoming, unit_rows, handle):
    total_rows = incoming[0].shape[0]
    block_count = total_rows // unit_rows
    block_rows = total_rows // block_count
    stacked = tuple(
        (member.reshape((block_count, block_rows) + member.shape[1:]) for member in incoming)
    )

    def visit(carried, element):
        block_index, members = element
        return (handle(carried, members, block_index * block_rows), None)

    running, unused = lax.scan(visit, running, (jnp.arange(block_count, dtype=jnp.int32), stacked))
    return running


def shards_general(
    tokens,
    lengths,
    norm_gain,
    norm_shift,
    inward_weight,
    inward_bias,
    outward_weight,
    gate_up_weight,
    down_weight,
    cotangent,
):
    group_len = tokens.shape[1]
    seq_count = tokens.shape[2]
    model_width = tokens.shape[3]
    row_total = group_len * seq_count
    block_total = lax.axis_size("blk")
    position = lax.axis_index("blk")
    own_start = position * group_len
    longest = jnp.max(lengths[0])
    active = own_start < longest
    gathered = (
        lax.all_gather(inward_weight.astype(jnp.bfloat16), ("bucket", "blk"), axis=0, tiled=True),
        lax.all_gather(outward_weight.astype(jnp.bfloat16), ("bucket", "blk"), axis=0, tiled=True),
        lax.all_gather(gate_up_weight.astype(jnp.bfloat16), ("bucket", "blk"), axis=0, tiled=True),
        lax.all_gather(down_weight.astype(jnp.bfloat16), ("bucket", "blk"), axis=0, tiled=True),
        lax.all_gather(norm_gain.astype(jnp.bfloat16), ("bucket", "blk"), axis=0, tiled=True),
        lax.all_gather(norm_shift.astype(jnp.bfloat16), ("bucket", "blk"), axis=0, tiled=True),
        lax.all_gather(inward_bias.astype(jnp.bfloat16), ("bucket", "blk"), axis=0, tiled=True),
    )
    inward_full, outward_full, gate_up_full, down_full, gain_full, shift_full, bias_full = gathered
    inputs = tokens.reshape(row_total, model_width).astype(jnp.float32)
    centred = inputs - jnp.mean(inputs, axis=-1, keepdims=True)
    variance = jnp.mean(centred * centred, axis=-1, keepdims=True)
    inverse = lax.rsqrt(variance + epsilon)
    normal_hat = centred * inverse
    normed_low = (
        normal_hat * gain_full.astype(jnp.float32) + shift_full.astype(jnp.float32)
    ).astype(jnp.bfloat16)
    bias_float = bias_full.astype(jnp.float32)
    key_bias = jnp.pad(
        bias_float[2 * model_width :].reshape(HEADS, ROT), ((0, 0), (0, HEAD_DIM - ROT))
    ).reshape(model_width)
    full_bias = jnp.concatenate(
        [bias_float[:model_width], key_bias, bias_float[model_width : 2 * model_width]]
    )
    projected = jnp.dot(normed_low, inward_full, preferred_element_type=jnp.float32) + full_bias
    projected = projected.reshape(group_len, seq_count, 3, HEADS, HEAD_DIM)
    cos_table, sine_table = rotary_tables(own_start + jnp.arange(group_len, dtype=jnp.int32))
    cos_table = cos_table[:, None, None, :]
    sine_table = sine_table[:, None, None, :]
    query_scale = HEAD_DIM ** (-0.5)
    queries = (rotate(projected[:, :, 0], cos_table, sine_table) * query_scale).astype(jnp.bfloat16)
    keys_low = rotate(projected[:, :, 1], cos_table, sine_table).astype(jnp.bfloat16)
    values_low = projected[:, :, 2].astype(jnp.bfloat16)
    packed = jnp.concatenate(
        [
            keys_low.reshape(group_len, seq_count, model_width),
            values_low.reshape(group_len, seq_count, model_width),
        ],
        axis=-1,
    )

    def forward_handle(carried, members, key_start):
        keys_part, values_part = split_pairs(members[0])
        needed = active & (key_start <= own_start + group_len - 1)

        def forward_compute(state_in):
            return forward_block(state_in, queries, keys_part, values_part, own_start, key_start)

        return lax.cond(needed, forward_compute, keep_same, carried)

    start_state = (
        jnp.full((seq_count, HEADS, group_len), masked_score, jnp.float32),
        jnp.zeros((seq_count, HEADS, group_len), jnp.float32),
        jnp.zeros((group_len, seq_count, HEADS, HEAD_DIM), jnp.float32),
    )
    running_max, running_sum, weighted = over_blocks(
        start_state, (lax.all_gather(packed, "blk", axis=0, tiled=True),), group_len, forward_handle
    )
    bounded = jnp.maximum(running_sum, 1.0)
    log_norm = running_max + jnp.log(bounded)
    attended = weighted / jnp.transpose(bounded, (2, 0, 1))[..., None]
    attended_rows = attended.astype(jnp.bfloat16).reshape(row_total, model_width)
    gate_up = jnp.dot(normed_low, gate_up_full, preferred_element_type=jnp.float32)
    ff_width = gate_up.shape[1] // 2
    gate_part = gate_up[:, :ff_width]
    up_part = gate_up[:, ff_width:]
    sigmoid_gate = jax.nn.sigmoid(gate_part)
    silu_gate = gate_part * sigmoid_gate
    hidden_low = (silu_gate * up_part).astype(jnp.bfloat16)
    branch = jnp.dot(attended_rows, outward_full, preferred_element_type=jnp.float32) + jnp.dot(
        hidden_low, down_full, preferred_element_type=jnp.float32
    )
    query_pos = own_start + jnp.arange(group_len, dtype=jnp.int32)
    valid_rows = (
        (query_pos[:, None] < lengths[0][None, :]).astype(jnp.float32).reshape(row_total, 1)
    )
    layer_out = (inputs + valid_rows * branch).astype(jnp.bfloat16).reshape(tokens.shape)
    inward_back = gathered[0]
    outward_back = gathered[1]
    gate_up_back = gathered[2]
    down_back = gathered[3]
    gain_float = gathered[4].astype(jnp.float32)
    cotangent_rows = cotangent.reshape(row_total, model_width).astype(jnp.float32)
    branch_grad = (cotangent_rows * valid_rows).astype(jnp.bfloat16)
    hidden_grad = transposed_times(branch_grad, down_back)
    gate_grad = hidden_grad * up_part * (sigmoid_gate + silu_gate * (1.0 - sigmoid_gate))
    up_grad = hidden_grad * silu_gate
    gate_up_grad_low = jnp.concatenate([gate_grad, up_grad], axis=-1).astype(jnp.bfloat16)
    down_term = times_transposed(hidden_low, branch_grad)
    gate_up_term = times_transposed(normed_low, gate_up_grad_low)
    gate_up_sum, down_sum = (
        lax.psum_scatter(gate_up_term, ("bucket", "blk"), scatter_dimension=0, tiled=True),
        lax.psum_scatter(down_term, ("bucket", "blk"), scatter_dimension=0, tiled=True),
    )
    normed_grad = transposed_times(gate_up_grad_low, gate_up_back)
    attended_grad = (
        transposed_times(branch_grad, outward_back)
        .astype(jnp.bfloat16)
        .reshape(group_len, seq_count, HEADS, HEAD_DIM)
    )
    outward_term = times_transposed(attended_rows, branch_grad)
    deltas = jnp.transpose(
        jnp.sum(attended_grad.astype(jnp.float32) * attended, axis=-1), (1, 2, 0)
    )
    grad_zeros = jnp.zeros((group_len, seq_count, 2 * model_width), jnp.float32)
    query_zeros = jnp.zeros((group_len, seq_count, HEADS, HEAD_DIM), jnp.float32)

    def cycle_turn(turn_index, carried):
        visiting, sums_now, grads_now = carried
        owner_index = (position - turn_index) % block_total
        key_start = owner_index * group_len
        needed = active & (owner_index <= position)

        def cycle_compute(sums_in):
            keys_part, values_part = split_pairs(visiting)
            query_part, key_part, value_part = pair_grads(
                queries,
                attended_grad,
                log_norm,
                deltas,
                keys_part,
                values_part,
                own_start,
                key_start,
            )
            merged = jnp.concatenate(
                [
                    key_part.reshape(group_len, seq_count, model_width),
                    value_part.reshape(group_len, seq_count, model_width),
                ],
                axis=-1,
            )
            return (sums_in[0] + merged, sums_in[1] + query_part)

        sums_now, grads_now = lax.cond(needed, cycle_compute, keep_same, (sums_now, grads_now))
        visiting = shifted(visiting, "blk", 1)
        sums_now = shifted_2(sums_now.astype(jnp.bfloat16), "blk", 1).astype(sums_now.dtype)
        return (visiting, sums_now, grads_now)

    unused, pair_sums, query_grads = lax.fori_loop(
        0, block_total, cycle_turn, (packed, grad_zeros, query_zeros)
    )
    key_grad = pair_sums[..., :model_width].reshape(group_len, seq_count, HEADS, HEAD_DIM)
    value_grad = pair_sums[..., model_width:].reshape(group_len, seq_count, HEADS, HEAD_DIM)
    back_sine = -sine_table
    query_back = rotate(query_grads * query_scale, cos_table, back_sine)
    key_back = rotate(key_grad, cos_table, back_sine)
    projected_grad = (
        jnp.stack([query_back, key_back, value_grad], axis=2)
        .reshape(row_total, 3 * model_width)
        .astype(jnp.bfloat16)
    )
    inward_term = times_transposed(normed_low, projected_grad)
    column_sums = jnp.sum(projected_grad.astype(jnp.float32), axis=0)
    key_bias_grad = (
        column_sums[model_width : 2 * model_width]
        .reshape(HEADS, HEAD_DIM)[:, :ROT]
        .reshape(HEADS * ROT)
    )
    bias_term = jnp.concatenate(
        [column_sums[:model_width], column_sums[2 * model_width :], key_bias_grad]
    )
    normed_grad = normed_grad + transposed_times(projected_grad, inward_back)
    gain_term = jnp.sum(normed_grad * normal_hat, axis=0)
    shift_term = jnp.sum(normed_grad, axis=0)
    scaled_grad = normed_grad * gain_float
    input_grad = inverse * (
        scaled_grad
        - jnp.mean(scaled_grad, axis=-1, keepdims=True)
        - normal_hat * jnp.mean(scaled_grad * normal_hat, axis=-1, keepdims=True)
    )
    tokens_grad = (cotangent_rows + input_grad).astype(jnp.bfloat16).reshape(tokens.shape)
    inward_sum, outward_sum, bias_sum, gain_sum, shift_sum = (
        lax.psum_scatter(inward_term, ("bucket", "blk"), scatter_dimension=0, tiled=True),
        lax.psum_scatter(outward_term, ("bucket", "blk"), scatter_dimension=0, tiled=True),
        lax.psum_scatter(bias_term, ("bucket", "blk"), scatter_dimension=0, tiled=True),
        lax.psum_scatter(gain_term, ("bucket", "blk"), scatter_dimension=0, tiled=True),
        lax.psum_scatter(shift_term, ("bucket", "blk"), scatter_dimension=0, tiled=True),
    )
    return (
        layer_out,
        tokens_grad,
        gain_sum,
        shift_sum,
        inward_sum,
        bias_sum,
        outward_sum,
        gate_up_sum,
        down_sum,
    )


DEPTH = 4
PIECES = 2 * DEPTH
ROWS = 256
GATE_STEP = 4
HALFWAY = 5
LOCAL_HEADS = 4
HEAD_COLS = LOCAL_HEADS * HEAD_DIM


MIB = 1024 * 1024


def fits_groups(mesh):
    return mesh.shape["bucket"] == 4 and mesh.shape["blk"] == 2 * DEPTH


def around(step):
    return [(z * 2 + y, ((z + step) % DEPTH) * 2 + y) for z in range(DEPTH) for y in range(2)]


def in_order(own, other, index, axis):
    return jnp.where(
        index == 0, jnp.stack([own, other], axis), jnp.stack([other, own], axis)
    )


def one_of(value, index, axis):
    return lax.dynamic_index_in_dim(value, index, axis, False)


def dot_rows(left, right):
    return lax.dot_general(
        left, right, (((1,), (0,)), ((), ())), preferred_element_type=jnp.float32
    )


def params(limit, **extra):
    return pltpu.CompilerParams(vmem_limit_bytes=limit * MIB, **extra)


def cost(flops, moved, exps=0):
    return pl.CostEstimate(flops=flops // 64, bytes_accessed=moved // 64, transcendentals=exps // 64)


def piece_spec(width):
    return pl.BlockSpec((1, ROWS, width), lambda i: (i, 0, 0))


def whole_spec(shape):
    return pl.BlockSpec(shape, lambda i: (0,) * len(shape))


def remote_to(src, dst, send_sem, recv_sem, device):
    return pltpu.make_async_remote_copy(
        src_ref=src,
        dst_ref=dst,
        send_sem=send_sem,
        recv_sem=recv_sem,
        device_id=device,
        device_id_type=pl.DeviceIdType.MESH,
    )


def remote(src, dst, sends, recvs, index, device):
    return remote_to(src, dst, sends.at[index], recvs.at[index], device)


def select(i, first, second, third):
    return jnp.where(i == 0, first, jnp.where(i == 1, second, jnp.where(i == 2, third, 0)))


class Chain:
    def __init__(self, src, out, x, core, z, y, sems):
        up_s, down_s, arrive, core_s, core_r, local = sems
        self.z = z
        self.out = out

        def hop(k, src, slot, sends, dz):
            return pltpu.make_async_remote_copy(
                src_ref=src,
                dst_ref=out.at[slot],
                send_sem=sends.at[k],
                recv_sem=arrive.at[slot],
                device_id=(x * 2 + core, (z + dz) * 2 + y),
                device_id_type=pl.DeviceIdType.MESH,
            )

        mate = (x * 2 + 1 - core, z * 2 + y)
        self.ups = [hop(k, src if k == 0 else out.at[k], k + 1, up_s, 1) for k in range(3)]
        self.downs = [
            hop(k, src if k == 0 else out.at[DEPTH - k], 3 - k, down_s, -1) for k in range(3)
        ]
        self.cores = [
            remote(src if k == 0 else out.at[k], out.at[DEPTH + k], core_s, core_r, k, mate)
            for k in range(DEPTH)
        ]
        self.local = pltpu.make_async_copy(src, out.at[0], local)
        inner = (z > 0) & (z < DEPTH - 1)
        self.sent = [
            (z < DEPTH - 1, self.ups[0]),
            (z > 0, self.downs[0]),
            (inner, self.ups[1]),
            (inner, self.downs[1]),
            (z == DEPTH - 2, self.ups[2]),
            (z == 1, self.downs[2]),
        ]

    def start(self, *numbers):
        for number in numbers:
            condition, copy = self.sent[number]
            pl.when(condition)(copy.start)

    def near(self):
        self.cores[0].start()
        self.local.start()

    def first(self):
        self.start(0, 1)

    def second(self):
        @pl.when(self.z > 0)
        def _():
            self.ups[0].wait_recv()
            self.cores[1].start()

        self.start(2)

        @pl.when(self.z < DEPTH - 1)
        def _():
            self.downs[0].wait_recv()
            self.cores[3].start()

        self.start(3)

    def third(self):
        self.ups[1].wait_recv()
        self.cores[2].start()
        self.start(4, 5)

    def fourth(self):
        @pl.when(self.z == DEPTH - 1)
        def _():
            self.ups[2].wait_recv()
            self.cores[3].start()

        @pl.when(self.z == 0)
        def _():
            self.downs[2].wait_recv()
            self.cores[1].start()

    def end(self, arrivals=True):
        if arrivals:
            for copy in self.cores:
                copy.wait_recv()
            self.local.wait()
        for copy in self.cores:
            copy.wait_send()
        for condition, copy in self.sent:
            pl.when(condition)(copy.wait_send)


def chain_sems():
    dma = pltpu.SemaphoreType.DMA
    return [dma((3,)), dma((3,)), dma((DEPTH,)), dma((DEPTH,)), dma((DEPTH,)), dma(())]


def greet(mates):
    barrier = pltpu.get_barrier_semaphore()
    for mate in mates:
        pl.semaphore_signal(
            barrier, inc=1, device_id=mate, device_id_type=pl.DeviceIdType.MESH
        )
    pl.semaphore_wait(barrier, len(mates))


def coordinates():
    bucket, blk = lax.axis_index("bucket"), lax.axis_index("blk")
    return bucket // 2, bucket % 2, blk // 2, blk % 2


def inward_rows(ref):
    blocks, rows, columns = ref.shape
    return ref[...].reshape(blocks * rows, columns)


def outward_rows(ref):
    blocks, rows, columns = ref.shape
    return ref[:, :HEAD_DIM].reshape(blocks * HEAD_DIM, columns)


def down_rows(ref):
    blocks, rows, columns = ref.shape
    return ref[:, HEAD_DIM:].reshape(blocks * (rows - HEAD_DIM), columns)


def normalised(rows):
    inputs = rows.astype(jnp.float32)
    centred = inputs - jnp.mean(inputs, axis=-1, keepdims=True)
    variance = jnp.mean(centred * centred, axis=-1, keepdims=True)
    inverse = lax.rsqrt(variance + epsilon)
    return centred * inverse, inverse


def turned(values, cos_ref, first_ref, second_ref, sign):
    half = ROT // 2
    cos = jnp.concatenate([cos_ref[0], cos_ref[0]], 0)
    first = jnp.concatenate([first_ref[0], first_ref[0]], 0)
    second = jnp.concatenate([second_ref[0], second_ref[0]], 0)
    ahead = pltpu.roll(values, HEAD_COLS - half, 1)
    behind = pltpu.roll(values, half, 1)
    return values * cos + sign * (ahead * first + behind * second)


def forward_kernel(
    tokens_ref,
    cot_ref,
    inward_ref,
    gate_up_ref,
    outward_ref,
    down_ref,
    valid_ref,
    shares_ref,
    bias_ref,
    frequency_ref,
    pieces,
    normed_out,
    gate_out,
    up_out,
    grads_out,
    wi_out,
    wg_out,
    ro_out,
    q_out,
    kv_out,
    okv_out,
    hidden_out,
    att_out,
    own_out,
    terms_out,
    cos_out,
    first_out,
    second_out,
    gain_out,
    vec_ref,
    wi_own,
    wg_own,
    wi_ref,
    wg_ref,
    rows_ref,
    cos_ref,
    first_ref,
    second_ref,
    gain_ref,
    shift_ref,
    bias_rows,
    own_bias,
    own_grad,
    q_ref,
    kv_ref,
    okv_ref,
    hidden_ref,
    att_ref,
    own_sum,
    terms,
    core_send,
    core_recv,
    group_s,
    group_r,
    across_s,
    across_r,
    rows_s,
    rows_r,
    kv_s,
    kv_r,
    core_s,
    core_r,
    local_sems,
    out_sems,
    *chains,
):
    x, core, z, y = coordinates()
    low, wide = jnp.bfloat16, jnp.float32

    def device(xx, cc, zz, yy):
        return (xx * 2 + cc, zz * 2 + yy)

    def at(xx, cc, zz, yy):
        return ((xx * 2 + cc) * DEPTH + zz) * 2 + yy

    x_mate, y_mate = device(1 - x, core, z, y), device(x, core, z, 1 - y)
    core_mate = device(x, 1 - core, z, y)
    members = [(flip, turn) for turn in (0, 1, 3, 2) for flip in (0, 1)]

    def target(flip, turn):
        return (core + flip) % 2, (z + turn) % DEPTH

    def source(flip, turn):
        return (core + flip) % 2, (z + DEPTH - turn) % DEPTH

    started = []
    written = []

    def begin(copy):
        copy.start()
        started.append(copy)
        return copy

    def write_out(*pairs):
        for src, dst in pairs:
            copy = pltpu.make_async_copy(src, dst, out_sems.at[len(written)])
            copy.start()
            written.append(copy)

    def group_copies(which, own, full):
        mine = at(x, core, z, y)
        copies = {}
        for flip, turn in members[1:]:
            cc, zz = target(flip, turn)
            copies[flip, turn] = remote(
                own.at[cc * DEPTH + zz],
                full.at[mine],
                group_s,
                group_r,
                (which, flip * DEPTH + turn),
                device(x, cc, zz, y),
            )
        return copies

    def vector_copies():
        mine = vec_ref.at[at(x, core, z, y)]
        copies = {}
        for flip, turn in members[1:]:
            copies[flip, turn] = remote(
                mine,
                mine,
                group_s,
                group_r,
                (2, flip * DEPTH + turn),
                device(x, *target(flip, turn), y),
            )
        return copies

    def rows_copies():
        mine = rows_ref.at[x * 2 + y]
        return [
            remote(mine, mine, rows_s, rows_r, way, mate) for way, mate in enumerate((x_mate, y_mate))
        ]

    tokens = Chain(tokens_ref, pieces, x, core, z, y, chains[:6])
    grads = Chain(own_grad, grads_out, x, core, z, y, chains[6:])
    position = lax.broadcasted_iota(jnp.int32, (ROWS // 2, HEAD_COLS), 0)
    lane = lax.broadcasted_iota(jnp.int32, (ROWS // 2, HEAD_COLS), 1) % HEAD_DIM
    half = ROT // 2

    share_lane = lax.broadcasted_iota(jnp.int32, shares_ref.shape, 1)
    share_row = lax.broadcasted_iota(jnp.int32, shares_ref.shape, 0)
    own_shares = jnp.where((share_lane // HEAD_DIM == y) | (share_row >= 2), shares_ref[...], 0.0)

    def prepare(inward_f32, gate_up_f32, outward_f32, down_f32):
        loads = [
            pltpu.make_async_copy(src, dst, local_sems.at[n])
            for n, (src, dst) in enumerate(
                (
                    (inward_ref, inward_f32),
                    (gate_up_ref, gate_up_f32),
                    (outward_ref, outward_f32),
                    (down_ref, down_f32),
                )
            )
        ]
        for load in loads:
            load.start()
        greet([device(x, *target(*m), y) for m in members[1:]] + [x_mate, y_mate])
        tokens.near()
        loads[0].wait()
        vec_ref[at(x, core, z, y)] = own_shares
        for copy in vector_copies().values():
            copy.start()
        pair = 2 * HEAD_DIM
        for n in range(PIECES):
            starts = [part * PIECES * pair + n * pair for part in range(6)]
            line = jnp.concatenate([inward_f32[:, c : c + pair] for c in starts], 1)
            wi_own[n] = line.astype(low)
        wi_ref[at(x, core, z, y)] = wi_own[core * DEPTH + z]
        for copy in group_copies(0, wi_own, wi_ref).values():
            copy.start()
        loads[1].wait()
        each = gate_up_f32.shape[1] // (4 * PIECES)
        for n in range(PIECES):
            starts = [part * PIECES * each + n * each for part in range(4)]
            line = jnp.concatenate([gate_up_f32[:, c : c + each] for c in starts], 1)
            wg_own[n] = line.astype(low)
        wg_ref[at(x, core, z, y)] = wg_own[core * DEPTH + z]
        loads[2].wait()
        loads[3].wait()
        rows_ref[x * 2 + y, :HEAD_DIM] = outward_f32[...].astype(low)
        rows_ref[x * 2 + y, HEAD_DIM:] = down_f32[...].astype(low)

    pl.run_scoped(
        prepare,
        *[
            pltpu.VMEM(r.shape, r.dtype)
            for r in (inward_ref, gate_up_ref, outward_ref, down_ref)
        ],
    )
    inward = group_copies(0, wi_own, wi_ref)
    gate_up = group_copies(1, wg_own, wg_ref)
    vectors = vector_copies()
    started += [*inward.values(), *gate_up.values(), *vectors.values()]

    def spread(which, full, copies, halfway=None):
        pairs = {}
        for member in members:
            if halfway is not None and member == members[HALFWAY]:
                halfway()
            flip, turn = member
            cc, zz = source(flip, turn)
            if member != (0, 0):
                copies[member].wait_recv()
            block = full.at[at(x, cc, zz, y)]
            number = flip * DEPTH + turn
            pairs[member] = tuple(
                begin(remote(block, block, across_s, across_r, (which, way, number), mate))
                for way, mate in enumerate((x_mate, y_mate))
            )
        return pairs

    def by_x(which, flip):
        return which != 1 or flip == 0

    def corner(which, full, pairs):
        copies = []
        for member in members:
            flip, turn = member
            cc, zz = source(flip, turn)
            number = flip * DEPTH + turn
            if by_x(which, flip):
                pairs[member][1].wait_recv()
                block, mate = full.at[at(x, cc, zz, 1 - y)], x_mate
            else:
                pairs[member][0].wait_recv()
                block, mate = full.at[at(1 - x, cc, zz, y)], y_mate
            copies.append(
                begin(remote(block, block, across_s, across_r, (which, 2, number), mate))
            )
        return copies

    def complete(which, pairs, copies):
        for flip, turn in members:
            pairs[flip, turn][0 if by_x(which, flip) else 1].wait_recv()
        for copy in copies:
            copy.wait_recv()

    frequency = frequency_ref[...]
    for k in range(DEPTH):
        first = (2 * lax.rem(z + DEPTH - k, DEPTH) + y) * (ROWS // 2)
        angles = (first + position).astype(wide) * frequency
        sine = jnp.sin(angles)
        cos_ref[k] = jnp.cos(angles)
        first_ref[k] = jnp.where(lane < half, -sine, 0.0)
        second_ref[k] = jnp.where((lane >= half) & (lane < ROT), sine, 0.0)
    own_grad[...] = (cot_ref[...].astype(wide) * valid_ref[...]).astype(low)
    write_out((cos_ref, cos_out), (first_ref, first_out), (second_ref, second_out))

    vector_pairs = spread(2, vec_ref, vectors)
    inward_pairs = spread(0, wi_ref, inward)
    for copy in gate_up.values():
        copy.start()
    vector_corner = corner(2, vec_ref, vector_pairs)
    inward_corner = corner(0, wi_ref, inward_pairs)
    gate_up_pairs = spread(1, wg_ref, gate_up, tokens.first)
    complete(2, vector_pairs, vector_corner)
    complete(0, inward_pairs, inward_corner)
    write_out((wi_ref, wi_out))

    shares = vec_ref[...].astype(low).astype(wide)
    for row, vector in ((0, gain_ref), (1, shift_ref)):
        line = shares[:, row]
        vector[...] = jnp.concatenate(
            [line[2 * i : 2 * i + 1] + line[2 * i + 1 : 2 * i + 2] for i in range(16)], 1
        )
    each = bias_ref.shape[1]
    biases = jnp.concatenate([shares[:, 2], shares[:, 3]], 1)
    flat = jnp.concatenate([biases[i : i + 1, :each] for i in range(32)], 1)
    for i in range(flat.shape[1] // 128):
        bias_rows[i : i + 1] = flat[:, i * 128 : (i + 1) * 128]
    query_bias, key_bias, value_bias = [], [], []
    gap = jnp.zeros((1, HEAD_DIM - ROT), wide)
    for i in range(2):
        row = i * PIECES + core * DEPTH + z
        query_bias.append(bias_rows[pl.ds(row, 1)])
        value_bias.append(bias_rows[pl.ds(2 * PIECES + row, 1)])
        line = bias_rows[pl.ds(4 * PIECES + i * 2 + core, 1)]
        heads = [line[:, 2 * ROT * j : 2 * ROT * (j + 1)] for j in range(DEPTH)]
        chosen = jnp.where(
            z == 0, heads[0], jnp.where(z == 1, heads[1], jnp.where(z == 2, heads[2], heads[3]))
        )
        key_bias += [chosen[:, :ROT], gap, chosen[:, ROT:], gap]
    own_bias[...] = jnp.concatenate(query_bias + key_bias + value_bias, 1)
    write_out((gain_ref, gain_out))

    def pair_copy(piece):
        return remote(kv_ref.at[piece], okv_ref.at[piece], kv_s, kv_r, piece, y_mate)

    def project(piece, tokens_part, normed):
        k = lax.rem(piece, DEPTH)
        hat, _ = normalised(tokens_part[0])
        narrow = (hat * gain_ref[...] + shift_ref[...]).astype(low)
        normed[0] = narrow
        projected = dot_rows(narrow, inward_rows(wi_ref)) + own_bias[...]
        tables = (cos_ref.at[pl.ds(k, 1)], first_ref.at[pl.ds(k, 1)], second_ref.at[pl.ds(k, 1)])
        query = turned(projected[:, :HEAD_COLS], *tables, 1.0) * (HEAD_DIM**-0.5)
        key = turned(projected[:, HEAD_COLS : 2 * HEAD_COLS], *tables, 1.0)
        kv_ref[piece] = jnp.concatenate([key, projected[:, 2 * HEAD_COLS :]], 1).astype(low)
        pair_copy(piece).start()
        q_ref[piece] = query.astype(low)

    def piece_at(first, i):
        turn = first + i // 2
        near = jnp.where(z == 0, DEPTH - 1, 1)
        k = jnp.where(
            turn == 0, 0, jnp.where(turn == 1, near, jnp.where(turn == 2, 2, DEPTH - near))
        )
        return k + DEPTH * (i % 2)

    def project_pieces(first, count):
        spec = pl.BlockSpec((1,) + pieces.shape[1:], lambda i: (piece_at(first, i), 0, 0))
        pltpu.emit_pipeline(
            lambda *refs: project(piece_at(first, pl.program_id(0)), *refs),
            grid=(2 * count,),
            in_specs=[spec],
            out_specs=[spec],
        )(pieces, normed_out)

    def feed(first, count):
        def body(normed, gate_part, up_part):
            piece = piece_at(first, pl.program_id(0))
            both = dot_rows(normed[0], wg_ref[...].reshape(normed.shape[2], wg_ref.shape[2]))
            hidden = both.shape[1] // 2
            gate, up = both[:, :hidden], both[:, hidden:]
            gate_part[0] = gate
            up_part[0] = up
            hidden_ref[piece] = (gate * jax.nn.sigmoid(gate) * up).astype(low)

        def spec(array):
            return pl.BlockSpec(
                (1,) + array.shape[1:], lambda i: (piece_at(first, i), 0, 0)
            )

        pltpu.emit_pipeline(
            body,
            grid=(2 * count,),
            in_specs=[spec(normed_out)],
            out_specs=[spec(gate_out), spec(up_out)],
        )(normed_out, gate_out, up_out)

    near = jnp.where(z == 0, DEPTH - 1, 1)
    far = DEPTH - near

    def core_arrived(k):
        remote(pieces.at[k], pieces.at[DEPTH + k], chains[3], chains[4], k, core_mate).wait_recv()

    tokens.local.wait()
    core_arrived(0)
    project_pieces(0, 1)
    tokens.second()
    core_arrived(near)
    project_pieces(1, 1)
    gate_up_corner = corner(1, wg_ref, gate_up_pairs)
    rows_x, rows_y = rows_copies()
    begin(rows_x)
    begin(rows_y)
    tokens.third()
    core_arrived(2)
    project_pieces(2, 1)
    complete(1, gate_up_pairs, gate_up_corner)
    feed(0, 2)
    tokens.fourth()
    grads.near()
    grads.first()
    core_arrived(far)
    project_pieces(3, 1)
    rows_y.wait_recv()
    block = rows_ref.at[x * 2 + 1 - y]
    rows_corner = begin(remote(block, block, rows_s, rows_r, 2, x_mate))
    feed(2, 2)
    grads.second()
    write_out((q_ref, q_out), (kv_ref, kv_out), (wg_ref, wg_out))

    for b in range(2):
        for j in range(DEPTH):
            pair_copy(b * DEPTH + j).wait_recv()

        def attend(t, carry):
            attend_one(Heads(b, t, z, y, q_ref, kv_ref, okv_ref), att_ref)
            return carry

        lax.fori_loop(0, 2 * LOCAL_HEADS // 2, attend, 0)
        if b == 0:
            grads.third()

    rows_x.wait_recv()
    rows_corner.wait_recv()
    write_out((hidden_ref, hidden_out), (att_ref, att_out), (okv_ref, okv_out), (rows_ref, ro_out))

    def core_copy(k):
        return remote(core_send.at[k % 2], core_recv.at[k], core_s, core_r, k, core_mate)

    def term(piece):
        return dot_rows(att_ref[piece], outward_rows(rows_ref)) + dot_rows(
            hidden_ref[piece], down_rows(rows_ref)
        )

    def branch(i, carry):
        k = DEPTH - 1 - i

        @pl.when(i >= 2)
        def _():
            core_copy(k + 2).wait_send()

        core_send[k % 2] = term(DEPTH + k).astype(low)
        core_copy(k).start()
        own = term(k)
        core_copy(k).wait_recv()
        both = own + core_recv[k].astype(wide)

        @pl.when(k > 0)
        def _():
            terms[k - 1] = both.astype(low)

        @pl.when(k == 0)
        def _():
            own_sum[...] = both

        return carry

    lax.fori_loop(0, DEPTH, branch, 0)
    write_out((own_sum, own_out), (terms, terms_out))
    grads.fourth()
    grads.end()
    tokens.end(False)
    for k in range(2):
        core_copy(k).wait_send()
    for piece in range(PIECES):
        pair_copy(piece).wait_send()
    for copy in started:
        copy.wait_send()
    for copy in written:
        copy.wait()


def forward(
    tokens, cot, inward, gate_up, outward, down, valid, shares, bias, frequency
):
    low, wide = jnp.bfloat16, jnp.float32
    rows, width = tokens.shape
    own_rows = inward.shape[0]
    group_columns = gate_up.shape[1] // PIECES
    hidden = group_columns // 2
    anywhere = pl.BlockSpec(memory_space=pl.ANY)
    inside = pl.BlockSpec(memory_space=pltpu.VMEM)
    shape = jax.ShapeDtypeStruct
    dma = pltpu.SemaphoreType.DMA
    wi_shape = shape((32, own_rows, 3 * HEAD_COLS), low)
    wg_shape = shape((32, own_rows, group_columns), low)
    ro_shape = shape((4, outward.shape[0] + down.shape[0], width), low)
    table = shape((DEPTH, ROWS // 2, HEAD_COLS), wide)
    heads = shape((PIECES, ROWS, HEAD_COLS), low)
    pairs = shape((PIECES, ROWS, 2 * HEAD_COLS), low)
    hidden_shape = shape((PIECES, ROWS, hidden), low)
    own_shape = shape((ROWS, width), wide)
    terms_shape = shape((DEPTH - 1, ROWS, width), low)
    vector = shape((1, width), wide)

    def scratch(*shapes):
        return [pltpu.VMEM(s.shape, s.dtype) for s in shapes]

    return pl.pallas_call(
        forward_kernel,
        in_specs=[anywhere] + [inside] + [anywhere] * 4 + [inside] * 4,
        out_specs=[anywhere] * 19,
        out_shape=[
            shape((PIECES, ROWS, width), low),
            shape((PIECES, ROWS, width), low),
            shape((PIECES, ROWS, hidden), wide),
            shape((PIECES, ROWS, hidden), wide),
            shape((PIECES, ROWS, width), low),
            wi_shape,
            wg_shape,
            ro_shape,
            heads,
            pairs,
            pairs,
            hidden_shape,
            heads,
            own_shape,
            terms_shape,
            table,
            table,
            table,
            vector,
        ],
        scratch_shapes=scratch(
            shape((32, 8, 128), wide),
            shape((PIECES,) + wi_shape.shape[1:], low),
            shape((PIECES,) + wg_shape.shape[1:], low),
            wi_shape,
            wg_shape,
            ro_shape,
            table,
            table,
            table,
            vector,
            vector,
            shape((40, 128), wide),
            shape((1, 3 * HEAD_COLS), wide),
            shape((ROWS, width), low),
            heads,
            pairs,
            pairs,
            hidden_shape,
            heads,
            own_shape,
            terms_shape,
            shape((2, ROWS, width), low),
            shape((DEPTH, ROWS, width), low),
        )
        + [
            dma((3, PIECES)),
            dma((3, PIECES)),
            dma((3, 3, PIECES)),
            dma((3, 3, PIECES)),
            dma((4,)),
            dma((4,)),
            dma((PIECES,)),
            dma((PIECES,)),
            dma((DEPTH,)),
            dma((DEPTH,)),
            dma((4,)),
            dma((14,)),
        ]
        + chain_sems()
        + chain_sems(),
        compiler_params=params(62, collective_id=0, has_side_effects=True),
        cost_estimate=cost(0, 64 * MIB),
        name="forward",
    )(tokens, cot, inward, gate_up, outward, down, valid, shares, bias, frequency)


def pair_rows(block):
    lane = lax.broadcasted_iota(jnp.int32, block.shape, 1)
    zero = jnp.zeros_like(block)
    return jnp.concatenate(
        [jnp.where(lane < HEAD_DIM, block, zero), jnp.where(lane < HEAD_DIM, zero, block)], 0
    )


def pair_lanes(rows):
    half = rows.shape[0] // 2
    lane = lax.broadcasted_iota(jnp.int32, (half, rows.shape[1]), 1)
    return jnp.where(lane < HEAD_DIM, rows[:half], rows[half:])


def block_probs(queries, keys, last, y):
    scores = transposed_times(queries, keys)
    rows, columns = scores.shape
    size = rows // 2
    row = lax.broadcasted_iota(jnp.int32, (rows, 2 * size), 0) % size
    column = lax.broadcasted_iota(jnp.int32, (rows, 2 * size), 1)
    allowed = (column <= row) | ((column >= size) & (y == 1))
    tail = jnp.where(allowed, scores[:, last * 2 * size :], masked_score)
    scores = tail if last == 0 else jnp.concatenate([scores[:, : last * 2 * size], tail], 1)
    weights = jnp.exp(scores - jnp.max(scores, axis=-1, keepdims=True))
    return weights * (1.0 / jnp.sum(weights, axis=-1, keepdims=True))


class Heads:
    def __init__(self, b, t, z, y, q_ref, kv_ref, okv_ref):
        size = ROWS // 2
        pair = 2 * HEAD_DIM
        self.b, self.z, self.y = b, z, y
        self.rows = pl.ds(pl.multiple_of((t // 2) * size, size), size)
        self.lanes = pl.ds(pl.multiple_of((t % 2) * pair, pair), pair)
        value_lanes = pl.ds(pl.multiple_of(HEAD_COLS + (t % 2) * pair, pair), pair)
        self.q_ref = q_ref

        def both(lanes):
            blocks = []
            for j in range(DEPTH):
                place = (self.piece(j), self.rows, lanes)
                blocks += [kv_ref[place], okv_ref[place]]
            return jnp.concatenate(blocks, 0)

        self.keys, self.values = both(self.lanes), both(value_lanes)

    def piece(self, j):
        return self.b * DEPTH + lax.rem(self.z + DEPTH - j, DEPTH)

    def place(self, j):
        return self.piece(j), self.rows, self.lanes

    def queries(self, j):
        return pair_rows(self.q_ref[self.place(j)])


def attend_one(heads, out_ref):
    for j in range(DEPTH):
        count = (j + 1) * ROWS
        probs = block_probs(heads.queries(j), heads.keys[:count], j, heads.y)
        out = dot_rows(probs.astype(jnp.bfloat16), heads.values[:count])
        out_ref[heads.place(j)] = pair_lanes(out).astype(jnp.bfloat16)


def attend_back_one(heads, grad_ref, dq_ref, dk_ref, dv_ref, odk_ref, odv_ref, key_sum, value_sum):
    half = ROWS // 2
    for j in reversed(range(DEPTH)):
        count = (j + 1) * ROWS
        queries = heads.queries(j)
        grads = pair_rows(grad_ref[heads.place(j)])
        keys, values = heads.keys[:count], heads.values[:count]
        probs = block_probs(queries, keys, j, heads.y)
        low = probs.astype(jnp.bfloat16)
        prob_grad = transposed_times(grads, values)
        delta = jnp.sum(low.astype(jnp.float32) * prob_grad, axis=-1, keepdims=True)
        score_grad = (probs * (prob_grad - delta)).astype(jnp.bfloat16)
        dq_ref[heads.place(j)] = pair_lanes(dot_rows(score_grad, keys))
        key_term = times_transposed(score_grad, queries)
        value_term = times_transposed(low, grads)
        if j == DEPTH - 1:
            key_sum[...] = key_term
            value_sum[...] = value_term
        else:
            key_sum[:count] += key_term
            value_sum[:count] += value_term
    for j in range(DEPTH):
        low = j * ROWS
        place = heads.place(j)
        dk_ref[place] = key_sum[low : low + half]
        dv_ref[place] = value_sum[low : low + half]
        odk_ref[place] = key_sum[low + half : low + ROWS].astype(jnp.bfloat16)
        odv_ref[place] = value_sum[low + half : low + ROWS].astype(jnp.bfloat16)


def backward_kernel(
    grads_ref,
    gate_ref,
    up_ref,
    normed_ref,
    pieces_ref,
    q_ref,
    kv_ref,
    okv_ref,
    hidden_ref,
    att_ref,
    rows_ref,
    own_sum,
    terms,
    valid_ref,
    gate_xs,
    gate_xk,
    gate_ys,
    gate_yk,
    gate_xr,
    gate_yr,
    gate_y2s,
    gate_x2s,
    gate_own_x,
    gate_own_y,
    heads_out,
    hidden_out,
    gu_ref,
    dq_ref,
    dk_ref,
    dv_ref,
    got_dk,
    got_dv,
    layer_out,
    attended_grad,
    odk_ref,
    odv_ref,
    key_sum,
    value_sum,
    z_recv,
    token_rows,
    z_s,
    z_r,
    pair_s,
    pair_r,
    stage_s,
    stage_r,
    local_sem,
):
    x, core, z, y = coordinates()
    low, wide = jnp.bfloat16, jnp.float32
    y_mate = (x * 2 + core, z * 2 + 1 - y)

    def z_mate(turn):
        return (x * 2 + core, lax.rem(z + turn, DEPTH) * 2 + y)

    x_mate = (2 - x * 2 + core, z * 2 + y)
    greet([x_mate, y_mate] + [z_mate(turn) for turn in range(1, DEPTH)])
    scattered = [
        remote(terms.at[k - 1], z_recv.at[k - 1], z_s, z_r, k - 1, z_mate(DEPTH - k))
        for k in range(1, DEPTH)
    ]
    for copy in scattered:
        copy.start()
    own_tokens = pltpu.make_async_copy(pieces_ref.at[0], token_rows, local_sem)
    own_tokens.start()

    def piece_body(grad_part, gate_part, up_part):
        piece = pl.program_id(0)
        grad = grad_part[0]
        attended_grad[piece] = transposed_times(grad, outward_rows(rows_ref)).astype(low)
        hidden_grad = transposed_times(grad, down_rows(rows_ref))
        gate = gate_part[0]
        sig = jax.nn.sigmoid(gate)
        silu = gate * sig
        gate_grad = hidden_grad * up_part[0] * (sig + silu * (1.0 - sig))
        up_grad = hidden_grad * silu
        gu_ref[piece] = jnp.concatenate([gate_grad, up_grad], 1).astype(low)

    pltpu.emit_pipeline(
        piece_body,
        grid=(PIECES,),
        in_specs=[piece_spec(r.shape[-1]) for r in (grads_ref, gate_ref, up_ref)],
    )(grads_ref, gate_ref, up_ref)

    def pair_copies(b, t):
        size, pair = ROWS // 2, 2 * HEAD_DIM
        at = (
            pl.ds(b * DEPTH, DEPTH),
            pl.ds(pl.multiple_of((t // 2) * size, size), size),
            pl.ds(pl.multiple_of((t % 2) * pair, pair), pair),
        )
        number = b * DEPTH + t
        return (
            remote(odk_ref.at[at], got_dk.at[at], pair_s, pair_r, (0, number), y_mate),
            remote(odv_ref.at[at], got_dv.at[at], pair_s, pair_r, (1, number), y_mate),
        )

    def attend_back(i, carry):
        b, t = i // DEPTH, i % DEPTH
        heads = Heads(b, t, z, y, q_ref, kv_ref, okv_ref)
        attend_back_one(
            heads, attended_grad, dq_ref, dk_ref, dv_ref, odk_ref, odv_ref, key_sum, value_sum
        )
        for copy in pair_copies(b, t):
            copy.start()
        return carry

    lax.fori_loop(0, PIECES, attend_back, 0)

    total, width = normed_ref.shape
    size = width // PIECES
    columns = gu_ref.shape[-1]
    cut = gate_xs.shape[-1]

    def right(first, last):
        return gu_ref[...].reshape(total, columns)[:, first:last]

    def whole_body(left, out):
        term = times_transposed(left[...], right(0, cut)).astype(out.dtype)
        out[...] = term.reshape(out.shape)

    def split_body(left, keep, send):
        split_rows(times_transposed(left[...], right(cut, columns)), y, keep, send)

    def from_block(base):
        return pl.BlockSpec((total, size), lambda i: (0, base + i))

    def block_of(array):
        return pl.BlockSpec((2,) + array.shape[1:], lambda i: (i,) + (0,) * (len(array.shape) - 1))

    pltpu.emit_pipeline(
        whole_body,
        grid=(DEPTH,),
        in_specs=[from_block((1 - x) * DEPTH)],
        out_specs=[block_of(gate_xs)],
    )(normed_ref, gate_xs)
    gate_x = remote(gate_xs, gate_xr, stage_s, stage_r, 0, x_mate)
    gate_x.start()
    pltpu.emit_pipeline(
        split_body,
        grid=(PIECES,),
        in_specs=[from_block(0)],
        out_specs=[block_of(gate_yk), block_of(gate_ys)],
    )(normed_ref, gate_yk, gate_ys)
    gate_y = remote(gate_ys, gate_yr, stage_s, stage_r, 1, y_mate)
    gate_y.start()

    flat_grads = grads_ref.reshape(total, width)
    wide_size = 2 * size

    def rows_body(right, heads, hidden):
        grad = right[...]
        attended = att_ref[...].reshape(total, HEAD_COLS)
        term = times_transposed(attended, grad).astype(low)
        heads[...] = term.reshape(heads.shape)
        hidden_rows = hidden_ref[...].reshape(total, hidden_ref.shape[-1])
        term = times_transposed(hidden_rows, grad).astype(low)
        hidden[...] = term.reshape(hidden.shape)

    def column_block(array):
        return pl.BlockSpec(array.shape[:2] + (wide_size,), lambda i: (0, 0, i))

    pltpu.emit_pipeline(
        rows_body,
        grid=(width // wide_size,),
        in_specs=[pl.BlockSpec((total, wide_size), lambda i: (0, i))],
        out_specs=[column_block(heads_out), column_block(hidden_out)],
    )(flat_grads, heads_out, hidden_out)

    pltpu.emit_pipeline(
        whole_body,
        grid=(DEPTH,),
        in_specs=[from_block(x * DEPTH)],
        out_specs=[block_of(gate_xk)],
    )(normed_ref, gate_xk)

    def sums_body(xk, xr, yk, yr, yk_own, yr_own, y2s, x2s, own_x, own_y):
        y2s[0] = (xk[0, 1 - y] + xr[0, 1 - y].astype(wide)).astype(low)
        own_x[0] = xk[0, y] + xr[0, y].astype(wide)
        x2s[0] = (yk[0] + yr[0].astype(wide)).astype(low)
        own_y[0] = yk_own[0] + yr_own[0].astype(wide)

    def one_block(array, base=0):
        return pl.BlockSpec(
            (1,) + array.shape[1:], lambda i: (base + i,) + (0,) * (len(array.shape) - 1)
        )

    gate_x.wait_recv()
    gate_y.wait_recv()
    theirs, ours = (1 - x) * PIECES, x * PIECES
    pltpu.emit_pipeline(
        sums_body,
        grid=(PIECES,),
        in_specs=[
            one_block(gate_xk),
            one_block(gate_xr),
            one_block(gate_yk, theirs),
            one_block(gate_yr, theirs),
            one_block(gate_yk, ours),
            one_block(gate_yr, ours),
        ],
        out_specs=[one_block(r) for r in (gate_y2s, gate_x2s, gate_own_x, gate_own_y)],
    )(
        gate_xk,
        gate_xr,
        gate_yk,
        gate_yr,
        gate_yk,
        gate_yr,
        gate_y2s,
        gate_x2s,
        gate_own_x,
        gate_own_y,
    )
    own_tokens.wait()
    for copy in scattered:
        copy.wait_recv()
    for first in range(0, ROWS, 64):
        rows = pl.ds(first, 64)
        branch = own_sum[rows]
        for k in range(DEPTH - 1):
            branch = branch + z_recv[k, rows].astype(wide)
        layer_out[rows] = (token_rows[rows].astype(wide) + valid_ref[rows] * branch).astype(low)

    for b in range(2):
        for t in range(DEPTH):
            for copy in pair_copies(b, t):
                copy.wait_recv()
                copy.wait_send()
    for copy in scattered:
        copy.wait_send()
    for copy in (gate_x, gate_y):
        copy.wait_send()


def backward(
    grads, gate, up, normed, pieces, queries, pairs, other_pairs, hidden, attended, rows_out,
    own_sum, terms, valid
):
    low, wide = jnp.bfloat16, jnp.float32
    width = pieces.shape[-1]
    each = hidden.shape[-1]
    columns = 2 * each
    cut = -(-columns // 256) * 128
    rows = width // 32
    head_rows = HEAD_DIM
    anywhere = pl.BlockSpec(memory_space=pl.ANY)
    inside = pl.BlockSpec(memory_space=pltpu.VMEM)
    shape = jax.ShapeDtypeStruct
    dma = pltpu.SemaphoreType.DMA
    return pl.pallas_call(
        backward_kernel,
        in_specs=[anywhere] * 5 + [inside] * 9,
        out_specs=[anywhere] * 12 + [inside] * 7,
        out_shape=[
            shape((PIECES, 2, rows, cut), low),
            shape((PIECES, 2, rows, cut), wide),
            shape((2 * PIECES, rows, columns - cut), low),
            shape((2 * PIECES, rows, columns - cut), wide),
            shape((PIECES, 2, rows, cut), low),
            shape((2 * PIECES, rows, columns - cut), low),
            shape((PIECES, rows, cut), low),
            shape((PIECES, rows, columns - cut), low),
            shape((PIECES, rows, cut), wide),
            shape((PIECES, rows, columns - cut), wide),
            shape((4, head_rows, width), low),
            shape((4, each // 4, width), low),
            shape((PIECES, ROWS, columns), low),
            shape((PIECES, ROWS, HEAD_COLS), wide),
            shape((PIECES, ROWS, HEAD_COLS), wide),
            shape((PIECES, ROWS, HEAD_COLS), wide),
            shape((PIECES, ROWS, HEAD_COLS), low),
            shape((PIECES, ROWS, HEAD_COLS), low),
            shape((ROWS, width), low),
        ],
        scratch_shapes=[
            pltpu.VMEM((PIECES, ROWS, HEAD_COLS), low),
            pltpu.VMEM((PIECES, ROWS, HEAD_COLS), low),
            pltpu.VMEM((PIECES, ROWS, HEAD_COLS), low),
            pltpu.VMEM((DEPTH * ROWS, 2 * HEAD_DIM), wide),
            pltpu.VMEM((DEPTH * ROWS, 2 * HEAD_DIM), wide),
            pltpu.VMEM((DEPTH - 1, ROWS, width), low),
            pltpu.VMEM((ROWS, width), low),
            dma((DEPTH - 1,)),
            dma((DEPTH - 1,)),
            dma((2, PIECES)),
            dma((2, PIECES)),
            dma((2,)),
            dma((2,)),
            dma(()),
        ],
        compiler_params=params(62, collective_id=3, has_side_effects=True),
        cost_estimate=cost(0, 64 * MIB),
        name="backward",
    )(
        grads, gate, up, normed, pieces, queries, pairs, other_pairs, hidden, attended, rows_out,
        own_sum, terms, valid
    )


def finish_kernel(
    dq_ref,
    dk_ref,
    dv_ref,
    odk_ref,
    odv_ref,
    gu_ref,
    pieces_ref,
    cos_ref,
    first_ref,
    second_ref,
    normed_ref,
    gate_y2s,
    gate_x2s,
    gate_sum_x,
    gate_sum_y,
    heads_term,
    hidden_term,
    wi_ref,
    wg_ref,
    gain_ref,
    cot_ref,
    tokens_out,
    heads_out,
    hidden_out,
    gate_rows,
    inward_rows_out,
    vec_out,
    heads_r,
    heads_2s,
    heads_2r,
    hidden_r,
    hidden_2s,
    hidden_2r,
    core_send,
    core_recv,
    z_send,
    below,
    above,
    own_sum,
    pg_ref,
    token_rows,
    vec_sum,
    vec_x,
    vec_y,
    gate_own_x,
    gate_own_y,
    gate_y2r,
    gate_x2r,
    gate_fin,
    inward_xs,
    inward_xr,
    inward_xk,
    inward_ys,
    inward_yr,
    inward_yk,
    inward_y2s,
    inward_y2r,
    inward_x2s,
    inward_x2r,
    inward_fin,
    core_s,
    core_r,
    up_s,
    down_s,
    below_r,
    above_r,
    stage_s,
    stage_r,
    rows_s,
    rows_r,
    vec_s,
    vec_r,
    local_sems,
):
    x, core, z, y = coordinates()
    low = jnp.bfloat16
    wide = jnp.float32

    def device(xx, cc, zz, yy):
        return (xx * 2 + cc, zz * 2 + yy)

    x_mate, y_mate = device(1 - x, core, z, y), device(x, core, z, 1 - y)
    core_mate = device(x, 1 - core, z, y)
    members = [(flip, turn) for turn in (2, 1, 3, 0) for flip in (1, 0)][:-1]

    def target(flip, turn):
        return (core + flip) % 2, (z + turn) % DEPTH

    greet([device(x, *target(*m), y) for m in members] + [x_mate, y_mate])

    started = []

    def begin(copy):
        copy.start()
        started.append(copy)
        return copy

    loads = [
        pltpu.make_async_copy(gate_sum_x, gate_own_x, local_sems.at[2]),
        pltpu.make_async_copy(gate_sum_y, gate_own_y, local_sems.at[3]),
    ]
    for load in loads:
        load.start()
    gate_y = begin(remote(gate_y2s, gate_y2r, stage_s, stage_r, (0, 2), y_mate))
    gate_x = begin(remote(gate_x2s, gate_x2r, stage_s, stage_r, (0, 3), x_mate))
    heads_x = begin(remote(heads_term.at[1 - x], heads_r, stage_s, stage_r, (2, 0), x_mate))
    hidden_y = [
        remote(hidden_term.at[i, 1 - y], hidden_r.at[i], stage_s, stage_r, (3, i), y_mate)
        for i in range(2)
    ]
    own_tokens = pltpu.make_async_copy(pieces_ref.at[0], token_rows, local_sems.at[4])
    own_tokens.start()

    vec_sum[...] = jnp.zeros_like(vec_sum)

    def core_copy(k):
        return remote(core_send.at[k % 2], core_recv.at[k], core_s, core_r, k, core_mate)

    def up_copy(slot, number):
        goal = device(x, core, z + 1, y)
        return remote_to(
            z_send.at[slot], below.at[number], up_s.at[slot], below_r.at[number], goal
        )

    def down_copy(slot, number):
        goal = device(x, core, z - 1, y)
        return remote_to(
            z_send.at[slot], above.at[number], down_s.at[slot], above_r.at[number], goal
        )

    def order(i):
        inner = jnp.where(z == 1, select(i, 2, 1, 3), select(i, 2, 3, 1))
        outer = jnp.where(z == 0, select(i, 1, 2, 3), select(i, 3, 2, 1))
        return jnp.where((z == 0) | (z == DEPTH - 1), outer, inner)

    def piece_of(i):
        return order(i // 2) + DEPTH * (1 - i % 2)

    def arrived(box, recvs, number):
        copy = remote_to(box.at[number], box.at[number], up_s.at[0], recvs.at[number], core_mate)
        copy.wait_recv()

    def add_and(slot, box, recvs, number, copy):
        arrived(box, recvs, number)
        z_send[slot] = (z_send[slot].astype(wide) + box[number].astype(wide)).astype(low)
        copy.start()

    def first_hop():
        @pl.when(z == 1)
        def _():
            add_and(0, below, below_r, 0, up_copy(0, 0))

        @pl.when(z == DEPTH - 2)
        def _():
            add_and(0, above, above_r, 0, down_copy(0, 0))

    def second_hop():
        @pl.when(z == 1)
        def _():
            add_and(2, below, below_r, 1, up_copy(2, 1))

        @pl.when(z == DEPTH - 2)
        def _():
            add_and(2, above, above_r, 1, down_copy(2, 1))

    def third_hop():
        @pl.when(z == 1)
        def _():
            add_and(1, above, above_r, 0, down_copy(1, 0))

        @pl.when(z == DEPTH - 2)
        def _():
            add_and(1, below, below_r, 0, up_copy(1, 0))

    def last_hop():
        @pl.when(z == 0)
        def _():
            arrived(above, above_r, 0)
            own_sum[...] += above[0].astype(wide)

        @pl.when(z == 1)
        def _():
            arrived(below, below_r, 2)
            arrived(above, above_r, 1)
            own_sum[...] += below[2].astype(wide) + above[1].astype(wide)

        @pl.when(z == DEPTH - 2)
        def _():
            arrived(below, below_r, 1)
            arrived(above, above_r, 2)
            own_sum[...] += below[1].astype(wide) + above[2].astype(wide)

        @pl.when(z == DEPTH - 1)
        def _():
            arrived(below, below_r, 0)
            own_sum[...] += below[0].astype(wide)

    def sent_all():
        @pl.when(z == 0)
        def _():
            for slot in range(DEPTH - 1):
                up_copy(slot, slot).wait_send()

        @pl.when(z == DEPTH - 1)
        def _():
            for slot in range(DEPTH - 1):
                down_copy(slot, slot).wait_send()

        @pl.when(z == 1)
        def _():
            up_copy(0, 0).wait_send()
            up_copy(2, 1).wait_send()
            down_copy(1, 0).wait_send()

        @pl.when(z == DEPTH - 2)
        def _():
            down_copy(0, 0).wait_send()
            down_copy(2, 1).wait_send()
            up_copy(1, 0).wait_send()

    def to_rows(which, fin, rows):
        slot = core * DEPTH + z
        copies = []
        for flip, turn in members:
            cc, zz = target(flip, turn)
            copies.append(
                remote(
                    fin.at[cc * DEPTH + zz],
                    rows.at[slot],
                    rows_s,
                    rows_r,
                    (which, flip * DEPTH + turn),
                    device(x, cc, zz, y),
                )
            )
        copies.append(pltpu.make_async_copy(fin.at[slot], rows.at[slot], local_sems.at[which]))
        return copies

    def gate_done():
        gate_y.wait_recv()
        gate_x.wait_recv()
        for load in loads:
            load.wait()
        gate_fin[...] = jnp.concatenate(
            [
                gate_own_x[...] + gate_y2r[...].astype(wide),
                gate_own_y[...] + gate_x2r[...].astype(wide),
            ],
            2,
        ).astype(low)
        for copy in to_rows(0, gate_fin, gate_rows) + hidden_y:
            copy.start()

    def piece_body(
        dq, dk, dv, odk, odv, gu, tokens, cos, first, second
    ):
        step = pl.program_id(0)
        turn = step // 2
        piece = piece_of(step)
        tables = (cos, first, second)
        query = turned(dq[0] * (HEAD_DIM**-0.5), *tables, -1.0)
        key = turned(dk[0] + odk[0].astype(wide), *tables, -1.0)
        value = dv[0] + odv[0].astype(wide)
        narrow = jnp.concatenate([query, key, value], 1).astype(low)
        pg_ref[piece] = narrow
        grad = transposed_times(narrow, inward_rows(wi_ref))
        grad += transposed_times(gu[0], wg_ref[...])
        hat, _ = normalised(tokens[0])
        half = grad.shape[1] // 2
        for row, total in (
            (0, jnp.sum(grad * hat, axis=0, keepdims=True)),
            (2, jnp.sum(grad, axis=0, keepdims=True)),
        ):
            vec_sum[row : row + 1] += total[:, :half]
            vec_sum[row + 1 : row + 2] += total[:, half:]
        vec_sum[4:5, : 3 * HEAD_COLS] += jnp.sum(narrow.astype(wide), axis=0, keepdims=True)

        pl.when(step == GATE_STEP)(gate_done)
        pl.when(step == PIECES - 1)(first_hop)

        @pl.when(step % 2 == 0)
        def _():
            @pl.when(turn >= 2)
            def _():
                core_copy(turn - 2).wait_send()

            core_send[turn % 2] = grad.astype(low)
            core_copy(turn).start()

        @pl.when(step % 2 == 1)
        def _():
            core_copy(turn).wait_recv()
            both = grad + core_recv[turn].astype(wide)

            @pl.when(turn < DEPTH - 1)
            def _():
                z_send[turn] = both.astype(low)

                @pl.when(z == 0)
                def _():
                    up_copy(turn, turn).start()

                @pl.when(z == DEPTH - 1)
                def _():
                    down_copy(turn, turn).start()

            @pl.when(turn == DEPTH - 1)
            def _():
                own_sum[...] = both

    def by_piece(width):
        return pl.BlockSpec((1, ROWS, width), lambda i: (piece_of(i), 0, 0))

    table_spec = pl.BlockSpec(
        (1,) + cos_ref.shape[1:], lambda i: (piece_of(i) % DEPTH, 0, 0)
    )
    pltpu.emit_pipeline(
        piece_body,
        grid=(PIECES,),
        in_specs=[by_piece(HEAD_COLS)] * 5
        + [by_piece(gu_ref.shape[-1]), by_piece(pieces_ref.shape[-1])]
        + [table_spec] * 3,
    )(
        dq_ref,
        dk_ref,
        dv_ref,
        odk_ref,
        odv_ref,
        gu_ref,
        pieces_ref,
        cos_ref,
        first_ref,
        second_ref,
    )
    vector_x = remote(vec_sum, vec_x, vec_s, vec_r, 0, x_mate)
    vector_x.start()

    total, width = normed_ref.shape
    size = width // PIECES
    cut = 3 * HEAD_COLS // 2

    def block(i):
        return jnp.where(i < DEPTH, (1 - x) * DEPTH + i, x * DEPTH + i - DEPTH)

    inward_x = remote(inward_xs, inward_xr, stage_s, stage_r, (1, 0), x_mate)

    def inward_body(left):
        i = pl.program_id(0)
        rhs = pg_ref[...].reshape(total, 3 * HEAD_COLS)
        term = times_transposed(left[...], rhs)
        first = term[:, :cut].reshape(2, 2, size // 4, cut)
        at = pl.ds((i % DEPTH) * 2, 2)

        @pl.when(i < DEPTH)
        def _():
            inward_xs[at] = first.astype(low)

        @pl.when(i >= DEPTH)
        def _():
            inward_xk[at] = first

        at = pl.ds(block(i) * 2, 2)
        split_rows(term[:, cut:], y, inward_yk.at[at], inward_ys.at[at])

        @pl.when(i == DEPTH - 1)
        def _():
            inward_x.start()

    pltpu.emit_pipeline(
        inward_body,
        grid=(PIECES,),
        in_specs=[pl.BlockSpec((total, size), lambda i: (0, block(i)))],
    )(normed_ref)
    started.append(inward_x)
    inward_y = begin(remote(inward_ys, inward_yr, stage_s, stage_r, (1, 1), y_mate))

    vector_x.wait_recv()
    vec_sum_x = vec_sum[...] + vec_x[...]
    vector_x.wait_send()
    vec_sum[...] = vec_sum_x
    vector_y = remote(vec_sum, vec_y, vec_s, vec_r, 1, y_mate)
    vector_y.start()

    def add_two(one, two, out):
        out[...] = (one[...].astype(wide) + two[...].astype(wide)).astype(out.dtype)

    second_hop()
    third_hop()

    chunk = heads_term.shape[-1] // 2

    def flat_spec(rows):
        return pl.BlockSpec((rows, chunk), lambda i: (0, i))

    def row_sum(one, two, out):
        spec = flat_spec(one.shape[0])
        pltpu.emit_pipeline(
            add_two, grid=(2,), in_specs=[spec, spec], out_specs=[spec]
        )(one, two, out)

    def row_total(one, two, three, out):
        spec = flat_spec(one.shape[0])

        def body(one, two, three, out):
            out[...] = one[...].astype(wide) + two[...].astype(wide) + three[...].astype(wide)

        pltpu.emit_pipeline(
            body, grid=(2,), in_specs=[spec] * 3, out_specs=[spec]
        )(one, two, three, out)

    heads_x.wait_recv()
    row_sum(heads_term.at[x, 1 - y], heads_r.at[1 - y], heads_2s)
    heads_y = begin(remote(heads_2s, heads_2r, stage_s, stage_r, (2, 2), y_mate))
    for copy in hidden_y:
        copy.wait_recv()
    row_sum(hidden_term.at[1 - x, y], hidden_r.at[1 - x], hidden_2s)
    hidden_x = begin(remote(hidden_2s, hidden_2r, stage_s, stage_r, (3, 2), x_mate))

    vector_y.wait_recv()
    vec_sum_y = vec_sum[...] + vec_y[...]
    vector_y.wait_send()
    slot = core * DEPTH + z
    vec_out[slot] = vec_sum_y
    vectors = []
    for flip, turn in members:
        cc, zz = target(flip, turn)
        vectors.append(
            begin(
                remote(
                    vec_out.at[slot],
                    vec_out.at[slot],
                    rows_s,
                    rows_r,
                    (2, flip * DEPTH + turn),
                    device(x, cc, zz, y),
                )
            )
        )

    inward_x.wait_recv()
    inward_y2s[...] = (inward_xk[:, 1 - y] + inward_xr[:, 1 - y].astype(wide)).astype(low)
    inward_over_y = begin(remote(inward_y2s, inward_y2r, stage_s, stage_r, (1, 2), y_mate))
    inward_y.wait_recv()
    other = pl.ds((1 - x) * PIECES, PIECES)
    inward_x2s[...] = (inward_yk[other] + inward_yr[other].astype(wide)).astype(low)
    inward_over_x = begin(remote(inward_x2s, inward_x2r, stage_s, stage_r, (1, 3), x_mate))
    heads_y.wait_recv()
    row_total(heads_term.at[x, y], heads_r.at[y], heads_2r, heads_out)
    hidden_x.wait_recv()
    row_total(hidden_term.at[x, y], hidden_r.at[x], hidden_2r, hidden_out)
    inward_over_y.wait_recv()
    inward_over_x.wait_recv()
    own = pl.ds(x * PIECES, PIECES)
    inward_fin[...] = jnp.concatenate(
        [
            inward_xk[:, y] + inward_xr[:, y].astype(wide) + inward_y2r[...].astype(wide),
            inward_yk[own] + inward_yr[own].astype(wide) + inward_x2r[...].astype(wide),
        ],
        2,
    ).astype(low)
    inward_rest = to_rows(1, inward_fin, inward_rows_out)
    for copy in inward_rest:
        copy.start()

    own_tokens.wait()
    last_hop()
    for first in range(0, ROWS, 64):
        rows = pl.ds(first, 64)
        grad = own_sum[rows]
        hat, inverse = normalised(token_rows[rows])
        scaled = grad * gain_ref[...]
        input_grad = inverse * (
            scaled
            - jnp.mean(scaled, axis=-1, keepdims=True)
            - hat * jnp.mean(scaled * hat, axis=-1, keepdims=True)
        )
        tokens_out[rows] = (cot_ref[rows].astype(wide) + input_grad).astype(low)

    for copy in to_rows(0, gate_fin, gate_rows) + inward_rest:
        copy.wait()
    for copy in hidden_y:
        copy.wait_send()
    for copy in vectors:
        copy.wait_recv()
    for copy in started:
        copy.wait_send()
    for turn in range(DEPTH - 2, DEPTH):
        core_copy(turn).wait_send()
    sent_all()


def finish(
    parts, gate_up_grad, pieces, tables, normed, gate_up, heads, hidden, weights, gain, cot
):
    low, wide = jnp.bfloat16, jnp.float32
    width = pieces.shape[-1]
    rows = width // 32
    anywhere = pl.BlockSpec(memory_space=pl.ANY)
    inside = pl.BlockSpec(memory_space=pltpu.VMEM)
    shape = jax.ShapeDtypeStruct
    half = 3 * HEAD_COLS // 2

    a, b = (value.shape[-1] for value in gate_up[:2])
    heads_rows, hidden_rows = heads.shape[2], hidden.shape[2]
    out_shapes = [
        shape((ROWS, width), low),
        shape((heads_rows, width), wide),
        shape((hidden_rows, width), wide),
        shape((PIECES, rows, a + b), low),
        shape((PIECES, rows, 2 * half), low),
        shape((PIECES, 8, width // 2), wide),
    ]
    out_shapes += [
        shape((2, heads_rows, width), low),
        shape((heads_rows, width), low),
        shape((heads_rows, width), low),
        shape((2, hidden_rows, width), low),
        shape((hidden_rows, width), low),
        shape((hidden_rows, width), low),
    ]
    out_specs = [inside] + [anywhere] * 4 + [inside] + [anywhere] * (len(out_shapes) - 6)
    dma = pltpu.SemaphoreType.DMA
    outs = pl.pallas_call(
        finish_kernel,
        in_specs=[anywhere] * 17 + [inside] * 4,
        out_specs=out_specs,
        out_shape=out_shapes,
        scratch_shapes=[
            pltpu.VMEM((2, ROWS, width), low),
            pltpu.VMEM((DEPTH, ROWS, width), low),
            pltpu.VMEM((DEPTH - 1, ROWS, width), low),
            pltpu.VMEM((DEPTH - 1, ROWS, width), low),
            pltpu.VMEM((DEPTH - 1, ROWS, width), low),
            pltpu.VMEM((ROWS, width), wide),
            pltpu.VMEM((PIECES, ROWS, 3 * HEAD_COLS), low),
            pltpu.VMEM((ROWS, width), low),
            pltpu.VMEM((8, width // 2), wide),
            pltpu.VMEM((8, width // 2), wide),
            pltpu.VMEM((8, width // 2), wide),
            pltpu.VMEM((PIECES, rows, a), wide),
            pltpu.VMEM((PIECES, rows, b), wide),
            pltpu.VMEM((PIECES, rows, a), low),
            pltpu.VMEM((PIECES, rows, b), low),
            pltpu.VMEM((PIECES, rows, a + b), low),
            pltpu.VMEM((PIECES, 2, rows, half), low),
            pltpu.VMEM((PIECES, 2, rows, half), low),
            pltpu.VMEM((PIECES, 2, rows, half), wide),
            pltpu.VMEM((2 * PIECES, rows, half), low),
            pltpu.VMEM((2 * PIECES, rows, half), low),
            pltpu.VMEM((2 * PIECES, rows, half), wide),
            pltpu.VMEM((PIECES, rows, half), low),
            pltpu.VMEM((PIECES, rows, half), low),
            pltpu.VMEM((PIECES, rows, half), low),
            pltpu.VMEM((PIECES, rows, half), low),
            pltpu.VMEM((PIECES, rows, 2 * half), low),
            dma((DEPTH,)),
            dma((DEPTH,)),
            dma((DEPTH - 1,)),
            dma((DEPTH - 1,)),
            dma((DEPTH - 1,)),
            dma((DEPTH - 1,)),
            dma((4, 4)),
            dma((4, 4)),
            dma((3, PIECES)),
            dma((3, PIECES)),
            dma((2,)),
            dma((2,)),
            dma((5,)),
        ],
        compiler_params=params(63, collective_id=1, has_side_effects=True),
        cost_estimate=cost(0, 64 * MIB),
        name="finish",
    )(
        *parts,
        gate_up_grad,
        pieces,
        *tables,
        normed,
        *gate_up,
        heads,
        hidden,
        *weights,
        gain,
        cot,
    )
    return outs[:6]


def split_rows(term, y, keep_ref, send_ref):
    rows = term.shape[0] // 4
    even = jnp.concatenate([term[:rows], term[2 * rows : 3 * rows]], 0)
    odd = jnp.concatenate([term[rows : 2 * rows], term[3 * rows :]], 0)
    keep_ref[...] = jnp.where(y == 0, even, odd).reshape(keep_ref.shape)
    send_ref[...] = jnp.where(y == 0, odd, even).astype(jnp.bfloat16).reshape(send_ref.shape)


def place_kernel(parts, in_ref, out_ref):
    each = in_ref.shape[2] // parts
    for part in range(parts):
        columns = slice(part * each, (part + 1) * each)
        line = jnp.concatenate([in_ref[n, :, columns] for n in range(PIECES)], 1)
        out_ref[:, part * PIECES * each : (part + 1) * PIECES * each] = line.astype(jnp.float32)


def place_rows(value, parts):
    rows, columns = value.shape[1], value.shape[2]
    return pl.pallas_call(
        functools.partial(place_kernel, parts),
        out_shape=jax.ShapeDtypeStruct((rows, PIECES * columns), jnp.float32),
        compiler_params=params(32),
        cost_estimate=cost(0, 4 * MIB),
        name="place_rows",
    )(value)


def shards_grouped(
    tokens,
    lengths,
    norm_gain,
    norm_shift,
    inward_weight,
    inward_bias,
    outward_weight,
    gate_up_weight,
    down_weight,
    cotangent,
):
    group_len, seqs, width = tokens.shape[1:]
    bucket, blk = lax.axis_index("bucket"), lax.axis_index("blk")

    gain_share, bias_share = norm_gain.shape[0], inward_bias.shape[0]
    shares = jnp.concatenate(
        [norm_gain, norm_gain, norm_shift, norm_shift, inward_bias, jnp.zeros((624,), jnp.float32)]
    ).reshape(8, 128)
    own_tokens = jnp.transpose(tokens[0], (1, 0, 2)).reshape(ROWS, width)
    own_cotangent = jnp.transpose(cotangent[0], (1, 0, 2)).reshape(ROWS, width)
    position = blk * group_len + jnp.arange(group_len, dtype=jnp.int32)
    valid = (position[None, :] < lengths[0][:, None]).astype(jnp.float32).reshape(ROWS, 1)
    lane = jnp.arange(HEAD_COLS, dtype=jnp.int32) % HEAD_DIM
    power = (lane % (ROT // 2)).astype(jnp.float32)
    frequency = jnp.where(lane < ROT, rotary_base ** (-(2.0 * power) / ROT), 0.0)
    (
        pieces,
        normed,
        gate,
        up,
        grads,
        inward,
        gate_up,
        rows_out,
        queries,
        pairs,
        other_pairs,
        hidden,
        attended,
        own_sum,
        terms,
        *tables,
        gain,
    ) = forward(
        own_tokens,
        own_cotangent,
        inward_weight,
        gate_up_weight,
        outward_weight,
        down_weight,
        valid,
        shares,
        inward_bias.reshape(1, -1),
        frequency.reshape(1, -1),
    )
    gate_up = gate_up.reshape(width, -1)
    normed = normed.reshape(PIECES * ROWS, width)
    outs = backward(
        grads,
        gate,
        up,
        normed,
        pieces,
        queries,
        pairs,
        other_pairs,
        hidden,
        attended,
        rows_out,
        own_sum,
        terms,
        valid,
    )
    heads_term, hidden_term, gate_up_grad, *parts, layer_out = outs[10:]
    tokens_grad, outward_sum, down_sum, gate_up_rows, inward_rows_own, vectors = finish(
        parts,
        gate_up_grad,
        pieces,
        tables,
        normed,
        outs[6:10],
        heads_term.reshape(2, 2, -1, width),
        hidden_term.reshape(2, 2, -1, width),
        (inward, gate_up),
        gain,
        own_cotangent,
    )
    gate_up_sum = place_rows(gate_up_rows, 4)
    inward_sum = place_rows(inward_rows_own, 6)

    device = bucket * 2 * DEPTH + blk
    sums = jnp.sum(vectors[:, :4], axis=0).reshape(2, -1, gain_share)
    gain_sum = one_of(sums[0], device, 0)
    shift_sum = one_of(sums[1], device, 0)
    columns_sum = vectors[:, 4, : 3 * HEAD_COLS].reshape(PIECES, 3, 2, 2 * HEAD_DIM)
    columns_sum = jnp.transpose(columns_sum, (1, 2, 0, 3)).reshape(3, -1)
    key_rot = columns_sum[1].reshape(HEADS, HEAD_DIM)[:, :ROT]
    bias_all = jnp.concatenate([columns_sum[0], columns_sum[2], key_rot.reshape(-1)])
    bias_sum = one_of(bias_all.reshape(-1, bias_share), device, 0)

    def placed(value):
        value = value.reshape(seqs, group_len, width)
        return jnp.transpose(value, (1, 0, 2)).reshape(tokens.shape)

    return (
        placed(layer_out),
        placed(tokens_grad),
        gain_sum,
        shift_sum,
        inward_sum,
        bias_sum,
        outward_sum,
        gate_up_sum,
        down_sum,
    )


def solution(mesh):
    in_specs = (
        P("bucket", "blk", None, None),
        P("bucket", None),
        P(("bucket", "blk")),
        P(("bucket", "blk")),
        P(("bucket", "blk"), None),
        P(("bucket", "blk")),
        P(("bucket", "blk"), None),
        P(("bucket", "blk"), None),
        P(("bucket", "blk"), None),
        P("bucket", "blk", None, None),
    )
    out_specs = (
        P("bucket", "blk", None, None),
        P("bucket", "blk", None, None),
        P(("bucket", "blk")),
        P(("bucket", "blk")),
        P(("bucket", "blk"), None),
        P(("bucket", "blk")),
        P(("bucket", "blk"), None),
        P(("bucket", "blk"), None),
        P(("bucket", "blk"), None),
    )
    body = shards_grouped if fits_groups(mesh) else shards_general
    return jax.shard_map(body, mesh=mesh, in_specs=in_specs, out_specs=out_specs, check_vma=False)
```

```python
import functools

import jax
import jax.numpy as jnp
from jax import lax
from jax.experimental import pallas as pl
from jax.experimental.pallas import tpu as pltpu
from jax.sharding import PartitionSpec as P

HEADS = 32
HEAD_DIM = 64
ROT = 16


epsilon = 1e-05
rotary_base = 10000.0
masked_score = -1e30


def shifted(value, axis, by):
    count = lax.axis_size(axis)
    pairs = [(i, i + by) for i in range(count) if 0 <= i + by < count]
    return lax.ppermute(value, axis, pairs)


def shifted_2(value, axis, steps):
    count = lax.axis_size(axis)
    pairs = [(source, (source + steps) % count) for source in range(count)]
    return lax.ppermute(value, axis, pairs)


def keep_same(value):
    return value


def transposed_times(left, right):
    return lax.dot_general(
        left, right, (((1,), (1,)), ((), ())), preferred_element_type=jnp.float32
    )


def times_transposed(left, right):
    return lax.dot_general(
        left, right, (((0,), (0,)), ((), ())), preferred_element_type=jnp.float32
    )


def rotary_tables(positions):
    half_rot = ROT // 2
    frequency = rotary_base ** (-(2.0 * jnp.arange(half_rot).astype(jnp.float32)) / ROT)
    angles = positions.astype(jnp.float32)[:, None] * frequency[None, :]
    return (jnp.cos(angles), jnp.sin(angles))


def rotate(values, cos_table, sine_table):
    half_rot = ROT // 2
    front_half = values[..., :half_rot]
    back_half = values[..., half_rot:ROT]
    return jnp.concatenate(
        [
            front_half * cos_table - back_half * sine_table,
            back_half * cos_table + front_half * sine_table,
            values[..., ROT:],
        ],
        axis=-1,
    )


def split_pairs(packed):
    rows_here, seq_count, both_width = packed.shape
    half_width = both_width // 2
    keys_part = packed[..., :half_width].reshape(rows_here, seq_count, HEADS, HEAD_DIM)
    values_part = packed[..., half_width:].reshape(rows_here, seq_count, HEADS, HEAD_DIM)
    return (keys_part, values_part)


def block_scores(queries, key_block, query_start, key_start):
    scores = jnp.einsum("tshd,ushd->shtu", queries, key_block, preferred_element_type=jnp.float32)
    query_pos = query_start + jnp.arange(queries.shape[0], dtype=jnp.int32)
    key_pos = key_start + jnp.arange(key_block.shape[0], dtype=jnp.int32)
    allowed = (key_pos[None, :] <= query_pos[:, None])[None, None]
    return (jnp.where(allowed, scores, masked_score), allowed)


def forward_block(carried, queries, key_block, value_block, query_start, key_start):
    running_max, running_sum, weighted = carried
    scores, allowed = block_scores(queries, key_block, query_start, key_start)
    new_max = jnp.maximum(running_max, jnp.max(scores, axis=-1))
    rescale = jnp.exp(running_max - new_max)
    weights = jnp.where(allowed, jnp.exp(scores - new_max[..., None]), 0.0)
    running_sum = running_sum * rescale + jnp.sum(weights, axis=-1)
    update = jnp.einsum(
        "shtu,ushd->tshd",
        weights.astype(jnp.bfloat16),
        value_block,
        preferred_element_type=jnp.float32,
    )
    weighted = weighted * jnp.transpose(rescale, (2, 0, 1))[..., None] + update
    return (new_max, running_sum, weighted)


def pair_grads(
    queries, out_grads, log_norm, deltas, key_block, value_block, query_start, key_start
):
    scores, allowed = block_scores(queries, key_block, query_start, key_start)
    probability = jnp.where(allowed, jnp.exp(scores - log_norm[..., None]), 0.0)
    value_grad = jnp.einsum(
        "shtu,tshd->ushd",
        probability.astype(jnp.bfloat16),
        out_grads,
        preferred_element_type=jnp.float32,
    )
    prob_grad = jnp.einsum(
        "tshd,ushd->shtu", out_grads, value_block, preferred_element_type=jnp.float32
    )
    score_grad = (probability * (prob_grad - deltas[..., None])).astype(jnp.bfloat16)
    query_grad = jnp.einsum(
        "shtu,ushd->tshd", score_grad, key_block, preferred_element_type=jnp.float32
    )
    key_grad = jnp.einsum(
        "shtu,tshd->ushd", score_grad, queries, preferred_element_type=jnp.float32
    )
    return (query_grad, key_grad, value_grad)


def over_blocks(running, incoming, unit_rows, handle):
    total_rows = incoming[0].shape[0]
    block_count = total_rows // unit_rows
    block_rows = total_rows // block_count
    stacked = tuple(
        (member.reshape((block_count, block_rows) + member.shape[1:]) for member in incoming)
    )

    def visit(carried, element):
        block_index, members = element
        return (handle(carried, members, block_index * block_rows), None)

    running, unused = lax.scan(visit, running, (jnp.arange(block_count, dtype=jnp.int32), stacked))
    return running


def shards_general(
    tokens,
    lengths,
    norm_gain,
    norm_shift,
    inward_weight,
    inward_bias,
    outward_weight,
    gate_up_weight,
    down_weight,
    cotangent,
):
    group_len = tokens.shape[1]
    seq_count = tokens.shape[2]
    model_width = tokens.shape[3]
    row_total = group_len * seq_count
    block_total = lax.axis_size("blk")
    position = lax.axis_index("blk")
    own_start = position * group_len
    longest = jnp.max(lengths[0])
    active = own_start < longest
    gathered = (
        lax.all_gather(inward_weight.astype(jnp.bfloat16), ("bucket", "blk"), axis=0, tiled=True),
        lax.all_gather(outward_weight.astype(jnp.bfloat16), ("bucket", "blk"), axis=0, tiled=True),
        lax.all_gather(gate_up_weight.astype(jnp.bfloat16), ("bucket", "blk"), axis=0, tiled=True),
        lax.all_gather(down_weight.astype(jnp.bfloat16), ("bucket", "blk"), axis=0, tiled=True),
        lax.all_gather(norm_gain.astype(jnp.bfloat16), ("bucket", "blk"), axis=0, tiled=True),
        lax.all_gather(norm_shift.astype(jnp.bfloat16), ("bucket", "blk"), axis=0, tiled=True),
        lax.all_gather(inward_bias.astype(jnp.bfloat16), ("bucket", "blk"), axis=0, tiled=True),
    )
    inward_full, outward_full, gate_up_full, down_full, gain_full, shift_full, bias_full = gathered
    inputs = tokens.reshape(row_total, model_width).astype(jnp.float32)
    centred = inputs - jnp.mean(inputs, axis=-1, keepdims=True)
    variance = jnp.mean(centred * centred, axis=-1, keepdims=True)
    inverse = lax.rsqrt(variance + epsilon)
    normal_hat = centred * inverse
    normed_low = (
        normal_hat * gain_full.astype(jnp.float32) + shift_full.astype(jnp.float32)
    ).astype(jnp.bfloat16)
    bias_float = bias_full.astype(jnp.float32)
    key_bias = jnp.pad(
        bias_float[2 * model_width :].reshape(HEADS, ROT), ((0, 0), (0, HEAD_DIM - ROT))
    ).reshape(model_width)
    full_bias = jnp.concatenate(
        [bias_float[:model_width], key_bias, bias_float[model_width : 2 * model_width]]
    )
    projected = jnp.dot(normed_low, inward_full, preferred_element_type=jnp.float32) + full_bias
    projected = projected.reshape(group_len, seq_count, 3, HEADS, HEAD_DIM)
    cos_table, sine_table = rotary_tables(own_start + jnp.arange(group_len, dtype=jnp.int32))
    cos_table = cos_table[:, None, None, :]
    sine_table = sine_table[:, None, None, :]
    query_scale = HEAD_DIM ** (-0.5)
    queries = (rotate(projected[:, :, 0], cos_table, sine_table) * query_scale).astype(jnp.bfloat16)
    keys_low = rotate(projected[:, :, 1], cos_table, sine_table).astype(jnp.bfloat16)
    values_low = projected[:, :, 2].astype(jnp.bfloat16)
    packed = jnp.concatenate(
        [
            keys_low.reshape(group_len, seq_count, model_width),
            values_low.reshape(group_len, seq_count, model_width),
        ],
        axis=-1,
    )

    def forward_handle(carried, members, key_start):
        keys_part, values_part = split_pairs(members[0])
        needed = active & (key_start <= own_start + group_len - 1)

        def forward_compute(state_in):
            return forward_block(state_in, queries, keys_part, values_part, own_start, key_start)

        return lax.cond(needed, forward_compute, keep_same, carried)

    start_state = (
        jnp.full((seq_count, HEADS, group_len), masked_score, jnp.float32),
        jnp.zeros((seq_count, HEADS, group_len), jnp.float32),
        jnp.zeros((group_len, seq_count, HEADS, HEAD_DIM), jnp.float32),
    )
    running_max, running_sum, weighted = over_blocks(
        start_state, (lax.all_gather(packed, "blk", axis=0, tiled=True),), group_len, forward_handle
    )
    bounded = jnp.maximum(running_sum, 1.0)
    log_norm = running_max + jnp.log(bounded)
    attended = weighted / jnp.transpose(bounded, (2, 0, 1))[..., None]
    attended_rows = attended.astype(jnp.bfloat16).reshape(row_total, model_width)
    gate_up = jnp.dot(normed_low, gate_up_full, preferred_element_type=jnp.float32)
    ff_width = gate_up.shape[1] // 2
    gate_part = gate_up[:, :ff_width]
    up_part = gate_up[:, ff_width:]
    sigmoid_gate = jax.nn.sigmoid(gate_part)
    silu_gate = gate_part * sigmoid_gate
    hidden_low = (silu_gate * up_part).astype(jnp.bfloat16)
    branch = jnp.dot(attended_rows, outward_full, preferred_element_type=jnp.float32) + jnp.dot(
        hidden_low, down_full, preferred_element_type=jnp.float32
    )
    query_pos = own_start + jnp.arange(group_len, dtype=jnp.int32)
    valid_rows = (
        (query_pos[:, None] < lengths[0][None, :]).astype(jnp.float32).reshape(row_total, 1)
    )
    layer_out = (inputs + valid_rows * branch).astype(jnp.bfloat16).reshape(tokens.shape)
    inward_back = gathered[0]
    outward_back = gathered[1]
    gate_up_back = gathered[2]
    down_back = gathered[3]
    gain_float = gathered[4].astype(jnp.float32)
    cotangent_rows = cotangent.reshape(row_total, model_width).astype(jnp.float32)
    branch_grad = (cotangent_rows * valid_rows).astype(jnp.bfloat16)
    hidden_grad = transposed_times(branch_grad, down_back)
    gate_grad = hidden_grad * up_part * (sigmoid_gate + silu_gate * (1.0 - sigmoid_gate))
    up_grad = hidden_grad * silu_gate
    gate_up_grad_low = jnp.concatenate([gate_grad, up_grad], axis=-1).astype(jnp.bfloat16)
    down_term = times_transposed(hidden_low, branch_grad)
    gate_up_term = times_transposed(normed_low, gate_up_grad_low)
    gate_up_sum, down_sum = (
        lax.psum_scatter(gate_up_term, ("bucket", "blk"), scatter_dimension=0, tiled=True),
        lax.psum_scatter(down_term, ("bucket", "blk"), scatter_dimension=0, tiled=True),
    )
    normed_grad = transposed_times(gate_up_grad_low, gate_up_back)
    attended_grad = (
        transposed_times(branch_grad, outward_back)
        .astype(jnp.bfloat16)
        .reshape(group_len, seq_count, HEADS, HEAD_DIM)
    )
    outward_term = times_transposed(attended_rows, branch_grad)
    deltas = jnp.transpose(
        jnp.sum(attended_grad.astype(jnp.float32) * attended, axis=-1), (1, 2, 0)
    )
    grad_zeros = jnp.zeros((group_len, seq_count, 2 * model_width), jnp.float32)
    query_zeros = jnp.zeros((group_len, seq_count, HEADS, HEAD_DIM), jnp.float32)

    def cycle_turn(turn_index, carried):
        visiting, sums_now, grads_now = carried
        owner_index = (position - turn_index) % block_total
        key_start = owner_index * group_len
        needed = active & (owner_index <= position)

        def cycle_compute(sums_in):
            keys_part, values_part = split_pairs(visiting)
            query_part, key_part, value_part = pair_grads(
                queries,
                attended_grad,
                log_norm,
                deltas,
                keys_part,
                values_part,
                own_start,
                key_start,
            )
            merged = jnp.concatenate(
                [
                    key_part.reshape(group_len, seq_count, model_width),
                    value_part.reshape(group_len, seq_count, model_width),
                ],
                axis=-1,
            )
            return (sums_in[0] + merged, sums_in[1] + query_part)

        sums_now, grads_now = lax.cond(needed, cycle_compute, keep_same, (sums_now, grads_now))
        visiting = shifted(visiting, "blk", 1)
        sums_now = shifted_2(sums_now.astype(jnp.bfloat16), "blk", 1).astype(sums_now.dtype)
        return (visiting, sums_now, grads_now)

    unused, pair_sums, query_grads = lax.fori_loop(
        0, block_total, cycle_turn, (packed, grad_zeros, query_zeros)
    )
    key_grad = pair_sums[..., :model_width].reshape(group_len, seq_count, HEADS, HEAD_DIM)
    value_grad = pair_sums[..., model_width:].reshape(group_len, seq_count, HEADS, HEAD_DIM)
    back_sine = -sine_table
    query_back = rotate(query_grads * query_scale, cos_table, back_sine)
    key_back = rotate(key_grad, cos_table, back_sine)
    projected_grad = (
        jnp.stack([query_back, key_back, value_grad], axis=2)
        .reshape(row_total, 3 * model_width)
        .astype(jnp.bfloat16)
    )
    inward_term = times_transposed(normed_low, projected_grad)
    column_sums = jnp.sum(projected_grad.astype(jnp.float32), axis=0)
    key_bias_grad = (
        column_sums[model_width : 2 * model_width]
        .reshape(HEADS, HEAD_DIM)[:, :ROT]
        .reshape(HEADS * ROT)
    )
    bias_term = jnp.concatenate(
        [column_sums[:model_width], column_sums[2 * model_width :], key_bias_grad]
    )
    normed_grad = normed_grad + transposed_times(projected_grad, inward_back)
    gain_term = jnp.sum(normed_grad * normal_hat, axis=0)
    shift_term = jnp.sum(normed_grad, axis=0)
    scaled_grad = normed_grad * gain_float
    input_grad = inverse * (
        scaled_grad
        - jnp.mean(scaled_grad, axis=-1, keepdims=True)
        - normal_hat * jnp.mean(scaled_grad * normal_hat, axis=-1, keepdims=True)
    )
    tokens_grad = (cotangent_rows + input_grad).astype(jnp.bfloat16).reshape(tokens.shape)
    inward_sum, outward_sum, bias_sum, gain_sum, shift_sum = (
        lax.psum_scatter(inward_term, ("bucket", "blk"), scatter_dimension=0, tiled=True),
        lax.psum_scatter(outward_term, ("bucket", "blk"), scatter_dimension=0, tiled=True),
        lax.psum_scatter(bias_term, ("bucket", "blk"), scatter_dimension=0, tiled=True),
        lax.psum_scatter(gain_term, ("bucket", "blk"), scatter_dimension=0, tiled=True),
        lax.psum_scatter(shift_term, ("bucket", "blk"), scatter_dimension=0, tiled=True),
    )
    return (
        layer_out,
        tokens_grad,
        gain_sum,
        shift_sum,
        inward_sum,
        bias_sum,
        outward_sum,
        gate_up_sum,
        down_sum,
    )


DEPTH = 4
PIECES = 2 * DEPTH
ROWS = 256
GATE_STEP = 6
HALFWAY = 5
LOCAL_HEADS = 4
HEAD_COLS = LOCAL_HEADS * HEAD_DIM


MIB = 1024 * 1024


def fits_groups(mesh):
    return mesh.shape["bucket"] == 4 and mesh.shape["blk"] == 2 * DEPTH


def around(step):
    return [(z * 2 + y, ((z + step) % DEPTH) * 2 + y) for z in range(DEPTH) for y in range(2)]


def in_order(own, other, index, axis):
    return jnp.where(
        index == 0, jnp.stack([own, other], axis), jnp.stack([other, own], axis)
    )


def one_of(value, index, axis):
    return lax.dynamic_index_in_dim(value, index, axis, False)


def dot_rows(left, right):
    return lax.dot_general(
        left, right, (((1,), (0,)), ((), ())), preferred_element_type=jnp.float32
    )


def params(limit, **extra):
    return pltpu.CompilerParams(vmem_limit_bytes=limit * MIB, **extra)


def cost(flops, moved, exps=0):
    return pl.CostEstimate(flops=flops // 64, bytes_accessed=moved // 64, transcendentals=exps // 64)


def piece_spec(width):
    return pl.BlockSpec((1, ROWS, width), lambda i: (i, 0, 0))


def whole_spec(shape):
    return pl.BlockSpec(shape, lambda i: (0,) * len(shape))


def remote_to(src, dst, send_sem, recv_sem, device):
    return pltpu.make_async_remote_copy(
        src_ref=src,
        dst_ref=dst,
        send_sem=send_sem,
        recv_sem=recv_sem,
        device_id=device,
        device_id_type=pl.DeviceIdType.MESH,
    )


def remote(src, dst, sends, recvs, index, device):
    return remote_to(src, dst, sends.at[index], recvs.at[index], device)


def select(i, first, second, third):
    return jnp.where(i == 0, first, jnp.where(i == 1, second, jnp.where(i == 2, third, 0)))


class Chain:
    def __init__(self, src, out, x, core, z, y, sems):
        up_s, down_s, arrive, core_s, core_r, local = sems
        self.z = z
        self.out = out

        def hop(k, src, slot, sends, dz):
            return pltpu.make_async_remote_copy(
                src_ref=src,
                dst_ref=out.at[slot],
                send_sem=sends.at[k],
                recv_sem=arrive.at[slot],
                device_id=(x * 2 + core, (z + dz) * 2 + y),
                device_id_type=pl.DeviceIdType.MESH,
            )

        mate = (x * 2 + 1 - core, z * 2 + y)
        self.ups = [hop(k, src if k == 0 else out.at[k], k + 1, up_s, 1) for k in range(3)]
        self.downs = [
            hop(k, src if k == 0 else out.at[DEPTH - k], 3 - k, down_s, -1) for k in range(3)
        ]
        self.cores = [
            remote(src if k == 0 else out.at[k], out.at[DEPTH + k], core_s, core_r, k, mate)
            for k in range(DEPTH)
        ]
        self.local = pltpu.make_async_copy(src, out.at[0], local)
        inner = (z > 0) & (z < DEPTH - 1)
        self.sent = [
            (z < DEPTH - 1, self.ups[0]),
            (z > 0, self.downs[0]),
            (inner, self.ups[1]),
            (inner, self.downs[1]),
            (z == DEPTH - 2, self.ups[2]),
            (z == 1, self.downs[2]),
        ]

    def start(self, *numbers):
        for number in numbers:
            condition, copy = self.sent[number]
            pl.when(condition)(copy.start)

    def near(self):
        self.cores[0].start()
        self.local.start()

    def first(self):
        self.start(0, 1)

    def second(self):
        @pl.when(self.z > 0)
        def _():
            self.ups[0].wait_recv()
            self.cores[1].start()

        self.start(2)

        @pl.when(self.z < DEPTH - 1)
        def _():
            self.downs[0].wait_recv()
            self.cores[3].start()

        self.start(3)

    def third(self):
        self.ups[1].wait_recv()
        self.cores[2].start()
        self.start(4, 5)

    def fourth(self):
        @pl.when(self.z == DEPTH - 1)
        def _():
            self.ups[2].wait_recv()
            self.cores[3].start()

        @pl.when(self.z == 0)
        def _():
            self.downs[2].wait_recv()
            self.cores[1].start()

    def end(self, arrivals=True):
        if arrivals:
            for copy in self.cores:
                copy.wait_recv()
            self.local.wait()
        for copy in self.cores:
            copy.wait_send()
        for condition, copy in self.sent:
            pl.when(condition)(copy.wait_send)


def far_first(i, z):
    inner = jnp.where(z == 1, select(i, 2, 1, 3), select(i, 2, 3, 1))
    outer = jnp.where(z == 0, select(i, 1, 2, 3), select(i, 3, 2, 1))
    return jnp.where((z == 0) | (z == DEPTH - 1), outer, inner)


class ChainSum:
    def __init__(self, send, below, above, own, x, core, z, y, sems):
        self.send, self.below, self.above, self.own = send, below, above, own
        self.z = z
        self.up_s, self.down_s, self.below_r, self.above_r = sems
        self.goal_up = (x * 2 + core, (z + 1) * 2 + y)
        self.goal_down = (x * 2 + core, (z - 1) * 2 + y)

    def up(self, slot, number):
        return remote_to(
            self.send.at[slot],
            self.below.at[number],
            self.up_s.at[slot],
            self.below_r.at[number],
            self.goal_up,
        )

    def down(self, slot, number):
        return remote_to(
            self.send.at[slot],
            self.above.at[number],
            self.down_s.at[slot],
            self.above_r.at[number],
            self.goal_down,
        )

    def when(self, z):
        return pl.when(self.z == z)

    def start(self, turn):
        @self.when(0)
        def _():
            self.up(turn, turn).start()

        @self.when(DEPTH - 1)
        def _():
            self.down(turn, turn).start()

    def wait_below(self, number):
        box = self.below.at[number]
        remote_to(box, box, self.up_s.at[0], self.below_r.at[number], self.goal_up).wait_recv()

    def wait_above(self, number):
        box = self.above.at[number]
        remote_to(box, box, self.down_s.at[0], self.above_r.at[number], self.goal_up).wait_recv()

    def add(self, slot, value):
        total = self.send[slot].astype(jnp.float32) + value.astype(jnp.float32)
        self.send[slot] = total.astype(jnp.bfloat16)

    def pass_up(self, slot, number, sent):
        self.wait_below(number)
        self.add(slot, self.below[number])
        self.up(slot, sent).start()

    def pass_down(self, slot, number, sent):
        self.wait_above(number)
        self.add(slot, self.above[number])
        self.down(slot, sent).start()

    def first_hop(self):
        self.when(1)(lambda: self.pass_up(0, 0, 0))
        self.when(DEPTH - 2)(lambda: self.pass_down(0, 0, 0))

    def second_hop(self):
        self.when(1)(lambda: self.pass_up(2, 1, 1))
        self.when(DEPTH - 2)(lambda: self.pass_down(2, 1, 1))

    def third_hop(self):
        self.when(1)(lambda: self.pass_down(1, 0, 0))
        self.when(DEPTH - 2)(lambda: self.pass_up(1, 0, 0))

    def last_hop(self):
        below, above, wide = self.below, self.above, jnp.float32

        @self.when(0)
        def _():
            self.wait_above(0)
            self.own[...] += above[0].astype(wide)

        @self.when(1)
        def _():
            self.wait_below(2)
            self.wait_above(1)
            self.own[...] += below[2].astype(wide) + above[1].astype(wide)

        @self.when(DEPTH - 2)
        def _():
            self.wait_below(1)
            self.wait_above(2)
            self.own[...] += below[1].astype(wide) + above[2].astype(wide)

        @self.when(DEPTH - 1)
        def _():
            self.wait_below(0)
            self.own[...] += below[0].astype(wide)

    def sent_all(self):
        @self.when(0)
        def _():
            for slot in range(DEPTH - 1):
                self.up(slot, slot).wait_send()

        @self.when(DEPTH - 1)
        def _():
            for slot in range(DEPTH - 1):
                self.down(slot, slot).wait_send()

        @self.when(1)
        def _():
            self.up(0, 0).wait_send()
            self.up(2, 1).wait_send()
            self.down(1, 0).wait_send()

        @self.when(DEPTH - 2)
        def _():
            self.down(0, 0).wait_send()
            self.down(2, 1).wait_send()
            self.up(1, 0).wait_send()


def chain_sems():
    dma = pltpu.SemaphoreType.DMA
    return [dma((3,)), dma((3,)), dma((DEPTH,)), dma((DEPTH,)), dma((DEPTH,)), dma(())]


def greet(mates):
    barrier = pltpu.get_barrier_semaphore()
    for mate in mates:
        pl.semaphore_signal(
            barrier, inc=1, device_id=mate, device_id_type=pl.DeviceIdType.MESH
        )
    pl.semaphore_wait(barrier, len(mates))


def coordinates():
    bucket, blk = lax.axis_index("bucket"), lax.axis_index("blk")
    return bucket // 2, bucket % 2, blk // 2, blk % 2


def inward_rows(ref):
    blocks, rows, columns = ref.shape
    return ref[...].reshape(blocks * rows, columns)


def outward_rows(ref):
    blocks, rows, columns = ref.shape
    return ref[:, :HEAD_DIM].reshape(blocks * HEAD_DIM, columns)


def down_rows(ref):
    blocks, rows, columns = ref.shape
    return ref[:, HEAD_DIM:].reshape(blocks * (rows - HEAD_DIM), columns)


def normalised(rows):
    inputs = rows.astype(jnp.float32)
    centred = inputs - jnp.mean(inputs, axis=-1, keepdims=True)
    variance = jnp.mean(centred * centred, axis=-1, keepdims=True)
    inverse = lax.rsqrt(variance + epsilon)
    return centred * inverse, inverse


def turned(values, cos_ref, first_ref, second_ref, sign):
    half = ROT // 2
    cos = jnp.concatenate([cos_ref[0], cos_ref[0]], 0)
    first = jnp.concatenate([first_ref[0], first_ref[0]], 0)
    second = jnp.concatenate([second_ref[0], second_ref[0]], 0)
    ahead = pltpu.roll(values, HEAD_COLS - half, 1)
    behind = pltpu.roll(values, half, 1)
    return values * cos + sign * (ahead * first + behind * second)


def forward_kernel(
    tokens_ref,
    cot_ref,
    inward_ref,
    gate_up_ref,
    outward_ref,
    down_ref,
    valid_ref,
    shares_ref,
    bias_ref,
    frequency_ref,
    pieces,
    normed_out,
    gate_out,
    up_out,
    grads_out,
    wi_out,
    wg_out,
    ro_out,
    q_out,
    kv_out,
    okv_out,
    hidden_out,
    att_out,
    own_out,
    terms_out,
    cos_out,
    first_out,
    second_out,
    gain_out,
    vec_ref,
    wi_own,
    wg_own,
    wi_ref,
    wg_ref,
    rows_ref,
    cos_ref,
    first_ref,
    second_ref,
    gain_ref,
    shift_ref,
    bias_rows,
    own_bias,
    own_grad,
    q_ref,
    kv_ref,
    okv_ref,
    hidden_ref,
    att_ref,
    own_sum,
    terms,
    core_send,
    core_recv,
    group_s,
    group_r,
    across_s,
    across_r,
    rows_s,
    rows_r,
    kv_s,
    kv_r,
    core_s,
    core_r,
    local_sems,
    out_sems,
    *chains,
):
    x, core, z, y = coordinates()
    low, wide = jnp.bfloat16, jnp.float32

    def device(xx, cc, zz, yy):
        return (xx * 2 + cc, zz * 2 + yy)

    def at(xx, cc, zz, yy):
        return ((xx * 2 + cc) * DEPTH + zz) * 2 + yy

    x_mate, y_mate = device(1 - x, core, z, y), device(x, core, z, 1 - y)
    core_mate = device(x, 1 - core, z, y)
    members = [(flip, turn) for turn in (0, 1, 3, 2) for flip in (0, 1)]

    def target(flip, turn):
        return (core + flip) % 2, (z + turn) % DEPTH

    def source(flip, turn):
        return (core + flip) % 2, (z + DEPTH - turn) % DEPTH

    started = []
    written = []

    def begin(copy):
        copy.start()
        started.append(copy)
        return copy

    def write_out(*pairs):
        for src, dst in pairs:
            copy = pltpu.make_async_copy(src, dst, out_sems.at[len(written)])
            copy.start()
            written.append(copy)

    def group_copies(which, own, full):
        mine = at(x, core, z, y)
        copies = {}
        for flip, turn in members[1:]:
            cc, zz = target(flip, turn)
            copies[flip, turn] = remote(
                own.at[cc * DEPTH + zz],
                full.at[mine],
                group_s,
                group_r,
                (which, flip * DEPTH + turn),
                device(x, cc, zz, y),
            )
        return copies

    def vector_copies():
        mine = vec_ref.at[at(x, core, z, y)]
        copies = {}
        for flip, turn in members[1:]:
            copies[flip, turn] = remote(
                mine,
                mine,
                group_s,
                group_r,
                (2, flip * DEPTH + turn),
                device(x, *target(flip, turn), y),
            )
        return copies

    def rows_copies():
        mine = rows_ref.at[x * 2 + y]
        return [
            remote(mine, mine, rows_s, rows_r, way, mate) for way, mate in enumerate((x_mate, y_mate))
        ]

    tokens = Chain(tokens_ref, pieces, x, core, z, y, chains[:6])
    grads = Chain(own_grad, grads_out, x, core, z, y, chains[6:])
    position = lax.broadcasted_iota(jnp.int32, (ROWS // 2, HEAD_COLS), 0)
    lane = lax.broadcasted_iota(jnp.int32, (ROWS // 2, HEAD_COLS), 1) % HEAD_DIM
    half = ROT // 2

    share_lane = lax.broadcasted_iota(jnp.int32, shares_ref.shape, 1)
    share_row = lax.broadcasted_iota(jnp.int32, shares_ref.shape, 0)
    own_shares = jnp.where((share_lane // HEAD_DIM == y) | (share_row >= 2), shares_ref[...], 0.0)

    def prepare(inward_f32, gate_up_f32, outward_f32, down_f32):
        loads = [
            pltpu.make_async_copy(src, dst, local_sems.at[n])
            for n, (src, dst) in enumerate(
                (
                    (inward_ref, inward_f32),
                    (gate_up_ref, gate_up_f32),
                    (outward_ref, outward_f32),
                    (down_ref, down_f32),
                )
            )
        ]
        for load in loads:
            load.start()
        greet([device(x, *target(*m), y) for m in members[1:]] + [x_mate, y_mate])
        tokens.near()
        loads[0].wait()
        vec_ref[at(x, core, z, y)] = own_shares
        for copy in vector_copies().values():
            copy.start()
        pair = 2 * HEAD_DIM
        for n in range(PIECES):
            starts = [part * PIECES * pair + n * pair for part in range(6)]
            line = jnp.concatenate([inward_f32[:, c : c + pair] for c in starts], 1)
            wi_own[n] = line.astype(low)
        wi_ref[at(x, core, z, y)] = wi_own[core * DEPTH + z]
        for copy in group_copies(0, wi_own, wi_ref).values():
            copy.start()
        loads[1].wait()
        each = gate_up_f32.shape[1] // (4 * PIECES)
        for n in range(PIECES):
            starts = [part * PIECES * each + n * each for part in range(4)]
            line = jnp.concatenate([gate_up_f32[:, c : c + each] for c in starts], 1)
            wg_own[n] = line.astype(low)
        wg_ref[at(x, core, z, y)] = wg_own[core * DEPTH + z]
        loads[2].wait()
        loads[3].wait()
        rows_ref[x * 2 + y, :HEAD_DIM] = outward_f32[...].astype(low)
        rows_ref[x * 2 + y, HEAD_DIM:] = down_f32[...].astype(low)

    pl.run_scoped(
        prepare,
        *[
            pltpu.VMEM(r.shape, r.dtype)
            for r in (inward_ref, gate_up_ref, outward_ref, down_ref)
        ],
    )
    inward = group_copies(0, wi_own, wi_ref)
    gate_up = group_copies(1, wg_own, wg_ref)
    vectors = vector_copies()
    started += [*inward.values(), *gate_up.values(), *vectors.values()]

    def spread(which, full, copies, halfway=None):
        pairs = {}
        for member in members:
            if halfway is not None and member == members[HALFWAY]:
                halfway()
            flip, turn = member
            cc, zz = source(flip, turn)
            if member != (0, 0):
                copies[member].wait_recv()
            block = full.at[at(x, cc, zz, y)]
            number = flip * DEPTH + turn
            pairs[member] = tuple(
                begin(remote(block, block, across_s, across_r, (which, way, number), mate))
                for way, mate in enumerate((x_mate, y_mate))
            )
        return pairs

    def by_x(which, flip):
        return which != 1 or flip == 0

    def corner(which, full, pairs):
        copies = []
        for member in members:
            flip, turn = member
            cc, zz = source(flip, turn)
            number = flip * DEPTH + turn
            if by_x(which, flip):
                pairs[member][1].wait_recv()
                block, mate = full.at[at(x, cc, zz, 1 - y)], x_mate
            else:
                pairs[member][0].wait_recv()
                block, mate = full.at[at(1 - x, cc, zz, y)], y_mate
            copies.append(
                begin(remote(block, block, across_s, across_r, (which, 2, number), mate))
            )
        return copies

    def complete(which, pairs, copies):
        for flip, turn in members:
            pairs[flip, turn][0 if by_x(which, flip) else 1].wait_recv()
        for copy in copies:
            copy.wait_recv()

    frequency = frequency_ref[...]
    for k in range(DEPTH):
        first = (2 * lax.rem(z + DEPTH - k, DEPTH) + y) * (ROWS // 2)
        angles = (first + position).astype(wide) * frequency
        sine = jnp.sin(angles)
        cos_ref[k] = jnp.cos(angles)
        first_ref[k] = jnp.where(lane < half, -sine, 0.0)
        second_ref[k] = jnp.where((lane >= half) & (lane < ROT), sine, 0.0)
    own_grad[...] = (cot_ref[...].astype(wide) * valid_ref[...]).astype(low)
    write_out((cos_ref, cos_out), (first_ref, first_out), (second_ref, second_out))

    vector_pairs = spread(2, vec_ref, vectors)
    inward_pairs = spread(0, wi_ref, inward)
    for copy in gate_up.values():
        copy.start()
    vector_corner = corner(2, vec_ref, vector_pairs)
    inward_corner = corner(0, wi_ref, inward_pairs)
    gate_up_pairs = spread(1, wg_ref, gate_up, tokens.first)
    complete(2, vector_pairs, vector_corner)
    complete(0, inward_pairs, inward_corner)
    write_out((wi_ref, wi_out))

    shares = vec_ref[...].astype(low).astype(wide)
    for row, vector in ((0, gain_ref), (1, shift_ref)):
        line = shares[:, row]
        vector[...] = jnp.concatenate(
            [line[2 * i : 2 * i + 1] + line[2 * i + 1 : 2 * i + 2] for i in range(16)], 1
        )
    each = bias_ref.shape[1]
    biases = jnp.concatenate([shares[:, 2], shares[:, 3]], 1)
    flat = jnp.concatenate([biases[i : i + 1, :each] for i in range(32)], 1)
    for i in range(flat.shape[1] // 128):
        bias_rows[i : i + 1] = flat[:, i * 128 : (i + 1) * 128]
    query_bias, key_bias, value_bias = [], [], []
    gap = jnp.zeros((1, HEAD_DIM - ROT), wide)
    for i in range(2):
        row = i * PIECES + core * DEPTH + z
        query_bias.append(bias_rows[pl.ds(row, 1)])
        value_bias.append(bias_rows[pl.ds(2 * PIECES + row, 1)])
        line = bias_rows[pl.ds(4 * PIECES + i * 2 + core, 1)]
        heads = [line[:, 2 * ROT * j : 2 * ROT * (j + 1)] for j in range(DEPTH)]
        chosen = jnp.where(
            z == 0, heads[0], jnp.where(z == 1, heads[1], jnp.where(z == 2, heads[2], heads[3]))
        )
        key_bias += [chosen[:, :ROT], gap, chosen[:, ROT:], gap]
    own_bias[...] = jnp.concatenate(query_bias + key_bias + value_bias, 1)
    write_out((gain_ref, gain_out))

    def pair_copy(piece):
        return remote(kv_ref.at[piece], okv_ref.at[piece], kv_s, kv_r, piece, y_mate)

    def project(piece, tokens_part, normed):
        k = lax.rem(piece, DEPTH)
        hat, _ = normalised(tokens_part[0])
        narrow = (hat * gain_ref[...] + shift_ref[...]).astype(low)
        normed[0] = narrow
        projected = dot_rows(narrow, inward_rows(wi_ref)) + own_bias[...]
        tables = (cos_ref.at[pl.ds(k, 1)], first_ref.at[pl.ds(k, 1)], second_ref.at[pl.ds(k, 1)])
        query = turned(projected[:, :HEAD_COLS], *tables, 1.0) * (HEAD_DIM**-0.5)
        key = turned(projected[:, HEAD_COLS : 2 * HEAD_COLS], *tables, 1.0)
        kv_ref[piece] = jnp.concatenate([key, projected[:, 2 * HEAD_COLS :]], 1).astype(low)
        pair_copy(piece).start()
        q_ref[piece] = query.astype(low)

    def piece_at(first, i):
        turn = first + i // 2
        near = jnp.where(z == 0, DEPTH - 1, 1)
        k = jnp.where(
            turn == 0, 0, jnp.where(turn == 1, near, jnp.where(turn == 2, 2, DEPTH - near))
        )
        return k + DEPTH * (i % 2)

    def project_pieces(first, count):
        spec = pl.BlockSpec((1,) + pieces.shape[1:], lambda i: (piece_at(first, i), 0, 0))
        pltpu.emit_pipeline(
            lambda *refs: project(piece_at(first, pl.program_id(0)), *refs),
            grid=(2 * count,),
            in_specs=[spec],
            out_specs=[spec],
        )(pieces, normed_out)

    def feed(first, count):
        def body(normed, gate_part, up_part):
            piece = piece_at(first, pl.program_id(0))
            both = dot_rows(normed[0], wg_ref[...].reshape(normed.shape[2], wg_ref.shape[2]))
            hidden = both.shape[1] // 2
            gate, up = both[:, :hidden], both[:, hidden:]
            gate_part[0] = gate
            up_part[0] = up
            hidden_ref[piece] = (gate * jax.nn.sigmoid(gate) * up).astype(low)

        def spec(array):
            return pl.BlockSpec(
                (1,) + array.shape[1:], lambda i: (piece_at(first, i), 0, 0)
            )

        pltpu.emit_pipeline(
            body,
            grid=(2 * count,),
            in_specs=[spec(normed_out)],
            out_specs=[spec(gate_out), spec(up_out)],
        )(normed_out, gate_out, up_out)

    near = jnp.where(z == 0, DEPTH - 1, 1)
    far = DEPTH - near

    def core_arrived(k):
        remote(pieces.at[k], pieces.at[DEPTH + k], chains[3], chains[4], k, core_mate).wait_recv()

    tokens.local.wait()
    core_arrived(0)
    project_pieces(0, 1)
    tokens.second()
    core_arrived(near)
    project_pieces(1, 1)
    gate_up_corner = corner(1, wg_ref, gate_up_pairs)
    rows_x, rows_y = rows_copies()
    begin(rows_x)
    begin(rows_y)
    tokens.third()
    core_arrived(2)
    project_pieces(2, 1)
    complete(1, gate_up_pairs, gate_up_corner)
    feed(0, 2)
    tokens.fourth()
    grads.near()
    grads.first()
    core_arrived(far)
    project_pieces(3, 1)
    rows_y.wait_recv()
    block = rows_ref.at[x * 2 + 1 - y]
    rows_corner = begin(remote(block, block, rows_s, rows_r, 2, x_mate))
    feed(2, 2)
    grads.second()
    write_out((q_ref, q_out), (kv_ref, kv_out), (wg_ref, wg_out))

    for b in range(2):
        for j in range(DEPTH):
            pair_copy(b * DEPTH + j).wait_recv()

        def attend(t, carry):
            attend_one(Heads(b, t, z, y, q_ref, kv_ref, okv_ref), att_ref)
            return carry

        lax.fori_loop(0, LOCAL_HEADS, attend, 0)

    rows_x.wait_recv()
    rows_corner.wait_recv()
    write_out((hidden_ref, hidden_out), (att_ref, att_out), (okv_ref, okv_out), (rows_ref, ro_out))

    def core_copy(k):
        return remote(core_send.at[k % 2], core_recv.at[k], core_s, core_r, k, core_mate)

    def term(piece):
        return dot_rows(att_ref[piece], outward_rows(rows_ref)) + dot_rows(
            hidden_ref[piece], down_rows(rows_ref)
        )

    def branch(i, carry):
        k = far_first(i, z)

        @pl.when(i >= 2)
        def _():
            core_copy(i - 2).wait_send()

        core_send[i % 2] = term(DEPTH + k).astype(low)
        core_copy(i).start()
        own = term(k)
        core_copy(i).wait_recv()
        both = own + core_recv[i].astype(wide)

        @pl.when(i < DEPTH - 1)
        def _():
            terms[i] = both.astype(low)

        @pl.when(i == DEPTH - 1)
        def _():
            own_sum[...] = both

        return carry

    grads.third()
    lax.fori_loop(0, DEPTH, branch, 0)
    write_out((own_sum, own_out), (terms, terms_out))
    grads.fourth()
    grads.end()
    tokens.end(False)
    for i in range(DEPTH - 2, DEPTH):
        core_copy(i).wait_send()
    for piece in range(PIECES):
        pair_copy(piece).wait_send()
    for copy in started:
        copy.wait_send()
    for copy in written:
        copy.wait()


def forward(
    tokens, cot, inward, gate_up, outward, down, valid, shares, bias, frequency
):
    low, wide = jnp.bfloat16, jnp.float32
    rows, width = tokens.shape
    own_rows = inward.shape[0]
    group_columns = gate_up.shape[1] // PIECES
    hidden = group_columns // 2
    anywhere = pl.BlockSpec(memory_space=pl.ANY)
    inside = pl.BlockSpec(memory_space=pltpu.VMEM)
    shape = jax.ShapeDtypeStruct
    dma = pltpu.SemaphoreType.DMA
    wi_shape = shape((32, own_rows, 3 * HEAD_COLS), low)
    wg_shape = shape((32, own_rows, group_columns), low)
    ro_shape = shape((4, outward.shape[0] + down.shape[0], width), low)
    table = shape((DEPTH, ROWS // 2, HEAD_COLS), wide)
    heads = shape((PIECES, ROWS, HEAD_COLS), low)
    pairs = shape((PIECES, ROWS, 2 * HEAD_COLS), low)
    hidden_shape = shape((PIECES, ROWS, hidden), low)
    own_shape = shape((ROWS, width), wide)
    terms_shape = shape((DEPTH - 1, ROWS, width), low)
    vector = shape((1, width), wide)

    def scratch(*shapes):
        return [pltpu.VMEM(s.shape, s.dtype) for s in shapes]

    return pl.pallas_call(
        forward_kernel,
        in_specs=[anywhere] + [inside] + [anywhere] * 4 + [inside] * 4,
        out_specs=[anywhere] * 19,
        out_shape=[
            shape((PIECES, ROWS, width), low),
            shape((PIECES, ROWS, width), low),
            shape((PIECES, ROWS, hidden), wide),
            shape((PIECES, ROWS, hidden), wide),
            shape((PIECES, ROWS, width), low),
            wi_shape,
            wg_shape,
            ro_shape,
            heads,
            pairs,
            pairs,
            hidden_shape,
            heads,
            own_shape,
            terms_shape,
            table,
            table,
            table,
            vector,
        ],
        scratch_shapes=scratch(
            shape((32, 8, 128), wide),
            shape((PIECES,) + wi_shape.shape[1:], low),
            shape((PIECES,) + wg_shape.shape[1:], low),
            wi_shape,
            wg_shape,
            ro_shape,
            table,
            table,
            table,
            vector,
            vector,
            shape((40, 128), wide),
            shape((1, 3 * HEAD_COLS), wide),
            shape((ROWS, width), low),
            heads,
            pairs,
            pairs,
            hidden_shape,
            heads,
            own_shape,
            terms_shape,
            shape((2, ROWS, width), low),
            shape((DEPTH, ROWS, width), low),
        )
        + [
            dma((3, PIECES)),
            dma((3, PIECES)),
            dma((3, 3, PIECES)),
            dma((3, 3, PIECES)),
            dma((4,)),
            dma((4,)),
            dma((PIECES,)),
            dma((PIECES,)),
            dma((DEPTH,)),
            dma((DEPTH,)),
            dma((4,)),
            dma((14,)),
        ]
        + chain_sems()
        + chain_sems(),
        compiler_params=params(62, collective_id=0, has_side_effects=True),
        cost_estimate=cost(0, 64 * MIB),
        name="forward",
    )(tokens, cot, inward, gate_up, outward, down, valid, shares, bias, frequency)


def pair_rows(block):
    lane = lax.broadcasted_iota(jnp.int32, block.shape, 1)
    zero = jnp.zeros_like(block)
    return jnp.concatenate(
        [jnp.where(lane < HEAD_DIM, block, zero), jnp.where(lane < HEAD_DIM, zero, block)], 0
    )


def pair_lanes(rows):
    half = rows.shape[0] // 2
    lane = lax.broadcasted_iota(jnp.int32, (half, rows.shape[1]), 1)
    return jnp.where(lane < HEAD_DIM, rows[:half], rows[half:])


def block_probs(queries, keys, last, y):
    scores = transposed_times(queries, keys)
    rows, columns = scores.shape
    size = rows // 2
    row = lax.broadcasted_iota(jnp.int32, (rows, 2 * size), 0) % size
    column = lax.broadcasted_iota(jnp.int32, (rows, 2 * size), 1)
    allowed = (column <= row) | ((column >= size) & (y == 1))
    tail = jnp.where(allowed, scores[:, last * 2 * size :], masked_score)
    scores = tail if last == 0 else jnp.concatenate([scores[:, : last * 2 * size], tail], 1)
    weights = jnp.exp(scores - jnp.max(scores, axis=-1, keepdims=True))
    return weights * (1.0 / jnp.sum(weights, axis=-1, keepdims=True))


class Heads:
    def __init__(self, b, t, z, y, q_ref, kv_ref, okv_ref):
        size = ROWS // 2
        pair = 2 * HEAD_DIM
        self.b, self.z, self.y = b, z, y
        self.rows = pl.ds(pl.multiple_of((t // 2) * size, size), size)
        self.lanes = pl.ds(pl.multiple_of((t % 2) * pair, pair), pair)
        value_lanes = pl.ds(pl.multiple_of(HEAD_COLS + (t % 2) * pair, pair), pair)
        self.q_ref = q_ref

        def both(lanes):
            blocks = []
            for j in range(DEPTH):
                place = (self.piece(j), self.rows, lanes)
                blocks += [kv_ref[place], okv_ref[place]]
            return jnp.concatenate(blocks, 0)

        self.keys, self.values = both(self.lanes), both(value_lanes)

    def piece(self, j):
        return self.b * DEPTH + lax.rem(self.z + DEPTH - j, DEPTH)

    def place(self, j):
        return self.piece(j), self.rows, self.lanes

    def queries(self, j):
        return pair_rows(self.q_ref[self.place(j)])


def attend_one(heads, out_ref):
    for j in range(DEPTH):
        count = (j + 1) * ROWS
        probs = block_probs(heads.queries(j), heads.keys[:count], j, heads.y)
        out = dot_rows(probs.astype(jnp.bfloat16), heads.values[:count])
        out_ref[heads.place(j)] = pair_lanes(out).astype(jnp.bfloat16)


def attend_back_one(heads, grad_ref, dq_ref, dk_ref, dv_ref, odk_ref, odv_ref, key_sum, value_sum):
    half = ROWS // 2
    for j in reversed(range(DEPTH)):
        count = (j + 1) * ROWS
        queries = heads.queries(j)
        grads = pair_rows(grad_ref[heads.place(j)])
        keys, values = heads.keys[:count], heads.values[:count]
        probs = block_probs(queries, keys, j, heads.y)
        low = probs.astype(jnp.bfloat16)
        prob_grad = transposed_times(grads, values)
        delta = jnp.sum(low.astype(jnp.float32) * prob_grad, axis=-1, keepdims=True)
        score_grad = (probs * (prob_grad - delta)).astype(jnp.bfloat16)
        dq_ref[heads.place(j)] = pair_lanes(dot_rows(score_grad, keys))
        key_term = times_transposed(score_grad, queries)
        value_term = times_transposed(low, grads)
        if j == DEPTH - 1:
            key_sum[...] = key_term
            value_sum[...] = value_term
        else:
            key_sum[:count] += key_term
            value_sum[:count] += value_term
    for j in range(DEPTH):
        low = j * ROWS
        place = heads.place(j)
        dk_ref[place] = key_sum[low : low + half]
        dv_ref[place] = value_sum[low : low + half]
        odk_ref[place] = key_sum[low + half : low + ROWS].astype(jnp.bfloat16)
        odv_ref[place] = value_sum[low + half : low + ROWS].astype(jnp.bfloat16)


def backward_kernel(
    grads_ref,
    gate_ref,
    up_ref,
    normed_ref,
    pieces_ref,
    q_in,
    kv_in,
    okv_in,
    rows_in,
    own_in,
    terms_in,
    valid_ref,
    gate_xs,
    gate_xk,
    gate_ys,
    gate_yk,
    gate_xr,
    gate_yr,
    gate_y2s,
    gate_x2s,
    gate_own_x,
    gate_own_y,
    gu_out,
    dq_out,
    dk_out,
    dv_out,
    got_dk,
    got_dv,
    layer_out,
    q_ref,
    kv_ref,
    okv_ref,
    rows_ref,
    own_sum,
    terms,
    gu_ref,
    dq_ref,
    dk_ref,
    dv_ref,
    attended_grad,
    odk_ref,
    odv_ref,
    key_sum,
    value_sum,
    below,
    above,
    token_rows,
    up_s,
    down_s,
    below_r,
    above_r,
    pair_s,
    pair_r,
    stage_s,
    stage_r,
    load_sems,
    out_sems,
):
    x, core, z, y = coordinates()
    low, wide = jnp.bfloat16, jnp.float32
    y_mate = (x * 2 + core, z * 2 + 1 - y)

    x_mate = (2 - x * 2 + core, z * 2 + y)
    loads = {}
    for src, dst in (
        (terms_in, terms),
        (rows_in, rows_ref),
        (q_in, q_ref),
        (kv_in, kv_ref),
        (okv_in, okv_ref),
        (own_in, own_sum),
        (pieces_ref.at[0], token_rows),
    ):
        load = pltpu.make_async_copy(src, dst, load_sems.at[len(loads)])
        load.start()
        loads[len(loads)] = load
    written = []

    def write_out(*pairs):
        for src, dst in pairs:
            copy = pltpu.make_async_copy(src, dst, out_sems.at[len(written)])
            copy.start()
            written.append(copy)

    below_mate = (x * 2 + core, lax.rem(z + DEPTH - 1, DEPTH) * 2 + y)
    above_mate = (x * 2 + core, lax.rem(z + 1, DEPTH) * 2 + y)
    greet([x_mate, y_mate, below_mate, above_mate])
    sums = ChainSum(terms, below, above, own_sum, x, core, z, y, (up_s, down_s, below_r, above_r))
    loads[0].wait()
    for turn in range(DEPTH - 1):
        sums.start(turn)
    loads[1].wait()

    def piece_body(grad_part, gate_part, up_part):
        piece = pl.program_id(0)
        grad = grad_part[0]
        attended_grad[piece] = transposed_times(grad, outward_rows(rows_ref)).astype(low)
        hidden_grad = transposed_times(grad, down_rows(rows_ref))
        gate = gate_part[0]
        sig = jax.nn.sigmoid(gate)
        silu = gate * sig
        gate_grad = hidden_grad * up_part[0] * (sig + silu * (1.0 - sig))
        up_grad = hidden_grad * silu
        gu_ref[piece] = jnp.concatenate([gate_grad, up_grad], 1).astype(low)

    pltpu.emit_pipeline(
        piece_body,
        grid=(PIECES,),
        in_specs=[piece_spec(r.shape[-1]) for r in (grads_ref, gate_ref, up_ref)],
    )(grads_ref, gate_ref, up_ref)

    write_out((gu_ref, gu_out))
    total, width = normed_ref.shape
    size = width // PIECES
    columns = gu_ref.shape[-1]
    cut = gate_xs.shape[-1]

    def right(first, last):
        return gu_ref[...].reshape(total, columns)[:, first:last]

    def whole_body(left, out):
        term = times_transposed(left[...], right(0, cut)).astype(out.dtype)
        out[...] = term.reshape(out.shape)

    def split_body(left, keep, send):
        split_rows(times_transposed(left[...], right(cut, columns)), y, keep, send)

    def from_block(base):
        return pl.BlockSpec((total, size), lambda i: (0, base + i))

    def block_of(array):
        return pl.BlockSpec((2,) + array.shape[1:], lambda i: (i,) + (0,) * (len(array.shape) - 1))

    pltpu.emit_pipeline(
        whole_body,
        grid=(DEPTH,),
        in_specs=[from_block((1 - x) * DEPTH)],
        out_specs=[block_of(gate_xs)],
    )(normed_ref, gate_xs)
    gate_x = remote(gate_xs, gate_xr, stage_s, stage_r, 0, x_mate)
    gate_x.start()
    sums.first_hop()
    for n in (2, 3, 4):
        loads[n].wait()

    def pair_copies(b, t):
        size, pair = ROWS // 2, 2 * HEAD_DIM
        at = (
            pl.ds(b * DEPTH, DEPTH),
            pl.ds(pl.multiple_of((t // 2) * size, size), size),
            pl.ds(pl.multiple_of((t % 2) * pair, pair), pair),
        )
        number = b * DEPTH + t
        return (
            remote(odk_ref.at[at], got_dk.at[at], pair_s, pair_r, (0, number), y_mate),
            remote(odv_ref.at[at], got_dv.at[at], pair_s, pair_r, (1, number), y_mate),
        )

    def attend_back(i, carry):
        b, t = i // DEPTH, i % DEPTH
        heads = Heads(b, t, z, y, q_ref, kv_ref, okv_ref)
        attend_back_one(
            heads, attended_grad, dq_ref, dk_ref, dv_ref, odk_ref, odv_ref, key_sum, value_sum
        )
        for copy in pair_copies(b, t):
            copy.start()
        return carry

    lax.fori_loop(0, PIECES, attend_back, 0)

    write_out((dq_ref, dq_out), (dk_ref, dk_out), (dv_ref, dv_out))
    sums.second_hop()
    sums.third_hop()

    pltpu.emit_pipeline(
        split_body,
        grid=(PIECES,),
        in_specs=[from_block(0)],
        out_specs=[block_of(gate_yk), block_of(gate_ys)],
    )(normed_ref, gate_yk, gate_ys)
    gate_y = remote(gate_ys, gate_yr, stage_s, stage_r, 1, y_mate)
    gate_y.start()

    pltpu.emit_pipeline(
        whole_body,
        grid=(DEPTH,),
        in_specs=[from_block(x * DEPTH)],
        out_specs=[block_of(gate_xk)],
    )(normed_ref, gate_xk)

    loads[5].wait()
    loads[6].wait()
    sums.last_hop()
    for first in range(0, ROWS, 64):
        rows = pl.ds(first, 64)
        layer = token_rows[rows].astype(wide) + valid_ref[rows] * own_sum[rows]
        layer_out[rows] = layer.astype(low)

    def sums_body(xk, xr, yk, yr, yk_own, yr_own, y2s, x2s, own_x, own_y):
        y2s[...] = (xk[:, 1 - y] + xr[:, 1 - y].astype(wide)).astype(low)
        own_x[...] = xk[:, y] + xr[:, y].astype(wide)
        x2s[...] = (yk[...] + yr[...].astype(wide)).astype(low)
        own_y[...] = yk_own[...] + yr_own[...].astype(wide)

    def two_blocks(array, base=0):
        return pl.BlockSpec(
            (2,) + array.shape[1:], lambda i: (base + i,) + (0,) * (len(array.shape) - 1)
        )

    gate_x.wait_recv()
    gate_y.wait_recv()
    theirs, ours = (1 - x) * DEPTH, x * DEPTH
    pltpu.emit_pipeline(
        sums_body,
        grid=(DEPTH,),
        in_specs=[
            two_blocks(gate_xk),
            two_blocks(gate_xr),
            two_blocks(gate_yk, theirs),
            two_blocks(gate_yr, theirs),
            two_blocks(gate_yk, ours),
            two_blocks(gate_yr, ours),
        ],
        out_specs=[two_blocks(r) for r in (gate_y2s, gate_x2s, gate_own_x, gate_own_y)],
    )(
        gate_xk,
        gate_xr,
        gate_yk,
        gate_yr,
        gate_yk,
        gate_yr,
        gate_y2s,
        gate_x2s,
        gate_own_x,
        gate_own_y,
    )
    for b in range(2):
        for t in range(DEPTH):
            for copy in pair_copies(b, t):
                copy.wait_recv()
                copy.wait_send()
    sums.sent_all()
    for copy in written:
        copy.wait()
    for copy in (gate_x, gate_y):
        copy.wait_send()


def backward(
    grads, gate, up, normed, pieces, queries, pairs, other_pairs, rows_out, own_sum, terms, valid
):
    low, wide = jnp.bfloat16, jnp.float32
    width = pieces.shape[-1]
    columns = 2 * gate.shape[-1]
    cut = columns - 128
    rows = width // 32
    anywhere = pl.BlockSpec(memory_space=pl.ANY)
    inside = pl.BlockSpec(memory_space=pltpu.VMEM)
    shape = jax.ShapeDtypeStruct
    dma = pltpu.SemaphoreType.DMA
    heads = shape((PIECES, ROWS, HEAD_COLS), wide)
    heads_low = shape((PIECES, ROWS, HEAD_COLS), low)
    gate_up = shape((PIECES, ROWS, columns), low)
    part = shape((DEPTH - 1, ROWS, width), low)
    half = shape((DEPTH * ROWS, 2 * HEAD_DIM), wide)
    return pl.pallas_call(
        backward_kernel,
        in_specs=[anywhere] * 11 + [inside],
        out_specs=[anywhere] * 16 + [inside],
        out_shape=[
            shape((PIECES, 2, rows, cut), low),
            shape((PIECES, 2, rows, cut), wide),
            shape((2 * PIECES, rows, columns - cut), low),
            shape((2 * PIECES, rows, columns - cut), wide),
            shape((PIECES, 2, rows, cut), low),
            shape((2 * PIECES, rows, columns - cut), low),
            shape((PIECES, rows, cut), low),
            shape((PIECES, rows, columns - cut), low),
            shape((PIECES, rows, cut), wide),
            shape((PIECES, rows, columns - cut), wide),
            gate_up,
            heads,
            heads,
            heads,
            heads_low,
            heads_low,
            shape((ROWS, width), low),
        ],
        scratch_shapes=[
            pltpu.VMEM(v.shape, v.dtype)
            for v in (
                queries,
                pairs,
                other_pairs,
                rows_out,
                own_sum,
                terms,
                gate_up,
                heads,
                heads,
                heads,
                heads_low,
                heads_low,
                heads_low,
                half,
                half,
                part,
                part,
                shape((ROWS, width), low),
            )
        ]
        + [
            dma((DEPTH - 1,)),
            dma((DEPTH - 1,)),
            dma((DEPTH - 1,)),
            dma((DEPTH - 1,)),
            dma((2, PIECES)),
            dma((2, PIECES)),
            dma((2,)),
            dma((2,)),
            dma((7,)),
            dma((4,)),
        ],
        compiler_params=params(62, collective_id=3, has_side_effects=True),
        cost_estimate=cost(0, 64 * MIB),
        name="backward",
    )(grads, gate, up, normed, pieces, queries, pairs, other_pairs, rows_out, own_sum, terms, valid)


def finish_kernel(
    dq_ref,
    dk_ref,
    dv_ref,
    odk_ref,
    odv_ref,
    gu_ref,
    pieces_ref,
    cos_ref,
    first_ref,
    second_ref,
    normed_ref,
    gate_y2s,
    gate_x2s,
    gate_sum_x,
    gate_sum_y,
    grads_ref,
    hidden_ref,
    att_ref,
    wi_ref,
    wg_ref,
    gain_ref,
    cot_ref,
    tokens_out,
    heads_out,
    hidden_out,
    gate_rows,
    inward_rows_out,
    vec_out,
    heads_term,
    hidden_term,
    heads_r,
    heads_2s,
    heads_2r,
    hidden_r,
    hidden_2s,
    hidden_2r,
    core_send,
    core_recv,
    z_send,
    below,
    above,
    own_sum,
    pg_ref,
    token_rows,
    vec_sum,
    vec_x,
    vec_y,
    gate_own_x,
    gate_own_y,
    gate_y2r,
    gate_x2r,
    gate_fin,
    inward_xs,
    inward_xr,
    inward_xk,
    inward_ys,
    inward_yr,
    inward_yk,
    inward_y2s,
    inward_y2r,
    inward_x2s,
    inward_x2r,
    inward_fin,
    core_s,
    core_r,
    up_s,
    down_s,
    below_r,
    above_r,
    stage_s,
    stage_r,
    rows_s,
    rows_r,
    vec_s,
    vec_r,
    local_sems,
):
    x, core, z, y = coordinates()
    low = jnp.bfloat16
    wide = jnp.float32

    def device(xx, cc, zz, yy):
        return (xx * 2 + cc, zz * 2 + yy)

    x_mate, y_mate = device(1 - x, core, z, y), device(x, core, z, 1 - y)
    core_mate = device(x, 1 - core, z, y)
    members = [(flip, turn) for turn in (2, 1, 3, 0) for flip in (1, 0)][:-1]

    def target(flip, turn):
        return (core + flip) % 2, (z + turn) % DEPTH

    greet([device(x, *target(*m), y) for m in members] + [x_mate, y_mate])

    started = []

    def begin(copy):
        copy.start()
        started.append(copy)
        return copy

    loads = [
        pltpu.make_async_copy(gate_sum_x, gate_own_x, local_sems.at[2]),
        pltpu.make_async_copy(gate_sum_y, gate_own_y, local_sems.at[3]),
    ]
    for load in loads:
        load.start()
    gate_y = begin(remote(gate_y2s, gate_y2r, stage_s, stage_r, (0, 2), y_mate))
    gate_x = begin(remote(gate_x2s, gate_x2r, stage_s, stage_r, (0, 3), x_mate))
    own_tokens = pltpu.make_async_copy(pieces_ref.at[0], token_rows, local_sems.at[4])
    own_tokens.start()

    vec_sum[...] = jnp.zeros_like(vec_sum)

    def core_copy(k):
        return remote(core_send.at[k % 2], core_recv.at[k], core_s, core_r, k, core_mate)

    sums = ChainSum(
        z_send, below, above, own_sum, x, core, z, y, (up_s, down_s, below_r, above_r)
    )

    def piece_of(i):
        return far_first(i // 2, z) + DEPTH * (1 - i % 2)

    def to_rows(which, fin, rows):
        slot = core * DEPTH + z
        copies = []
        for flip, turn in members:
            cc, zz = target(flip, turn)
            copies.append(
                remote(
                    fin.at[cc * DEPTH + zz],
                    rows.at[slot],
                    rows_s,
                    rows_r,
                    (which, flip * DEPTH + turn),
                    device(x, cc, zz, y),
                )
            )
        copies.append(pltpu.make_async_copy(fin.at[slot], rows.at[slot], local_sems.at[which]))
        return copies

    def gate_done():
        gate_y.wait_recv()
        gate_x.wait_recv()
        for load in loads:
            load.wait()
        gate_fin[...] = jnp.concatenate(
            [
                gate_own_x[...] + gate_y2r[...].astype(wide),
                gate_own_y[...] + gate_x2r[...].astype(wide),
            ],
            2,
        ).astype(low)
        for copy in to_rows(0, gate_fin, gate_rows):
            copy.start()

    def piece_body(
        dq, dk, dv, odk, odv, gu, tokens, cos, first, second
    ):
        step = pl.program_id(0)
        turn = step // 2
        piece = piece_of(step)
        tables = (cos, first, second)
        query = turned(dq[0] * (HEAD_DIM**-0.5), *tables, -1.0)
        key = turned(dk[0] + odk[0].astype(wide), *tables, -1.0)
        value = dv[0] + odv[0].astype(wide)
        narrow = jnp.concatenate([query, key, value], 1).astype(low)
        pg_ref[piece] = narrow
        grad = transposed_times(narrow, inward_rows(wi_ref))
        grad += transposed_times(gu[0], wg_ref[...])
        hat, _ = normalised(tokens[0])
        half = grad.shape[1] // 2
        for row, total in (
            (0, jnp.sum(grad * hat, axis=0, keepdims=True)),
            (2, jnp.sum(grad, axis=0, keepdims=True)),
        ):
            vec_sum[row : row + 1] += total[:, :half]
            vec_sum[row + 1 : row + 2] += total[:, half:]
        vec_sum[4:5, : 3 * HEAD_COLS] += jnp.sum(narrow.astype(wide), axis=0, keepdims=True)

        pl.when(step == GATE_STEP)(gate_done)
        pl.when(step == PIECES - 1)(sums.first_hop)

        @pl.when(step % 2 == 0)
        def _():
            @pl.when(turn >= 2)
            def _():
                core_copy(turn - 2).wait_send()

            core_send[turn % 2] = grad.astype(low)
            core_copy(turn).start()

        @pl.when(step % 2 == 1)
        def _():
            core_copy(turn).wait_recv()
            both = grad + core_recv[turn].astype(wide)

            @pl.when(turn < DEPTH - 1)
            def _():
                z_send[turn] = both.astype(low)
                sums.start(turn)

            @pl.when(turn == DEPTH - 1)
            def _():
                own_sum[...] = both

    def by_piece(width):
        return pl.BlockSpec((1, ROWS, width), lambda i: (piece_of(i), 0, 0))

    table_spec = pl.BlockSpec(
        (1,) + cos_ref.shape[1:], lambda i: (piece_of(i) % DEPTH, 0, 0)
    )
    pltpu.emit_pipeline(
        piece_body,
        grid=(PIECES,),
        in_specs=[by_piece(HEAD_COLS)] * 5
        + [by_piece(gu_ref.shape[-1]), by_piece(pieces_ref.shape[-1])]
        + [table_spec] * 3,
    )(
        dq_ref,
        dk_ref,
        dv_ref,
        odk_ref,
        odv_ref,
        gu_ref,
        pieces_ref,
        cos_ref,
        first_ref,
        second_ref,
    )
    vector_x = remote(vec_sum, vec_x, vec_s, vec_r, 0, x_mate)
    vector_x.start()

    total, width = normed_ref.shape
    size = width // PIECES
    cut = 3 * HEAD_COLS // 2

    def block(i):
        return jnp.where(i < DEPTH, (1 - x) * DEPTH + i, x * DEPTH + i - DEPTH)

    inward_x = remote(inward_xs, inward_xr, stage_s, stage_r, (1, 0), x_mate)

    def inward_body(left):
        i = pl.program_id(0)
        rhs = pg_ref[...].reshape(total, 3 * HEAD_COLS)
        term = times_transposed(left[...], rhs)
        first = term[:, :cut].reshape(2, 2, size // 4, cut)
        at = pl.ds((i % DEPTH) * 2, 2)

        @pl.when(i < DEPTH)
        def _():
            inward_xs[at] = first.astype(low)

        @pl.when(i >= DEPTH)
        def _():
            inward_xk[at] = first

        at = pl.ds(block(i) * 2, 2)
        split_rows(term[:, cut:], y, inward_yk.at[at], inward_ys.at[at])

        @pl.when(i == DEPTH - 1)
        def _():
            inward_x.start()

    pltpu.emit_pipeline(
        inward_body,
        grid=(PIECES,),
        in_specs=[pl.BlockSpec((total, size), lambda i: (0, block(i)))],
    )(normed_ref)
    started.append(inward_x)
    inward_y = begin(remote(inward_ys, inward_yr, stage_s, stage_r, (1, 1), y_mate))

    def rows_grads(att, hidden):
        loads = [
            pltpu.make_async_copy(att_ref, att, local_sems.at[5]),
            pltpu.make_async_copy(hidden_ref, hidden, local_sems.at[6]),
        ]
        for load in loads:
            load.start()
        for load in loads:
            load.wait()

        def body(right, heads_part, hidden_part):
            grad = right[...]
            term = times_transposed(att[...].reshape(total, att.shape[2]), grad)
            heads_part[...] = term.astype(low).reshape(heads_part.shape)
            term = times_transposed(hidden[...].reshape(total, hidden.shape[2]), grad)
            hidden_part[...] = term.astype(low).reshape(hidden_part.shape)

        def columns_of(array):
            return pl.BlockSpec(array.shape[:3] + (2 * size,), lambda i: (0, 0, 0, i))

        pltpu.emit_pipeline(
            body,
            grid=(width // (2 * size),),
            in_specs=[pl.BlockSpec((total, 2 * size), lambda i: (0, i))],
            out_specs=[columns_of(heads_term), columns_of(hidden_term)],
        )(grads_ref, heads_term, hidden_term)

    sums.second_hop()
    pl.run_scoped(
        rows_grads, *[pltpu.VMEM(r.shape, r.dtype) for r in (att_ref, hidden_ref)]
    )
    inward_x.wait_recv()
    inward_y2s[...] = (inward_xk[:, 1 - y] + inward_xr[:, 1 - y].astype(wide)).astype(low)
    inward_over_y = begin(remote(inward_y2s, inward_y2r, stage_s, stage_r, (1, 2), y_mate))
    inward_y.wait_recv()
    other = pl.ds((1 - x) * PIECES, PIECES)
    inward_x2s[...] = (inward_yk[other] + inward_yr[other].astype(wide)).astype(low)
    inward_over_x = begin(remote(inward_x2s, inward_x2r, stage_s, stage_r, (1, 3), x_mate))
    left, right = pl.ds(0, width // 2), pl.ds(width // 2, width // 2)
    heads_x = begin(remote(heads_term.at[1 - x], heads_r, stage_s, stage_r, (2, 0), x_mate))
    hidden_x = begin(
        remote(
            hidden_term.at[1 - x, :, :, left],
            hidden_r.at[pl.ds(0, 2)],
            stage_s,
            stage_r,
            (3, 0),
            x_mate,
        )
    )
    hidden_y = [
        begin(
            remote(
                hidden_term.at[n, 1 - y, :, right],
                hidden_r.at[2 + n],
                stage_s,
                stage_r,
                (3, 1 + n),
                y_mate,
            )
        )
        for n in range(2)
    ]
    sums.third_hop()

    vector_x.wait_recv()
    vec_sum_x = vec_sum[...] + vec_x[...]
    vector_x.wait_send()
    vec_sum[...] = vec_sum_x
    vector_y = remote(vec_sum, vec_y, vec_s, vec_r, 1, y_mate)
    vector_y.start()

    inward_over_y.wait_recv()
    inward_over_x.wait_recv()
    own = pl.ds(x * PIECES, PIECES)
    inward_fin[...] = jnp.concatenate(
        [
            inward_xk[:, y] + inward_xr[:, y].astype(wide) + inward_y2r[...].astype(wide),
            inward_yk[own] + inward_yr[own].astype(wide) + inward_x2r[...].astype(wide),
        ],
        2,
    ).astype(low)
    inward_rest = to_rows(1, inward_fin, inward_rows_out)
    for copy in inward_rest:
        copy.start()

    vector_y.wait_recv()
    vec_sum_y = vec_sum[...] + vec_y[...]
    vector_y.wait_send()
    slot = core * DEPTH + z
    vec_out[slot] = vec_sum_y
    vectors = []
    for flip, turn in members:
        cc, zz = target(flip, turn)
        vectors.append(
            begin(
                remote(
                    vec_out.at[slot],
                    vec_out.at[slot],
                    rows_s,
                    rows_r,
                    (2, flip * DEPTH + turn),
                    device(x, cc, zz, y),
                )
            )
        )

    def row_sum(*refs):
        spec = pl.BlockSpec((refs[0].shape[0], refs[0].shape[1] // 2), lambda i: (0, i))

        def body(*parts):
            total = parts[0][...].astype(wide)
            for part in parts[1:-1]:
                total = total + part[...].astype(wide)
            parts[-1][...] = total.astype(parts[-1].dtype)

        pltpu.emit_pipeline(
            body, grid=(2,), in_specs=[spec] * (len(refs) - 1), out_specs=[spec]
        )(*refs)

    heads_x.wait_recv()
    row_sum(heads_term.at[x, 1 - y], heads_r.at[1 - y], heads_2s)
    heads_y = begin(remote(heads_2s, heads_2r, stage_s, stage_r, (2, 2), y_mate))
    for copy in hidden_y:
        copy.wait_recv()
    row_sum(hidden_term.at[1 - x, y, :, right], hidden_r.at[2 + 1 - x], hidden_2s.at[1])
    over_x = begin(remote(hidden_2s.at[1], hidden_2r.at[1], stage_s, stage_r, (2, 3), x_mate))
    hidden_x.wait_recv()
    row_sum(hidden_term.at[x, 1 - y, :, left], hidden_r.at[1 - y], hidden_2s.at[0])
    over_y = begin(remote(hidden_2s.at[0], hidden_2r.at[0], stage_s, stage_r, (3, 3), y_mate))
    heads_y.wait_recv()
    row_sum(heads_term.at[x, y], heads_r.at[y], heads_2r, heads_out)
    over_x.wait_recv()
    row_sum(
        hidden_term.at[x, y, :, right], hidden_r.at[2 + x], hidden_2r.at[1], hidden_out.at[:, right]
    )
    over_y.wait_recv()
    row_sum(hidden_term.at[x, y, :, left], hidden_r.at[y], hidden_2r.at[0], hidden_out.at[:, left])

    own_tokens.wait()
    sums.last_hop()
    for first in range(0, ROWS, 64):
        rows = pl.ds(first, 64)
        grad = own_sum[rows]
        hat, inverse = normalised(token_rows[rows])
        scaled = grad * gain_ref[...]
        input_grad = inverse * (
            scaled
            - jnp.mean(scaled, axis=-1, keepdims=True)
            - hat * jnp.mean(scaled * hat, axis=-1, keepdims=True)
        )
        tokens_out[rows] = (cot_ref[rows].astype(wide) + input_grad).astype(low)

    for copy in to_rows(0, gate_fin, gate_rows) + inward_rest:
        copy.wait()
    for copy in vectors:
        copy.wait_recv()
    for copy in started:
        copy.wait_send()
    for turn in range(DEPTH - 2, DEPTH):
        core_copy(turn).wait_send()
    sums.sent_all()


def finish(
    parts, gate_up_grad, pieces, tables, normed, gate_up, grads, hidden, attended, weights, gain, cot
):
    low, wide = jnp.bfloat16, jnp.float32
    width = pieces.shape[-1]
    rows = width // 32
    anywhere = pl.BlockSpec(memory_space=pl.ANY)
    inside = pl.BlockSpec(memory_space=pltpu.VMEM)
    shape = jax.ShapeDtypeStruct
    half = 3 * HEAD_COLS // 2

    a, b = (value.shape[-1] for value in gate_up[:2])
    heads_rows, hidden_rows = HEAD_DIM, hidden.shape[2] // 4
    out_shapes = [
        shape((ROWS, width), low),
        shape((heads_rows, width), wide),
        shape((hidden_rows, width), wide),
        shape((PIECES, rows, a + b), low),
        shape((PIECES, rows, 2 * half), low),
        shape((PIECES, 8, width // 2), wide),
    ]
    out_shapes += [
        shape((2, 2, heads_rows, width), low),
        shape((2, 2, hidden_rows, width), low),
        shape((2, heads_rows, width), low),
        shape((heads_rows, width), low),
        shape((heads_rows, width), low),
        shape((4, hidden_rows, width // 2), low),
        shape((2, hidden_rows, width // 2), low),
        shape((2, hidden_rows, width // 2), low),
    ]
    out_specs = [inside] + [anywhere] * 4 + [inside] + [anywhere] * (len(out_shapes) - 6)
    dma = pltpu.SemaphoreType.DMA
    outs = pl.pallas_call(
        finish_kernel,
        in_specs=[anywhere] * 18 + [inside] * 4,
        out_specs=out_specs,
        out_shape=out_shapes,
        scratch_shapes=[
            pltpu.VMEM((2, ROWS, width), low),
            pltpu.VMEM((DEPTH, ROWS, width), low),
            pltpu.VMEM((DEPTH - 1, ROWS, width), low),
            pltpu.VMEM((DEPTH - 1, ROWS, width), low),
            pltpu.VMEM((DEPTH - 1, ROWS, width), low),
            pltpu.VMEM((ROWS, width), wide),
            pltpu.VMEM((PIECES, ROWS, 3 * HEAD_COLS), low),
            pltpu.VMEM((ROWS, width), low),
            pltpu.VMEM((8, width // 2), wide),
            pltpu.VMEM((8, width // 2), wide),
            pltpu.VMEM((8, width // 2), wide),
            pltpu.VMEM((PIECES, rows, a), wide),
            pltpu.VMEM((PIECES, rows, b), wide),
            pltpu.VMEM((PIECES, rows, a), low),
            pltpu.VMEM((PIECES, rows, b), low),
            pltpu.VMEM((PIECES, rows, a + b), low),
            pltpu.VMEM((PIECES, 2, rows, half), low),
            pltpu.VMEM((PIECES, 2, rows, half), low),
            pltpu.VMEM((PIECES, 2, rows, half), wide),
            pltpu.VMEM((2 * PIECES, rows, half), low),
            pltpu.VMEM((2 * PIECES, rows, half), low),
            pltpu.VMEM((2 * PIECES, rows, half), wide),
            pltpu.VMEM((PIECES, rows, half), low),
            pltpu.VMEM((PIECES, rows, half), low),
            pltpu.VMEM((PIECES, rows, half), low),
            pltpu.VMEM((PIECES, rows, half), low),
            pltpu.VMEM((PIECES, rows, 2 * half), low),
            dma((DEPTH,)),
            dma((DEPTH,)),
            dma((DEPTH - 1,)),
            dma((DEPTH - 1,)),
            dma((DEPTH - 1,)),
            dma((DEPTH - 1,)),
            dma((4, 4)),
            dma((4, 4)),
            dma((3, PIECES)),
            dma((3, PIECES)),
            dma((2,)),
            dma((2,)),
            dma((7,)),
        ],
        compiler_params=params(63, collective_id=1, has_side_effects=True),
        cost_estimate=cost(0, 64 * MIB),
        name="finish",
    )(
        *parts,
        gate_up_grad,
        pieces,
        *tables,
        normed,
        *gate_up,
        grads,
        hidden,
        attended,
        *weights,
        gain,
        cot,
    )
    return outs[:6]


def split_rows(term, y, keep_ref, send_ref):
    rows = term.shape[0] // 4
    even = jnp.concatenate([term[:rows], term[2 * rows : 3 * rows]], 0)
    odd = jnp.concatenate([term[rows : 2 * rows], term[3 * rows :]], 0)
    keep_ref[...] = jnp.where(y == 0, even, odd).reshape(keep_ref.shape)
    send_ref[...] = jnp.where(y == 0, odd, even).astype(jnp.bfloat16).reshape(send_ref.shape)


def place_kernel(parts, in_ref, out_ref):
    each = in_ref.shape[2] // parts
    for part in range(parts):
        columns = slice(part * each, (part + 1) * each)
        line = jnp.concatenate([in_ref[n, :, columns] for n in range(PIECES)], 1)
        out_ref[:, part * PIECES * each : (part + 1) * PIECES * each] = line.astype(jnp.float32)


def place_rows(value, parts):
    rows, columns = value.shape[1], value.shape[2]
    return pl.pallas_call(
        functools.partial(place_kernel, parts),
        out_shape=jax.ShapeDtypeStruct((rows, PIECES * columns), jnp.float32),
        compiler_params=params(32),
        cost_estimate=cost(0, 4 * MIB),
        name="place_rows",
    )(value)


def shards_grouped(
    tokens,
    lengths,
    norm_gain,
    norm_shift,
    inward_weight,
    inward_bias,
    outward_weight,
    gate_up_weight,
    down_weight,
    cotangent,
):
    group_len, seqs, width = tokens.shape[1:]
    bucket, blk = lax.axis_index("bucket"), lax.axis_index("blk")

    gain_share, bias_share = norm_gain.shape[0], inward_bias.shape[0]
    shares = jnp.concatenate(
        [norm_gain, norm_gain, norm_shift, norm_shift, inward_bias, jnp.zeros((624,), jnp.float32)]
    ).reshape(8, 128)
    own_tokens = jnp.transpose(tokens[0], (1, 0, 2)).reshape(ROWS, width)
    own_cotangent = jnp.transpose(cotangent[0], (1, 0, 2)).reshape(ROWS, width)
    position = blk * group_len + jnp.arange(group_len, dtype=jnp.int32)
    valid = (position[None, :] < lengths[0][:, None]).astype(jnp.float32).reshape(ROWS, 1)
    lane = jnp.arange(HEAD_COLS, dtype=jnp.int32) % HEAD_DIM
    power = (lane % (ROT // 2)).astype(jnp.float32)
    frequency = jnp.where(lane < ROT, rotary_base ** (-(2.0 * power) / ROT), 0.0)
    (
        pieces,
        normed,
        gate,
        up,
        grads,
        inward,
        gate_up,
        rows_out,
        queries,
        pairs,
        other_pairs,
        hidden,
        attended,
        own_sum,
        terms,
        *tables,
        gain,
    ) = forward(
        own_tokens,
        own_cotangent,
        inward_weight,
        gate_up_weight,
        outward_weight,
        down_weight,
        valid,
        shares,
        inward_bias.reshape(1, -1),
        frequency.reshape(1, -1),
    )
    gate_up = gate_up.reshape(width, -1)
    normed = normed.reshape(PIECES * ROWS, width)
    def placed(value):
        value = value.reshape(seqs, group_len, width)
        return jnp.transpose(value, (1, 0, 2)).reshape(tokens.shape)

    outs = backward(
        grads,
        gate,
        up,
        normed,
        pieces,
        queries,
        pairs,
        other_pairs,
        rows_out,
        own_sum,
        terms,
        valid,
    )
    gate_up_grad, *parts, layer_out = outs[10:]
    layer_out, normed = lax.optimization_barrier((placed(layer_out), normed))
    tokens_grad, outward_sum, down_sum, gate_up_rows, inward_rows_own, vectors = finish(
        parts,
        gate_up_grad,
        pieces,
        tables,
        normed,
        outs[6:10],
        grads.reshape(PIECES * ROWS, width),
        hidden,
        attended,
        (inward, gate_up),
        gain,
        own_cotangent,
    )
    gate_up_sum = place_rows(gate_up_rows, 4)
    inward_sum = place_rows(inward_rows_own, 6)

    device = bucket * 2 * DEPTH + blk
    sums = jnp.sum(vectors[:, :4], axis=0).reshape(2, -1, gain_share)
    gain_sum = one_of(sums[0], device, 0)
    shift_sum = one_of(sums[1], device, 0)
    columns_sum = vectors[:, 4, : 3 * HEAD_COLS].reshape(PIECES, 3, 2, 2 * HEAD_DIM)
    columns_sum = jnp.transpose(columns_sum, (1, 2, 0, 3)).reshape(3, -1)
    key_rot = columns_sum[1].reshape(HEADS, HEAD_DIM)[:, :ROT]
    bias_all = jnp.concatenate([columns_sum[0], columns_sum[2], key_rot.reshape(-1)])
    bias_sum = one_of(bias_all.reshape(-1, bias_share), device, 0)

    return (
        layer_out,
        placed(tokens_grad),
        gain_sum,
        shift_sum,
        inward_sum,
        bias_sum,
        outward_sum,
        gate_up_sum,
        down_sum,
    )


def solution(mesh):
    in_specs = (
        P("bucket", "blk", None, None),
        P("bucket", None),
        P(("bucket", "blk")),
        P(("bucket", "blk")),
        P(("bucket", "blk"), None),
        P(("bucket", "blk")),
        P(("bucket", "blk"), None),
        P(("bucket", "blk"), None),
        P(("bucket", "blk"), None),
        P("bucket", "blk", None, None),
    )
    out_specs = (
        P("bucket", "blk", None, None),
        P("bucket", "blk", None, None),
        P(("bucket", "blk")),
        P(("bucket", "blk")),
        P(("bucket", "blk"), None),
        P(("bucket", "blk")),
        P(("bucket", "blk"), None),
        P(("bucket", "blk"), None),
        P(("bucket", "blk"), None),
    )
    body = shards_grouped if fits_groups(mesh) else shards_general
    return jax.shard_map(body, mesh=mesh, in_specs=in_specs, out_specs=out_specs, check_vma=False)
```

```python
import functools

import jax
import jax.numpy as jnp
from jax import lax
from jax.experimental import pallas as pl
from jax.experimental.pallas import tpu as pltpu
from jax.sharding import PartitionSpec as P

HEADS = 32
HEAD_DIM = 64
ROT = 16


epsilon = 1e-05
rotary_base = 10000.0
masked_score = -1e30


def shifted(value, axis, by):
    count = lax.axis_size(axis)
    pairs = [(i, i + by) for i in range(count) if 0 <= i + by < count]
    return lax.ppermute(value, axis, pairs)


def shifted_2(value, axis, steps):
    count = lax.axis_size(axis)
    pairs = [(source, (source + steps) % count) for source in range(count)]
    return lax.ppermute(value, axis, pairs)


def keep_same(value):
    return value


def transposed_times(left, right):
    return lax.dot_general(
        left, right, (((1,), (1,)), ((), ())), preferred_element_type=jnp.float32
    )


def times_transposed(left, right):
    return lax.dot_general(
        left, right, (((0,), (0,)), ((), ())), preferred_element_type=jnp.float32
    )


def rotary_tables(positions):
    half_rot = ROT // 2
    frequency = rotary_base ** (-(2.0 * jnp.arange(half_rot).astype(jnp.float32)) / ROT)
    angles = positions.astype(jnp.float32)[:, None] * frequency[None, :]
    return (jnp.cos(angles), jnp.sin(angles))


def rotate(values, cos_table, sine_table):
    half_rot = ROT // 2
    front_half = values[..., :half_rot]
    back_half = values[..., half_rot:ROT]
    return jnp.concatenate(
        [
            front_half * cos_table - back_half * sine_table,
            back_half * cos_table + front_half * sine_table,
            values[..., ROT:],
        ],
        axis=-1,
    )


def split_pairs(packed):
    rows_here, seq_count, both_width = packed.shape
    half_width = both_width // 2
    keys_part = packed[..., :half_width].reshape(rows_here, seq_count, HEADS, HEAD_DIM)
    values_part = packed[..., half_width:].reshape(rows_here, seq_count, HEADS, HEAD_DIM)
    return (keys_part, values_part)


def block_scores(queries, key_block, query_start, key_start):
    scores = jnp.einsum("tshd,ushd->shtu", queries, key_block, preferred_element_type=jnp.float32)
    query_pos = query_start + jnp.arange(queries.shape[0], dtype=jnp.int32)
    key_pos = key_start + jnp.arange(key_block.shape[0], dtype=jnp.int32)
    allowed = (key_pos[None, :] <= query_pos[:, None])[None, None]
    return (jnp.where(allowed, scores, masked_score), allowed)


def forward_block(carried, queries, key_block, value_block, query_start, key_start):
    running_max, running_sum, weighted = carried
    scores, allowed = block_scores(queries, key_block, query_start, key_start)
    new_max = jnp.maximum(running_max, jnp.max(scores, axis=-1))
    rescale = jnp.exp(running_max - new_max)
    weights = jnp.where(allowed, jnp.exp(scores - new_max[..., None]), 0.0)
    running_sum = running_sum * rescale + jnp.sum(weights, axis=-1)
    update = jnp.einsum(
        "shtu,ushd->tshd",
        weights.astype(jnp.bfloat16),
        value_block,
        preferred_element_type=jnp.float32,
    )
    weighted = weighted * jnp.transpose(rescale, (2, 0, 1))[..., None] + update
    return (new_max, running_sum, weighted)


def pair_grads(
    queries, out_grads, log_norm, deltas, key_block, value_block, query_start, key_start
):
    scores, allowed = block_scores(queries, key_block, query_start, key_start)
    probability = jnp.where(allowed, jnp.exp(scores - log_norm[..., None]), 0.0)
    value_grad = jnp.einsum(
        "shtu,tshd->ushd",
        probability.astype(jnp.bfloat16),
        out_grads,
        preferred_element_type=jnp.float32,
    )
    prob_grad = jnp.einsum(
        "tshd,ushd->shtu", out_grads, value_block, preferred_element_type=jnp.float32
    )
    score_grad = (probability * (prob_grad - deltas[..., None])).astype(jnp.bfloat16)
    query_grad = jnp.einsum(
        "shtu,ushd->tshd", score_grad, key_block, preferred_element_type=jnp.float32
    )
    key_grad = jnp.einsum(
        "shtu,tshd->ushd", score_grad, queries, preferred_element_type=jnp.float32
    )
    return (query_grad, key_grad, value_grad)


def over_blocks(running, incoming, unit_rows, handle):
    total_rows = incoming[0].shape[0]
    block_count = total_rows // unit_rows
    block_rows = total_rows // block_count
    stacked = tuple(
        (member.reshape((block_count, block_rows) + member.shape[1:]) for member in incoming)
    )

    def visit(carried, element):
        block_index, members = element
        return (handle(carried, members, block_index * block_rows), None)

    running, unused = lax.scan(visit, running, (jnp.arange(block_count, dtype=jnp.int32), stacked))
    return running


def shards_general(
    tokens,
    lengths,
    norm_gain,
    norm_shift,
    inward_weight,
    inward_bias,
    outward_weight,
    gate_up_weight,
    down_weight,
    cotangent,
):
    group_len = tokens.shape[1]
    seq_count = tokens.shape[2]
    model_width = tokens.shape[3]
    row_total = group_len * seq_count
    block_total = lax.axis_size("blk")
    position = lax.axis_index("blk")
    own_start = position * group_len
    longest = jnp.max(lengths[0])
    active = own_start < longest
    gathered = (
        lax.all_gather(inward_weight.astype(jnp.bfloat16), ("bucket", "blk"), axis=0, tiled=True),
        lax.all_gather(outward_weight.astype(jnp.bfloat16), ("bucket", "blk"), axis=0, tiled=True),
        lax.all_gather(gate_up_weight.astype(jnp.bfloat16), ("bucket", "blk"), axis=0, tiled=True),
        lax.all_gather(down_weight.astype(jnp.bfloat16), ("bucket", "blk"), axis=0, tiled=True),
        lax.all_gather(norm_gain.astype(jnp.bfloat16), ("bucket", "blk"), axis=0, tiled=True),
        lax.all_gather(norm_shift.astype(jnp.bfloat16), ("bucket", "blk"), axis=0, tiled=True),
        lax.all_gather(inward_bias.astype(jnp.bfloat16), ("bucket", "blk"), axis=0, tiled=True),
    )
    inward_full, outward_full, gate_up_full, down_full, gain_full, shift_full, bias_full = gathered
    inputs = tokens.reshape(row_total, model_width).astype(jnp.float32)
    centred = inputs - jnp.mean(inputs, axis=-1, keepdims=True)
    variance = jnp.mean(centred * centred, axis=-1, keepdims=True)
    inverse = lax.rsqrt(variance + epsilon)
    normal_hat = centred * inverse
    normed_low = (
        normal_hat * gain_full.astype(jnp.float32) + shift_full.astype(jnp.float32)
    ).astype(jnp.bfloat16)
    bias_float = bias_full.astype(jnp.float32)
    key_bias = jnp.pad(
        bias_float[2 * model_width :].reshape(HEADS, ROT), ((0, 0), (0, HEAD_DIM - ROT))
    ).reshape(model_width)
    full_bias = jnp.concatenate(
        [bias_float[:model_width], key_bias, bias_float[model_width : 2 * model_width]]
    )
    projected = jnp.dot(normed_low, inward_full, preferred_element_type=jnp.float32) + full_bias
    projected = projected.reshape(group_len, seq_count, 3, HEADS, HEAD_DIM)
    cos_table, sine_table = rotary_tables(own_start + jnp.arange(group_len, dtype=jnp.int32))
    cos_table = cos_table[:, None, None, :]
    sine_table = sine_table[:, None, None, :]
    query_scale = HEAD_DIM ** (-0.5)
    queries = (rotate(projected[:, :, 0], cos_table, sine_table) * query_scale).astype(jnp.bfloat16)
    keys_low = rotate(projected[:, :, 1], cos_table, sine_table).astype(jnp.bfloat16)
    values_low = projected[:, :, 2].astype(jnp.bfloat16)
    packed = jnp.concatenate(
        [
            keys_low.reshape(group_len, seq_count, model_width),
            values_low.reshape(group_len, seq_count, model_width),
        ],
        axis=-1,
    )

    def forward_handle(carried, members, key_start):
        keys_part, values_part = split_pairs(members[0])
        needed = active & (key_start <= own_start + group_len - 1)

        def forward_compute(state_in):
            return forward_block(state_in, queries, keys_part, values_part, own_start, key_start)

        return lax.cond(needed, forward_compute, keep_same, carried)

    start_state = (
        jnp.full((seq_count, HEADS, group_len), masked_score, jnp.float32),
        jnp.zeros((seq_count, HEADS, group_len), jnp.float32),
        jnp.zeros((group_len, seq_count, HEADS, HEAD_DIM), jnp.float32),
    )
    running_max, running_sum, weighted = over_blocks(
        start_state, (lax.all_gather(packed, "blk", axis=0, tiled=True),), group_len, forward_handle
    )
    bounded = jnp.maximum(running_sum, 1.0)
    log_norm = running_max + jnp.log(bounded)
    attended = weighted / jnp.transpose(bounded, (2, 0, 1))[..., None]
    attended_rows = attended.astype(jnp.bfloat16).reshape(row_total, model_width)
    gate_up = jnp.dot(normed_low, gate_up_full, preferred_element_type=jnp.float32)
    ff_width = gate_up.shape[1] // 2
    gate_part = gate_up[:, :ff_width]
    up_part = gate_up[:, ff_width:]
    sigmoid_gate = jax.nn.sigmoid(gate_part)
    silu_gate = gate_part * sigmoid_gate
    hidden_low = (silu_gate * up_part).astype(jnp.bfloat16)
    branch = jnp.dot(attended_rows, outward_full, preferred_element_type=jnp.float32) + jnp.dot(
        hidden_low, down_full, preferred_element_type=jnp.float32
    )
    query_pos = own_start + jnp.arange(group_len, dtype=jnp.int32)
    valid_rows = (
        (query_pos[:, None] < lengths[0][None, :]).astype(jnp.float32).reshape(row_total, 1)
    )
    layer_out = (inputs + valid_rows * branch).astype(jnp.bfloat16).reshape(tokens.shape)
    inward_back = gathered[0]
    outward_back = gathered[1]
    gate_up_back = gathered[2]
    down_back = gathered[3]
    gain_float = gathered[4].astype(jnp.float32)
    cotangent_rows = cotangent.reshape(row_total, model_width).astype(jnp.float32)
    branch_grad = (cotangent_rows * valid_rows).astype(jnp.bfloat16)
    hidden_grad = transposed_times(branch_grad, down_back)
    gate_grad = hidden_grad * up_part * (sigmoid_gate + silu_gate * (1.0 - sigmoid_gate))
    up_grad = hidden_grad * silu_gate
    gate_up_grad_low = jnp.concatenate([gate_grad, up_grad], axis=-1).astype(jnp.bfloat16)
    down_term = times_transposed(hidden_low, branch_grad)
    gate_up_term = times_transposed(normed_low, gate_up_grad_low)
    gate_up_sum, down_sum = (
        lax.psum_scatter(gate_up_term, ("bucket", "blk"), scatter_dimension=0, tiled=True),
        lax.psum_scatter(down_term, ("bucket", "blk"), scatter_dimension=0, tiled=True),
    )
    normed_grad = transposed_times(gate_up_grad_low, gate_up_back)
    attended_grad = (
        transposed_times(branch_grad, outward_back)
        .astype(jnp.bfloat16)
        .reshape(group_len, seq_count, HEADS, HEAD_DIM)
    )
    outward_term = times_transposed(attended_rows, branch_grad)
    deltas = jnp.transpose(
        jnp.sum(attended_grad.astype(jnp.float32) * attended, axis=-1), (1, 2, 0)
    )
    grad_zeros = jnp.zeros((group_len, seq_count, 2 * model_width), jnp.float32)
    query_zeros = jnp.zeros((group_len, seq_count, HEADS, HEAD_DIM), jnp.float32)

    def cycle_turn(turn_index, carried):
        visiting, sums_now, grads_now = carried
        owner_index = (position - turn_index) % block_total
        key_start = owner_index * group_len
        needed = active & (owner_index <= position)

        def cycle_compute(sums_in):
            keys_part, values_part = split_pairs(visiting)
            query_part, key_part, value_part = pair_grads(
                queries,
                attended_grad,
                log_norm,
                deltas,
                keys_part,
                values_part,
                own_start,
                key_start,
            )
            merged = jnp.concatenate(
                [
                    key_part.reshape(group_len, seq_count, model_width),
                    value_part.reshape(group_len, seq_count, model_width),
                ],
                axis=-1,
            )
            return (sums_in[0] + merged, sums_in[1] + query_part)

        sums_now, grads_now = lax.cond(needed, cycle_compute, keep_same, (sums_now, grads_now))
        visiting = shifted(visiting, "blk", 1)
        sums_now = shifted_2(sums_now.astype(jnp.bfloat16), "blk", 1).astype(sums_now.dtype)
        return (visiting, sums_now, grads_now)

    unused, pair_sums, query_grads = lax.fori_loop(
        0, block_total, cycle_turn, (packed, grad_zeros, query_zeros)
    )
    key_grad = pair_sums[..., :model_width].reshape(group_len, seq_count, HEADS, HEAD_DIM)
    value_grad = pair_sums[..., model_width:].reshape(group_len, seq_count, HEADS, HEAD_DIM)
    back_sine = -sine_table
    query_back = rotate(query_grads * query_scale, cos_table, back_sine)
    key_back = rotate(key_grad, cos_table, back_sine)
    projected_grad = (
        jnp.stack([query_back, key_back, value_grad], axis=2)
        .reshape(row_total, 3 * model_width)
        .astype(jnp.bfloat16)
    )
    inward_term = times_transposed(normed_low, projected_grad)
    column_sums = jnp.sum(projected_grad.astype(jnp.float32), axis=0)
    key_bias_grad = (
        column_sums[model_width : 2 * model_width]
        .reshape(HEADS, HEAD_DIM)[:, :ROT]
        .reshape(HEADS * ROT)
    )
    bias_term = jnp.concatenate(
        [column_sums[:model_width], column_sums[2 * model_width :], key_bias_grad]
    )
    normed_grad = normed_grad + transposed_times(projected_grad, inward_back)
    gain_term = jnp.sum(normed_grad * normal_hat, axis=0)
    shift_term = jnp.sum(normed_grad, axis=0)
    scaled_grad = normed_grad * gain_float
    input_grad = inverse * (
        scaled_grad
        - jnp.mean(scaled_grad, axis=-1, keepdims=True)
        - normal_hat * jnp.mean(scaled_grad * normal_hat, axis=-1, keepdims=True)
    )
    tokens_grad = (cotangent_rows + input_grad).astype(jnp.bfloat16).reshape(tokens.shape)
    inward_sum, outward_sum, bias_sum, gain_sum, shift_sum = (
        lax.psum_scatter(inward_term, ("bucket", "blk"), scatter_dimension=0, tiled=True),
        lax.psum_scatter(outward_term, ("bucket", "blk"), scatter_dimension=0, tiled=True),
        lax.psum_scatter(bias_term, ("bucket", "blk"), scatter_dimension=0, tiled=True),
        lax.psum_scatter(gain_term, ("bucket", "blk"), scatter_dimension=0, tiled=True),
        lax.psum_scatter(shift_term, ("bucket", "blk"), scatter_dimension=0, tiled=True),
    )
    return (
        layer_out,
        tokens_grad,
        gain_sum,
        shift_sum,
        inward_sum,
        bias_sum,
        outward_sum,
        gate_up_sum,
        down_sum,
    )


DEPTH = 4
PIECES = 2 * DEPTH
ROWS = 256
GATE_STEP = 6
HALFWAY = 5
LOCAL_HEADS = 4
HEAD_COLS = LOCAL_HEADS * HEAD_DIM


MIB = 1024 * 1024


def fits_groups(mesh):
    return mesh.shape["bucket"] == 4 and mesh.shape["blk"] == 2 * DEPTH


def around(step):
    return [(z * 2 + y, ((z + step) % DEPTH) * 2 + y) for z in range(DEPTH) for y in range(2)]


def in_order(own, other, index, axis):
    return jnp.where(
        index == 0, jnp.stack([own, other], axis), jnp.stack([other, own], axis)
    )


def one_of(value, index, axis):
    return lax.dynamic_index_in_dim(value, index, axis, False)


def dot_rows(left, right):
    return lax.dot_general(
        left, right, (((1,), (0,)), ((), ())), preferred_element_type=jnp.float32
    )


def params(limit, **extra):
    return pltpu.CompilerParams(vmem_limit_bytes=limit * MIB, **extra)


def cost(flops, moved, exps=0):
    return pl.CostEstimate(flops=flops // 64, bytes_accessed=moved // 64, transcendentals=exps // 64)


def piece_spec(width):
    return pl.BlockSpec((1, ROWS, width), lambda i: (i, 0, 0))


def whole_spec(shape):
    return pl.BlockSpec(shape, lambda i: (0,) * len(shape))


def remote_to(src, dst, send_sem, recv_sem, device):
    return pltpu.make_async_remote_copy(
        src_ref=src,
        dst_ref=dst,
        send_sem=send_sem,
        recv_sem=recv_sem,
        device_id=device,
        device_id_type=pl.DeviceIdType.MESH,
    )


def remote(src, dst, sends, recvs, index, device):
    return remote_to(src, dst, sends.at[index], recvs.at[index], device)


def select(i, first, second, third):
    return jnp.where(i == 0, first, jnp.where(i == 1, second, jnp.where(i == 2, third, 0)))


class Chain:
    def __init__(self, src, out, x, core, z, y, sems):
        up_s, down_s, arrive, core_s, core_r, local = sems
        self.z = z
        self.out = out

        def hop(k, src, slot, sends, dz):
            return pltpu.make_async_remote_copy(
                src_ref=src,
                dst_ref=out.at[slot],
                send_sem=sends.at[k],
                recv_sem=arrive.at[slot],
                device_id=(x * 2 + core, (z + dz) * 2 + y),
                device_id_type=pl.DeviceIdType.MESH,
            )

        mate = (x * 2 + 1 - core, z * 2 + y)
        self.ups = [hop(k, src if k == 0 else out.at[k], k + 1, up_s, 1) for k in range(3)]
        self.downs = [
            hop(k, src if k == 0 else out.at[DEPTH - k], 3 - k, down_s, -1) for k in range(3)
        ]
        self.cores = [
            remote(src if k == 0 else out.at[k], out.at[DEPTH + k], core_s, core_r, k, mate)
            for k in range(DEPTH)
        ]
        self.local = pltpu.make_async_copy(src, out.at[0], local)
        inner = (z > 0) & (z < DEPTH - 1)
        self.sent = [
            (z < DEPTH - 1, self.ups[0]),
            (z > 0, self.downs[0]),
            (inner, self.ups[1]),
            (inner, self.downs[1]),
            (z == DEPTH - 2, self.ups[2]),
            (z == 1, self.downs[2]),
        ]

    def start(self, *numbers):
        for number in numbers:
            condition, copy = self.sent[number]
            pl.when(condition)(copy.start)

    def near(self):
        self.cores[0].start()
        self.local.start()

    def first(self):
        self.start(0, 1)

    def first_apart(self):
        pl.when(self.z < DEPTH // 2)(self.ups[0].start)
        pl.when(self.z >= DEPTH // 2)(self.downs[0].start)

    def first_rest(self):
        pl.when(self.z == DEPTH // 2)(self.ups[0].start)
        pl.when(self.z == DEPTH // 2 - 1)(self.downs[0].start)

    def inner(self, step):
        pl.when((self.z > 0) & (self.z < DEPTH - 1))(step)

    def outer(self, step):
        pl.when((self.z == 0) | (self.z == DEPTH - 1))(step)

    def second(self):
        @pl.when(self.z > 0)
        def _():
            self.ups[0].wait_recv()
            self.cores[1].start()

        self.start(2)

        @pl.when(self.z < DEPTH - 1)
        def _():
            self.downs[0].wait_recv()
            self.cores[3].start()

        self.start(3)

    def third(self):
        self.ups[1].wait_recv()
        self.cores[2].start()
        self.start(4, 5)

    def fourth(self):
        @pl.when(self.z == DEPTH - 1)
        def _():
            self.ups[2].wait_recv()
            self.cores[3].start()

        @pl.when(self.z == 0)
        def _():
            self.downs[2].wait_recv()
            self.cores[1].start()

    def end(self, arrivals=True):
        if arrivals:
            for copy in self.cores:
                copy.wait_recv()
            self.local.wait()
        for copy in self.cores:
            copy.wait_send()
        for condition, copy in self.sent:
            pl.when(condition)(copy.wait_send)


def far_first(i, z):
    inner = jnp.where(z == 1, select(i, 2, 1, 3), select(i, 2, 3, 1))
    outer = jnp.where(z == 0, select(i, 1, 2, 3), select(i, 3, 2, 1))
    return jnp.where((z == 0) | (z == DEPTH - 1), outer, inner)


class ChainSum:
    def __init__(self, send, below, above, own, x, core, z, y, sems):
        self.send, self.below, self.above, self.own = send, below, above, own
        self.z = z
        self.up_s, self.down_s, self.below_r, self.above_r = sems
        self.goal_up = (x * 2 + core, (z + 1) * 2 + y)
        self.goal_down = (x * 2 + core, (z - 1) * 2 + y)

    def up(self, slot, number):
        return remote_to(
            self.send.at[slot],
            self.below.at[number],
            self.up_s.at[slot],
            self.below_r.at[number],
            self.goal_up,
        )

    def down(self, slot, number):
        return remote_to(
            self.send.at[slot],
            self.above.at[number],
            self.down_s.at[slot],
            self.above_r.at[number],
            self.goal_down,
        )

    def when(self, z):
        return pl.when(self.z == z)

    def start(self, turn):
        @self.when(0)
        def _():
            self.up(turn, turn).start()

        @self.when(DEPTH - 1)
        def _():
            self.down(turn, turn).start()

    def wait_below(self, number):
        box = self.below.at[number]
        remote_to(box, box, self.up_s.at[0], self.below_r.at[number], self.goal_up).wait_recv()

    def wait_above(self, number):
        box = self.above.at[number]
        remote_to(box, box, self.down_s.at[0], self.above_r.at[number], self.goal_up).wait_recv()

    def add(self, slot, value):
        total = self.send[slot].astype(jnp.float32) + value.astype(jnp.float32)
        self.send[slot] = total.astype(jnp.bfloat16)

    def pass_up(self, slot, number, sent):
        self.wait_below(number)
        self.add(slot, self.below[number])
        self.up(slot, sent).start()

    def pass_down(self, slot, number, sent):
        self.wait_above(number)
        self.add(slot, self.above[number])
        self.down(slot, sent).start()

    def first_hop(self):
        self.when(1)(lambda: self.pass_up(0, 0, 0))
        self.when(DEPTH - 2)(lambda: self.pass_down(0, 0, 0))

    def second_hop(self):
        self.when(1)(lambda: self.pass_up(2, 1, 1))
        self.when(DEPTH - 2)(lambda: self.pass_down(2, 1, 1))

    def third_hop(self):
        self.when(1)(lambda: self.pass_down(1, 0, 0))
        self.when(DEPTH - 2)(lambda: self.pass_up(1, 0, 0))

    def last_hop(self):
        below, above, wide = self.below, self.above, jnp.float32

        @self.when(0)
        def _():
            self.wait_above(0)
            self.own[...] += above[0].astype(wide)

        @self.when(1)
        def _():
            self.wait_below(2)
            self.wait_above(1)
            self.own[...] += below[2].astype(wide) + above[1].astype(wide)

        @self.when(DEPTH - 2)
        def _():
            self.wait_below(1)
            self.wait_above(2)
            self.own[...] += below[1].astype(wide) + above[2].astype(wide)

        @self.when(DEPTH - 1)
        def _():
            self.wait_below(0)
            self.own[...] += below[0].astype(wide)

    def sent_all(self):
        @self.when(0)
        def _():
            for slot in range(DEPTH - 1):
                self.up(slot, slot).wait_send()

        @self.when(DEPTH - 1)
        def _():
            for slot in range(DEPTH - 1):
                self.down(slot, slot).wait_send()

        @self.when(1)
        def _():
            self.up(0, 0).wait_send()
            self.up(2, 1).wait_send()
            self.down(1, 0).wait_send()

        @self.when(DEPTH - 2)
        def _():
            self.down(0, 0).wait_send()
            self.down(2, 1).wait_send()
            self.up(1, 0).wait_send()


def chain_sems():
    dma = pltpu.SemaphoreType.DMA
    return [dma((3,)), dma((3,)), dma((DEPTH,)), dma((DEPTH,)), dma((DEPTH,)), dma(())]


def greet(mates):
    barrier = pltpu.get_barrier_semaphore()
    for mate in mates:
        pl.semaphore_signal(
            barrier, inc=1, device_id=mate, device_id_type=pl.DeviceIdType.MESH
        )
    pl.semaphore_wait(barrier, len(mates))


def coordinates():
    bucket, blk = lax.axis_index("bucket"), lax.axis_index("blk")
    return bucket // 2, bucket % 2, blk // 2, blk % 2


def inward_rows(ref):
    blocks, rows, columns = ref.shape
    return ref[...].reshape(blocks * rows, columns)


def outward_rows(ref):
    blocks, rows, columns = ref.shape
    return ref[:, :HEAD_DIM].reshape(blocks * HEAD_DIM, columns)


def down_rows(ref):
    blocks, rows, columns = ref.shape
    return ref[:, HEAD_DIM:].reshape(blocks * (rows - HEAD_DIM), columns)


def normalised(rows):
    inputs = rows.astype(jnp.float32)
    centred = inputs - jnp.mean(inputs, axis=-1, keepdims=True)
    variance = jnp.mean(centred * centred, axis=-1, keepdims=True)
    inverse = lax.rsqrt(variance + epsilon)
    return centred * inverse, inverse


def turned(values, cos_ref, first_ref, second_ref, sign):
    half = ROT // 2
    cos = jnp.concatenate([cos_ref[0], cos_ref[0]], 0)
    first = jnp.concatenate([first_ref[0], first_ref[0]], 0)
    second = jnp.concatenate([second_ref[0], second_ref[0]], 0)
    ahead = pltpu.roll(values, HEAD_COLS - half, 1)
    behind = pltpu.roll(values, half, 1)
    return values * cos + sign * (ahead * first + behind * second)


def forward_kernel(
    tokens_ref,
    cot_ref,
    inward_ref,
    gate_up_ref,
    outward_ref,
    down_ref,
    valid_ref,
    shares_ref,
    bias_ref,
    frequency_ref,
    pieces,
    normed_out,
    gate_out,
    up_out,
    grads_out,
    wi_out,
    wg_out,
    ro_out,
    q_out,
    kv_out,
    okv_out,
    hidden_out,
    att_out,
    own_out,
    terms_out,
    cos_out,
    first_out,
    second_out,
    gain_out,
    vec_ref,
    wi_own,
    wg_own,
    wi_ref,
    wg_ref,
    rows_ref,
    cos_ref,
    first_ref,
    second_ref,
    gain_ref,
    shift_ref,
    bias_rows,
    own_bias,
    own_grad,
    q_ref,
    kv_ref,
    okv_ref,
    hidden_ref,
    att_ref,
    own_sum,
    terms,
    core_send,
    core_recv,
    group_s,
    group_r,
    across_s,
    across_r,
    rows_s,
    rows_r,
    kv_s,
    kv_r,
    core_s,
    core_r,
    local_sems,
    out_sems,
    *chains,
):
    x, core, z, y = coordinates()
    low, wide = jnp.bfloat16, jnp.float32

    def device(xx, cc, zz, yy):
        return (xx * 2 + cc, zz * 2 + yy)

    def at(xx, cc, zz, yy):
        return ((xx * 2 + cc) * DEPTH + zz) * 2 + yy

    x_mate, y_mate = device(1 - x, core, z, y), device(x, core, z, 1 - y)
    core_mate = device(x, 1 - core, z, y)
    members = [(flip, turn) for turn in (0, 1, 3, 2) for flip in (0, 1)]

    def target(flip, turn):
        return (core + flip) % 2, (z + turn) % DEPTH

    def source(flip, turn):
        return (core + flip) % 2, (z + DEPTH - turn) % DEPTH

    started = []
    written = []

    def begin(copy):
        copy.start()
        started.append(copy)
        return copy

    def write_out(*pairs):
        for src, dst in pairs:
            copy = pltpu.make_async_copy(src, dst, out_sems.at[len(written)])
            copy.start()
            written.append(copy)

    def group_copies(which, own, full):
        mine = at(x, core, z, y)
        copies = {}
        for flip, turn in members[1:]:
            cc, zz = target(flip, turn)
            copies[flip, turn] = remote(
                own.at[cc * DEPTH + zz],
                full.at[mine],
                group_s,
                group_r,
                (which, flip * DEPTH + turn),
                device(x, cc, zz, y),
            )
        return copies

    def vector_copies():
        mine = vec_ref.at[at(x, core, z, y)]
        copies = {}
        for flip, turn in members[1:]:
            copies[flip, turn] = remote(
                mine,
                mine,
                group_s,
                group_r,
                (2, flip * DEPTH + turn),
                device(x, *target(flip, turn), y),
            )
        return copies

    def rows_copies():
        mine = rows_ref.at[x * 2 + y]
        return [
            remote(mine, mine, rows_s, rows_r, way, mate) for way, mate in enumerate((x_mate, y_mate))
        ]

    tokens = Chain(tokens_ref, pieces, x, core, z, y, chains[:6])
    grads = Chain(own_grad, grads_out, x, core, z, y, chains[6:])
    position = lax.broadcasted_iota(jnp.int32, (ROWS // 2, HEAD_COLS), 0)
    lane = lax.broadcasted_iota(jnp.int32, (ROWS // 2, HEAD_COLS), 1) % HEAD_DIM
    half = ROT // 2

    share_lane = lax.broadcasted_iota(jnp.int32, shares_ref.shape, 1)
    share_row = lax.broadcasted_iota(jnp.int32, shares_ref.shape, 0)
    own_shares = jnp.where((share_lane // HEAD_DIM == y) | (share_row >= 2), shares_ref[...], 0.0)

    def prepare(inward_f32, gate_up_f32, outward_f32, down_f32):
        loads = [
            pltpu.make_async_copy(src, dst, local_sems.at[n])
            for n, (src, dst) in enumerate(
                (
                    (inward_ref, inward_f32),
                    (gate_up_ref, gate_up_f32),
                    (outward_ref, outward_f32),
                    (down_ref, down_f32),
                )
            )
        ]
        for load in loads:
            load.start()
        greet([device(x, *target(*m), y) for m in members[1:]] + [x_mate, y_mate])
        tokens.near()
        loads[0].wait()
        vec_ref[at(x, core, z, y)] = own_shares
        for copy in vector_copies().values():
            copy.start()
        pair = 2 * HEAD_DIM
        for n in range(PIECES):
            starts = [part * PIECES * pair + n * pair for part in range(6)]
            line = jnp.concatenate([inward_f32[:, c : c + pair] for c in starts], 1)
            wi_own[n] = line.astype(low)
        wi_ref[at(x, core, z, y)] = wi_own[core * DEPTH + z]
        for copy in group_copies(0, wi_own, wi_ref).values():
            copy.start()
        loads[1].wait()
        each = gate_up_f32.shape[1] // (4 * PIECES)
        for n in range(PIECES):
            starts = [part * PIECES * each + n * each for part in range(4)]
            line = jnp.concatenate([gate_up_f32[:, c : c + each] for c in starts], 1)
            wg_own[n] = line.astype(low)
        wg_ref[at(x, core, z, y)] = wg_own[core * DEPTH + z]
        loads[2].wait()
        loads[3].wait()
        rows_ref[x * 2 + y, :HEAD_DIM] = outward_f32[...].astype(low)
        rows_ref[x * 2 + y, HEAD_DIM:] = down_f32[...].astype(low)

    pl.run_scoped(
        prepare,
        *[
            pltpu.VMEM(r.shape, r.dtype)
            for r in (inward_ref, gate_up_ref, outward_ref, down_ref)
        ],
    )
    inward = group_copies(0, wi_own, wi_ref)
    gate_up = group_copies(1, wg_own, wg_ref)
    vectors = vector_copies()
    started += [*inward.values(), *gate_up.values(), *vectors.values()]

    def spread(which, full, copies, halfway=None):
        pairs = {}
        for member in members:
            if halfway is not None and member == members[HALFWAY]:
                halfway()
            flip, turn = member
            cc, zz = source(flip, turn)
            if member != (0, 0):
                copies[member].wait_recv()
            block = full.at[at(x, cc, zz, y)]
            number = flip * DEPTH + turn
            pairs[member] = tuple(
                begin(remote(block, block, across_s, across_r, (which, way, number), mate))
                for way, mate in enumerate((x_mate, y_mate))
            )
        return pairs

    def by_x(which, flip):
        return which != 1 or flip == 0

    def corner(which, full, pairs):
        copies = []
        for member in members:
            flip, turn = member
            cc, zz = source(flip, turn)
            number = flip * DEPTH + turn
            if by_x(which, flip):
                pairs[member][1].wait_recv()
                block, mate = full.at[at(x, cc, zz, 1 - y)], x_mate
            else:
                pairs[member][0].wait_recv()
                block, mate = full.at[at(1 - x, cc, zz, y)], y_mate
            copies.append(
                begin(remote(block, block, across_s, across_r, (which, 2, number), mate))
            )
        return copies

    def complete(which, pairs, copies):
        for flip, turn in members:
            pairs[flip, turn][0 if by_x(which, flip) else 1].wait_recv()
        for copy in copies:
            copy.wait_recv()

    frequency = frequency_ref[...]
    for k in range(DEPTH):
        first = (2 * lax.rem(z + DEPTH - k, DEPTH) + y) * (ROWS // 2)
        angles = (first + position).astype(wide) * frequency
        sine = jnp.sin(angles)
        cos_ref[k] = jnp.cos(angles)
        first_ref[k] = jnp.where(lane < half, -sine, 0.0)
        second_ref[k] = jnp.where((lane >= half) & (lane < ROT), sine, 0.0)
    own_grad[...] = (cot_ref[...].astype(wide) * valid_ref[...]).astype(low)
    write_out((cos_ref, cos_out), (first_ref, first_out), (second_ref, second_out))

    vector_pairs = spread(2, vec_ref, vectors)
    inward_pairs = spread(0, wi_ref, inward)
    for copy in gate_up.values():
        copy.start()
    vector_corner = corner(2, vec_ref, vector_pairs)
    inward_corner = corner(0, wi_ref, inward_pairs)
    gate_up_pairs = spread(1, wg_ref, gate_up, tokens.first)
    complete(2, vector_pairs, vector_corner)
    complete(0, inward_pairs, inward_corner)
    write_out((wi_ref, wi_out))

    shares = vec_ref[...].astype(low).astype(wide)
    for row, vector in ((0, gain_ref), (1, shift_ref)):
        line = shares[:, row]
        vector[...] = jnp.concatenate(
            [line[2 * i : 2 * i + 1] + line[2 * i + 1 : 2 * i + 2] for i in range(16)], 1
        )
    each = bias_ref.shape[1]
    biases = jnp.concatenate([shares[:, 2], shares[:, 3]], 1)
    flat = jnp.concatenate([biases[i : i + 1, :each] for i in range(32)], 1)
    for i in range(flat.shape[1] // 128):
        bias_rows[i : i + 1] = flat[:, i * 128 : (i + 1) * 128]
    query_bias, key_bias, value_bias = [], [], []
    gap = jnp.zeros((1, HEAD_DIM - ROT), wide)
    for i in range(2):
        row = i * PIECES + core * DEPTH + z
        query_bias.append(bias_rows[pl.ds(row, 1)])
        value_bias.append(bias_rows[pl.ds(2 * PIECES + row, 1)])
        line = bias_rows[pl.ds(4 * PIECES + i * 2 + core, 1)]
        heads = [line[:, 2 * ROT * j : 2 * ROT * (j + 1)] for j in range(DEPTH)]
        chosen = jnp.where(
            z == 0, heads[0], jnp.where(z == 1, heads[1], jnp.where(z == 2, heads[2], heads[3]))
        )
        key_bias += [chosen[:, :ROT], gap, chosen[:, ROT:], gap]
    own_bias[...] = jnp.concatenate(query_bias + key_bias + value_bias, 1)
    write_out((gain_ref, gain_out))

    def pair_copy(piece):
        return remote(kv_ref.at[piece], okv_ref.at[piece], kv_s, kv_r, piece, y_mate)

    def project(piece, tokens_part, normed):
        k = lax.rem(piece, DEPTH)
        hat, _ = normalised(tokens_part[0])
        narrow = (hat * gain_ref[...] + shift_ref[...]).astype(low)
        normed[0] = narrow
        projected = dot_rows(narrow, inward_rows(wi_ref)) + own_bias[...]
        tables = (cos_ref.at[pl.ds(k, 1)], first_ref.at[pl.ds(k, 1)], second_ref.at[pl.ds(k, 1)])
        query = turned(projected[:, :HEAD_COLS], *tables, 1.0) * (HEAD_DIM**-0.5)
        key = turned(projected[:, HEAD_COLS : 2 * HEAD_COLS], *tables, 1.0)
        kv_ref[piece] = jnp.concatenate([key, projected[:, 2 * HEAD_COLS :]], 1).astype(low)
        pair_copy(piece).start()
        q_ref[piece] = query.astype(low)

    def piece_at(first, i):
        turn = first + i // 2
        near = jnp.where(z == 0, DEPTH - 1, 1)
        k = jnp.where(
            turn == 0, 0, jnp.where(turn == 1, near, jnp.where(turn == 2, 2, DEPTH - near))
        )
        return k + DEPTH * (i % 2)

    def project_pieces(first, count):
        spec = pl.BlockSpec((1,) + pieces.shape[1:], lambda i: (piece_at(first, i), 0, 0))
        pltpu.emit_pipeline(
            lambda *refs: project(piece_at(first, pl.program_id(0)), *refs),
            grid=(2 * count,),
            in_specs=[spec],
            out_specs=[spec],
        )(pieces, normed_out)

    def feed(first, count):
        def body(normed, gate_part, up_part):
            piece = piece_at(first, pl.program_id(0))
            both = dot_rows(normed[0], wg_ref[...].reshape(normed.shape[2], wg_ref.shape[2]))
            hidden = both.shape[1] // 2
            gate, up = both[:, :hidden], both[:, hidden:]
            gate_part[0] = gate
            up_part[0] = up
            hidden_ref[piece] = (gate * jax.nn.sigmoid(gate) * up).astype(low)

        def spec(array):
            return pl.BlockSpec(
                (1,) + array.shape[1:], lambda i: (piece_at(first, i), 0, 0)
            )

        pltpu.emit_pipeline(
            body,
            grid=(2 * count,),
            in_specs=[spec(normed_out)],
            out_specs=[spec(gate_out), spec(up_out)],
        )(normed_out, gate_out, up_out)

    near = jnp.where(z == 0, DEPTH - 1, 1)
    far = DEPTH - near

    def core_arrived(k):
        remote(pieces.at[k], pieces.at[DEPTH + k], chains[3], chains[4], k, core_mate).wait_recv()

    tokens.local.wait()
    core_arrived(0)
    project_pieces(0, 1)
    tokens.second()
    core_arrived(near)
    project_pieces(1, 1)
    gate_up_corner = corner(1, wg_ref, gate_up_pairs)
    rows_x, rows_y = rows_copies()
    begin(rows_x)
    begin(rows_y)
    tokens.third()
    grads.near()
    grads.first_apart()
    core_arrived(2)
    project_pieces(2, 1)
    complete(1, gate_up_pairs, gate_up_corner)
    feed(0, 2)
    tokens.fourth()
    grads.first_rest()
    core_arrived(far)
    project_pieces(3, 1)
    grads.inner(grads.second)
    rows_y.wait_recv()
    block = rows_ref.at[x * 2 + 1 - y]
    rows_corner = begin(remote(block, block, rows_s, rows_r, 2, x_mate))
    feed(2, 2)
    write_out((q_ref, q_out), (kv_ref, kv_out), (wg_ref, wg_out))

    for b in range(2):
        for j in range(DEPTH):
            pair_copy(b * DEPTH + j).wait_recv()

        def attend(t, carry):
            attend_one(Heads(b, t, z, y, q_ref, kv_ref, okv_ref), att_ref)
            return carry

        lax.fori_loop(0, LOCAL_HEADS, attend, 0)

    rows_x.wait_recv()
    rows_corner.wait_recv()
    write_out((hidden_ref, hidden_out), (att_ref, att_out), (okv_ref, okv_out), (rows_ref, ro_out))

    def core_copy(k):
        return remote(core_send.at[k % 2], core_recv.at[k], core_s, core_r, k, core_mate)

    def term(piece):
        return dot_rows(att_ref[piece], outward_rows(rows_ref)) + dot_rows(
            hidden_ref[piece], down_rows(rows_ref)
        )

    def branch(i, carry):
        k = far_first(i, z)

        @pl.when(i >= 2)
        def _():
            core_copy(i - 2).wait_send()

        core_send[i % 2] = term(DEPTH + k).astype(low)
        core_copy(i).start()
        own = term(k)
        core_copy(i).wait_recv()
        both = own + core_recv[i].astype(wide)

        @pl.when(i < DEPTH - 1)
        def _():
            terms[i] = both.astype(low)

        @pl.when(i == DEPTH - 1)
        def _():
            own_sum[...] = both

        return carry

    grads.inner(grads.third)
    lax.fori_loop(0, DEPTH, branch, 0)
    write_out((own_sum, own_out), (terms, terms_out))
    grads.outer(grads.second)
    grads.outer(grads.third)
    grads.fourth()
    grads.end()
    tokens.end(False)
    for i in range(DEPTH - 2, DEPTH):
        core_copy(i).wait_send()
    for piece in range(PIECES):
        pair_copy(piece).wait_send()
    for copy in started:
        copy.wait_send()
    for copy in written:
        copy.wait()


def forward(
    tokens, cot, inward, gate_up, outward, down, valid, shares, bias, frequency
):
    low, wide = jnp.bfloat16, jnp.float32
    rows, width = tokens.shape
    own_rows = inward.shape[0]
    group_columns = gate_up.shape[1] // PIECES
    hidden = group_columns // 2
    anywhere = pl.BlockSpec(memory_space=pl.ANY)
    inside = pl.BlockSpec(memory_space=pltpu.VMEM)
    shape = jax.ShapeDtypeStruct
    dma = pltpu.SemaphoreType.DMA
    wi_shape = shape((32, own_rows, 3 * HEAD_COLS), low)
    wg_shape = shape((32, own_rows, group_columns), low)
    ro_shape = shape((4, outward.shape[0] + down.shape[0], width), low)
    table = shape((DEPTH, ROWS // 2, HEAD_COLS), wide)
    heads = shape((PIECES, ROWS, HEAD_COLS), low)
    pairs = shape((PIECES, ROWS, 2 * HEAD_COLS), low)
    hidden_shape = shape((PIECES, ROWS, hidden), low)
    own_shape = shape((ROWS, width), wide)
    terms_shape = shape((DEPTH - 1, ROWS, width), low)
    vector = shape((1, width), wide)

    def scratch(*shapes):
        return [pltpu.VMEM(s.shape, s.dtype) for s in shapes]

    return pl.pallas_call(
        forward_kernel,
        in_specs=[anywhere] + [inside] + [anywhere] * 4 + [inside] * 4,
        out_specs=[anywhere] * 19,
        out_shape=[
            shape((PIECES, ROWS, width), low),
            shape((PIECES, ROWS, width), low),
            shape((PIECES, ROWS, hidden), wide),
            shape((PIECES, ROWS, hidden), wide),
            shape((PIECES, ROWS, width), low),
            wi_shape,
            wg_shape,
            ro_shape,
            heads,
            pairs,
            pairs,
            hidden_shape,
            heads,
            own_shape,
            terms_shape,
            table,
            table,
            table,
            vector,
        ],
        scratch_shapes=scratch(
            shape((32, 8, 128), wide),
            shape((PIECES,) + wi_shape.shape[1:], low),
            shape((PIECES,) + wg_shape.shape[1:], low),
            wi_shape,
            wg_shape,
            ro_shape,
            table,
            table,
            table,
            vector,
            vector,
            shape((40, 128), wide),
            shape((1, 3 * HEAD_COLS), wide),
            shape((ROWS, width), low),
            heads,
            pairs,
            pairs,
            hidden_shape,
            heads,
            own_shape,
            terms_shape,
            shape((2, ROWS, width), low),
            shape((DEPTH, ROWS, width), low),
        )
        + [
            dma((3, PIECES)),
            dma((3, PIECES)),
            dma((3, 3, PIECES)),
            dma((3, 3, PIECES)),
            dma((4,)),
            dma((4,)),
            dma((PIECES,)),
            dma((PIECES,)),
            dma((DEPTH,)),
            dma((DEPTH,)),
            dma((4,)),
            dma((14,)),
        ]
        + chain_sems()
        + chain_sems(),
        compiler_params=params(62, collective_id=0, has_side_effects=True),
        cost_estimate=cost(0, 64 * MIB),
        name="forward",
    )(tokens, cot, inward, gate_up, outward, down, valid, shares, bias, frequency)


def pair_rows(block):
    lane = lax.broadcasted_iota(jnp.int32, block.shape, 1)
    zero = jnp.zeros_like(block)
    return jnp.concatenate(
        [jnp.where(lane < HEAD_DIM, block, zero), jnp.where(lane < HEAD_DIM, zero, block)], 0
    )


def pair_lanes(rows):
    half = rows.shape[0] // 2
    lane = lax.broadcasted_iota(jnp.int32, (half, rows.shape[1]), 1)
    return jnp.where(lane < HEAD_DIM, rows[:half], rows[half:])


def block_probs(queries, keys, last, y):
    scores = transposed_times(queries, keys)
    rows, columns = scores.shape
    size = rows // 2
    row = lax.broadcasted_iota(jnp.int32, (rows, 2 * size), 0) % size
    column = lax.broadcasted_iota(jnp.int32, (rows, 2 * size), 1)
    allowed = (column <= row) | ((column >= size) & (y == 1))
    tail = jnp.where(allowed, scores[:, last * 2 * size :], masked_score)
    scores = tail if last == 0 else jnp.concatenate([scores[:, : last * 2 * size], tail], 1)
    weights = jnp.exp(scores - jnp.max(scores, axis=-1, keepdims=True))
    return weights * (1.0 / jnp.sum(weights, axis=-1, keepdims=True))


class Heads:
    def __init__(self, b, t, z, y, q_ref, kv_ref, okv_ref):
        size = ROWS // 2
        pair = 2 * HEAD_DIM
        self.b, self.z, self.y = b, z, y
        self.rows = pl.ds(pl.multiple_of((t // 2) * size, size), size)
        self.lanes = pl.ds(pl.multiple_of((t % 2) * pair, pair), pair)
        value_lanes = pl.ds(pl.multiple_of(HEAD_COLS + (t % 2) * pair, pair), pair)
        self.q_ref = q_ref

        def both(lanes):
            blocks = []
            for j in range(DEPTH):
                place = (self.piece(j), self.rows, lanes)
                blocks += [kv_ref[place], okv_ref[place]]
            return jnp.concatenate(blocks, 0)

        self.keys, self.values = both(self.lanes), both(value_lanes)

    def piece(self, j):
        return self.b * DEPTH + lax.rem(self.z + DEPTH - j, DEPTH)

    def place(self, j):
        return self.piece(j), self.rows, self.lanes

    def queries(self, j):
        return pair_rows(self.q_ref[self.place(j)])


def attend_one(heads, out_ref):
    for j in range(DEPTH):
        count = (j + 1) * ROWS
        probs = block_probs(heads.queries(j), heads.keys[:count], j, heads.y)
        out = dot_rows(probs.astype(jnp.bfloat16), heads.values[:count])
        out_ref[heads.place(j)] = pair_lanes(out).astype(jnp.bfloat16)


def attend_back_one(heads, grad_ref, dq_ref, dk_ref, dv_ref, odk_ref, odv_ref, key_sum, value_sum):
    half = ROWS // 2
    for j in reversed(range(DEPTH)):
        count = (j + 1) * ROWS
        queries = heads.queries(j)
        grads = pair_rows(grad_ref[heads.place(j)])
        keys, values = heads.keys[:count], heads.values[:count]
        probs = block_probs(queries, keys, j, heads.y)
        low = probs.astype(jnp.bfloat16)
        prob_grad = transposed_times(grads, values)
        delta = jnp.sum(low.astype(jnp.float32) * prob_grad, axis=-1, keepdims=True)
        score_grad = (probs * (prob_grad - delta)).astype(jnp.bfloat16)
        dq_ref[heads.place(j)] = pair_lanes(dot_rows(score_grad, keys))
        key_term = times_transposed(score_grad, queries)
        value_term = times_transposed(low, grads)
        if j == DEPTH - 1:
            key_sum[...] = key_term
            value_sum[...] = value_term
        else:
            key_sum[:count] += key_term
            value_sum[:count] += value_term
    for j in range(DEPTH):
        low = j * ROWS
        place = heads.place(j)
        dk_ref[place] = key_sum[low : low + half]
        dv_ref[place] = value_sum[low : low + half]
        odk_ref[place] = key_sum[low + half : low + ROWS].astype(jnp.bfloat16)
        odv_ref[place] = value_sum[low + half : low + ROWS].astype(jnp.bfloat16)


def backward_kernel(
    grads_ref,
    gate_ref,
    up_ref,
    normed_ref,
    pieces_ref,
    q_in,
    kv_in,
    okv_in,
    rows_in,
    own_in,
    terms_in,
    valid_ref,
    gate_xs,
    gate_xk,
    gate_ys,
    gate_yk,
    gate_xr,
    gate_yr,
    gate_y2s,
    gate_x2s,
    gate_own_x,
    gate_own_y,
    gu_out,
    dq_out,
    dk_out,
    dv_out,
    got_dk,
    got_dv,
    layer_out,
    q_ref,
    kv_ref,
    okv_ref,
    rows_ref,
    own_sum,
    terms,
    gu_ref,
    dq_ref,
    dk_ref,
    dv_ref,
    attended_grad,
    odk_ref,
    odv_ref,
    key_sum,
    value_sum,
    below,
    above,
    token_rows,
    up_s,
    down_s,
    below_r,
    above_r,
    pair_s,
    pair_r,
    stage_s,
    stage_r,
    load_sems,
    out_sems,
):
    x, core, z, y = coordinates()
    low, wide = jnp.bfloat16, jnp.float32
    y_mate = (x * 2 + core, z * 2 + 1 - y)

    x_mate = (2 - x * 2 + core, z * 2 + y)
    loads = {}
    for src, dst in (
        (terms_in, terms),
        (rows_in, rows_ref),
        (q_in, q_ref),
        (kv_in, kv_ref),
        (okv_in, okv_ref),
        (own_in, own_sum),
        (pieces_ref.at[0], token_rows),
    ):
        load = pltpu.make_async_copy(src, dst, load_sems.at[len(loads)])
        load.start()
        loads[len(loads)] = load
    written = []

    def write_out(*pairs):
        for src, dst in pairs:
            copy = pltpu.make_async_copy(src, dst, out_sems.at[len(written)])
            copy.start()
            written.append(copy)

    below_mate = (x * 2 + core, lax.rem(z + DEPTH - 1, DEPTH) * 2 + y)
    above_mate = (x * 2 + core, lax.rem(z + 1, DEPTH) * 2 + y)
    greet([x_mate, y_mate, below_mate, above_mate])
    sums = ChainSum(terms, below, above, own_sum, x, core, z, y, (up_s, down_s, below_r, above_r))
    loads[0].wait()
    for turn in range(DEPTH - 1):
        sums.start(turn)
    loads[1].wait()

    def piece_body(grad_part, gate_part, up_part):
        piece = pl.program_id(0)
        grad = grad_part[0]
        attended_grad[piece] = transposed_times(grad, outward_rows(rows_ref)).astype(low)
        hidden_grad = transposed_times(grad, down_rows(rows_ref))
        gate = gate_part[0]
        sig = jax.nn.sigmoid(gate)
        silu = gate * sig
        gate_grad = hidden_grad * up_part[0] * (sig + silu * (1.0 - sig))
        up_grad = hidden_grad * silu
        gu_ref[piece] = jnp.concatenate([gate_grad, up_grad], 1).astype(low)

    pltpu.emit_pipeline(
        piece_body,
        grid=(PIECES,),
        in_specs=[piece_spec(r.shape[-1]) for r in (grads_ref, gate_ref, up_ref)],
    )(grads_ref, gate_ref, up_ref)

    write_out((gu_ref, gu_out))
    total, width = normed_ref.shape
    size = width // PIECES
    columns = gu_ref.shape[-1]
    cut = gate_xs.shape[-1]

    def right(first, last):
        return gu_ref[...].reshape(total, columns)[:, first:last]

    def whole_body(left, out):
        term = times_transposed(left[...], right(0, cut)).astype(out.dtype)
        out[...] = term.reshape(out.shape)

    def split_body(left, keep, send):
        split_rows(times_transposed(left[...], right(cut, columns)), y, keep, send)

    def from_block(base):
        return pl.BlockSpec((total, size), lambda i: (0, base + i))

    def block_of(array):
        return pl.BlockSpec((2,) + array.shape[1:], lambda i: (i,) + (0,) * (len(array.shape) - 1))

    pltpu.emit_pipeline(
        whole_body,
        grid=(DEPTH,),
        in_specs=[from_block((1 - x) * DEPTH)],
        out_specs=[block_of(gate_xs)],
    )(normed_ref, gate_xs)
    gate_x = remote(gate_xs, gate_xr, stage_s, stage_r, 0, x_mate)
    gate_x.start()
    sums.first_hop()
    for n in (2, 3, 4):
        loads[n].wait()

    def pair_copies(b, t):
        size, pair = ROWS // 2, 2 * HEAD_DIM
        at = (
            pl.ds(b * DEPTH, DEPTH),
            pl.ds(pl.multiple_of((t // 2) * size, size), size),
            pl.ds(pl.multiple_of((t % 2) * pair, pair), pair),
        )
        number = b * DEPTH + t
        return (
            remote(odk_ref.at[at], got_dk.at[at], pair_s, pair_r, (0, number), y_mate),
            remote(odv_ref.at[at], got_dv.at[at], pair_s, pair_r, (1, number), y_mate),
        )

    def attend_back(i, carry):
        b, t = i // DEPTH, i % DEPTH
        heads = Heads(b, t, z, y, q_ref, kv_ref, okv_ref)
        attend_back_one(
            heads, attended_grad, dq_ref, dk_ref, dv_ref, odk_ref, odv_ref, key_sum, value_sum
        )
        for copy in pair_copies(b, t):
            copy.start()
        return carry

    lax.fori_loop(0, PIECES, attend_back, 0)

    write_out((dq_ref, dq_out), (dk_ref, dk_out), (dv_ref, dv_out))
    sums.second_hop()
    sums.third_hop()

    pltpu.emit_pipeline(
        split_body,
        grid=(PIECES,),
        in_specs=[from_block(0)],
        out_specs=[block_of(gate_yk), block_of(gate_ys)],
    )(normed_ref, gate_yk, gate_ys)
    gate_y = remote(gate_ys, gate_yr, stage_s, stage_r, 1, y_mate)
    gate_y.start()

    pltpu.emit_pipeline(
        whole_body,
        grid=(DEPTH,),
        in_specs=[from_block(x * DEPTH)],
        out_specs=[block_of(gate_xk)],
    )(normed_ref, gate_xk)

    loads[5].wait()
    loads[6].wait()
    sums.last_hop()
    for first in range(0, ROWS, 64):
        rows = pl.ds(first, 64)
        layer = token_rows[rows].astype(wide) + valid_ref[rows] * own_sum[rows]
        layer_out[rows] = layer.astype(low)

    def sums_body(xk, xr, yk, yr, yk_own, yr_own, y2s, x2s, own_x, own_y):
        y2s[...] = (xk[:, 1 - y] + xr[:, 1 - y].astype(wide)).astype(low)
        own_x[...] = xk[:, y] + xr[:, y].astype(wide)
        x2s[...] = (yk[...] + yr[...].astype(wide)).astype(low)
        own_y[...] = yk_own[...] + yr_own[...].astype(wide)

    def two_blocks(array, base=0):
        return pl.BlockSpec(
            (2,) + array.shape[1:], lambda i: (base + i,) + (0,) * (len(array.shape) - 1)
        )

    gate_x.wait_recv()
    gate_y.wait_recv()
    theirs, ours = (1 - x) * DEPTH, x * DEPTH
    pltpu.emit_pipeline(
        sums_body,
        grid=(DEPTH,),
        in_specs=[
            two_blocks(gate_xk),
            two_blocks(gate_xr),
            two_blocks(gate_yk, theirs),
            two_blocks(gate_yr, theirs),
            two_blocks(gate_yk, ours),
            two_blocks(gate_yr, ours),
        ],
        out_specs=[two_blocks(r) for r in (gate_y2s, gate_x2s, gate_own_x, gate_own_y)],
    )(
        gate_xk,
        gate_xr,
        gate_yk,
        gate_yr,
        gate_yk,
        gate_yr,
        gate_y2s,
        gate_x2s,
        gate_own_x,
        gate_own_y,
    )
    for b in range(2):
        for t in range(DEPTH):
            for copy in pair_copies(b, t):
                copy.wait_recv()
                copy.wait_send()
    sums.sent_all()
    for copy in written:
        copy.wait()
    for copy in (gate_x, gate_y):
        copy.wait_send()


def backward(
    grads, gate, up, normed, pieces, queries, pairs, other_pairs, rows_out, own_sum, terms, valid
):
    low, wide = jnp.bfloat16, jnp.float32
    width = pieces.shape[-1]
    columns = 2 * gate.shape[-1]
    cut = columns - 128
    rows = width // 32
    anywhere = pl.BlockSpec(memory_space=pl.ANY)
    inside = pl.BlockSpec(memory_space=pltpu.VMEM)
    shape = jax.ShapeDtypeStruct
    dma = pltpu.SemaphoreType.DMA
    heads = shape((PIECES, ROWS, HEAD_COLS), wide)
    heads_low = shape((PIECES, ROWS, HEAD_COLS), low)
    gate_up = shape((PIECES, ROWS, columns), low)
    part = shape((DEPTH - 1, ROWS, width), low)
    half = shape((DEPTH * ROWS, 2 * HEAD_DIM), wide)
    return pl.pallas_call(
        backward_kernel,
        in_specs=[anywhere] * 11 + [inside],
        out_specs=[anywhere] * 16 + [inside],
        out_shape=[
            shape((PIECES, 2, rows, cut), low),
            shape((PIECES, 2, rows, cut), wide),
            shape((2 * PIECES, rows, columns - cut), low),
            shape((2 * PIECES, rows, columns - cut), wide),
            shape((PIECES, 2, rows, cut), low),
            shape((2 * PIECES, rows, columns - cut), low),
            shape((PIECES, rows, cut), low),
            shape((PIECES, rows, columns - cut), low),
            shape((PIECES, rows, cut), wide),
            shape((PIECES, rows, columns - cut), wide),
            gate_up,
            heads,
            heads,
            heads,
            heads_low,
            heads_low,
            shape((ROWS, width), low),
        ],
        scratch_shapes=[
            pltpu.VMEM(v.shape, v.dtype)
            for v in (
                queries,
                pairs,
                other_pairs,
                rows_out,
                own_sum,
                terms,
                gate_up,
                heads,
                heads,
                heads,
                heads_low,
                heads_low,
                heads_low,
                half,
                half,
                part,
                part,
                shape((ROWS, width), low),
            )
        ]
        + [
            dma((DEPTH - 1,)),
            dma((DEPTH - 1,)),
            dma((DEPTH - 1,)),
            dma((DEPTH - 1,)),
            dma((2, PIECES)),
            dma((2, PIECES)),
            dma((2,)),
            dma((2,)),
            dma((7,)),
            dma((4,)),
        ],
        compiler_params=params(62, collective_id=3, has_side_effects=True),
        cost_estimate=cost(0, 64 * MIB),
        name="backward",
    )(grads, gate, up, normed, pieces, queries, pairs, other_pairs, rows_out, own_sum, terms, valid)


def finish_kernel(
    dq_ref,
    dk_ref,
    dv_ref,
    odk_ref,
    odv_ref,
    gu_ref,
    pieces_ref,
    cos_ref,
    first_ref,
    second_ref,
    normed_ref,
    gate_y2s,
    gate_x2s,
    gate_sum_x,
    gate_sum_y,
    grads_ref,
    hidden_ref,
    att_ref,
    wi_ref,
    wg_ref,
    gain_ref,
    cot_ref,
    tokens_out,
    heads_out,
    hidden_out,
    gate_rows,
    inward_rows_out,
    vec_out,
    heads_term,
    hidden_term,
    heads_r,
    heads_2s,
    heads_2r,
    hidden_r,
    hidden_2s,
    hidden_2r,
    core_send,
    core_recv,
    z_send,
    below,
    above,
    own_sum,
    pg_ref,
    token_rows,
    vec_sum,
    vec_x,
    vec_y,
    gate_own_x,
    gate_own_y,
    gate_y2r,
    gate_x2r,
    gate_fin,
    inward_xs,
    inward_xr,
    inward_xk,
    inward_ys,
    inward_yr,
    inward_yk,
    inward_y2s,
    inward_y2r,
    inward_x2s,
    inward_x2r,
    inward_fin,
    core_s,
    core_r,
    up_s,
    down_s,
    below_r,
    above_r,
    stage_s,
    stage_r,
    rows_s,
    rows_r,
    vec_s,
    vec_r,
    local_sems,
):
    x, core, z, y = coordinates()
    low = jnp.bfloat16
    wide = jnp.float32

    def device(xx, cc, zz, yy):
        return (xx * 2 + cc, zz * 2 + yy)

    x_mate, y_mate = device(1 - x, core, z, y), device(x, core, z, 1 - y)
    core_mate = device(x, 1 - core, z, y)
    members = [(flip, turn) for turn in (2, 1, 3, 0) for flip in (1, 0)][:-1]

    def target(flip, turn):
        return (core + flip) % 2, (z + turn) % DEPTH

    greet([device(x, *target(*m), y) for m in members] + [x_mate, y_mate])

    started = []

    def begin(copy):
        copy.start()
        started.append(copy)
        return copy

    loads = [
        pltpu.make_async_copy(gate_sum_x, gate_own_x, local_sems.at[2]),
        pltpu.make_async_copy(gate_sum_y, gate_own_y, local_sems.at[3]),
    ]
    for load in loads:
        load.start()
    gate_y = begin(remote(gate_y2s, gate_y2r, stage_s, stage_r, (0, 2), y_mate))
    gate_x = begin(remote(gate_x2s, gate_x2r, stage_s, stage_r, (0, 3), x_mate))
    own_tokens = pltpu.make_async_copy(pieces_ref.at[0], token_rows, local_sems.at[4])
    own_tokens.start()

    vec_sum[...] = jnp.zeros_like(vec_sum)

    def core_copy(k):
        return remote(core_send.at[k % 2], core_recv.at[k], core_s, core_r, k, core_mate)

    sums = ChainSum(
        z_send, below, above, own_sum, x, core, z, y, (up_s, down_s, below_r, above_r)
    )

    def piece_of(i):
        return far_first(i // 2, z) + DEPTH * (1 - i % 2)

    def to_rows(which, fin, rows):
        slot = core * DEPTH + z
        copies = []
        for flip, turn in members:
            cc, zz = target(flip, turn)
            copies.append(
                remote(
                    fin.at[cc * DEPTH + zz],
                    rows.at[slot],
                    rows_s,
                    rows_r,
                    (which, flip * DEPTH + turn),
                    device(x, cc, zz, y),
                )
            )
        copies.append(pltpu.make_async_copy(fin.at[slot], rows.at[slot], local_sems.at[which]))
        return copies

    def gate_done():
        gate_y.wait_recv()
        gate_x.wait_recv()
        for load in loads:
            load.wait()
        gate_fin[...] = jnp.concatenate(
            [
                gate_own_x[...] + gate_y2r[...].astype(wide),
                gate_own_y[...] + gate_x2r[...].astype(wide),
            ],
            2,
        ).astype(low)
        for copy in to_rows(0, gate_fin, gate_rows):
            copy.start()

    def piece_body(
        dq, dk, dv, odk, odv, gu, tokens, cos, first, second
    ):
        step = pl.program_id(0)
        turn = step // 2
        piece = piece_of(step)
        tables = (cos, first, second)
        query = turned(dq[0] * (HEAD_DIM**-0.5), *tables, -1.0)
        key = turned(dk[0] + odk[0].astype(wide), *tables, -1.0)
        value = dv[0] + odv[0].astype(wide)
        narrow = jnp.concatenate([query, key, value], 1).astype(low)
        pg_ref[piece] = narrow
        grad = transposed_times(narrow, inward_rows(wi_ref))
        grad += transposed_times(gu[0], wg_ref[...])
        hat, _ = normalised(tokens[0])
        half = grad.shape[1] // 2
        for row, total in (
            (0, jnp.sum(grad * hat, axis=0, keepdims=True)),
            (2, jnp.sum(grad, axis=0, keepdims=True)),
        ):
            vec_sum[row : row + 1] += total[:, :half]
            vec_sum[row + 1 : row + 2] += total[:, half:]
        vec_sum[4:5, : 3 * HEAD_COLS] += jnp.sum(narrow.astype(wide), axis=0, keepdims=True)

        pl.when(step == GATE_STEP)(gate_done)
        pl.when(step == PIECES - 1)(sums.first_hop)

        @pl.when(step % 2 == 0)
        def _():
            @pl.when(turn >= 2)
            def _():
                core_copy(turn - 2).wait_send()

            core_send[turn % 2] = grad.astype(low)
            core_copy(turn).start()

        @pl.when(step % 2 == 1)
        def _():
            core_copy(turn).wait_recv()
            both = grad + core_recv[turn].astype(wide)

            @pl.when(turn < DEPTH - 1)
            def _():
                z_send[turn] = both.astype(low)
                sums.start(turn)

            @pl.when(turn == DEPTH - 1)
            def _():
                own_sum[...] = both

    def by_piece(width):
        return pl.BlockSpec((1, ROWS, width), lambda i: (piece_of(i), 0, 0))

    table_spec = pl.BlockSpec(
        (1,) + cos_ref.shape[1:], lambda i: (piece_of(i) % DEPTH, 0, 0)
    )
    pltpu.emit_pipeline(
        piece_body,
        grid=(PIECES,),
        in_specs=[by_piece(HEAD_COLS)] * 5
        + [by_piece(gu_ref.shape[-1]), by_piece(pieces_ref.shape[-1])]
        + [table_spec] * 3,
    )(
        dq_ref,
        dk_ref,
        dv_ref,
        odk_ref,
        odv_ref,
        gu_ref,
        pieces_ref,
        cos_ref,
        first_ref,
        second_ref,
    )
    vector_x = remote(vec_sum, vec_x, vec_s, vec_r, 0, x_mate)
    vector_x.start()

    total, width = normed_ref.shape
    size = width // PIECES
    cut = 3 * HEAD_COLS // 2

    def block(i):
        return jnp.where(i < DEPTH, (1 - x) * DEPTH + i, x * DEPTH + i - DEPTH)

    inward_x = remote(inward_xs, inward_xr, stage_s, stage_r, (1, 0), x_mate)

    def inward_body(left):
        i = pl.program_id(0)
        rhs = pg_ref[...].reshape(total, 3 * HEAD_COLS)
        term = times_transposed(left[...], rhs)
        first = term[:, :cut].reshape(2, 2, size // 4, cut)
        at = pl.ds((i % DEPTH) * 2, 2)

        @pl.when(i < DEPTH)
        def _():
            inward_xs[at] = first.astype(low)

        @pl.when(i >= DEPTH)
        def _():
            inward_xk[at] = first

        at = pl.ds(block(i) * 2, 2)
        split_rows(term[:, cut:], y, inward_yk.at[at], inward_ys.at[at])

        @pl.when(i == DEPTH - 1)
        def _():
            inward_x.start()

    pltpu.emit_pipeline(
        inward_body,
        grid=(PIECES,),
        in_specs=[pl.BlockSpec((total, size), lambda i: (0, block(i)))],
    )(normed_ref)
    started.append(inward_x)
    vector_x.wait_recv()
    vec_sum_x = vec_sum[...] + vec_x[...]
    vector_x.wait_send()
    vec_sum[...] = vec_sum_x
    vector_y = remote(vec_sum, vec_y, vec_s, vec_r, 1, y_mate)
    vector_y.start()
    inward_y = begin(remote(inward_ys, inward_yr, stage_s, stage_r, (1, 1), y_mate))

    def rows_grads(att, hidden):
        loads = [
            pltpu.make_async_copy(att_ref, att, local_sems.at[5]),
            pltpu.make_async_copy(hidden_ref, hidden, local_sems.at[6]),
        ]
        for load in loads:
            load.start()
        for load in loads:
            load.wait()

        def body(right, heads_part, hidden_part):
            grad = right[...]
            term = times_transposed(att[...].reshape(total, att.shape[2]), grad)
            heads_part[...] = term.astype(low).reshape(heads_part.shape)
            term = times_transposed(hidden[...].reshape(total, hidden.shape[2]), grad)
            hidden_part[...] = term.astype(low).reshape(hidden_part.shape)

        def columns_of(array):
            return pl.BlockSpec(array.shape[:3] + (2 * size,), lambda i: (0, 0, 0, i))

        pltpu.emit_pipeline(
            body,
            grid=(width // (2 * size),),
            in_specs=[pl.BlockSpec((total, 2 * size), lambda i: (0, i))],
            out_specs=[columns_of(heads_term), columns_of(hidden_term)],
        )(grads_ref, heads_term, hidden_term)

    pl.run_scoped(
        rows_grads, *[pltpu.VMEM(r.shape, r.dtype) for r in (att_ref, hidden_ref)]
    )
    vector_y.wait_recv()
    vec_sum_y = vec_sum[...] + vec_y[...]
    vector_y.wait_send()
    slot = core * DEPTH + z
    vec_out[slot] = vec_sum_y
    vectors = []
    for flip, turn in members:
        cc, zz = target(flip, turn)
        vectors.append(
            begin(
                remote(
                    vec_out.at[slot],
                    vec_out.at[slot],
                    rows_s,
                    rows_r,
                    (2, flip * DEPTH + turn),
                    device(x, cc, zz, y),
                )
            )
        )

    sums.second_hop()
    inward_x.wait_recv()
    inward_y2s[...] = (inward_xk[:, 1 - y] + inward_xr[:, 1 - y].astype(wide)).astype(low)
    inward_over_y = begin(remote(inward_y2s, inward_y2r, stage_s, stage_r, (1, 2), y_mate))
    inward_y.wait_recv()
    other = pl.ds((1 - x) * PIECES, PIECES)
    inward_x2s[...] = (inward_yk[other] + inward_yr[other].astype(wide)).astype(low)
    inward_over_x = begin(remote(inward_x2s, inward_x2r, stage_s, stage_r, (1, 3), x_mate))
    left, right = pl.ds(0, width // 2), pl.ds(width // 2, width // 2)
    heads_x = begin(remote(heads_term.at[1 - x], heads_r, stage_s, stage_r, (2, 0), x_mate))
    hidden_x = begin(
        remote(
            hidden_term.at[1 - x, :, :, left],
            hidden_r.at[pl.ds(0, 2)],
            stage_s,
            stage_r,
            (3, 0),
            x_mate,
        )
    )
    hidden_y = [
        begin(
            remote(
                hidden_term.at[n, 1 - y, :, right],
                hidden_r.at[2 + n],
                stage_s,
                stage_r,
                (3, 1 + n),
                y_mate,
            )
        )
        for n in range(2)
    ]
    sums.third_hop()

    inward_over_y.wait_recv()
    inward_over_x.wait_recv()
    own = pl.ds(x * PIECES, PIECES)
    inward_fin[...] = jnp.concatenate(
        [
            inward_xk[:, y] + inward_xr[:, y].astype(wide) + inward_y2r[...].astype(wide),
            inward_yk[own] + inward_yr[own].astype(wide) + inward_x2r[...].astype(wide),
        ],
        2,
    ).astype(low)
    inward_rest = to_rows(1, inward_fin, inward_rows_out)
    for copy in inward_rest:
        copy.start()

    def row_sum(*refs):
        spec = pl.BlockSpec((refs[0].shape[0], refs[0].shape[1] // 2), lambda i: (0, i))

        def body(*parts):
            total = parts[0][...].astype(wide)
            for part in parts[1:-1]:
                total = total + part[...].astype(wide)
            parts[-1][...] = total.astype(parts[-1].dtype)

        pltpu.emit_pipeline(
            body, grid=(2,), in_specs=[spec] * (len(refs) - 1), out_specs=[spec]
        )(*refs)

    heads_x.wait_recv()
    row_sum(heads_term.at[x, 1 - y], heads_r.at[1 - y], heads_2s)
    heads_y = begin(remote(heads_2s, heads_2r, stage_s, stage_r, (2, 2), y_mate))
    for copy in hidden_y:
        copy.wait_recv()
    row_sum(hidden_term.at[1 - x, y, :, right], hidden_r.at[2 + 1 - x], hidden_2s.at[1])
    over_x = begin(remote(hidden_2s.at[1], hidden_2r.at[1], stage_s, stage_r, (2, 3), x_mate))
    hidden_x.wait_recv()
    row_sum(hidden_term.at[x, 1 - y, :, left], hidden_r.at[1 - y], hidden_2s.at[0])
    over_y = begin(remote(hidden_2s.at[0], hidden_2r.at[0], stage_s, stage_r, (3, 3), y_mate))
    heads_y.wait_recv()
    row_sum(heads_term.at[x, y], heads_r.at[y], heads_2r, heads_out)
    over_x.wait_recv()
    row_sum(
        hidden_term.at[x, y, :, right], hidden_r.at[2 + x], hidden_2r.at[1], hidden_out.at[:, right]
    )
    over_y.wait_recv()
    row_sum(hidden_term.at[x, y, :, left], hidden_r.at[y], hidden_2r.at[0], hidden_out.at[:, left])

    own_tokens.wait()
    sums.last_hop()
    for first in range(0, ROWS, 64):
        rows = pl.ds(first, 64)
        grad = own_sum[rows]
        hat, inverse = normalised(token_rows[rows])
        scaled = grad * gain_ref[...]
        input_grad = inverse * (
            scaled
            - jnp.mean(scaled, axis=-1, keepdims=True)
            - hat * jnp.mean(scaled * hat, axis=-1, keepdims=True)
        )
        tokens_out[rows] = (cot_ref[rows].astype(wide) + input_grad).astype(low)

    for copy in to_rows(0, gate_fin, gate_rows) + inward_rest:
        copy.wait()
    for copy in vectors:
        copy.wait_recv()
    for copy in started:
        copy.wait_send()
    for turn in range(DEPTH - 2, DEPTH):
        core_copy(turn).wait_send()
    sums.sent_all()


def finish(
    parts, gate_up_grad, pieces, tables, normed, gate_up, grads, hidden, attended, weights, gain, cot
):
    low, wide = jnp.bfloat16, jnp.float32
    width = pieces.shape[-1]
    rows = width // 32
    anywhere = pl.BlockSpec(memory_space=pl.ANY)
    inside = pl.BlockSpec(memory_space=pltpu.VMEM)
    shape = jax.ShapeDtypeStruct
    half = 3 * HEAD_COLS // 2

    a, b = (value.shape[-1] for value in gate_up[:2])
    heads_rows, hidden_rows = HEAD_DIM, hidden.shape[2] // 4
    out_shapes = [
        shape((ROWS, width), low),
        shape((heads_rows, width), wide),
        shape((hidden_rows, width), wide),
        shape((PIECES, rows, a + b), low),
        shape((PIECES, rows, 2 * half), low),
        shape((PIECES, 8, width // 2), wide),
    ]
    out_shapes += [
        shape((2, 2, heads_rows, width), low),
        shape((2, 2, hidden_rows, width), low),
        shape((2, heads_rows, width), low),
        shape((heads_rows, width), low),
        shape((heads_rows, width), low),
        shape((4, hidden_rows, width // 2), low),
        shape((2, hidden_rows, width // 2), low),
        shape((2, hidden_rows, width // 2), low),
    ]
    out_specs = [inside] + [anywhere] * 4 + [inside] + [anywhere] * (len(out_shapes) - 6)
    dma = pltpu.SemaphoreType.DMA
    outs = pl.pallas_call(
        finish_kernel,
        in_specs=[anywhere] * 18 + [inside] * 4,
        out_specs=out_specs,
        out_shape=out_shapes,
        scratch_shapes=[
            pltpu.VMEM((2, ROWS, width), low),
            pltpu.VMEM((DEPTH, ROWS, width), low),
            pltpu.VMEM((DEPTH - 1, ROWS, width), low),
            pltpu.VMEM((DEPTH - 1, ROWS, width), low),
            pltpu.VMEM((DEPTH - 1, ROWS, width), low),
            pltpu.VMEM((ROWS, width), wide),
            pltpu.VMEM((PIECES, ROWS, 3 * HEAD_COLS), low),
            pltpu.VMEM((ROWS, width), low),
            pltpu.VMEM((8, width // 2), wide),
            pltpu.VMEM((8, width // 2), wide),
            pltpu.VMEM((8, width // 2), wide),
            pltpu.VMEM((PIECES, rows, a), wide),
            pltpu.VMEM((PIECES, rows, b), wide),
            pltpu.VMEM((PIECES, rows, a), low),
            pltpu.VMEM((PIECES, rows, b), low),
            pltpu.VMEM((PIECES, rows, a + b), low),
            pltpu.VMEM((PIECES, 2, rows, half), low),
            pltpu.VMEM((PIECES, 2, rows, half), low),
            pltpu.VMEM((PIECES, 2, rows, half), wide),
            pltpu.VMEM((2 * PIECES, rows, half), low),
            pltpu.VMEM((2 * PIECES, rows, half), low),
            pltpu.VMEM((2 * PIECES, rows, half), wide),
            pltpu.VMEM((PIECES, rows, half), low),
            pltpu.VMEM((PIECES, rows, half), low),
            pltpu.VMEM((PIECES, rows, half), low),
            pltpu.VMEM((PIECES, rows, half), low),
            pltpu.VMEM((PIECES, rows, 2 * half), low),
            dma((DEPTH,)),
            dma((DEPTH,)),
            dma((DEPTH - 1,)),
            dma((DEPTH - 1,)),
            dma((DEPTH - 1,)),
            dma((DEPTH - 1,)),
            dma((4, 4)),
            dma((4, 4)),
            dma((3, PIECES)),
            dma((3, PIECES)),
            dma((2,)),
            dma((2,)),
            dma((7,)),
        ],
        compiler_params=params(63, collective_id=1, has_side_effects=True),
        cost_estimate=cost(0, 64 * MIB),
        name="finish",
    )(
        *parts,
        gate_up_grad,
        pieces,
        *tables,
        normed,
        *gate_up,
        grads,
        hidden,
        attended,
        *weights,
        gain,
        cot,
    )
    return outs[:6]


def split_rows(term, y, keep_ref, send_ref):
    rows = term.shape[0] // 4
    even = jnp.concatenate([term[:rows], term[2 * rows : 3 * rows]], 0)
    odd = jnp.concatenate([term[rows : 2 * rows], term[3 * rows :]], 0)
    keep_ref[...] = jnp.where(y == 0, even, odd).reshape(keep_ref.shape)
    send_ref[...] = jnp.where(y == 0, odd, even).astype(jnp.bfloat16).reshape(send_ref.shape)


def place_kernel(parts, in_ref, out_ref):
    each = in_ref.shape[2] // parts
    for part in range(parts):
        columns = slice(part * each, (part + 1) * each)
        line = jnp.concatenate([in_ref[n, :, columns] for n in range(PIECES)], 1)
        out_ref[:, part * PIECES * each : (part + 1) * PIECES * each] = line.astype(jnp.float32)


def place_rows(value, parts):
    rows, columns = value.shape[1], value.shape[2]
    return pl.pallas_call(
        functools.partial(place_kernel, parts),
        out_shape=jax.ShapeDtypeStruct((rows, PIECES * columns), jnp.float32),
        compiler_params=params(32),
        cost_estimate=cost(0, 4 * MIB),
        name="place_rows",
    )(value)


def shards_grouped(
    tokens,
    lengths,
    norm_gain,
    norm_shift,
    inward_weight,
    inward_bias,
    outward_weight,
    gate_up_weight,
    down_weight,
    cotangent,
):
    group_len, seqs, width = tokens.shape[1:]
    bucket, blk = lax.axis_index("bucket"), lax.axis_index("blk")

    gain_share, bias_share = norm_gain.shape[0], inward_bias.shape[0]
    shares = jnp.concatenate(
        [norm_gain, norm_gain, norm_shift, norm_shift, inward_bias, jnp.zeros((624,), jnp.float32)]
    ).reshape(8, 128)
    own_tokens = jnp.transpose(tokens[0], (1, 0, 2)).reshape(ROWS, width)
    own_cotangent = jnp.transpose(cotangent[0], (1, 0, 2)).reshape(ROWS, width)
    position = blk * group_len + jnp.arange(group_len, dtype=jnp.int32)
    valid = (position[None, :] < lengths[0][:, None]).astype(jnp.float32).reshape(ROWS, 1)
    lane = jnp.arange(HEAD_COLS, dtype=jnp.int32) % HEAD_DIM
    power = (lane % (ROT // 2)).astype(jnp.float32)
    frequency = jnp.where(lane < ROT, rotary_base ** (-(2.0 * power) / ROT), 0.0)
    (
        pieces,
        normed,
        gate,
        up,
        grads,
        inward,
        gate_up,
        rows_out,
        queries,
        pairs,
        other_pairs,
        hidden,
        attended,
        own_sum,
        terms,
        *tables,
        gain,
    ) = forward(
        own_tokens,
        own_cotangent,
        inward_weight,
        gate_up_weight,
        outward_weight,
        down_weight,
        valid,
        shares,
        inward_bias.reshape(1, -1),
        frequency.reshape(1, -1),
    )
    gate_up = gate_up.reshape(width, -1)
    normed = normed.reshape(PIECES * ROWS, width)
    def placed(value):
        value = value.reshape(seqs, group_len, width)
        return jnp.transpose(value, (1, 0, 2)).reshape(tokens.shape)

    outs = backward(
        grads,
        gate,
        up,
        normed,
        pieces,
        queries,
        pairs,
        other_pairs,
        rows_out,
        own_sum,
        terms,
        valid,
    )
    gate_up_grad, *parts, layer_out = outs[10:]
    layer_out, normed = lax.optimization_barrier((placed(layer_out), normed))
    tokens_grad, outward_sum, down_sum, gate_up_rows, inward_rows_own, vectors = finish(
        parts,
        gate_up_grad,
        pieces,
        tables,
        normed,
        outs[6:10],
        grads.reshape(PIECES * ROWS, width),
        hidden,
        attended,
        (inward, gate_up),
        gain,
        own_cotangent,
    )
    gate_up_sum = place_rows(gate_up_rows, 4)
    inward_sum = place_rows(inward_rows_own, 6)

    device = bucket * 2 * DEPTH + blk
    sums = jnp.sum(vectors[:, :4], axis=0).reshape(2, -1, gain_share)
    gain_sum = one_of(sums[0], device, 0)
    shift_sum = one_of(sums[1], device, 0)
    columns_sum = vectors[:, 4, : 3 * HEAD_COLS].reshape(PIECES, 3, 2, 2 * HEAD_DIM)
    columns_sum = jnp.transpose(columns_sum, (1, 2, 0, 3)).reshape(3, -1)
    key_rot = columns_sum[1].reshape(HEADS, HEAD_DIM)[:, :ROT]
    bias_all = jnp.concatenate([columns_sum[0], columns_sum[2], key_rot.reshape(-1)])
    bias_sum = one_of(bias_all.reshape(-1, bias_share), device, 0)

    return (
        layer_out,
        placed(tokens_grad),
        gain_sum,
        shift_sum,
        inward_sum,
        bias_sum,
        outward_sum,
        gate_up_sum,
        down_sum,
    )


def solution(mesh):
    in_specs = (
        P("bucket", "blk", None, None),
        P("bucket", None),
        P(("bucket", "blk")),
        P(("bucket", "blk")),
        P(("bucket", "blk"), None),
        P(("bucket", "blk")),
        P(("bucket", "blk"), None),
        P(("bucket", "blk"), None),
        P(("bucket", "blk"), None),
        P("bucket", "blk", None, None),
    )
    out_specs = (
        P("bucket", "blk", None, None),
        P("bucket", "blk", None, None),
        P(("bucket", "blk")),
        P(("bucket", "blk")),
        P(("bucket", "blk"), None),
        P(("bucket", "blk")),
        P(("bucket", "blk"), None),
        P(("bucket", "blk"), None),
        P(("bucket", "blk"), None),
    )
    body = shards_grouped if fits_groups(mesh) else shards_general
    return jax.shard_map(body, mesh=mesh, in_specs=in_specs, out_specs=out_specs, check_vma=False)
```

```python
import functools

import jax
import jax.numpy as jnp
from jax import lax
from jax.experimental import pallas as pl
from jax.experimental.pallas import tpu as pltpu
from jax.sharding import PartitionSpec as P

HEADS = 32
HEAD_DIM = 64
ROT = 16


epsilon = 1e-05
rotary_base = 10000.0
masked_score = -1e30


def shifted(value, axis, by):
    count = lax.axis_size(axis)
    pairs = [(i, i + by) for i in range(count) if 0 <= i + by < count]
    return lax.ppermute(value, axis, pairs)


def shifted_2(value, axis, steps):
    count = lax.axis_size(axis)
    pairs = [(source, (source + steps) % count) for source in range(count)]
    return lax.ppermute(value, axis, pairs)


def keep_same(value):
    return value


def transposed_times(left, right):
    return lax.dot_general(
        left, right, (((1,), (1,)), ((), ())), preferred_element_type=jnp.float32
    )


def times_transposed(left, right):
    return lax.dot_general(
        left, right, (((0,), (0,)), ((), ())), preferred_element_type=jnp.float32
    )


def rotary_tables(positions):
    half_rot = ROT // 2
    frequency = rotary_base ** (-(2.0 * jnp.arange(half_rot).astype(jnp.float32)) / ROT)
    angles = positions.astype(jnp.float32)[:, None] * frequency[None, :]
    return (jnp.cos(angles), jnp.sin(angles))


def rotate(values, cos_table, sine_table):
    half_rot = ROT // 2
    front_half = values[..., :half_rot]
    back_half = values[..., half_rot:ROT]
    return jnp.concatenate(
        [
            front_half * cos_table - back_half * sine_table,
            back_half * cos_table + front_half * sine_table,
            values[..., ROT:],
        ],
        axis=-1,
    )


def split_pairs(packed):
    rows_here, seq_count, both_width = packed.shape
    half_width = both_width // 2
    keys_part = packed[..., :half_width].reshape(rows_here, seq_count, HEADS, HEAD_DIM)
    values_part = packed[..., half_width:].reshape(rows_here, seq_count, HEADS, HEAD_DIM)
    return (keys_part, values_part)


def block_scores(queries, key_block, query_start, key_start):
    scores = jnp.einsum("tshd,ushd->shtu", queries, key_block, preferred_element_type=jnp.float32)
    query_pos = query_start + jnp.arange(queries.shape[0], dtype=jnp.int32)
    key_pos = key_start + jnp.arange(key_block.shape[0], dtype=jnp.int32)
    allowed = (key_pos[None, :] <= query_pos[:, None])[None, None]
    return (jnp.where(allowed, scores, masked_score), allowed)


def forward_block(carried, queries, key_block, value_block, query_start, key_start):
    running_max, running_sum, weighted = carried
    scores, allowed = block_scores(queries, key_block, query_start, key_start)
    new_max = jnp.maximum(running_max, jnp.max(scores, axis=-1))
    rescale = jnp.exp(running_max - new_max)
    weights = jnp.where(allowed, jnp.exp(scores - new_max[..., None]), 0.0)
    running_sum = running_sum * rescale + jnp.sum(weights, axis=-1)
    update = jnp.einsum(
        "shtu,ushd->tshd",
        weights.astype(jnp.bfloat16),
        value_block,
        preferred_element_type=jnp.float32,
    )
    weighted = weighted * jnp.transpose(rescale, (2, 0, 1))[..., None] + update
    return (new_max, running_sum, weighted)


def pair_grads(
    queries, out_grads, log_norm, deltas, key_block, value_block, query_start, key_start
):
    scores, allowed = block_scores(queries, key_block, query_start, key_start)
    probability = jnp.where(allowed, jnp.exp(scores - log_norm[..., None]), 0.0)
    value_grad = jnp.einsum(
        "shtu,tshd->ushd",
        probability.astype(jnp.bfloat16),
        out_grads,
        preferred_element_type=jnp.float32,
    )
    prob_grad = jnp.einsum(
        "tshd,ushd->shtu", out_grads, value_block, preferred_element_type=jnp.float32
    )
    score_grad = (probability * (prob_grad - deltas[..., None])).astype(jnp.bfloat16)
    query_grad = jnp.einsum(
        "shtu,ushd->tshd", score_grad, key_block, preferred_element_type=jnp.float32
    )
    key_grad = jnp.einsum(
        "shtu,tshd->ushd", score_grad, queries, preferred_element_type=jnp.float32
    )
    return (query_grad, key_grad, value_grad)


def over_blocks(running, incoming, unit_rows, handle):
    total_rows = incoming[0].shape[0]
    block_count = total_rows // unit_rows
    block_rows = total_rows // block_count
    stacked = tuple(
        (member.reshape((block_count, block_rows) + member.shape[1:]) for member in incoming)
    )

    def visit(carried, element):
        block_index, members = element
        return (handle(carried, members, block_index * block_rows), None)

    running, unused = lax.scan(visit, running, (jnp.arange(block_count, dtype=jnp.int32), stacked))
    return running


def shards_general(
    tokens,
    lengths,
    norm_gain,
    norm_shift,
    inward_weight,
    inward_bias,
    outward_weight,
    gate_up_weight,
    down_weight,
    cotangent,
):
    group_len = tokens.shape[1]
    seq_count = tokens.shape[2]
    model_width = tokens.shape[3]
    row_total = group_len * seq_count
    block_total = lax.axis_size("blk")
    position = lax.axis_index("blk")
    own_start = position * group_len
    longest = jnp.max(lengths[0])
    active = own_start < longest
    gathered = (
        lax.all_gather(inward_weight.astype(jnp.bfloat16), ("bucket", "blk"), axis=0, tiled=True),
        lax.all_gather(outward_weight.astype(jnp.bfloat16), ("bucket", "blk"), axis=0, tiled=True),
        lax.all_gather(gate_up_weight.astype(jnp.bfloat16), ("bucket", "blk"), axis=0, tiled=True),
        lax.all_gather(down_weight.astype(jnp.bfloat16), ("bucket", "blk"), axis=0, tiled=True),
        lax.all_gather(norm_gain.astype(jnp.bfloat16), ("bucket", "blk"), axis=0, tiled=True),
        lax.all_gather(norm_shift.astype(jnp.bfloat16), ("bucket", "blk"), axis=0, tiled=True),
        lax.all_gather(inward_bias.astype(jnp.bfloat16), ("bucket", "blk"), axis=0, tiled=True),
    )
    inward_full, outward_full, gate_up_full, down_full, gain_full, shift_full, bias_full = gathered
    inputs = tokens.reshape(row_total, model_width).astype(jnp.float32)
    centred = inputs - jnp.mean(inputs, axis=-1, keepdims=True)
    variance = jnp.mean(centred * centred, axis=-1, keepdims=True)
    inverse = lax.rsqrt(variance + epsilon)
    normal_hat = centred * inverse
    normed_low = (
        normal_hat * gain_full.astype(jnp.float32) + shift_full.astype(jnp.float32)
    ).astype(jnp.bfloat16)
    bias_float = bias_full.astype(jnp.float32)
    key_bias = jnp.pad(
        bias_float[2 * model_width :].reshape(HEADS, ROT), ((0, 0), (0, HEAD_DIM - ROT))
    ).reshape(model_width)
    full_bias = jnp.concatenate(
        [bias_float[:model_width], key_bias, bias_float[model_width : 2 * model_width]]
    )
    projected = jnp.dot(normed_low, inward_full, preferred_element_type=jnp.float32) + full_bias
    projected = projected.reshape(group_len, seq_count, 3, HEADS, HEAD_DIM)
    cos_table, sine_table = rotary_tables(own_start + jnp.arange(group_len, dtype=jnp.int32))
    cos_table = cos_table[:, None, None, :]
    sine_table = sine_table[:, None, None, :]
    query_scale = HEAD_DIM ** (-0.5)
    queries = (rotate(projected[:, :, 0], cos_table, sine_table) * query_scale).astype(jnp.bfloat16)
    keys_low = rotate(projected[:, :, 1], cos_table, sine_table).astype(jnp.bfloat16)
    values_low = projected[:, :, 2].astype(jnp.bfloat16)
    packed = jnp.concatenate(
        [
            keys_low.reshape(group_len, seq_count, model_width),
            values_low.reshape(group_len, seq_count, model_width),
        ],
        axis=-1,
    )

    def forward_handle(carried, members, key_start):
        keys_part, values_part = split_pairs(members[0])
        needed = active & (key_start <= own_start + group_len - 1)

        def forward_compute(state_in):
            return forward_block(state_in, queries, keys_part, values_part, own_start, key_start)

        return lax.cond(needed, forward_compute, keep_same, carried)

    start_state = (
        jnp.full((seq_count, HEADS, group_len), masked_score, jnp.float32),
        jnp.zeros((seq_count, HEADS, group_len), jnp.float32),
        jnp.zeros((group_len, seq_count, HEADS, HEAD_DIM), jnp.float32),
    )
    running_max, running_sum, weighted = over_blocks(
        start_state, (lax.all_gather(packed, "blk", axis=0, tiled=True),), group_len, forward_handle
    )
    bounded = jnp.maximum(running_sum, 1.0)
    log_norm = running_max + jnp.log(bounded)
    attended = weighted / jnp.transpose(bounded, (2, 0, 1))[..., None]
    attended_rows = attended.astype(jnp.bfloat16).reshape(row_total, model_width)
    gate_up = jnp.dot(normed_low, gate_up_full, preferred_element_type=jnp.float32)
    ff_width = gate_up.shape[1] // 2
    gate_part = gate_up[:, :ff_width]
    up_part = gate_up[:, ff_width:]
    sigmoid_gate = jax.nn.sigmoid(gate_part)
    silu_gate = gate_part * sigmoid_gate
    hidden_low = (silu_gate * up_part).astype(jnp.bfloat16)
    branch = jnp.dot(attended_rows, outward_full, preferred_element_type=jnp.float32) + jnp.dot(
        hidden_low, down_full, preferred_element_type=jnp.float32
    )
    query_pos = own_start + jnp.arange(group_len, dtype=jnp.int32)
    valid_rows = (
        (query_pos[:, None] < lengths[0][None, :]).astype(jnp.float32).reshape(row_total, 1)
    )
    layer_out = (inputs + valid_rows * branch).astype(jnp.bfloat16).reshape(tokens.shape)
    inward_back = gathered[0]
    outward_back = gathered[1]
    gate_up_back = gathered[2]
    down_back = gathered[3]
    gain_float = gathered[4].astype(jnp.float32)
    cotangent_rows = cotangent.reshape(row_total, model_width).astype(jnp.float32)
    branch_grad = (cotangent_rows * valid_rows).astype(jnp.bfloat16)
    hidden_grad = transposed_times(branch_grad, down_back)
    gate_grad = hidden_grad * up_part * (sigmoid_gate + silu_gate * (1.0 - sigmoid_gate))
    up_grad = hidden_grad * silu_gate
    gate_up_grad_low = jnp.concatenate([gate_grad, up_grad], axis=-1).astype(jnp.bfloat16)
    down_term = times_transposed(hidden_low, branch_grad)
    gate_up_term = times_transposed(normed_low, gate_up_grad_low)
    gate_up_sum, down_sum = (
        lax.psum_scatter(gate_up_term, ("bucket", "blk"), scatter_dimension=0, tiled=True),
        lax.psum_scatter(down_term, ("bucket", "blk"), scatter_dimension=0, tiled=True),
    )
    normed_grad = transposed_times(gate_up_grad_low, gate_up_back)
    attended_grad = (
        transposed_times(branch_grad, outward_back)
        .astype(jnp.bfloat16)
        .reshape(group_len, seq_count, HEADS, HEAD_DIM)
    )
    outward_term = times_transposed(attended_rows, branch_grad)
    deltas = jnp.transpose(
        jnp.sum(attended_grad.astype(jnp.float32) * attended, axis=-1), (1, 2, 0)
    )
    grad_zeros = jnp.zeros((group_len, seq_count, 2 * model_width), jnp.float32)
    query_zeros = jnp.zeros((group_len, seq_count, HEADS, HEAD_DIM), jnp.float32)

    def cycle_turn(turn_index, carried):
        visiting, sums_now, grads_now = carried
        owner_index = (position - turn_index) % block_total
        key_start = owner_index * group_len
        needed = active & (owner_index <= position)

        def cycle_compute(sums_in):
            keys_part, values_part = split_pairs(visiting)
            query_part, key_part, value_part = pair_grads(
                queries,
                attended_grad,
                log_norm,
                deltas,
                keys_part,
                values_part,
                own_start,
                key_start,
            )
            merged = jnp.concatenate(
                [
                    key_part.reshape(group_len, seq_count, model_width),
                    value_part.reshape(group_len, seq_count, model_width),
                ],
                axis=-1,
            )
            return (sums_in[0] + merged, sums_in[1] + query_part)

        sums_now, grads_now = lax.cond(needed, cycle_compute, keep_same, (sums_now, grads_now))
        visiting = shifted(visiting, "blk", 1)
        sums_now = shifted_2(sums_now.astype(jnp.bfloat16), "blk", 1).astype(sums_now.dtype)
        return (visiting, sums_now, grads_now)

    unused, pair_sums, query_grads = lax.fori_loop(
        0, block_total, cycle_turn, (packed, grad_zeros, query_zeros)
    )
    key_grad = pair_sums[..., :model_width].reshape(group_len, seq_count, HEADS, HEAD_DIM)
    value_grad = pair_sums[..., model_width:].reshape(group_len, seq_count, HEADS, HEAD_DIM)
    back_sine = -sine_table
    query_back = rotate(query_grads * query_scale, cos_table, back_sine)
    key_back = rotate(key_grad, cos_table, back_sine)
    projected_grad = (
        jnp.stack([query_back, key_back, value_grad], axis=2)
        .reshape(row_total, 3 * model_width)
        .astype(jnp.bfloat16)
    )
    inward_term = times_transposed(normed_low, projected_grad)
    column_sums = jnp.sum(projected_grad.astype(jnp.float32), axis=0)
    key_bias_grad = (
        column_sums[model_width : 2 * model_width]
        .reshape(HEADS, HEAD_DIM)[:, :ROT]
        .reshape(HEADS * ROT)
    )
    bias_term = jnp.concatenate(
        [column_sums[:model_width], column_sums[2 * model_width :], key_bias_grad]
    )
    normed_grad = normed_grad + transposed_times(projected_grad, inward_back)
    gain_term = jnp.sum(normed_grad * normal_hat, axis=0)
    shift_term = jnp.sum(normed_grad, axis=0)
    scaled_grad = normed_grad * gain_float
    input_grad = inverse * (
        scaled_grad
        - jnp.mean(scaled_grad, axis=-1, keepdims=True)
        - normal_hat * jnp.mean(scaled_grad * normal_hat, axis=-1, keepdims=True)
    )
    tokens_grad = (cotangent_rows + input_grad).astype(jnp.bfloat16).reshape(tokens.shape)
    inward_sum, outward_sum, bias_sum, gain_sum, shift_sum = (
        lax.psum_scatter(inward_term, ("bucket", "blk"), scatter_dimension=0, tiled=True),
        lax.psum_scatter(outward_term, ("bucket", "blk"), scatter_dimension=0, tiled=True),
        lax.psum_scatter(bias_term, ("bucket", "blk"), scatter_dimension=0, tiled=True),
        lax.psum_scatter(gain_term, ("bucket", "blk"), scatter_dimension=0, tiled=True),
        lax.psum_scatter(shift_term, ("bucket", "blk"), scatter_dimension=0, tiled=True),
    )
    return (
        layer_out,
        tokens_grad,
        gain_sum,
        shift_sum,
        inward_sum,
        bias_sum,
        outward_sum,
        gate_up_sum,
        down_sum,
    )


DEPTH = 4
PIECES = 2 * DEPTH
ROWS = 256
GATE_STEP = 5
HALFWAY = 5
LOCAL_HEADS = 4
HEAD_COLS = LOCAL_HEADS * HEAD_DIM


MIB = 1024 * 1024


def fits_groups(mesh):
    return mesh.shape["bucket"] == 4 and mesh.shape["blk"] == 2 * DEPTH


def around(step):
    return [(z * 2 + y, ((z + step) % DEPTH) * 2 + y) for z in range(DEPTH) for y in range(2)]


def in_order(own, other, index, axis):
    return jnp.where(
        index == 0, jnp.stack([own, other], axis), jnp.stack([other, own], axis)
    )


def one_of(value, index, axis):
    return lax.dynamic_index_in_dim(value, index, axis, False)


def dot_rows(left, right):
    return lax.dot_general(
        left, right, (((1,), (0,)), ((), ())), preferred_element_type=jnp.float32
    )


def params(limit, **extra):
    return pltpu.CompilerParams(vmem_limit_bytes=limit * MIB, **extra)


def cost(flops, moved, exps=0):
    return pl.CostEstimate(flops=flops // 64, bytes_accessed=moved // 64, transcendentals=exps // 64)


def piece_spec(width):
    return pl.BlockSpec((1, ROWS, width), lambda i: (i, 0, 0))


def whole_spec(shape):
    return pl.BlockSpec(shape, lambda i: (0,) * len(shape))


def remote_to(src, dst, send_sem, recv_sem, device):
    return pltpu.make_async_remote_copy(
        src_ref=src,
        dst_ref=dst,
        send_sem=send_sem,
        recv_sem=recv_sem,
        device_id=device,
        device_id_type=pl.DeviceIdType.MESH,
    )


def remote(src, dst, sends, recvs, index, device):
    return remote_to(src, dst, sends.at[index], recvs.at[index], device)


def select(i, first, second, third):
    return jnp.where(i == 0, first, jnp.where(i == 1, second, jnp.where(i == 2, third, 0)))


class Chain:
    def __init__(self, src, out, x, core, z, y, sems):
        up_s, down_s, arrive, core_s, core_r, local = sems
        self.z = z
        self.out = out

        def hop(k, src, slot, sends, dz):
            return pltpu.make_async_remote_copy(
                src_ref=src,
                dst_ref=out.at[slot],
                send_sem=sends.at[k],
                recv_sem=arrive.at[slot],
                device_id=(x * 2 + core, (z + dz) * 2 + y),
                device_id_type=pl.DeviceIdType.MESH,
            )

        mate = (x * 2 + 1 - core, z * 2 + y)
        self.ups = [hop(k, src if k == 0 else out.at[k], k + 1, up_s, 1) for k in range(3)]
        self.downs = [
            hop(k, src if k == 0 else out.at[DEPTH - k], 3 - k, down_s, -1) for k in range(3)
        ]
        self.cores = [
            remote(src if k == 0 else out.at[k], out.at[DEPTH + k], core_s, core_r, k, mate)
            for k in range(DEPTH)
        ]
        self.local = pltpu.make_async_copy(src, out.at[0], local)
        inner = (z > 0) & (z < DEPTH - 1)
        self.sent = [
            (z < DEPTH - 1, self.ups[0]),
            (z > 0, self.downs[0]),
            (inner, self.ups[1]),
            (inner, self.downs[1]),
            (z == DEPTH - 2, self.ups[2]),
            (z == 1, self.downs[2]),
        ]

    def start(self, *numbers):
        for number in numbers:
            condition, copy = self.sent[number]
            pl.when(condition)(copy.start)

    def near(self):
        self.cores[0].start()
        self.local.start()

    def first(self):
        self.start(0, 1)

    def first_apart(self):
        pl.when(self.z < DEPTH // 2)(self.ups[0].start)
        pl.when(self.z >= DEPTH // 2)(self.downs[0].start)

    def first_rest(self):
        pl.when(self.z == DEPTH // 2)(self.ups[0].start)
        pl.when(self.z == DEPTH // 2 - 1)(self.downs[0].start)

    def inner(self, step):
        pl.when((self.z > 0) & (self.z < DEPTH - 1))(step)

    def outer(self, step):
        pl.when((self.z == 0) | (self.z == DEPTH - 1))(step)

    def second(self):
        @pl.when(self.z > 0)
        def _():
            self.ups[0].wait_recv()
            self.cores[1].start()

        self.start(2)

        @pl.when(self.z < DEPTH - 1)
        def _():
            self.downs[0].wait_recv()
            self.cores[3].start()

        self.start(3)

    def third(self):
        self.ups[1].wait_recv()
        self.cores[2].start()
        self.start(4, 5)

    def fourth(self):
        @pl.when(self.z == DEPTH - 1)
        def _():
            self.ups[2].wait_recv()
            self.cores[3].start()

        @pl.when(self.z == 0)
        def _():
            self.downs[2].wait_recv()
            self.cores[1].start()

    def end(self, arrivals=True):
        if arrivals:
            for copy in self.cores:
                copy.wait_recv()
            self.local.wait()
        for copy in self.cores:
            copy.wait_send()
        for condition, copy in self.sent:
            pl.when(condition)(copy.wait_send)


def far_first(i, z):
    inner = jnp.where(z == 1, select(i, 2, 1, 3), select(i, 2, 3, 1))
    outer = jnp.where(z == 0, select(i, 1, 2, 3), select(i, 3, 2, 1))
    return jnp.where((z == 0) | (z == DEPTH - 1), outer, inner)


class ChainSum:
    def __init__(self, send, below, above, own, x, core, z, y, sems):
        self.send, self.below, self.above, self.own = send, below, above, own
        self.z = z
        self.up_s, self.down_s, self.below_r, self.above_r = sems
        self.goal_up = (x * 2 + core, (z + 1) * 2 + y)
        self.goal_down = (x * 2 + core, (z - 1) * 2 + y)

    def up(self, slot, number):
        return remote_to(
            self.send.at[slot],
            self.below.at[number],
            self.up_s.at[slot],
            self.below_r.at[number],
            self.goal_up,
        )

    def down(self, slot, number):
        return remote_to(
            self.send.at[slot],
            self.above.at[number],
            self.down_s.at[slot],
            self.above_r.at[number],
            self.goal_down,
        )

    def when(self, z):
        return pl.when(self.z == z)

    def start(self, turn):
        @self.when(0)
        def _():
            self.up(turn, turn).start()

        @self.when(DEPTH - 1)
        def _():
            self.down(turn, turn).start()

    def wait_below(self, number):
        box = self.below.at[number]
        remote_to(box, box, self.up_s.at[0], self.below_r.at[number], self.goal_up).wait_recv()

    def wait_above(self, number):
        box = self.above.at[number]
        remote_to(box, box, self.down_s.at[0], self.above_r.at[number], self.goal_up).wait_recv()

    def add(self, slot, value):
        total = self.send[slot].astype(jnp.float32) + value.astype(jnp.float32)
        self.send[slot] = total.astype(jnp.bfloat16)

    def pass_up(self, slot, number, sent):
        self.wait_below(number)
        self.add(slot, self.below[number])
        self.up(slot, sent).start()

    def pass_down(self, slot, number, sent):
        self.wait_above(number)
        self.add(slot, self.above[number])
        self.down(slot, sent).start()

    def first_hop(self):
        self.when(1)(lambda: self.pass_up(0, 0, 0))
        self.when(DEPTH - 2)(lambda: self.pass_down(0, 0, 0))

    def second_hop(self):
        self.when(1)(lambda: self.pass_up(2, 1, 1))
        self.when(DEPTH - 2)(lambda: self.pass_down(2, 1, 1))

    def third_hop(self):
        self.when(1)(lambda: self.pass_down(1, 0, 0))
        self.when(DEPTH - 2)(lambda: self.pass_up(1, 0, 0))

    def last_hop(self):
        below, above, wide = self.below, self.above, jnp.float32

        @self.when(0)
        def _():
            self.wait_above(0)
            self.own[...] += above[0].astype(wide)

        @self.when(1)
        def _():
            self.wait_below(2)
            self.wait_above(1)
            self.own[...] += below[2].astype(wide) + above[1].astype(wide)

        @self.when(DEPTH - 2)
        def _():
            self.wait_below(1)
            self.wait_above(2)
            self.own[...] += below[1].astype(wide) + above[2].astype(wide)

        @self.when(DEPTH - 1)
        def _():
            self.wait_below(0)
            self.own[...] += below[0].astype(wide)

    def sent_all(self):
        @self.when(0)
        def _():
            for slot in range(DEPTH - 1):
                self.up(slot, slot).wait_send()

        @self.when(DEPTH - 1)
        def _():
            for slot in range(DEPTH - 1):
                self.down(slot, slot).wait_send()

        @self.when(1)
        def _():
            self.up(0, 0).wait_send()
            self.up(2, 1).wait_send()
            self.down(1, 0).wait_send()

        @self.when(DEPTH - 2)
        def _():
            self.down(0, 0).wait_send()
            self.down(2, 1).wait_send()
            self.up(1, 0).wait_send()


def chain_sems():
    dma = pltpu.SemaphoreType.DMA
    return [dma((3,)), dma((3,)), dma((DEPTH,)), dma((DEPTH,)), dma((DEPTH,)), dma(())]


def greet(mates):
    barrier = pltpu.get_barrier_semaphore()
    for mate in mates:
        pl.semaphore_signal(
            barrier, inc=1, device_id=mate, device_id_type=pl.DeviceIdType.MESH
        )
    pl.semaphore_wait(barrier, len(mates))


def coordinates():
    bucket, blk = lax.axis_index("bucket"), lax.axis_index("blk")
    return bucket // 2, bucket % 2, blk // 2, blk % 2


def inward_rows(ref):
    blocks, rows, columns = ref.shape
    return ref[...].reshape(blocks * rows, columns)


def outward_rows(ref):
    blocks, rows, columns = ref.shape
    return ref[:, :HEAD_DIM].reshape(blocks * HEAD_DIM, columns)


def down_rows(ref):
    blocks, rows, columns = ref.shape
    return ref[:, HEAD_DIM:].reshape(blocks * (rows - HEAD_DIM), columns)


def normalised(rows):
    inputs = rows.astype(jnp.float32)
    centred = inputs - jnp.mean(inputs, axis=-1, keepdims=True)
    variance = jnp.mean(centred * centred, axis=-1, keepdims=True)
    inverse = lax.rsqrt(variance + epsilon)
    return centred * inverse, inverse


def turned(values, cos_ref, first_ref, second_ref, sign):
    half = ROT // 2
    cos = jnp.concatenate([cos_ref[0], cos_ref[0]], 0)
    first = jnp.concatenate([first_ref[0], first_ref[0]], 0)
    second = jnp.concatenate([second_ref[0], second_ref[0]], 0)
    ahead = pltpu.roll(values, HEAD_COLS - half, 1)
    behind = pltpu.roll(values, half, 1)
    return values * cos + sign * (ahead * first + behind * second)


def forward_kernel(
    tokens_ref,
    cot_ref,
    inward_ref,
    gate_up_ref,
    outward_ref,
    down_ref,
    valid_ref,
    shares_ref,
    bias_ref,
    frequency_ref,
    pieces,
    normed_out,
    gate_out,
    up_out,
    grads_out,
    wi_out,
    wg_out,
    ro_out,
    q_out,
    kv_out,
    okv_out,
    hidden_out,
    att_out,
    own_out,
    terms_out,
    cos_out,
    first_out,
    second_out,
    gain_out,
    vec_ref,
    wi_own,
    wg_own,
    wi_ref,
    wg_ref,
    rows_ref,
    cos_ref,
    first_ref,
    second_ref,
    gain_ref,
    shift_ref,
    bias_rows,
    own_bias,
    own_grad,
    q_ref,
    kv_ref,
    okv_ref,
    hidden_ref,
    att_ref,
    own_sum,
    terms,
    core_send,
    core_recv,
    group_s,
    group_r,
    across_s,
    across_r,
    rows_s,
    rows_r,
    kv_s,
    kv_r,
    core_s,
    core_r,
    local_sems,
    out_sems,
    *chains,
):
    x, core, z, y = coordinates()
    low, wide = jnp.bfloat16, jnp.float32

    def device(xx, cc, zz, yy):
        return (xx * 2 + cc, zz * 2 + yy)

    def at(xx, cc, zz, yy):
        return ((xx * 2 + cc) * DEPTH + zz) * 2 + yy

    x_mate, y_mate = device(1 - x, core, z, y), device(x, core, z, 1 - y)
    core_mate = device(x, 1 - core, z, y)
    members = [(flip, turn) for turn in (0, 1, 3, 2) for flip in (0, 1)]

    def target(flip, turn):
        return (core + flip) % 2, (z + turn) % DEPTH

    def source(flip, turn):
        return (core + flip) % 2, (z + DEPTH - turn) % DEPTH

    started = []
    written = []

    def begin(copy):
        copy.start()
        started.append(copy)
        return copy

    def write_out(*pairs):
        for src, dst in pairs:
            copy = pltpu.make_async_copy(src, dst, out_sems.at[len(written)])
            copy.start()
            written.append(copy)

    def group_copies(which, own, full):
        mine = at(x, core, z, y)
        copies = {}
        for flip, turn in members[1:]:
            cc, zz = target(flip, turn)
            copies[flip, turn] = remote(
                own.at[cc * DEPTH + zz],
                full.at[mine],
                group_s,
                group_r,
                (which, flip * DEPTH + turn),
                device(x, cc, zz, y),
            )
        return copies

    def vector_copies():
        mine = vec_ref.at[at(x, core, z, y)]
        copies = {}
        for flip, turn in members[1:]:
            copies[flip, turn] = remote(
                mine,
                mine,
                group_s,
                group_r,
                (2, flip * DEPTH + turn),
                device(x, *target(flip, turn), y),
            )
        return copies

    def rows_copies():
        mine = rows_ref.at[x * 2 + y]
        return [
            remote(mine, mine, rows_s, rows_r, way, mate) for way, mate in enumerate((x_mate, y_mate))
        ]

    tokens = Chain(tokens_ref, pieces, x, core, z, y, chains[:6])
    grads = Chain(own_grad, grads_out, x, core, z, y, chains[6:])
    position = lax.broadcasted_iota(jnp.int32, (ROWS // 2, HEAD_COLS), 0)
    lane = lax.broadcasted_iota(jnp.int32, (ROWS // 2, HEAD_COLS), 1) % HEAD_DIM
    half = ROT // 2

    share_lane = lax.broadcasted_iota(jnp.int32, shares_ref.shape, 1)
    share_row = lax.broadcasted_iota(jnp.int32, shares_ref.shape, 0)
    own_shares = jnp.where((share_lane // HEAD_DIM == y) | (share_row >= 2), shares_ref[...], 0.0)

    def prepare(inward_f32, gate_up_f32, outward_f32, down_f32):
        loads = [
            pltpu.make_async_copy(src, dst, local_sems.at[n])
            for n, (src, dst) in enumerate(
                (
                    (inward_ref, inward_f32),
                    (gate_up_ref, gate_up_f32),
                    (outward_ref, outward_f32),
                    (down_ref, down_f32),
                )
            )
        ]
        for load in loads:
            load.start()
        greet([device(x, *target(*m), y) for m in members[1:]] + [x_mate, y_mate])
        tokens.near()
        loads[0].wait()
        vec_ref[at(x, core, z, y)] = own_shares
        for copy in vector_copies().values():
            copy.start()
        pair = 2 * HEAD_DIM
        for n in range(PIECES):
            starts = [part * PIECES * pair + n * pair for part in range(6)]
            line = jnp.concatenate([inward_f32[:, c : c + pair] for c in starts], 1)
            wi_own[n] = line.astype(low)
        wi_ref[at(x, core, z, y)] = wi_own[core * DEPTH + z]
        for copy in group_copies(0, wi_own, wi_ref).values():
            copy.start()
        loads[1].wait()
        each = gate_up_f32.shape[1] // (4 * PIECES)
        for n in range(PIECES):
            starts = [part * PIECES * each + n * each for part in range(4)]
            line = jnp.concatenate([gate_up_f32[:, c : c + each] for c in starts], 1)
            wg_own[n] = line.astype(low)
        wg_ref[at(x, core, z, y)] = wg_own[core * DEPTH + z]
        loads[2].wait()
        loads[3].wait()
        rows_ref[x * 2 + y, :HEAD_DIM] = outward_f32[...].astype(low)
        rows_ref[x * 2 + y, HEAD_DIM:] = down_f32[...].astype(low)

    pl.run_scoped(
        prepare,
        *[
            pltpu.VMEM(r.shape, r.dtype)
            for r in (inward_ref, gate_up_ref, outward_ref, down_ref)
        ],
    )
    inward = group_copies(0, wi_own, wi_ref)
    gate_up = group_copies(1, wg_own, wg_ref)
    vectors = vector_copies()
    started += [*inward.values(), *gate_up.values(), *vectors.values()]

    def spread(which, full, copies, halfway=None):
        pairs = {}
        for member in members:
            if halfway is not None and member == members[HALFWAY]:
                halfway()
            flip, turn = member
            cc, zz = source(flip, turn)
            if member != (0, 0):
                copies[member].wait_recv()
            block = full.at[at(x, cc, zz, y)]
            number = flip * DEPTH + turn
            pairs[member] = tuple(
                begin(remote(block, block, across_s, across_r, (which, way, number), mate))
                for way, mate in enumerate((x_mate, y_mate))
            )
        return pairs

    def by_x(which, flip):
        return which != 1 or flip == 0

    def corner(which, full, pairs):
        copies = []
        for member in members:
            flip, turn = member
            cc, zz = source(flip, turn)
            number = flip * DEPTH + turn
            if by_x(which, flip):
                pairs[member][1].wait_recv()
                block, mate = full.at[at(x, cc, zz, 1 - y)], x_mate
            else:
                pairs[member][0].wait_recv()
                block, mate = full.at[at(1 - x, cc, zz, y)], y_mate
            copies.append(
                begin(remote(block, block, across_s, across_r, (which, 2, number), mate))
            )
        return copies

    def complete(which, pairs, copies):
        for flip, turn in members:
            pairs[flip, turn][0 if by_x(which, flip) else 1].wait_recv()
        for copy in copies:
            copy.wait_recv()

    frequency = frequency_ref[...]
    for k in range(DEPTH):
        first = (2 * lax.rem(z + DEPTH - k, DEPTH) + y) * (ROWS // 2)
        angles = (first + position).astype(wide) * frequency
        sine = jnp.sin(angles)
        cos_ref[k] = jnp.cos(angles)
        first_ref[k] = jnp.where(lane < half, -sine, 0.0)
        second_ref[k] = jnp.where((lane >= half) & (lane < ROT), sine, 0.0)
    own_grad[...] = (cot_ref[...].astype(wide) * valid_ref[...]).astype(low)
    write_out((cos_ref, cos_out), (first_ref, first_out), (second_ref, second_out))

    vector_pairs = spread(2, vec_ref, vectors)
    inward_pairs = spread(0, wi_ref, inward)
    for copy in gate_up.values():
        copy.start()
    vector_corner = corner(2, vec_ref, vector_pairs)
    inward_corner = corner(0, wi_ref, inward_pairs)
    gate_up_pairs = spread(1, wg_ref, gate_up, tokens.first)
    complete(2, vector_pairs, vector_corner)
    complete(0, inward_pairs, inward_corner)
    write_out((wi_ref, wi_out))

    shares = vec_ref[...].astype(low).astype(wide)
    for row, vector in ((0, gain_ref), (1, shift_ref)):
        line = shares[:, row]
        vector[...] = jnp.concatenate(
            [line[2 * i : 2 * i + 1] + line[2 * i + 1 : 2 * i + 2] for i in range(16)], 1
        )
    each = bias_ref.shape[1]
    biases = jnp.concatenate([shares[:, 2], shares[:, 3]], 1)
    flat = jnp.concatenate([biases[i : i + 1, :each] for i in range(32)], 1)
    for i in range(flat.shape[1] // 128):
        bias_rows[i : i + 1] = flat[:, i * 128 : (i + 1) * 128]
    query_bias, key_bias, value_bias = [], [], []
    gap = jnp.zeros((1, HEAD_DIM - ROT), wide)
    for i in range(2):
        row = i * PIECES + core * DEPTH + z
        query_bias.append(bias_rows[pl.ds(row, 1)])
        value_bias.append(bias_rows[pl.ds(2 * PIECES + row, 1)])
        line = bias_rows[pl.ds(4 * PIECES + i * 2 + core, 1)]
        heads = [line[:, 2 * ROT * j : 2 * ROT * (j + 1)] for j in range(DEPTH)]
        chosen = jnp.where(
            z == 0, heads[0], jnp.where(z == 1, heads[1], jnp.where(z == 2, heads[2], heads[3]))
        )
        key_bias += [chosen[:, :ROT], gap, chosen[:, ROT:], gap]
    own_bias[...] = jnp.concatenate(query_bias + key_bias + value_bias, 1)
    write_out((gain_ref, gain_out))

    def pair_copy(piece):
        return remote(kv_ref.at[piece], okv_ref.at[piece], kv_s, kv_r, piece, y_mate)

    def project(piece, tokens_part, normed):
        k = lax.rem(piece, DEPTH)
        hat, _ = normalised(tokens_part[0])
        narrow = (hat * gain_ref[...] + shift_ref[...]).astype(low)
        normed[0] = narrow
        projected = dot_rows(narrow, inward_rows(wi_ref)) + own_bias[...]
        tables = (cos_ref.at[pl.ds(k, 1)], first_ref.at[pl.ds(k, 1)], second_ref.at[pl.ds(k, 1)])
        query = turned(projected[:, :HEAD_COLS], *tables, 1.0) * (HEAD_DIM**-0.5)
        key = turned(projected[:, HEAD_COLS : 2 * HEAD_COLS], *tables, 1.0)
        kv_ref[piece] = jnp.concatenate([key, projected[:, 2 * HEAD_COLS :]], 1).astype(low)
        pair_copy(piece).start()
        q_ref[piece] = query.astype(low)

    def piece_at(first, i):
        turn = first + i // 2
        near = jnp.where(z == 0, DEPTH - 1, 1)
        k = jnp.where(
            turn == 0, 0, jnp.where(turn == 1, near, jnp.where(turn == 2, 2, DEPTH - near))
        )
        return k + DEPTH * (i % 2)

    def project_pieces(first, count):
        spec = pl.BlockSpec((1,) + pieces.shape[1:], lambda i: (piece_at(first, i), 0, 0))
        pltpu.emit_pipeline(
            lambda *refs: project(piece_at(first, pl.program_id(0)), *refs),
            grid=(2 * count,),
            in_specs=[spec],
            out_specs=[spec],
        )(pieces, normed_out)

    def feed(first, count):
        def body(normed, gate_part, up_part):
            piece = piece_at(first, pl.program_id(0))
            both = dot_rows(normed[0], wg_ref[...].reshape(normed.shape[2], wg_ref.shape[2]))
            hidden = both.shape[1] // 2
            gate, up = both[:, :hidden], both[:, hidden:]
            gate_part[0] = gate
            up_part[0] = up
            hidden_ref[piece] = (gate * jax.nn.sigmoid(gate) * up).astype(low)

        def spec(array):
            return pl.BlockSpec(
                (1,) + array.shape[1:], lambda i: (piece_at(first, i), 0, 0)
            )

        pltpu.emit_pipeline(
            body,
            grid=(2 * count,),
            in_specs=[spec(normed_out)],
            out_specs=[spec(gate_out), spec(up_out)],
        )(normed_out, gate_out, up_out)

    near = jnp.where(z == 0, DEPTH - 1, 1)
    far = DEPTH - near

    def core_arrived(k):
        remote(pieces.at[k], pieces.at[DEPTH + k], chains[3], chains[4], k, core_mate).wait_recv()

    tokens.local.wait()
    core_arrived(0)
    project_pieces(0, 1)
    tokens.second()
    core_arrived(near)
    project_pieces(1, 1)
    gate_up_corner = corner(1, wg_ref, gate_up_pairs)
    rows_x, rows_y = rows_copies()
    begin(rows_x)
    begin(rows_y)
    tokens.third()
    grads.near()
    grads.first_apart()
    core_arrived(2)
    project_pieces(2, 1)
    complete(1, gate_up_pairs, gate_up_corner)
    feed(0, 2)
    tokens.fourth()
    grads.first_rest()
    core_arrived(far)
    project_pieces(3, 1)
    grads.inner(grads.second)
    rows_y.wait_recv()
    block = rows_ref.at[x * 2 + 1 - y]
    rows_corner = begin(remote(block, block, rows_s, rows_r, 2, x_mate))
    feed(2, 2)
    write_out((q_ref, q_out), (kv_ref, kv_out), (wg_ref, wg_out))

    for b in range(2):
        for j in range(DEPTH):
            pair_copy(b * DEPTH + j).wait_recv()

        def attend(t, carry):
            attend_one(Heads(b, t, z, y, q_ref, kv_ref, okv_ref), att_ref)
            return carry

        lax.fori_loop(0, LOCAL_HEADS, attend, 0)

    rows_x.wait_recv()
    rows_corner.wait_recv()
    write_out((hidden_ref, hidden_out), (att_ref, att_out), (okv_ref, okv_out), (rows_ref, ro_out))

    def core_copy(k):
        return remote(core_send.at[k % 2], core_recv.at[k], core_s, core_r, k, core_mate)

    def term(piece):
        return dot_rows(att_ref[piece], outward_rows(rows_ref)) + dot_rows(
            hidden_ref[piece], down_rows(rows_ref)
        )

    def branch(i, carry):
        k = far_first(i, z)

        @pl.when(i >= 2)
        def _():
            core_copy(i - 2).wait_send()

        core_send[i % 2] = term(DEPTH + k).astype(low)
        core_copy(i).start()
        own = term(k)
        core_copy(i).wait_recv()
        both = own + core_recv[i].astype(wide)

        @pl.when(i < DEPTH - 1)
        def _():
            terms[i] = both.astype(low)

        @pl.when(i == DEPTH - 1)
        def _():
            own_sum[...] = both

        return carry

    grads.inner(grads.third)
    lax.fori_loop(0, DEPTH, branch, 0)
    write_out((own_sum, own_out), (terms, terms_out))
    grads.outer(grads.second)
    grads.outer(grads.third)
    grads.fourth()
    grads.end()
    tokens.end(False)
    for i in range(DEPTH - 2, DEPTH):
        core_copy(i).wait_send()
    for piece in range(PIECES):
        pair_copy(piece).wait_send()
    for copy in started:
        copy.wait_send()
    for copy in written:
        copy.wait()


def forward(
    tokens, cot, inward, gate_up, outward, down, valid, shares, bias, frequency
):
    low, wide = jnp.bfloat16, jnp.float32
    rows, width = tokens.shape
    own_rows = inward.shape[0]
    group_columns = gate_up.shape[1] // PIECES
    hidden = group_columns // 2
    anywhere = pl.BlockSpec(memory_space=pl.ANY)
    inside = pl.BlockSpec(memory_space=pltpu.VMEM)
    shape = jax.ShapeDtypeStruct
    dma = pltpu.SemaphoreType.DMA
    wi_shape = shape((32, own_rows, 3 * HEAD_COLS), low)
    wg_shape = shape((32, own_rows, group_columns), low)
    ro_shape = shape((4, outward.shape[0] + down.shape[0], width), low)
    table = shape((DEPTH, ROWS // 2, HEAD_COLS), wide)
    heads = shape((PIECES, ROWS, HEAD_COLS), low)
    pairs = shape((PIECES, ROWS, 2 * HEAD_COLS), low)
    hidden_shape = shape((PIECES, ROWS, hidden), low)
    own_shape = shape((ROWS, width), wide)
    terms_shape = shape((DEPTH - 1, ROWS, width), low)
    vector = shape((1, width), wide)

    def scratch(*shapes):
        return [pltpu.VMEM(s.shape, s.dtype) for s in shapes]

    return pl.pallas_call(
        forward_kernel,
        in_specs=[anywhere] + [inside] + [anywhere] * 4 + [inside] * 4,
        out_specs=[anywhere] * 19,
        out_shape=[
            shape((PIECES, ROWS, width), low),
            shape((PIECES, ROWS, width), low),
            shape((PIECES, ROWS, hidden), wide),
            shape((PIECES, ROWS, hidden), wide),
            shape((PIECES, ROWS, width), low),
            wi_shape,
            wg_shape,
            ro_shape,
            heads,
            pairs,
            pairs,
            hidden_shape,
            heads,
            own_shape,
            terms_shape,
            table,
            table,
            table,
            vector,
        ],
        scratch_shapes=scratch(
            shape((32, 8, 128), wide),
            shape((PIECES,) + wi_shape.shape[1:], low),
            shape((PIECES,) + wg_shape.shape[1:], low),
            wi_shape,
            wg_shape,
            ro_shape,
            table,
            table,
            table,
            vector,
            vector,
            shape((40, 128), wide),
            shape((1, 3 * HEAD_COLS), wide),
            shape((ROWS, width), low),
            heads,
            pairs,
            pairs,
            hidden_shape,
            heads,
            own_shape,
            terms_shape,
            shape((2, ROWS, width), low),
            shape((DEPTH, ROWS, width), low),
        )
        + [
            dma((3, PIECES)),
            dma((3, PIECES)),
            dma((3, 3, PIECES)),
            dma((3, 3, PIECES)),
            dma((4,)),
            dma((4,)),
            dma((PIECES,)),
            dma((PIECES,)),
            dma((DEPTH,)),
            dma((DEPTH,)),
            dma((4,)),
            dma((14,)),
        ]
        + chain_sems()
        + chain_sems(),
        compiler_params=params(62, collective_id=0, has_side_effects=True),
        cost_estimate=cost(0, 64 * MIB),
        name="forward",
    )(tokens, cot, inward, gate_up, outward, down, valid, shares, bias, frequency)


def pair_rows(block):
    lane = lax.broadcasted_iota(jnp.int32, block.shape, 1)
    zero = jnp.zeros_like(block)
    return jnp.concatenate(
        [jnp.where(lane < HEAD_DIM, block, zero), jnp.where(lane < HEAD_DIM, zero, block)], 0
    )


def pair_lanes(rows):
    half = rows.shape[0] // 2
    lane = lax.broadcasted_iota(jnp.int32, (half, rows.shape[1]), 1)
    return jnp.where(lane < HEAD_DIM, rows[:half], rows[half:])


def block_probs(queries, keys, last, y):
    scores = transposed_times(queries, keys)
    rows, columns = scores.shape
    size = rows // 2
    row = lax.broadcasted_iota(jnp.int32, (rows, 2 * size), 0) % size
    column = lax.broadcasted_iota(jnp.int32, (rows, 2 * size), 1)
    allowed = (column <= row) | ((column >= size) & (y == 1))
    tail = jnp.where(allowed, scores[:, last * 2 * size :], masked_score)
    scores = tail if last == 0 else jnp.concatenate([scores[:, : last * 2 * size], tail], 1)
    weights = jnp.exp(scores - jnp.max(scores, axis=-1, keepdims=True))
    return weights * (1.0 / jnp.sum(weights, axis=-1, keepdims=True))


class Heads:
    def __init__(self, b, t, z, y, q_ref, kv_ref, okv_ref):
        size = ROWS // 2
        pair = 2 * HEAD_DIM
        self.b, self.z, self.y = b, z, y
        self.rows = pl.ds(pl.multiple_of((t // 2) * size, size), size)
        self.lanes = pl.ds(pl.multiple_of((t % 2) * pair, pair), pair)
        value_lanes = pl.ds(pl.multiple_of(HEAD_COLS + (t % 2) * pair, pair), pair)
        self.q_ref = q_ref

        def both(lanes):
            blocks = []
            for j in range(DEPTH):
                place = (self.piece(j), self.rows, lanes)
                blocks += [kv_ref[place], okv_ref[place]]
            return jnp.concatenate(blocks, 0)

        self.keys, self.values = both(self.lanes), both(value_lanes)

    def piece(self, j):
        return self.b * DEPTH + lax.rem(self.z + DEPTH - j, DEPTH)

    def place(self, j):
        return self.piece(j), self.rows, self.lanes

    def queries(self, j):
        return pair_rows(self.q_ref[self.place(j)])


def attend_one(heads, out_ref):
    for j in range(DEPTH):
        count = (j + 1) * ROWS
        probs = block_probs(heads.queries(j), heads.keys[:count], j, heads.y)
        out = dot_rows(probs.astype(jnp.bfloat16), heads.values[:count])
        out_ref[heads.place(j)] = pair_lanes(out).astype(jnp.bfloat16)


def attend_back_one(heads, grad_ref, dq_ref, dk_ref, dv_ref, odk_ref, odv_ref, key_sum, value_sum):
    half = ROWS // 2
    for j in reversed(range(DEPTH)):
        count = (j + 1) * ROWS
        queries = heads.queries(j)
        grads = pair_rows(grad_ref[heads.place(j)])
        keys, values = heads.keys[:count], heads.values[:count]
        probs = block_probs(queries, keys, j, heads.y)
        low = probs.astype(jnp.bfloat16)
        prob_grad = transposed_times(grads, values)
        delta = jnp.sum(low.astype(jnp.float32) * prob_grad, axis=-1, keepdims=True)
        score_grad = (probs * (prob_grad - delta)).astype(jnp.bfloat16)
        dq_ref[heads.place(j)] = pair_lanes(dot_rows(score_grad, keys))
        key_term = times_transposed(score_grad, queries)
        value_term = times_transposed(low, grads)
        if j == DEPTH - 1:
            key_sum[...] = key_term
            value_sum[...] = value_term
        else:
            key_sum[:count] += key_term
            value_sum[:count] += value_term
    for j in range(DEPTH):
        low = j * ROWS
        place = heads.place(j)
        dk_ref[place] = key_sum[low : low + half]
        dv_ref[place] = value_sum[low : low + half]
        odk_ref[place] = key_sum[low + half : low + ROWS].astype(jnp.bfloat16)
        odv_ref[place] = value_sum[low + half : low + ROWS].astype(jnp.bfloat16)


def backward_kernel(
    grads_ref,
    gate_ref,
    up_ref,
    normed_ref,
    pieces_ref,
    q_in,
    kv_in,
    okv_in,
    rows_in,
    own_in,
    terms_in,
    valid_ref,
    gate_xs,
    gate_xk,
    gate_ys,
    gate_yk,
    gate_xr,
    gate_yr,
    gate_y2s,
    gate_x2s,
    gate_own_x,
    gate_own_y,
    gu_out,
    dq_out,
    dk_out,
    dv_out,
    got_dk,
    got_dv,
    layer_out,
    q_ref,
    kv_ref,
    okv_ref,
    rows_ref,
    own_sum,
    terms,
    gu_ref,
    dq_ref,
    dk_ref,
    dv_ref,
    attended_grad,
    odk_ref,
    odv_ref,
    key_sum,
    value_sum,
    below,
    above,
    token_rows,
    up_s,
    down_s,
    below_r,
    above_r,
    pair_s,
    pair_r,
    stage_s,
    stage_r,
    load_sems,
    out_sems,
):
    x, core, z, y = coordinates()
    low, wide = jnp.bfloat16, jnp.float32
    y_mate = (x * 2 + core, z * 2 + 1 - y)

    x_mate = (2 - x * 2 + core, z * 2 + y)
    loads = {}
    for src, dst in (
        (terms_in, terms),
        (rows_in, rows_ref),
        (q_in, q_ref),
        (kv_in, kv_ref),
        (okv_in, okv_ref),
        (own_in, own_sum),
        (pieces_ref.at[0], token_rows),
    ):
        load = pltpu.make_async_copy(src, dst, load_sems.at[len(loads)])
        loads[len(loads)] = load
    loads[0].start()
    loads[1].start()
    written = []

    def write_out(*pairs):
        for src, dst in pairs:
            copy = pltpu.make_async_copy(src, dst, out_sems.at[len(written)])
            copy.start()
            written.append(copy)

    below_mate = (x * 2 + core, lax.rem(z + DEPTH - 1, DEPTH) * 2 + y)
    above_mate = (x * 2 + core, lax.rem(z + 1, DEPTH) * 2 + y)
    greet([x_mate, y_mate, below_mate, above_mate])
    sums = ChainSum(terms, below, above, own_sum, x, core, z, y, (up_s, down_s, below_r, above_r))
    loads[0].wait()
    for turn in range(DEPTH - 1):
        sums.start(turn)
    loads[1].wait()
    for n in range(2, len(loads)):
        loads[n].start()

    def piece_body(grad_part, gate_part, up_part):
        piece = pl.program_id(0)
        grad = grad_part[0]
        attended_grad[piece] = transposed_times(grad, outward_rows(rows_ref)).astype(low)
        hidden_grad = transposed_times(grad, down_rows(rows_ref))
        gate = gate_part[0]
        sig = jax.nn.sigmoid(gate)
        silu = gate * sig
        gate_grad = hidden_grad * up_part[0] * (sig + silu * (1.0 - sig))
        up_grad = hidden_grad * silu
        gu_ref[piece] = jnp.concatenate([gate_grad, up_grad], 1).astype(low)

    pltpu.emit_pipeline(
        piece_body,
        grid=(PIECES,),
        in_specs=[piece_spec(r.shape[-1]) for r in (grads_ref, gate_ref, up_ref)],
    )(grads_ref, gate_ref, up_ref)

    write_out((gu_ref, gu_out))
    total, width = normed_ref.shape
    size = width // PIECES
    columns = gu_ref.shape[-1]
    cut = gate_xs.shape[-1]

    def right(first, last):
        return gu_ref[...].reshape(total, columns)[:, first:last]

    def whole_body(left, out):
        term = times_transposed(left[...], right(0, cut)).astype(out.dtype)
        out[...] = term.reshape(out.shape)

    def split_body(left, keep, send):
        split_rows(times_transposed(left[...], right(cut, columns)), y, keep, send)

    def from_block(base):
        return pl.BlockSpec((total, size), lambda i: (0, base + i))

    def block_of(array):
        return pl.BlockSpec((2,) + array.shape[1:], lambda i: (i,) + (0,) * (len(array.shape) - 1))

    pltpu.emit_pipeline(
        whole_body,
        grid=(DEPTH,),
        in_specs=[from_block((1 - x) * DEPTH)],
        out_specs=[block_of(gate_xs)],
    )(normed_ref, gate_xs)
    gate_x = remote(gate_xs, gate_xr, stage_s, stage_r, 0, x_mate)
    gate_x.start()
    sums.first_hop()
    for n in (2, 3, 4):
        loads[n].wait()

    def pair_copies(b, t):
        size, pair = ROWS // 2, 2 * HEAD_DIM
        at = (
            pl.ds(b * DEPTH, DEPTH),
            pl.ds(pl.multiple_of((t // 2) * size, size), size),
            pl.ds(pl.multiple_of((t % 2) * pair, pair), pair),
        )
        number = b * DEPTH + t
        return (
            remote(odk_ref.at[at], got_dk.at[at], pair_s, pair_r, (0, number), y_mate),
            remote(odv_ref.at[at], got_dv.at[at], pair_s, pair_r, (1, number), y_mate),
        )

    def attend_back(i, carry):
        b, t = i // DEPTH, i % DEPTH
        heads = Heads(b, t, z, y, q_ref, kv_ref, okv_ref)
        attend_back_one(
            heads, attended_grad, dq_ref, dk_ref, dv_ref, odk_ref, odv_ref, key_sum, value_sum
        )
        for copy in pair_copies(b, t):
            copy.start()
        return carry

    lax.fori_loop(0, PIECES, attend_back, 0)

    write_out((dq_ref, dq_out), (dk_ref, dk_out), (dv_ref, dv_out))
    sums.second_hop()
    sums.third_hop()

    pltpu.emit_pipeline(
        split_body,
        grid=(PIECES,),
        in_specs=[from_block(0)],
        out_specs=[block_of(gate_yk), block_of(gate_ys)],
    )(normed_ref, gate_yk, gate_ys)
    gate_y = remote(gate_ys, gate_yr, stage_s, stage_r, 1, y_mate)
    gate_y.start()

    pltpu.emit_pipeline(
        whole_body,
        grid=(DEPTH,),
        in_specs=[from_block(x * DEPTH)],
        out_specs=[block_of(gate_xk)],
    )(normed_ref, gate_xk)

    loads[5].wait()
    loads[6].wait()
    sums.last_hop()
    for first in range(0, ROWS, 64):
        rows = pl.ds(first, 64)
        layer = token_rows[rows].astype(wide) + valid_ref[rows] * own_sum[rows]
        layer_out[rows] = layer.astype(low)

    def sums_body(xk, xr, yk, yr, yk_own, yr_own, y2s, x2s, own_x, own_y):
        y2s[...] = (xk[:, 1 - y] + xr[:, 1 - y].astype(wide)).astype(low)
        own_x[...] = xk[:, y] + xr[:, y].astype(wide)
        x2s[...] = (yk[...] + yr[...].astype(wide)).astype(low)
        own_y[...] = yk_own[...] + yr_own[...].astype(wide)

    def two_blocks(array, base=0):
        return pl.BlockSpec(
            (2,) + array.shape[1:], lambda i: (base + i,) + (0,) * (len(array.shape) - 1)
        )

    gate_x.wait_recv()
    gate_y.wait_recv()
    theirs, ours = (1 - x) * DEPTH, x * DEPTH
    pltpu.emit_pipeline(
        sums_body,
        grid=(DEPTH,),
        in_specs=[
            two_blocks(gate_xk),
            two_blocks(gate_xr),
            two_blocks(gate_yk, theirs),
            two_blocks(gate_yr, theirs),
            two_blocks(gate_yk, ours),
            two_blocks(gate_yr, ours),
        ],
        out_specs=[two_blocks(r) for r in (gate_y2s, gate_x2s, gate_own_x, gate_own_y)],
    )(
        gate_xk,
        gate_xr,
        gate_yk,
        gate_yr,
        gate_yk,
        gate_yr,
        gate_y2s,
        gate_x2s,
        gate_own_x,
        gate_own_y,
    )
    for b in range(2):
        for t in range(DEPTH):
            for copy in pair_copies(b, t):
                copy.wait_recv()
                copy.wait_send()
    sums.sent_all()
    for copy in written:
        copy.wait()
    for copy in (gate_x, gate_y):
        copy.wait_send()


def backward(
    grads, gate, up, normed, pieces, queries, pairs, other_pairs, rows_out, own_sum, terms, valid
):
    low, wide = jnp.bfloat16, jnp.float32
    width = pieces.shape[-1]
    columns = 2 * gate.shape[-1]
    cut = columns - 256
    rows = width // 32
    anywhere = pl.BlockSpec(memory_space=pl.ANY)
    inside = pl.BlockSpec(memory_space=pltpu.VMEM)
    shape = jax.ShapeDtypeStruct
    dma = pltpu.SemaphoreType.DMA
    heads = shape((PIECES, ROWS, HEAD_COLS), wide)
    heads_low = shape((PIECES, ROWS, HEAD_COLS), low)
    gate_up = shape((PIECES, ROWS, columns), low)
    part = shape((DEPTH - 1, ROWS, width), low)
    half = shape((DEPTH * ROWS, 2 * HEAD_DIM), wide)
    return pl.pallas_call(
        backward_kernel,
        in_specs=[anywhere] * 11 + [inside],
        out_specs=[anywhere] * 16 + [inside],
        out_shape=[
            shape((PIECES, 2, rows, cut), low),
            shape((PIECES, 2, rows, cut), wide),
            shape((2 * PIECES, rows, columns - cut), low),
            shape((2 * PIECES, rows, columns - cut), wide),
            shape((PIECES, 2, rows, cut), low),
            shape((2 * PIECES, rows, columns - cut), low),
            shape((PIECES, rows, cut), low),
            shape((PIECES, rows, columns - cut), low),
            shape((PIECES, rows, cut), wide),
            shape((PIECES, rows, columns - cut), wide),
            gate_up,
            heads,
            heads,
            heads,
            heads_low,
            heads_low,
            shape((ROWS, width), low),
        ],
        scratch_shapes=[
            pltpu.VMEM(v.shape, v.dtype)
            for v in (
                queries,
                pairs,
                other_pairs,
                rows_out,
                own_sum,
                terms,
                gate_up,
                heads,
                heads,
                heads,
                heads_low,
                heads_low,
                heads_low,
                half,
                half,
                part,
                part,
                shape((ROWS, width), low),
            )
        ]
        + [
            dma((DEPTH - 1,)),
            dma((DEPTH - 1,)),
            dma((DEPTH - 1,)),
            dma((DEPTH - 1,)),
            dma((2, PIECES)),
            dma((2, PIECES)),
            dma((2,)),
            dma((2,)),
            dma((7,)),
            dma((4,)),
        ],
        compiler_params=params(62, collective_id=3, has_side_effects=True),
        cost_estimate=cost(0, 64 * MIB),
        name="backward",
    )(grads, gate, up, normed, pieces, queries, pairs, other_pairs, rows_out, own_sum, terms, valid)


def finish_kernel(
    dq_ref,
    dk_ref,
    dv_ref,
    odk_ref,
    odv_ref,
    gu_ref,
    pieces_ref,
    cos_ref,
    first_ref,
    second_ref,
    normed_ref,
    gate_y2s,
    gate_x2s,
    gate_sum_x,
    gate_sum_y,
    grads_ref,
    hidden_ref,
    att_ref,
    wi_ref,
    wg_ref,
    gain_ref,
    cot_ref,
    tokens_out,
    heads_out,
    hidden_out,
    gate_rows,
    inward_rows_out,
    vec_out,
    heads_term,
    hidden_term,
    heads_r,
    heads_2s,
    heads_2r,
    hidden_r,
    hidden_2s,
    hidden_2r,
    core_send,
    core_recv,
    z_send,
    below,
    above,
    own_sum,
    pg_ref,
    token_rows,
    vec_sum,
    vec_x,
    vec_y,
    gate_own_x,
    gate_own_y,
    gate_y2r,
    gate_x2r,
    gate_fin,
    inward_xs,
    inward_xr,
    inward_xk,
    inward_ys,
    inward_yr,
    inward_yk,
    inward_y2s,
    inward_y2r,
    inward_x2s,
    inward_x2r,
    inward_fin,
    core_s,
    core_r,
    up_s,
    down_s,
    below_r,
    above_r,
    stage_s,
    stage_r,
    rows_s,
    rows_r,
    vec_s,
    vec_r,
    local_sems,
):
    x, core, z, y = coordinates()
    low = jnp.bfloat16
    wide = jnp.float32

    def device(xx, cc, zz, yy):
        return (xx * 2 + cc, zz * 2 + yy)

    x_mate, y_mate = device(1 - x, core, z, y), device(x, core, z, 1 - y)
    core_mate = device(x, 1 - core, z, y)
    members = [(flip, turn) for turn in (2, 1, 3, 0) for flip in (1, 0)][:-1]

    def target(flip, turn):
        return (core + flip) % 2, (z + turn) % DEPTH

    greet([device(x, *target(*m), y) for m in members] + [x_mate, y_mate])

    started = []

    def begin(copy):
        copy.start()
        started.append(copy)
        return copy

    loads = [
        pltpu.make_async_copy(gate_sum_x, gate_own_x, local_sems.at[2]),
        pltpu.make_async_copy(gate_sum_y, gate_own_y, local_sems.at[3]),
    ]
    for load in loads:
        load.start()
    gate_y = begin(remote(gate_y2s, gate_y2r, stage_s, stage_r, (0, 2), y_mate))
    gate_x = begin(remote(gate_x2s, gate_x2r, stage_s, stage_r, (0, 3), x_mate))
    own_tokens = pltpu.make_async_copy(pieces_ref.at[0], token_rows, local_sems.at[4])
    own_tokens.start()

    vec_sum[...] = jnp.zeros_like(vec_sum)

    def core_copy(k):
        return remote(core_send.at[k % 2], core_recv.at[k], core_s, core_r, k, core_mate)

    sums = ChainSum(
        z_send, below, above, own_sum, x, core, z, y, (up_s, down_s, below_r, above_r)
    )

    def piece_of(i):
        return far_first(i // 2, z) + DEPTH * (1 - i % 2)

    def to_rows(which, fin, rows):
        slot = core * DEPTH + z
        copies = []
        for flip, turn in members:
            cc, zz = target(flip, turn)
            copies.append(
                remote(
                    fin.at[cc * DEPTH + zz],
                    rows.at[slot],
                    rows_s,
                    rows_r,
                    (which, flip * DEPTH + turn),
                    device(x, cc, zz, y),
                )
            )
        copies.append(pltpu.make_async_copy(fin.at[slot], rows.at[slot], local_sems.at[which]))
        return copies

    def gate_done():
        gate_y.wait_recv()
        gate_x.wait_recv()
        for load in loads:
            load.wait()
        gate_fin[...] = jnp.concatenate(
            [
                gate_own_x[...] + gate_y2r[...].astype(wide),
                gate_own_y[...] + gate_x2r[...].astype(wide),
            ],
            2,
        ).astype(low)
        for copy in to_rows(0, gate_fin, gate_rows):
            copy.start()

    def piece_body(
        dq, dk, dv, odk, odv, gu, tokens, cos, first, second
    ):
        step = pl.program_id(0)
        turn = step // 2
        piece = piece_of(step)
        tables = (cos, first, second)
        query = turned(dq[0] * (HEAD_DIM**-0.5), *tables, -1.0)
        key = turned(dk[0] + odk[0].astype(wide), *tables, -1.0)
        value = dv[0] + odv[0].astype(wide)
        narrow = jnp.concatenate([query, key, value], 1).astype(low)
        pg_ref[piece] = narrow
        grad = transposed_times(narrow, inward_rows(wi_ref))
        grad += transposed_times(gu[0], wg_ref[...])
        hat, _ = normalised(tokens[0])
        half = grad.shape[1] // 2
        for row, total in (
            (0, jnp.sum(grad * hat, axis=0, keepdims=True)),
            (2, jnp.sum(grad, axis=0, keepdims=True)),
        ):
            vec_sum[row : row + 1] += total[:, :half]
            vec_sum[row + 1 : row + 2] += total[:, half:]
        vec_sum[4:5, : 3 * HEAD_COLS] += jnp.sum(narrow.astype(wide), axis=0, keepdims=True)

        pl.when(step == GATE_STEP)(gate_done)
        pl.when(step == PIECES - 1)(sums.first_hop)

        @pl.when(step % 2 == 0)
        def _():
            @pl.when(turn >= 2)
            def _():
                core_copy(turn - 2).wait_send()

            core_send[turn % 2] = grad.astype(low)
            core_copy(turn).start()

        @pl.when(step % 2 == 1)
        def _():
            core_copy(turn).wait_recv()
            both = grad + core_recv[turn].astype(wide)

            @pl.when(turn < DEPTH - 1)
            def _():
                z_send[turn] = both.astype(low)
                sums.start(turn)

            @pl.when(turn == DEPTH - 1)
            def _():
                own_sum[...] = both

    def by_piece(width):
        return pl.BlockSpec((1, ROWS, width), lambda i: (piece_of(i), 0, 0))

    table_spec = pl.BlockSpec(
        (1,) + cos_ref.shape[1:], lambda i: (piece_of(i) % DEPTH, 0, 0)
    )
    pltpu.emit_pipeline(
        piece_body,
        grid=(PIECES,),
        in_specs=[by_piece(HEAD_COLS)] * 5
        + [by_piece(gu_ref.shape[-1]), by_piece(pieces_ref.shape[-1])]
        + [table_spec] * 3,
    )(
        dq_ref,
        dk_ref,
        dv_ref,
        odk_ref,
        odv_ref,
        gu_ref,
        pieces_ref,
        cos_ref,
        first_ref,
        second_ref,
    )
    vector_x = remote(vec_sum, vec_x, vec_s, vec_r, 0, x_mate)
    vector_x.start()

    total, width = normed_ref.shape
    size = width // PIECES
    cut = 3 * HEAD_COLS // 2

    def block(i):
        return jnp.where(i < DEPTH, (1 - x) * DEPTH + i, x * DEPTH + i - DEPTH)

    inward_x = remote(inward_xs, inward_xr, stage_s, stage_r, (1, 0), x_mate)

    def inward_body(left):
        i = pl.program_id(0)
        rhs = pg_ref[...].reshape(total, 3 * HEAD_COLS)
        term = times_transposed(left[...], rhs)
        first = term[:, :cut].reshape(2, 2, size // 4, cut)
        at = pl.ds((i % DEPTH) * 2, 2)

        @pl.when(i < DEPTH)
        def _():
            inward_xs[at] = first.astype(low)

        @pl.when(i >= DEPTH)
        def _():
            inward_xk[at] = first

        at = pl.ds(block(i) * 2, 2)
        split_rows(term[:, cut:], y, inward_yk.at[at], inward_ys.at[at])

        @pl.when(i == DEPTH - 1)
        def _():
            inward_x.start()

    pltpu.emit_pipeline(
        inward_body,
        grid=(PIECES,),
        in_specs=[pl.BlockSpec((total, size), lambda i: (0, block(i)))],
    )(normed_ref)
    started.append(inward_x)
    vector_x.wait_recv()
    vec_sum_x = vec_sum[...] + vec_x[...]
    vector_x.wait_send()
    vec_sum[...] = vec_sum_x
    vector_y = remote(vec_sum, vec_y, vec_s, vec_r, 1, y_mate)
    vector_y.start()
    inward_y = begin(remote(inward_ys, inward_yr, stage_s, stage_r, (1, 1), y_mate))

    def rows_grads(att, hidden):
        loads = [
            pltpu.make_async_copy(att_ref, att, local_sems.at[5]),
            pltpu.make_async_copy(hidden_ref, hidden, local_sems.at[6]),
        ]
        for load in loads:
            load.start()
        for load in loads:
            load.wait()

        def body(right, heads_part, hidden_part):
            grad = right[...]
            term = times_transposed(att[...].reshape(total, att.shape[2]), grad)
            heads_part[...] = term.astype(low).reshape(heads_part.shape)
            term = times_transposed(hidden[...].reshape(total, hidden.shape[2]), grad)
            hidden_part[...] = term.astype(low).reshape(hidden_part.shape)

        def columns_of(array):
            return pl.BlockSpec(array.shape[:3] + (2 * size,), lambda i: (0, 0, 0, i))

        pltpu.emit_pipeline(
            body,
            grid=(width // (2 * size),),
            in_specs=[pl.BlockSpec((total, 2 * size), lambda i: (0, i))],
            out_specs=[columns_of(heads_term), columns_of(hidden_term)],
        )(grads_ref, heads_term, hidden_term)

    pl.run_scoped(
        rows_grads, *[pltpu.VMEM(r.shape, r.dtype) for r in (att_ref, hidden_ref)]
    )
    vector_y.wait_recv()
    vec_sum_y = vec_sum[...] + vec_y[...]
    vector_y.wait_send()
    slot = core * DEPTH + z
    vec_out[slot] = vec_sum_y
    vectors = []
    for flip, turn in members:
        cc, zz = target(flip, turn)
        vectors.append(
            begin(
                remote(
                    vec_out.at[slot],
                    vec_out.at[slot],
                    rows_s,
                    rows_r,
                    (2, flip * DEPTH + turn),
                    device(x, cc, zz, y),
                )
            )
        )

    sums.second_hop()
    inward_x.wait_recv()
    inward_y2s[...] = (inward_xk[:, 1 - y] + inward_xr[:, 1 - y].astype(wide)).astype(low)
    inward_over_y = begin(remote(inward_y2s, inward_y2r, stage_s, stage_r, (1, 2), y_mate))
    inward_y.wait_recv()
    other = pl.ds((1 - x) * PIECES, PIECES)
    inward_x2s[...] = (inward_yk[other] + inward_yr[other].astype(wide)).astype(low)
    inward_over_x = begin(remote(inward_x2s, inward_x2r, stage_s, stage_r, (1, 3), x_mate))
    left, right = pl.ds(0, width // 2), pl.ds(width // 2, width // 2)
    heads_x = begin(remote(heads_term.at[1 - x], heads_r, stage_s, stage_r, (2, 0), x_mate))
    hidden_x = begin(
        remote(
            hidden_term.at[1 - x, :, :, left],
            hidden_r.at[pl.ds(0, 2)],
            stage_s,
            stage_r,
            (3, 0),
            x_mate,
        )
    )
    hidden_y = [
        begin(
            remote(
                hidden_term.at[n, 1 - y, :, right],
                hidden_r.at[2 + n],
                stage_s,
                stage_r,
                (3, 1 + n),
                y_mate,
            )
        )
        for n in range(2)
    ]
    sums.third_hop()

    inward_over_y.wait_recv()
    inward_over_x.wait_recv()
    own = pl.ds(x * PIECES, PIECES)
    inward_fin[...] = jnp.concatenate(
        [
            inward_xk[:, y] + inward_xr[:, y].astype(wide) + inward_y2r[...].astype(wide),
            inward_yk[own] + inward_yr[own].astype(wide) + inward_x2r[...].astype(wide),
        ],
        2,
    ).astype(low)
    inward_rest = to_rows(1, inward_fin, inward_rows_out)
    for copy in inward_rest:
        copy.start()

    def row_sum(*refs):
        spec = pl.BlockSpec((refs[0].shape[0], refs[0].shape[1] // 2), lambda i: (0, i))

        def body(*parts):
            total = parts[0][...].astype(wide)
            for part in parts[1:-1]:
                total = total + part[...].astype(wide)
            parts[-1][...] = total.astype(parts[-1].dtype)

        pltpu.emit_pipeline(
            body, grid=(2,), in_specs=[spec] * (len(refs) - 1), out_specs=[spec]
        )(*refs)

    heads_x.wait_recv()
    row_sum(heads_term.at[x, 1 - y], heads_r.at[1 - y], heads_2s)
    heads_y = begin(remote(heads_2s, heads_2r, stage_s, stage_r, (2, 2), y_mate))
    for copy in hidden_y:
        copy.wait_recv()
    row_sum(hidden_term.at[1 - x, y, :, right], hidden_r.at[2 + 1 - x], hidden_2s.at[1])
    over_x = begin(remote(hidden_2s.at[1], hidden_2r.at[1], stage_s, stage_r, (2, 3), x_mate))
    hidden_x.wait_recv()
    row_sum(hidden_term.at[x, 1 - y, :, left], hidden_r.at[1 - y], hidden_2s.at[0])
    over_y = begin(remote(hidden_2s.at[0], hidden_2r.at[0], stage_s, stage_r, (3, 3), y_mate))
    heads_y.wait_recv()
    row_sum(heads_term.at[x, y], heads_r.at[y], heads_2r, heads_out)
    over_x.wait_recv()
    row_sum(
        hidden_term.at[x, y, :, right], hidden_r.at[2 + x], hidden_2r.at[1], hidden_out.at[:, right]
    )
    over_y.wait_recv()
    row_sum(hidden_term.at[x, y, :, left], hidden_r.at[y], hidden_2r.at[0], hidden_out.at[:, left])

    own_tokens.wait()
    sums.last_hop()
    for first in range(0, ROWS, 64):
        rows = pl.ds(first, 64)
        grad = own_sum[rows]
        hat, inverse = normalised(token_rows[rows])
        scaled = grad * gain_ref[...]
        input_grad = inverse * (
            scaled
            - jnp.mean(scaled, axis=-1, keepdims=True)
            - hat * jnp.mean(scaled * hat, axis=-1, keepdims=True)
        )
        tokens_out[rows] = (cot_ref[rows].astype(wide) + input_grad).astype(low)

    for copy in to_rows(0, gate_fin, gate_rows) + inward_rest:
        copy.wait()
    for copy in vectors:
        copy.wait_recv()
    for copy in started:
        copy.wait_send()
    for turn in range(DEPTH - 2, DEPTH):
        core_copy(turn).wait_send()
    sums.sent_all()


def finish(
    parts, gate_up_grad, pieces, tables, normed, gate_up, grads, hidden, attended, weights, gain, cot
):
    low, wide = jnp.bfloat16, jnp.float32
    width = pieces.shape[-1]
    rows = width // 32
    anywhere = pl.BlockSpec(memory_space=pl.ANY)
    inside = pl.BlockSpec(memory_space=pltpu.VMEM)
    shape = jax.ShapeDtypeStruct
    half = 3 * HEAD_COLS // 2

    a, b = (value.shape[-1] for value in gate_up[:2])
    heads_rows, hidden_rows = HEAD_DIM, hidden.shape[2] // 4
    out_shapes = [
        shape((ROWS, width), low),
        shape((heads_rows, width), wide),
        shape((hidden_rows, width), wide),
        shape((PIECES, rows, a + b), low),
        shape((PIECES, rows, 2 * half), low),
        shape((PIECES, 8, width // 2), wide),
    ]
    out_shapes += [
        shape((2, 2, heads_rows, width), low),
        shape((2, 2, hidden_rows, width), low),
        shape((2, heads_rows, width), low),
        shape((heads_rows, width), low),
        shape((heads_rows, width), low),
        shape((4, hidden_rows, width // 2), low),
        shape((2, hidden_rows, width // 2), low),
        shape((2, hidden_rows, width // 2), low),
    ]
    out_specs = [inside] + [anywhere] * 4 + [inside] + [anywhere] * (len(out_shapes) - 6)
    dma = pltpu.SemaphoreType.DMA
    outs = pl.pallas_call(
        finish_kernel,
        in_specs=[anywhere] * 18 + [inside] * 4,
        out_specs=out_specs,
        out_shape=out_shapes,
        scratch_shapes=[
            pltpu.VMEM((2, ROWS, width), low),
            pltpu.VMEM((DEPTH, ROWS, width), low),
            pltpu.VMEM((DEPTH - 1, ROWS, width), low),
            pltpu.VMEM((DEPTH - 1, ROWS, width), low),
            pltpu.VMEM((DEPTH - 1, ROWS, width), low),
            pltpu.VMEM((ROWS, width), wide),
            pltpu.VMEM((PIECES, ROWS, 3 * HEAD_COLS), low),
            pltpu.VMEM((ROWS, width), low),
            pltpu.VMEM((8, width // 2), wide),
            pltpu.VMEM((8, width // 2), wide),
            pltpu.VMEM((8, width // 2), wide),
            pltpu.VMEM((PIECES, rows, a), wide),
            pltpu.VMEM((PIECES, rows, b), wide),
            pltpu.VMEM((PIECES, rows, a), low),
            pltpu.VMEM((PIECES, rows, b), low),
            pltpu.VMEM((PIECES, rows, a + b), low),
            pltpu.VMEM((PIECES, 2, rows, half), low),
            pltpu.VMEM((PIECES, 2, rows, half), low),
            pltpu.VMEM((PIECES, 2, rows, half), wide),
            pltpu.VMEM((2 * PIECES, rows, half), low),
            pltpu.VMEM((2 * PIECES, rows, half), low),
            pltpu.VMEM((2 * PIECES, rows, half), wide),
            pltpu.VMEM((PIECES, rows, half), low),
            pltpu.VMEM((PIECES, rows, half), low),
            pltpu.VMEM((PIECES, rows, half), low),
            pltpu.VMEM((PIECES, rows, half), low),
            pltpu.VMEM((PIECES, rows, 2 * half), low),
            dma((DEPTH,)),
            dma((DEPTH,)),
            dma((DEPTH - 1,)),
            dma((DEPTH - 1,)),
            dma((DEPTH - 1,)),
            dma((DEPTH - 1,)),
            dma((4, 4)),
            dma((4, 4)),
            dma((3, PIECES)),
            dma((3, PIECES)),
            dma((2,)),
            dma((2,)),
            dma((7,)),
        ],
        compiler_params=params(63, collective_id=1, has_side_effects=True),
        cost_estimate=cost(0, 64 * MIB),
        name="finish",
    )(
        *parts,
        gate_up_grad,
        pieces,
        *tables,
        normed,
        *gate_up,
        grads,
        hidden,
        attended,
        *weights,
        gain,
        cot,
    )
    return outs[:6]


def split_rows(term, y, keep_ref, send_ref):
    rows = term.shape[0] // 4
    even = jnp.concatenate([term[:rows], term[2 * rows : 3 * rows]], 0)
    odd = jnp.concatenate([term[rows : 2 * rows], term[3 * rows :]], 0)
    keep_ref[...] = jnp.where(y == 0, even, odd).reshape(keep_ref.shape)
    send_ref[...] = jnp.where(y == 0, odd, even).astype(jnp.bfloat16).reshape(send_ref.shape)


def place_kernel(parts, in_ref, out_ref):
    each = in_ref.shape[2] // parts
    for part in range(parts):
        columns = slice(part * each, (part + 1) * each)
        line = jnp.concatenate([in_ref[n, :, columns] for n in range(PIECES)], 1)
        out_ref[:, part * PIECES * each : (part + 1) * PIECES * each] = line.astype(jnp.float32)


def place_rows(value, parts):
    rows, columns = value.shape[1], value.shape[2]
    return pl.pallas_call(
        functools.partial(place_kernel, parts),
        out_shape=jax.ShapeDtypeStruct((rows, PIECES * columns), jnp.float32),
        compiler_params=params(32),
        cost_estimate=cost(0, 4 * MIB),
        name="place_rows",
    )(value)


def shards_grouped(
    tokens,
    lengths,
    norm_gain,
    norm_shift,
    inward_weight,
    inward_bias,
    outward_weight,
    gate_up_weight,
    down_weight,
    cotangent,
):
    group_len, seqs, width = tokens.shape[1:]
    bucket, blk = lax.axis_index("bucket"), lax.axis_index("blk")

    gain_share, bias_share = norm_gain.shape[0], inward_bias.shape[0]
    shares = jnp.concatenate(
        [norm_gain, norm_gain, norm_shift, norm_shift, inward_bias, jnp.zeros((624,), jnp.float32)]
    ).reshape(8, 128)
    own_tokens = jnp.transpose(tokens[0], (1, 0, 2)).reshape(ROWS, width)
    own_cotangent = jnp.transpose(cotangent[0], (1, 0, 2)).reshape(ROWS, width)
    position = blk * group_len + jnp.arange(group_len, dtype=jnp.int32)
    valid = (position[None, :] < lengths[0][:, None]).astype(jnp.float32).reshape(ROWS, 1)
    lane = jnp.arange(HEAD_COLS, dtype=jnp.int32) % HEAD_DIM
    power = (lane % (ROT // 2)).astype(jnp.float32)
    frequency = jnp.where(lane < ROT, rotary_base ** (-(2.0 * power) / ROT), 0.0)
    (
        pieces,
        normed,
        gate,
        up,
        grads,
        inward,
        gate_up,
        rows_out,
        queries,
        pairs,
        other_pairs,
        hidden,
        attended,
        own_sum,
        terms,
        *tables,
        gain,
    ) = forward(
        own_tokens,
        own_cotangent,
        inward_weight,
        gate_up_weight,
        outward_weight,
        down_weight,
        valid,
        shares,
        inward_bias.reshape(1, -1),
        frequency.reshape(1, -1),
    )
    gate_up = gate_up.reshape(width, -1)
    normed = normed.reshape(PIECES * ROWS, width)
    def placed(value):
        value = value.reshape(seqs, group_len, width)
        return jnp.transpose(value, (1, 0, 2)).reshape(tokens.shape)

    outs = backward(
        grads,
        gate,
        up,
        normed,
        pieces,
        queries,
        pairs,
        other_pairs,
        rows_out,
        own_sum,
        terms,
        valid,
    )
    gate_up_grad, *parts, layer_out = outs[10:]
    layer_out, normed = lax.optimization_barrier((placed(layer_out), normed))
    tokens_grad, outward_sum, down_sum, gate_up_rows, inward_rows_own, vectors = finish(
        parts,
        gate_up_grad,
        pieces,
        tables,
        normed,
        outs[6:10],
        grads.reshape(PIECES * ROWS, width),
        hidden,
        attended,
        (inward, gate_up),
        gain,
        own_cotangent,
    )
    gate_up_sum = place_rows(gate_up_rows, 4)
    inward_sum = place_rows(inward_rows_own, 6)

    device = bucket * 2 * DEPTH + blk
    sums = jnp.sum(vectors[:, :4], axis=0).reshape(2, -1, gain_share)
    gain_sum = one_of(sums[0], device, 0)
    shift_sum = one_of(sums[1], device, 0)
    columns_sum = vectors[:, 4, : 3 * HEAD_COLS].reshape(PIECES, 3, 2, 2 * HEAD_DIM)
    columns_sum = jnp.transpose(columns_sum, (1, 2, 0, 3)).reshape(3, -1)
    key_rot = columns_sum[1].reshape(HEADS, HEAD_DIM)[:, :ROT]
    bias_all = jnp.concatenate([columns_sum[0], columns_sum[2], key_rot.reshape(-1)])
    bias_sum = one_of(bias_all.reshape(-1, bias_share), device, 0)

    return (
        layer_out,
        placed(tokens_grad),
        gain_sum,
        shift_sum,
        inward_sum,
        bias_sum,
        outward_sum,
        gate_up_sum,
        down_sum,
    )


def solution(mesh):
    in_specs = (
        P("bucket", "blk", None, None),
        P("bucket", None),
        P(("bucket", "blk")),
        P(("bucket", "blk")),
        P(("bucket", "blk"), None),
        P(("bucket", "blk")),
        P(("bucket", "blk"), None),
        P(("bucket", "blk"), None),
        P(("bucket", "blk"), None),
        P("bucket", "blk", None, None),
    )
    out_specs = (
        P("bucket", "blk", None, None),
        P("bucket", "blk", None, None),
        P(("bucket", "blk")),
        P(("bucket", "blk")),
        P(("bucket", "blk"), None),
        P(("bucket", "blk")),
        P(("bucket", "blk"), None),
        P(("bucket", "blk"), None),
        P(("bucket", "blk"), None),
    )
    body = shards_grouped if fits_groups(mesh) else shards_general
    return jax.shard_map(body, mesh=mesh, in_specs=in_specs, out_specs=out_specs, check_vma=False)
```
